32 devices in a mesh: group: 2 (over y), replica: 8 (over z, x), tensor: 2 (over core).
Axes of the slice: x: 2, y: 2, z: 4, core: 2. Of those that a mesh axis runs over, the one named last changes fastest.
Arguments:
- queries: bfloat16 [4096, 4096], P(('group', 'replica'), 'tensor'), parts along dimension 0, may hold values from -12 to 12
- keys: bfloat16 [4096, 512], P(('group', 'replica'), 'tensor'), parts along dimension 0, may hold values from -6 to 6
- values: bfloat16 [4096, 512], P(('group', 'replica'), 'tensor'), parts along dimension 0, may hold values from -6 to 6
- lengths: int32 [16], P('group'), parts along dimension 0, may hold values from 1 to 8, as said below
- slot_prompt: int32 [16, 2], P('group'), parts along dimension 0, may hold values from 0 to 7, as said below
- slot_span: int32 [16, 2], P('group'), parts along dimension 0, may hold values from 0 to 7
Outputs:
- attention: bfloat16 [16384, 4096], P(('group', 'replica'), 'tensor'), parts along dimension 0
- cache_keys: bfloat16 [16384, 512], P(('group', 'replica'), 'tensor'), parts along dimension 0
- cache_values: bfloat16 [16384, 512], P(('group', 'replica'), 'tensor'), parts along dimension 0
The draws below stay inside these ranges and needn't reach their ends.
There are 2 independent parts, one for each index of `group`. The reference program is written for one: setup_inputs(seed, part) draws one part's arguments, and reference() takes and returns one part's arrays. A program takes and returns all parts, laid end to end along the dimension named above; each array names one. Nothing has to cross between parts.
Inputs may be any that keep to these rules, and one draw needn't show every extreme that they name: The lengths sum to 16, and some prompt has exactly 8 spans. Every slot holds one span: each pair of a prompt p and a span m < lengths[p] is named by exactly one slot through slot_prompt and slot_span, and no other pair is named. Span m < min(lengths[p], 2) of prompt p sits in slot m of replica p.
All inputs are finite; a program needn't handle non-finite values.
Results may differ from the reference program's by a relative error of at most 0.0047.
Values may be sent and summed in bfloat16 or wider, within the bound.
No kernel may reach another device: no remote copies, remote signals or barrier semaphores. Data moves between devices by JAX's collectives and lax.ppermute only.
A program may use at most 128 MiB of HBM per device.

```python
import math
import jax
import jax.numpy as jnp
from jax import lax

HDIM = 128
QHEADS = 32
KVHEADS = 4
SPAN = 128
SLOTS = 2
MAXC = 8
ROWS = 2048
QWIDTH = 4096
KWIDTH = 512
N_REPLICA = 8


def placement(key):
    spare = MAXC - 1
    extra = N_REPLICA * SLOTS - N_REPLICA - spare
    key_top, key_units, key_order = jax.random.split(key, 3)
    longest = jax.random.randint(key_top, (), 0, N_REPLICA).astype(jnp.int32)
    units = jax.random.permutation(key_units, (N_REPLICA - 2) * spare)[:extra].astype(jnp.int32)
    owners = (longest + 2 + units // spare) % N_REPLICA
    replica_ids = jnp.arange(N_REPLICA, dtype=jnp.int32)
    extras = jnp.sum((owners[:, None] == replica_ids[None, :]).astype(jnp.int32), axis=0)
    lengths = 1 + extras + jnp.where(replica_ids == longest, spare, 0)
    span_ids = jnp.arange(MAXC, dtype=jnp.int32)
    slot_ids = jnp.arange(SLOTS, dtype=jnp.int32)
    overflow = (span_ids[None, :] >= SLOTS) & (span_ids[None, :] < lengths[:, None])
    overflow_flat = overflow.reshape(-1)
    overflow_rank = jnp.cumsum(overflow_flat.astype(jnp.int32)) - 1
    order = jax.random.permutation(key_order, N_REPLICA).astype(jnp.int32)
    vacant = slot_ids[None, :] >= lengths[:, None]
    vacant_order = vacant[order]
    rank_order = (jnp.cumsum(vacant_order.reshape(-1).astype(jnp.int32)) - 1).reshape(N_REPLICA, SLOTS)
    inverse = jnp.argsort(order)
    vacant_rank = rank_order[inverse].reshape(-1)
    vacant_flat = vacant.reshape(-1)
    paired = (overflow_rank[None, :] == vacant_rank[:, None]) & overflow_flat[None, :] & vacant_flat[:, None]
    flat_prompt_ids = jnp.repeat(replica_ids, MAXC)
    flat_span_ids = jnp.tile(span_ids, N_REPLICA)
    moved_prompt = jnp.sum(jnp.where(paired, flat_prompt_ids[None, :], 0), axis=1).reshape(N_REPLICA, SLOTS)
    moved_span = jnp.sum(jnp.where(paired, flat_span_ids[None, :], 0), axis=1).reshape(N_REPLICA, SLOTS)
    slot_prompt = jnp.where(vacant, moved_prompt, replica_ids[:, None])
    slot_span = jnp.where(vacant, moved_span, slot_ids[None, :])
    return (lengths.astype(jnp.int32), slot_prompt.astype(jnp.int32), slot_span.astype(jnp.int32))


def draw_lengths(key, part):
    shared = placement(key)
    return shared[0]


def draw_slot_prompt(key, part):
    shared = placement(key)
    return shared[1]


def draw_slot_span(key, part):
    shared = placement(key)
    return shared[2]


def draw_keys(key, part):
    key = jax.random.fold_in(key, 11)
    result = jnp.clip(jax.random.normal(key, (ROWS, KWIDTH), jnp.float32), -6.0, 6.0)
    return result.astype(jnp.bfloat16)


def draw_queries(key, part):
    key = jax.random.fold_in(key, 12)
    result = jnp.clip(jax.random.normal(key, (ROWS, QWIDTH), jnp.float32), -6.0, 6.0)
    return result.astype(jnp.bfloat16)


def steps_of(own_key, extent, shards, least, top_value):
    loudness = 1.0
    for axis_at, blocks in shards:
        heights = jax.random.uniform(jax.random.fold_in(jax.random.fold_in(own_key, 6), axis_at), (blocks,), jnp.float32, least / len(shards), top_value / len(shards))
        loudness = loudness * jnp.repeat(jnp.exp(heights), extent[axis_at] // blocks).reshape((-1,) + (1,) * (len(extent) - 1 - axis_at))
    return loudness


def scatter_about(key, dims, width, most, pieces=(), kind=jnp.bfloat16):
    values = width * jax.random.normal(key, dims, jnp.float32)
    if pieces:
        values = values * steps_of(key, dims, pieces, -0.22, 0.18)
    return jnp.clip(values, -most, most).astype(kind)


def setup_inputs(seed: int = 0, part: int = 0) -> dict:
    key_of = jax.random.split(jax.random.key(seed), 7)
    own_keys = jax.random.split(jax.random.fold_in(key_of[6], part), 7)
    return {
        "queries": draw_queries(jax.random.fold_in(jax.random.fold_in(key_of[6], part), 71), part),
        "keys": draw_keys(jax.random.fold_in(jax.random.fold_in(key_of[6], part), 71), part),
        "values": scatter_about(own_keys[2], (ROWS, KWIDTH), 1.0, 6.0, ((0, 8), (1, 2))),
        "lengths": draw_lengths(jax.random.fold_in(jax.random.fold_in(key_of[6], part), 71), part),
        "slot_prompt": draw_slot_prompt(jax.random.fold_in(jax.random.fold_in(key_of[6], part), 71), part),
        "slot_span": draw_slot_span(jax.random.fold_in(jax.random.fold_in(key_of[6], part), 71), part),
    }


def reference(queries, keys, values, lengths, slot_prompt, slot_span):
    replicas = N_REPLICA
    kv_group = QHEADS // KVHEADS
    home_rows = MAXC * SPAN
    slabs_q = queries.reshape(replicas * SLOTS, SPAN, QHEADS * HDIM)
    slabs_k = keys.reshape(replicas * SLOTS, SPAN, KVHEADS * HDIM)
    slabs_v = values.reshape(replicas * SLOTS, SPAN, KVHEADS * HDIM)
    flat_prompt = slot_prompt.reshape(-1).astype(jnp.int32)
    flat_span = slot_span.reshape(-1).astype(jnp.int32)
    slot_ids = jnp.arange(replicas * SLOTS, dtype=jnp.int32)
    span_ids = jnp.arange(MAXC, dtype=jnp.int32)
    positions = jnp.arange(home_rows, dtype=jnp.int32)
    visible = positions[None, :] <= positions[:, None]
    score_scale = 1.0 / math.sqrt(HDIM)

    def one_prompt(prompt):
        matches = (flat_prompt[None, :] == prompt) & (flat_span[None, :] == span_ids[:, None])
        present = jnp.any(matches, axis=1)
        where_slot = lax.optimization_barrier(jnp.sum(jnp.where(matches, slot_ids[None, :], 0), axis=1)).astype(jnp.int32)

        def gather_home(slabs):
            picked = jnp.take(slabs, where_slot, axis=0)
            kept = jnp.where(present[:, None, None], picked, jnp.zeros((), slabs.dtype))
            return kept.reshape(home_rows, slabs.shape[2])
        home_q = gather_home(slabs_q)
        home_k = gather_home(slabs_k)
        home_v = gather_home(slabs_v)
        query_f = home_q.astype(jnp.float32).reshape(home_rows, KVHEADS, kv_group, HDIM)
        key_f = home_k.astype(jnp.float32).reshape(home_rows, KVHEADS, HDIM)
        value_f = home_v.astype(jnp.float32).reshape(home_rows, KVHEADS, HDIM)
        scores = jnp.einsum('qkgd,tkd->kgqt', query_f, key_f) * score_scale
        masked = jnp.where(visible, scores, -jnp.inf)
        row_max = lax.optimization_barrier(jnp.max(masked, axis=-1, keepdims=True))
        shifted = jnp.exp(masked - row_max)
        probability = (shifted / lax.optimization_barrier(jnp.sum(shifted, axis=-1, keepdims=True))).astype(jnp.bfloat16)
        mixed_rows = jnp.einsum('kgqt,tkd->qkgd', probability.astype(jnp.float32), value_f)
        mixed_rows = mixed_rows.reshape(home_rows, QHEADS * HDIM)
        live_rows = positions // SPAN < lengths[prompt]
        attention = jnp.where(live_rows[:, None], mixed_rows, 0.0).astype(jnp.bfloat16)
        return (attention, home_k, home_v)
    attention, cache_keys, cache_values = lax.map(one_prompt, jnp.arange(replicas, dtype=jnp.int32))
    return (attention.reshape(replicas * home_rows, QHEADS * HDIM), cache_keys.reshape(replicas * home_rows, KVHEADS * HDIM), cache_values.reshape(replicas * home_rows, KVHEADS * HDIM))
```

```python
import math

import jax
import jax.numpy as jnp
from jax import lax
from jax.experimental import pallas as pl
from jax.experimental.pallas import tpu as pltpu
from jax.sharding import PartitionSpec as P

HDIM = 128
SPAN = 128
SLOTS = 2
MAXC = 8
STACK = 2
LOG2E = 1.0 / math.log(2.0)


def locate_slots(slot_prompt, slot_span, replicas):
    flat_prompt = slot_prompt.reshape(-1)
    flat_span = slot_span.reshape(-1)
    slot_ids = jnp.arange(flat_prompt.shape[0], dtype=jnp.int32)
    prompt_ids = jnp.arange(replicas, dtype=jnp.int32)
    span_ids = jnp.arange(MAXC, dtype=jnp.int32)
    matches = (flat_prompt[None, None, :] == prompt_ids[:, None, None]) & (
        flat_span[None, None, :] == span_ids[None, :, None]
    )
    present = jnp.any(matches, axis=2)
    slot_index = jnp.sum(jnp.where(matches, slot_ids[None, None, :], 0), axis=2)
    return (present, slot_index)


def attend_span(span, q_ref, k_ref, v_ref, o_ref):
    heads = q_ref.shape[-1] // HDIM
    before = span * SPAN
    scale = LOG2E / math.sqrt(HDIM)
    row = lax.broadcasted_iota(jnp.int32, (STACK * SPAN, SPAN), 0) % SPAN
    column = lax.broadcasted_iota(jnp.int32, (STACK * SPAN, SPAN), 1)
    visible = column <= row
    contract = (((1,), (1,)), ((), ()))

    def some_heads(step, carry):
        columns = [
            pl.ds(pl.multiple_of((step * STACK + h) * HDIM, HDIM), HDIM) for h in range(STACK)
        ]
        q = jnp.concatenate([q_ref[:, c] for c in columns], axis=0)
        edge = lax.dot_general(
            q, k_ref[before : before + SPAN, :], contract, preferred_element_type=jnp.float32
        )
        edge = jnp.where(visible, edge, -jnp.inf)
        top = jnp.max(edge, axis=1, keepdims=True)
        if span:
            full = lax.dot_general(
                q, k_ref[:before, :], contract, preferred_element_type=jnp.float32
            )
            top = jnp.maximum(top, jnp.max(full, axis=1, keepdims=True))
        edge = jnp.exp2((edge - top) * scale)
        total = jnp.sum(edge, axis=1, keepdims=True)
        mixed = jnp.dot(
            edge.astype(jnp.bfloat16),
            v_ref[before : before + SPAN, :],
            preferred_element_type=jnp.float32,
        )
        if span:
            full = jnp.exp2((full - top) * scale)
            total = total + jnp.sum(full, axis=1, keepdims=True)
            mixed = mixed + jnp.dot(
                full.astype(jnp.bfloat16), v_ref[:before, :], preferred_element_type=jnp.float32
            )
        mixed = (mixed * (1.0 / total)).astype(o_ref.dtype)
        for h in range(STACK):
            o_ref[:, columns[h]] = mixed[h * SPAN : (h + 1) * SPAN, :]
        return carry

    lax.fori_loop(0, heads // STACK, some_heads, 0)


def attend_kernel(meta_ref, first_ref, later_ref, k_ref, v_ref, o_ref):
    at = pl.program_id(1)
    live = meta_ref[0]
    for span in range(MAXC):
        q_ref = first_ref if span == 0 else later_ref.at[0]

        @pl.when((at == span) & (span < live))
        def _(span=span, q_ref=q_ref):
            attend_span(span, q_ref, k_ref, v_ref, o_ref)

    @pl.when(at >= live)
    def _():
        o_ref[...] = jnp.zeros_like(o_ref)


def attend(live, source, first, later, cache_keys, cache_values):
    home_rows, key_width = cache_keys.shape
    width = first.shape[1]
    groups = key_width // HDIM
    part = width // groups
    meta = jnp.concatenate([live.reshape(1), source]).astype(jnp.int32)
    return pl.pallas_call(
        attend_kernel,
        out_shape=jax.ShapeDtypeStruct((home_rows, width), first.dtype),
        grid_spec=pltpu.PrefetchScalarGridSpec(
            num_scalar_prefetch=1,
            grid=(groups, MAXC),
            in_specs=[
                pl.BlockSpec((SPAN, part), lambda g, m, meta: (0, g)),
                pl.BlockSpec((1, SPAN, part), lambda g, m, meta: (meta[1 + m], 0, g)),
                pl.BlockSpec((home_rows, HDIM), lambda g, m, meta: (0, g)),
                pl.BlockSpec((home_rows, HDIM), lambda g, m, meta: (0, g)),
            ],
            out_specs=pl.BlockSpec((SPAN, part), lambda g, m, meta: (m, g)),
        ),
        compiler_params=pltpu.CompilerParams(vmem_limit_bytes=48 * 1024 * 1024),
        cost_estimate=pl.CostEstimate(
            flops=4 * width * home_rows * home_rows // 2,
            bytes_accessed=2 * (2 * home_rows * width + 2 * home_rows * key_width),
            transcendentals=width // HDIM * home_rows * home_rows // 2,
        ),
    )(meta, first, later, cache_keys, cache_values)


def per_device(queries, keys, values, lengths, slot_prompt, slot_span):
    replicas = lax.axis_size("replica")
    mine = lax.axis_index("replica")
    query_width = queries.shape[1]
    key_width = keys.shape[1]
    home_rows = MAXC * SPAN
    present, slot_index = locate_slots(slot_prompt, slot_span, replicas)
    live = lengths[mine]
    here = present[mine]
    source = jnp.where(here, slot_index[mine] // SLOTS, 0)
    last = jnp.max(jnp.where(jnp.arange(MAXC) < live, jnp.arange(MAXC), 0))
    source = jnp.where(jnp.arange(MAXC) < live, source, source[last])
    slots_k = lax.all_gather(keys[SPAN:], "replica")
    slots_v = lax.all_gather(values[SPAN:], "replica")
    slots_q = lax.all_gather(queries[SPAN:], "replica")

    def in_order(first, slots):
        picked = jnp.take(slots, source, axis=0)
        kept = jnp.where(here[:, None, None], picked, jnp.zeros((), slots.dtype))
        return jnp.concatenate([first, kept[1:].reshape(home_rows - SPAN, key_width)], axis=0)

    cache_keys = in_order(keys[:SPAN], slots_k)
    cache_values = in_order(values[:SPAN], slots_v)
    attention = attend(live, source, queries[:SPAN], slots_q, cache_keys, cache_values)
    return (attention, cache_keys, cache_values)


def solution(mesh):
    in_specs = (
        P(("group", "replica"), "tensor"),
        P(("group", "replica"), "tensor"),
        P(("group", "replica"), "tensor"),
        P("group"),
        P("group", None),
        P("group", None),
    )
    out_specs = (
        P(("group", "replica"), "tensor"),
        P(("group", "replica"), "tensor"),
        P(("group", "replica"), "tensor"),
    )
    return jax.shard_map(
        per_device, mesh=mesh, in_specs=in_specs, out_specs=out_specs, check_vma=False
    )
```

```python
import math

import jax
import jax.numpy as jnp
from jax import lax
from jax.experimental import pallas as pl
from jax.experimental.pallas import tpu as pltpu
from jax.sharding import PartitionSpec as P

HDIM = 128
SPAN = 128
SLOTS = 2
MAXC = 8
STACK = 2
LOG2E = 1.0 / math.log(2.0)
VMEM_BYTES = 48 * 1024 * 1024
ANY = pl.BlockSpec(memory_space=pl.ANY)
SMEM = pl.BlockSpec(memory_space=pltpu.SMEM)
VMEM = pl.BlockSpec(memory_space=pltpu.VMEM)


def attend_span(span, q_ref, k_ref, v_ref, o_ref):
    width = q_ref.shape[-1]
    group = width // k_ref.shape[-1]
    before = span * SPAN
    scale = LOG2E / math.sqrt(HDIM)
    row = lax.broadcasted_iota(jnp.int32, (STACK * SPAN, SPAN), 0) % SPAN
    column = lax.broadcasted_iota(jnp.int32, (STACK * SPAN, SPAN), 1)
    visible = column <= row
    contract = (((1,), (1,)), ((), ()))

    def some_heads(step, carry):
        columns = [
            pl.ds(pl.multiple_of((step * STACK + h) * HDIM, HDIM), HDIM) for h in range(STACK)
        ]
        shared = pl.ds(pl.multiple_of(step * STACK // group * HDIM, HDIM), HDIM)
        q = jnp.concatenate([q_ref[:, c] for c in columns], axis=0)
        edge = lax.dot_general(
            q,
            k_ref[before : before + SPAN, shared],
            contract,
            preferred_element_type=jnp.float32,
        )
        edge = jnp.where(visible, edge, -jnp.inf)
        top = jnp.max(edge, axis=1, keepdims=True)
        if span:
            full = lax.dot_general(
                q, k_ref[:before, shared], contract, preferred_element_type=jnp.float32
            )
            top = jnp.maximum(top, jnp.max(full, axis=1, keepdims=True))
        edge = jnp.exp2((edge - top) * scale)
        total = jnp.sum(edge, axis=1, keepdims=True)
        mixed = jnp.dot(
            edge.astype(jnp.bfloat16),
            v_ref[before : before + SPAN, shared],
            preferred_element_type=jnp.float32,
        )
        if span:
            full = jnp.exp2((full - top) * scale)
            total = total + jnp.sum(full, axis=1, keepdims=True)
            mixed = mixed + jnp.dot(
                full.astype(jnp.bfloat16),
                v_ref[:before, shared],
                preferred_element_type=jnp.float32,
            )
        mixed = (mixed * (1.0 / total)).astype(o_ref.dtype)
        for h in range(STACK):
            o_ref[:, columns[h]] = mixed[h * SPAN : (h + 1) * SPAN, :]
        return carry

    lax.fori_loop(0, width // (STACK * HDIM), some_heads, 0)


def rows_of(span):
    return pl.ds(pl.multiple_of(span * SPAN, SPAN), SPAN)


def local_kernel(live_ref, q_ref, k_ref, v_ref, o_ref, mixed, zeros, sems):
    live = live_ref[0]
    zeros[...] = jnp.zeros_like(zeros)
    for span in range(1, MAXC):

        @pl.when(span >= live)
        def _(span=span):
            pltpu.make_async_copy(zeros, o_ref.at[rows_of(span)], sems.at[span]).start()

    attend_span(0, q_ref.at[:SPAN], k_ref, v_ref, mixed.at[0])
    first = pltpu.make_async_copy(mixed.at[0], o_ref.at[rows_of(0)], sems.at[0])
    first.start()

    @pl.when(live > 1)
    def _():
        attend_span(1, q_ref.at[SPAN:], k_ref, v_ref, mixed.at[1])
        second = pltpu.make_async_copy(mixed.at[1], o_ref.at[rows_of(1)], sems.at[MAXC])
        second.start()
        second.wait()

    first.wait()
    for span in range(1, MAXC):

        @pl.when(span >= live)
        def _(span=span):
            pltpu.make_async_copy(zeros, o_ref.at[rows_of(span)], sems.at[span]).wait()


def attend_local(live, queries, keys, values):
    width = queries.shape[1]
    return pl.pallas_call(
        local_kernel,
        out_shape=jax.ShapeDtypeStruct((MAXC * SPAN, width), queries.dtype),
        in_specs=[SMEM, VMEM, VMEM, VMEM],
        out_specs=ANY,
        scratch_shapes=[
            pltpu.VMEM((SLOTS, SPAN, width), queries.dtype),
            pltpu.VMEM((SPAN, width), queries.dtype),
            pltpu.SemaphoreType.DMA((MAXC + 1,)),
        ],
        compiler_params=pltpu.CompilerParams(vmem_limit_bytes=VMEM_BYTES),
        cost_estimate=pl.CostEstimate(
            flops=12 * SPAN * SPAN * width, bytes_accessed=12 * SPAN * width, transcendentals=0
        ),
    )(live.reshape(1), queries, keys, values)


def arrived_kernel(count, dest_ref, *refs):
    q_refs, (k_hbm, v_hbm, _, o_ref, k_ref, v_ref, q_buf, mixed, sems) = refs[:count], refs[count:]
    wanted = dest_ref[0] >= 0
    for j in range(1, count):
        wanted |= dest_ref[j] >= 0

    @pl.when(wanted)
    def _():
        copy_k = pltpu.make_async_copy(k_hbm, k_ref, sems.at[2 * count])
        copy_v = pltpu.make_async_copy(v_hbm, v_ref, sems.at[2 * count + 1])
        copy_k.start()
        copy_v.start()
        for j in range(count):

            @pl.when(dest_ref[j] >= 0)
            def _(j=j):
                pltpu.make_async_copy(q_refs[j], q_buf.at[j], sems.at[j]).start()

        copy_k.wait()
        copy_v.wait()

        def one(j, carry):
            dest = dest_ref[j]

            @pl.when(dest >= 0)
            def _():
                pltpu.make_async_copy(q_buf.at[j], q_buf.at[j], sems.at[j]).wait()
                for span in range(1, MAXC):

                    @pl.when(dest == span)
                    def _(span=span):
                        attend_span(span, q_buf.at[j], k_ref, v_ref, mixed.at[j])

                pltpu.make_async_copy(
                    mixed.at[j], o_ref.at[rows_of(dest)], sems.at[count + j]
                ).start()

            return carry

        lax.fori_loop(0, count, one, 0)
        for j in range(count):

            @pl.when(dest_ref[j] >= 0)
            def _(j=j):
                pltpu.make_async_copy(
                    mixed.at[j], o_ref.at[rows_of(dest_ref[j])], sems.at[count + j]
                ).wait()


def attend_arrived(dest, blocks, cache_keys, cache_values, attention):
    count = len(blocks)
    width = attention.shape[1]
    return pl.pallas_call(
        lambda *refs: arrived_kernel(count, *refs),
        out_shape=jax.ShapeDtypeStruct(attention.shape, attention.dtype),
        in_specs=[SMEM] + [ANY] * (count + 3),
        out_specs=ANY,
        input_output_aliases={count + 3: 0},
        scratch_shapes=[
            pltpu.VMEM(cache_keys.shape, cache_keys.dtype),
            pltpu.VMEM(cache_values.shape, cache_values.dtype),
            pltpu.VMEM((count, SPAN, width), attention.dtype),
            pltpu.VMEM((count, SPAN, width), attention.dtype),
            pltpu.SemaphoreType.DMA((2 * count + 2,)),
        ],
        compiler_params=pltpu.CompilerParams(vmem_limit_bytes=VMEM_BYTES),
        cost_estimate=pl.CostEstimate(
            flops=16 * SPAN * SPAN * width * count,
            bytes_accessed=4 * SPAN * width * count,
            transcendentals=0,
        ),
    )(dest, *blocks, cache_keys, cache_values, attention)


def order_kernel(count, dest_ref, live_ref, own_k, own_v, *refs):
    blocks, (o_k, o_v, zeros, sems) = refs[:count], refs[count:]
    live = live_ref[0]
    zeros[...] = jnp.zeros_like(zeros)

    def copies():
        yield None, own_k.at[:SPAN], o_k.at[rows_of(0)]
        yield None, own_v.at[:SPAN], o_v.at[rows_of(0)]
        yield live > 1, own_k.at[SPAN:], o_k.at[rows_of(1)]
        yield live > 1, own_v.at[SPAN:], o_v.at[rows_of(1)]
        for span in range(1, MAXC):
            yield span >= live, zeros, o_k.at[rows_of(span)]
            yield span >= live, zeros, o_v.at[rows_of(span)]
        for j in range(count):
            dest = dest_ref[j]
            yield dest >= 0, blocks[j].at[:SPAN], o_k.at[rows_of(jnp.maximum(dest, 0))]
            yield dest >= 0, blocks[j].at[SPAN:], o_v.at[rows_of(jnp.maximum(dest, 0))]

    for act in ("start", "wait"):
        for n, (needed, here, there) in enumerate(copies()):
            copy = pltpu.make_async_copy(here, there, sems.at[n])
            if needed is None:
                getattr(copy, act)()
            else:
                pl.when(needed)(getattr(copy, act))


def put_in_order(dest, live, keys, values, blocks):
    count = len(blocks)
    shape = jax.ShapeDtypeStruct((MAXC * SPAN, keys.shape[1]), keys.dtype)
    return pl.pallas_call(
        lambda *refs: order_kernel(count, *refs),
        out_shape=(shape, shape),
        in_specs=[SMEM, SMEM] + [ANY] * (count + 2),
        out_specs=(ANY, ANY),
        scratch_shapes=[
            pltpu.VMEM((SPAN, keys.shape[1]), keys.dtype),
            pltpu.SemaphoreType.DMA((4 + 2 * (MAXC - 1) + 2 * count,)),
        ],
        compiler_params=pltpu.CompilerParams(vmem_limit_bytes=VMEM_BYTES),
        cost_estimate=pl.CostEstimate(
            flops=0, bytes_accessed=8 * MAXC * SPAN * keys.shape[1], transcendentals=0
        ),
    )(dest, live.reshape(1), keys, values, *blocks)


def gathered_kernel(meta_ref, first_ref, later_ref, k_ref, v_ref, o_ref):
    at = pl.program_id(1)
    live = meta_ref[0]
    for span in range(MAXC):
        q_ref = first_ref if span == 0 else later_ref.at[0]

        @pl.when((at == span) & (span < live))
        def _(span=span, q_ref=q_ref):
            attend_span(span, q_ref, k_ref, v_ref, o_ref)

    @pl.when(at >= live)
    def _():
        o_ref[...] = jnp.zeros_like(o_ref)


def attend_gathered(live, source, first, later, cache_keys, cache_values):
    home_rows, key_width = cache_keys.shape
    width = first.shape[1]
    groups = key_width // HDIM
    part = width // groups
    meta = jnp.concatenate([live.reshape(1), source]).astype(jnp.int32)
    return pl.pallas_call(
        gathered_kernel,
        out_shape=jax.ShapeDtypeStruct((home_rows, width), first.dtype),
        grid_spec=pltpu.PrefetchScalarGridSpec(
            num_scalar_prefetch=1,
            grid=(groups, MAXC),
            in_specs=[
                pl.BlockSpec((SPAN, part), lambda g, m, meta: (0, g)),
                pl.BlockSpec((1, SPAN, part), lambda g, m, meta: (meta[1 + m], 0, g)),
                pl.BlockSpec((home_rows, HDIM), lambda g, m, meta: (0, g)),
                pl.BlockSpec((home_rows, HDIM), lambda g, m, meta: (0, g)),
            ],
            out_specs=pl.BlockSpec((SPAN, part), lambda g, m, meta: (m, g)),
        ),
        compiler_params=pltpu.CompilerParams(vmem_limit_bytes=VMEM_BYTES),
    )(meta, first, later, cache_keys, cache_values)


def gather_all(queries, keys, values, lengths, slot_prompt, slot_span):
    mine = lax.axis_index("replica")
    home_rows, key_width = MAXC * SPAN, keys.shape[1]
    live = lengths[mine]
    spans = jnp.arange(MAXC, dtype=jnp.int32)
    matches = (slot_prompt[None, :, 1] == mine) & (slot_span[None, :, 1] == spans[:, None])
    here = jnp.any(matches, axis=1)
    source = jnp.argmax(matches, axis=1).astype(jnp.int32)
    slots_k = lax.all_gather(keys[SPAN:], "replica")
    slots_v = lax.all_gather(values[SPAN:], "replica")
    slots_q = lax.all_gather(queries[SPAN:], "replica")

    def in_order(first, slots):
        picked = jnp.take(slots, source, axis=0)
        kept = jnp.where(here[:, None, None], picked, jnp.zeros((), slots.dtype))
        return jnp.concatenate([first, kept[1:].reshape(home_rows - SPAN, key_width)], axis=0)

    cache_keys = in_order(keys[:SPAN], slots_k)
    cache_values = in_order(values[:SPAN], slots_v)
    attention = attend_gathered(live, source, queries[:SPAN], slots_q, cache_keys, cache_values)
    return (attention, cache_keys, cache_values)


def per_device(queries, keys, values, lengths, slot_prompt, slot_span):
    replicas = lax.axis_size("replica")
    if replicas != 8:
        return gather_all(queries, keys, values, lengths, slot_prompt, slot_span)
    mine = lax.axis_index("replica")
    live = lengths[mine]
    dest = jnp.where(slot_prompt[:, 1] == mine, slot_span[:, 1], -1)
    depth = replicas // 2
    z = mine // 2

    def along_z(block, step):
        pairs = [
            (a, a + 2 * step) for a in range(replicas) if 0 <= a + 2 * step < replicas
        ]
        return lax.ppermute(block, "replica", pairs)

    def along_x(block):
        return lax.ppermute(block, "replica", [(a, a ^ 1) for a in range(replicas)])

    def chain(block, step):
        found = []
        for _ in range(depth - 1):
            block = along_z(block, step)
            found.append(block)
        return found

    def dest_of(dx, dz):
        at = z + dz
        other = jnp.clip(2 * at + jnp.where(dx, (mine % 2) ^ 1, mine % 2), 0, replicas - 1)
        return jnp.where((at >= 0) & (at < depth), dest[other], -1)

    own_kv = jnp.concatenate([keys[SPAN:], values[SPAN:]], axis=0)
    own_q = queries[SPAN:]
    kv, kv_dest = [], []
    side_kv = along_x(own_kv)
    kv.append(side_kv)
    kv_dest.append(dest_of(1, 0))
    for dx, block in ((0, own_kv), (1, side_kv)):
        for step in (1, -1):
            kv += chain(block, step)
            kv_dest += [dest_of(dx, -step * (n + 1)) for n in range(depth - 1)]
    cache_keys, cache_values = put_in_order(jnp.stack(kv_dest), live, keys, values, kv)

    attention = attend_local(live, queries, keys, values)
    up, down = chain(own_q, 1), chain(own_q, -1)
    send = [
        own_q,
        jnp.where(z == 0, down[0], up[0]),
        jnp.where(z == 0, down[1], jnp.where(z == depth - 1, up[1], down[0])),
        jnp.where(z == 0, down[2], jnp.where(z == depth - 1, up[2], jnp.where(z == 1, down[1], up[1]))),
    ]
    offset = [
        jnp.zeros((), jnp.int32),
        jnp.where(z == 0, 1, -1),
        jnp.where(z == 0, 2, jnp.where(z == depth - 1, -2, 1)),
        jnp.where(z == 0, 3, jnp.where(z == depth - 1, -3, jnp.where(z == 1, 2, -2))),
    ]
    side = [along_x(block) for block in send]
    stages = [
        [(up[0], dest_of(0, -1)), (down[0], dest_of(0, 1)), (side[0], dest_of(1, 0))],
        [(up[1], dest_of(0, -2)), (down[1], dest_of(0, 2)), (side[1], dest_of(1, offset[1]))],
        [(up[2], dest_of(0, -3)), (down[2], dest_of(0, 3)), (side[2], dest_of(1, offset[2]))],
        [(side[3], dest_of(1, offset[3]))],
    ]
    for stage in stages:
        blocks, places = zip(*stage)
        attention = attend_arrived(
            jnp.stack(places), blocks, cache_keys, cache_values, attention
        )
    return (attention, cache_keys, cache_values)


def solution(mesh):
    in_specs = (
        P(("group", "replica"), "tensor"),
        P(("group", "replica"), "tensor"),
        P(("group", "replica"), "tensor"),
        P("group"),
        P("group", None),
        P("group", None),
    )
    out_specs = (
        P(("group", "replica"), "tensor"),
        P(("group", "replica"), "tensor"),
        P(("group", "replica"), "tensor"),
    )
    return jax.shard_map(
        per_device, mesh=mesh, in_specs=in_specs, out_specs=out_specs, check_vma=False
    )
```

```python
import math

import jax
import jax.numpy as jnp
from jax import lax
from jax.experimental import pallas as pl
from jax.experimental.pallas import tpu as pltpu
from jax.sharding import PartitionSpec as P

HDIM = 128
SPAN = 128
SLOTS = 2
MAXC = 8
STACK = 2
CHAINS = 2
LOG2E = 1.0 / math.log(2.0)
VMEM_BYTES = 48 * 1024 * 1024
ANY = pl.BlockSpec(memory_space=pl.ANY)
SMEM = pl.BlockSpec(memory_space=pltpu.SMEM)
VMEM = pl.BlockSpec(memory_space=pltpu.VMEM)


def widen(v_ref, wide_ref):
    for at in range(0, v_ref.shape[-1], HDIM):
        wide_ref[:, 2 * at : 2 * at + HDIM] = v_ref[:, at : at + HDIM]
        wide_ref[:, 2 * at + HDIM : 2 * at + 2 * HDIM] = jnp.ones(
            (v_ref.shape[0], HDIM), v_ref.dtype
        )


def attend_span(span, q_ref, k_ref, wide_ref, o_ref):
    width = q_ref.shape[-1]
    group = width // k_ref.shape[-1]
    before = span * SPAN
    seen = before + SPAN
    scale = LOG2E / math.sqrt(HDIM)
    row = lax.broadcasted_iota(jnp.int32, (STACK * SPAN, SPAN), 0) % SPAN
    column = lax.broadcasted_iota(jnp.int32, (STACK * SPAN, SPAN), 1)
    visible = column <= row

    def stack(first):
        columns = [pl.ds(pl.multiple_of((first + h) * HDIM, HDIM), HDIM) for h in range(STACK)]
        shared = first // group
        q = jnp.concatenate([q_ref[:, c] for c in columns], axis=0)
        k = k_ref[:seen, pl.ds(pl.multiple_of(shared * HDIM, HDIM), HDIM)]
        wide = wide_ref[:seen, pl.ds(pl.multiple_of(shared * 2 * HDIM, HDIM), 2 * HDIM)]
        scores = lax.dot_general(
            q, k, (((1,), (1,)), ((), ())), preferred_element_type=jnp.float32
        )
        edge = jnp.where(visible, scores[:, before:], -jnp.inf)
        if span:
            scores = jnp.concatenate([scores[:, :before], edge], axis=1)
        else:
            scores = edge
        top = jnp.max(scores, axis=1, keepdims=True)
        weights = jnp.exp2((scores - top) * scale).astype(jnp.bfloat16)
        mixed = jnp.dot(weights, wide, preferred_element_type=jnp.float32)
        mixed = (mixed[:, :HDIM] / mixed[:, HDIM:]).astype(o_ref.dtype)
        for h in range(STACK):
            o_ref[:, columns[h]] = mixed[h * SPAN : (h + 1) * SPAN, :]

    def some_heads(step, carry):
        for n in range(CHAINS):
            stack((step * CHAINS + n) * STACK)
        return carry

    lax.fori_loop(0, width // (CHAINS * STACK * HDIM), some_heads, 0)


def rows_of(span):
    return pl.ds(pl.multiple_of(span * SPAN, SPAN), SPAN)


def local_kernel(live_ref, q_ref, k_ref, v_ref, o_ref, wide, mixed, zeros, sems):
    live = live_ref[0]
    zeros[...] = jnp.zeros_like(zeros)
    for span in range(1, MAXC):

        @pl.when(span >= live)
        def _(span=span):
            pltpu.make_async_copy(zeros, o_ref.at[rows_of(span)], sems.at[span]).start()

    widen(v_ref, wide)
    attend_span(0, q_ref.at[:SPAN], k_ref, wide, mixed.at[0])
    first = pltpu.make_async_copy(mixed.at[0], o_ref.at[rows_of(0)], sems.at[0])
    first.start()

    @pl.when(live > 1)
    def _():
        attend_span(1, q_ref.at[SPAN:], k_ref, wide, mixed.at[1])
        second = pltpu.make_async_copy(mixed.at[1], o_ref.at[rows_of(1)], sems.at[MAXC])
        second.start()
        second.wait()

    first.wait()
    for span in range(1, MAXC):

        @pl.when(span >= live)
        def _(span=span):
            pltpu.make_async_copy(zeros, o_ref.at[rows_of(span)], sems.at[span]).wait()


def attend_local(live, queries, keys, values):
    width = queries.shape[1]
    return pl.pallas_call(
        local_kernel,
        out_shape=jax.ShapeDtypeStruct((MAXC * SPAN, width), queries.dtype),
        in_specs=[SMEM, VMEM, VMEM, VMEM],
        out_specs=ANY,
        scratch_shapes=[
            pltpu.VMEM((SLOTS * SPAN, 2 * keys.shape[1]), keys.dtype),
            pltpu.VMEM((SLOTS, SPAN, width), queries.dtype),
            pltpu.VMEM((SPAN, width), queries.dtype),
            pltpu.SemaphoreType.DMA((MAXC + 1,)),
        ],
        compiler_params=pltpu.CompilerParams(vmem_limit_bytes=VMEM_BYTES),
        cost_estimate=pl.CostEstimate(
            flops=12 * SPAN * SPAN * width, bytes_accessed=12 * SPAN * width, transcendentals=0
        ),
    )(live.reshape(1), queries, keys, values)


def arrived_kernel(pieces, dest_ref, *refs):
    count, parts = len(pieces), sum(pieces)
    q_refs, (k_hbm, v_hbm, _, o_ref, k_ref, v_ref, wide, q_buf, mixed, sems) = (
        refs[:parts],
        refs[parts:],
    )
    wanted = dest_ref[0] >= 0
    for j in range(1, count):
        wanted |= dest_ref[j] >= 0

    @pl.when(wanted)
    def _():
        copy_k = pltpu.make_async_copy(k_hbm, k_ref, sems.at[2 * count])
        copy_v = pltpu.make_async_copy(v_hbm, v_ref, sems.at[2 * count + 1])
        copy_k.start()
        copy_v.start()
        for j in range(count):

            @pl.when(dest_ref[j] >= 0)
            def _(j=j):
                rows = SPAN // pieces[j]
                for n in range(pieces[j]):
                    pltpu.make_async_copy(
                        q_refs[sum(pieces[:j]) + n],
                        q_buf.at[j, n * rows : (n + 1) * rows],
                        sems.at[j],
                    ).start()

        copy_k.wait()
        copy_v.wait()
        widen(v_ref, wide)

        def one(j, carry):
            dest = dest_ref[j]

            @pl.when(dest >= 0)
            def _():
                pltpu.make_async_copy(q_buf.at[j], q_buf.at[j], sems.at[j]).wait()
                for span in range(1, MAXC):

                    @pl.when(dest == span)
                    def _(span=span):
                        attend_span(span, q_buf.at[j], k_ref, wide, mixed.at[j])

                pltpu.make_async_copy(
                    mixed.at[j], o_ref.at[rows_of(dest)], sems.at[count + j]
                ).start()

            return carry

        lax.fori_loop(0, count, one, 0)
        for j in range(count):

            @pl.when(dest_ref[j] >= 0)
            def _(j=j):
                pltpu.make_async_copy(
                    mixed.at[j], o_ref.at[rows_of(dest_ref[j])], sems.at[count + j]
                ).wait()


def attend_arrived(dest, blocks, cache_keys, cache_values, attention):
    pieces = [len(block) for block in blocks]
    count, parts = len(pieces), sum(pieces)
    width = attention.shape[1]
    return pl.pallas_call(
        lambda *refs: arrived_kernel(pieces, *refs),
        out_shape=jax.ShapeDtypeStruct(attention.shape, attention.dtype),
        in_specs=[SMEM] + [ANY] * (parts + 3),
        out_specs=ANY,
        input_output_aliases={parts + 3: 0},
        scratch_shapes=[
            pltpu.VMEM(cache_keys.shape, cache_keys.dtype),
            pltpu.VMEM(cache_values.shape, cache_values.dtype),
            pltpu.VMEM((cache_keys.shape[0], 2 * cache_keys.shape[1]), cache_keys.dtype),
            pltpu.VMEM((count, SPAN, width), attention.dtype),
            pltpu.VMEM((count, SPAN, width), attention.dtype),
            pltpu.SemaphoreType.DMA((2 * count + 2,)),
        ],
        compiler_params=pltpu.CompilerParams(vmem_limit_bytes=VMEM_BYTES),
        cost_estimate=pl.CostEstimate(
            flops=16 * SPAN * SPAN * width * count,
            bytes_accessed=4 * SPAN * width * count,
            transcendentals=0,
        ),
    )(dest, *[part for block in blocks for part in block], cache_keys, cache_values, attention)


def order_kernel(dest_ref, live_ref, own_k, own_v, slots, o_k, o_v, k_buf, v_buf, in_sems, out_sems):
    live = live_ref[0]

    def fetches():
        yield None, own_k.at[:SPAN], k_buf.at[rows_of(0)]
        yield None, own_v.at[:SPAN], v_buf.at[rows_of(0)]
        for j in range(slots.shape[0]):
            there = rows_of(jnp.maximum(dest_ref[j], 0))
            yield dest_ref[j] >= 0, slots.at[j, :SPAN], k_buf.at[there]
            yield dest_ref[j] >= 0, slots.at[j, SPAN:], v_buf.at[there]

    for span in range(1, MAXC):

        @pl.when(span >= live)
        def _(span=span):
            k_buf[rows_of(span), :] = jnp.zeros((SPAN, k_buf.shape[1]), k_buf.dtype)
            v_buf[rows_of(span), :] = jnp.zeros((SPAN, v_buf.shape[1]), v_buf.dtype)

    for act in ("start", "wait"):
        for n, (needed, here, there) in enumerate(fetches()):
            copy = pltpu.make_async_copy(here, there, in_sems.at[n])
            if needed is None:
                getattr(copy, act)()
            else:
                pl.when(needed)(getattr(copy, act))
    copy_k = pltpu.make_async_copy(k_buf, o_k, out_sems.at[0])
    copy_v = pltpu.make_async_copy(v_buf, o_v, out_sems.at[1])
    copy_k.start()
    copy_v.start()
    copy_k.wait()
    copy_v.wait()


def put_in_order(dest, live, keys, values, slots):
    shape = (MAXC * SPAN, keys.shape[1])
    out = jax.ShapeDtypeStruct(shape, keys.dtype)
    return pl.pallas_call(
        order_kernel,
        out_shape=(out, out),
        in_specs=[SMEM, SMEM] + [ANY] * 3,
        out_specs=(ANY, ANY),
        scratch_shapes=[
            pltpu.VMEM(shape, keys.dtype),
            pltpu.VMEM(shape, keys.dtype),
            pltpu.SemaphoreType.DMA((2 + 2 * slots.shape[0],)),
            pltpu.SemaphoreType.DMA((2,)),
        ],
        compiler_params=pltpu.CompilerParams(vmem_limit_bytes=VMEM_BYTES),
        cost_estimate=pl.CostEstimate(
            flops=0, bytes_accessed=8 * MAXC * SPAN * keys.shape[1], transcendentals=0
        ),
    )(dest, live.reshape(1), keys, values, slots)


def gathered_kernel(meta_ref, first_ref, later_ref, k_ref, v_ref, o_ref, wide):
    at = pl.program_id(1)
    live = meta_ref[0]
    widen(v_ref, wide)
    for span in range(MAXC):
        q_ref = first_ref if span == 0 else later_ref.at[0]

        @pl.when((at == span) & (span < live))
        def _(span=span, q_ref=q_ref):
            attend_span(span, q_ref, k_ref, wide, o_ref)

    @pl.when(at >= live)
    def _():
        o_ref[...] = jnp.zeros_like(o_ref)


def attend_gathered(live, source, first, later, cache_keys, cache_values):
    home_rows, key_width = cache_keys.shape
    width = first.shape[1]
    groups = key_width // HDIM
    part = width // groups
    meta = jnp.concatenate([live.reshape(1), source]).astype(jnp.int32)
    return pl.pallas_call(
        gathered_kernel,
        out_shape=jax.ShapeDtypeStruct((home_rows, width), first.dtype),
        grid_spec=pltpu.PrefetchScalarGridSpec(
            num_scalar_prefetch=1,
            grid=(groups, MAXC),
            in_specs=[
                pl.BlockSpec((SPAN, part), lambda g, m, meta: (0, g)),
                pl.BlockSpec((1, SPAN, part), lambda g, m, meta: (meta[1 + m], 0, g)),
                pl.BlockSpec((home_rows, HDIM), lambda g, m, meta: (0, g)),
                pl.BlockSpec((home_rows, HDIM), lambda g, m, meta: (0, g)),
            ],
            out_specs=pl.BlockSpec((SPAN, part), lambda g, m, meta: (m, g)),
            scratch_shapes=[pltpu.VMEM((home_rows, 2 * HDIM), cache_keys.dtype)],
        ),
        compiler_params=pltpu.CompilerParams(vmem_limit_bytes=VMEM_BYTES),
    )(meta, first, later, cache_keys, cache_values)


def gather_all(queries, keys, values, lengths, slot_prompt, slot_span):
    mine = lax.axis_index("replica")
    home_rows, key_width = MAXC * SPAN, keys.shape[1]
    live = lengths[mine]
    spans = jnp.arange(MAXC, dtype=jnp.int32)
    matches = (slot_prompt[None, :, 1] == mine) & (slot_span[None, :, 1] == spans[:, None])
    here = jnp.any(matches, axis=1)
    source = jnp.argmax(matches, axis=1).astype(jnp.int32)
    slots_k = lax.all_gather(keys[SPAN:], "replica")
    slots_v = lax.all_gather(values[SPAN:], "replica")
    slots_q = lax.all_gather(queries[SPAN:], "replica")

    def in_order(first, slots):
        picked = jnp.take(slots, source, axis=0)
        kept = jnp.where(here[:, None, None], picked, jnp.zeros((), slots.dtype))
        return jnp.concatenate([first, kept[1:].reshape(home_rows - SPAN, key_width)], axis=0)

    cache_keys = in_order(keys[:SPAN], slots_k)
    cache_values = in_order(values[:SPAN], slots_v)
    attention = attend_gathered(live, source, queries[:SPAN], slots_q, cache_keys, cache_values)
    return (attention, cache_keys, cache_values)


def per_device(queries, keys, values, lengths, slot_prompt, slot_span):
    replicas = lax.axis_size("replica")
    if replicas != 8:
        return gather_all(queries, keys, values, lengths, slot_prompt, slot_span)
    mine = lax.axis_index("replica")
    live = lengths[mine]
    dest = jnp.where(slot_prompt[:, 1] == mine, slot_span[:, 1], -1)
    ring = list(range(0, replicas, 2)) + list(range(replicas - 1, 0, -2))
    place = jnp.where(mine % 2 == 0, mine // 2, replicas - 1 - mine // 2)

    def shift(block, step):
        pairs = [(r, ring[(n + step) % replicas]) for n, r in enumerate(ring)]
        return lax.ppermute(block, "replica", pairs)

    def dest_from(step):
        at = (place - step) % replicas
        return dest[jnp.where(at < replicas // 2, 2 * at, 2 * (replicas - at) - 1)]

    own_kv = jnp.concatenate([keys[SPAN:], values[SPAN:]], axis=0)
    own_kv, queries = lax.optimization_barrier((own_kv, queries))
    slots_kv = lax.all_gather(own_kv, "replica")
    own_q = queries[SPAN:]
    ups, downs = [own_q], [own_q]

    def go_on():
        ups.append(shift(ups[-1], 1))
        downs.append(shift(downs[-1], -1))

    def attend(steps, attention):
        blocks = [(block,) for step in steps for block in (ups[step], downs[step])]
        places = [dest_from(way * step) for step in steps for way in (1, -1)]
        return attend_arrived(jnp.stack(places), blocks, cache_keys, cache_values, attention)

    go_on()
    attention = attend_local(live, queries, keys, values)
    ups[1], downs[1], attention = lax.optimization_barrier((ups[1], downs[1], attention))
    go_on()
    cache_keys, cache_values = put_in_order(dest, live, keys, values, slots_kv)
    ups[2], downs[2], cache_keys = lax.optimization_barrier((ups[2], downs[2], cache_keys))
    go_on()
    attention = attend((1, 2), attention)
    up, down, attention = lax.optimization_barrier((ups[3], downs[3], attention))
    half = SPAN // 2
    farthest = (shift(up[:half], 1), shift(down[half:], -1))
    attention = attend((3,), attention)
    attention = attend_arrived(
        dest_from(replicas // 2).reshape(1), [farthest], cache_keys, cache_values, attention
    )
    return (attention, cache_keys, cache_values)


def solution(mesh):
    in_specs = (
        P(("group", "replica"), "tensor"),
        P(("group", "replica"), "tensor"),
        P(("group", "replica"), "tensor"),
        P("group"),
        P("group", None),
        P("group", None),
    )
    out_specs = (
        P(("group", "replica"), "tensor"),
        P(("group", "replica"), "tensor"),
        P(("group", "replica"), "tensor"),
    )
    return jax.shard_map(
        per_device, mesh=mesh, in_specs=in_specs, out_specs=out_specs, check_vma=False
    )
```

```python
import math

import jax
import jax.numpy as jnp
from jax import lax
from jax.experimental import pallas as pl
from jax.experimental.pallas import tpu as pltpu
from jax.sharding import PartitionSpec as P

HDIM = 128
SPAN = 128
SLOTS = 2
MAXC = 8
STACK = 4
CHAINS = 1
LOG2E = 1.0 / math.log(2.0)
VMEM_BYTES = 48 * 1024 * 1024
ANY = pl.BlockSpec(memory_space=pl.ANY)
SMEM = pl.BlockSpec(memory_space=pltpu.SMEM)
VMEM = pl.BlockSpec(memory_space=pltpu.VMEM)


def column_ring(replicas):
    return list(range(0, replicas, 2)) + list(range(replicas - 1, 0, -2))


def pack_kernel(length_ref, prompt_ref, span_ref, q_ref, k_ref, v_ref, o_q, o_kv, meta_ref, sems):
    copies = [
        pltpu.make_async_copy(q_ref.at[SPAN:], o_q, sems.at[0]),
        pltpu.make_async_copy(k_ref.at[SPAN:], o_kv.at[:SPAN], sems.at[1]),
        pltpu.make_async_copy(v_ref.at[SPAN:], o_kv.at[SPAN:], sems.at[2]),
    ]
    for copy in copies:
        copy.start()
    replicas = length_ref.shape[0]
    mine = lax.axis_index("replica")
    meta_ref[0] = length_ref[mine]
    place = jnp.where(mine % 2 == 0, mine // 2, replicas - 1 - mine // 2)
    for n in range(1, replicas):
        at = (place + replicas - n) % replicas
        other = jnp.where(at < replicas // 2, 2 * at, 2 * (replicas - at) - 1)
        meta_ref[n] = jnp.where(prompt_ref[other, 1] == mine, span_ref[other, 1], -1)
    for copy in copies:
        copy.wait()


def pack(queries, keys, values, lengths, slot_prompt, slot_span):
    width = keys.shape[1]
    return pl.pallas_call(
        pack_kernel,
        out_shape=(
            jax.ShapeDtypeStruct((SPAN, queries.shape[1]), queries.dtype),
            jax.ShapeDtypeStruct((2 * SPAN, width), keys.dtype),
            jax.ShapeDtypeStruct(lengths.shape, jnp.int32),
        ),
        in_specs=[SMEM] * 3 + [ANY] * 3,
        out_specs=(ANY, ANY, SMEM),
        scratch_shapes=[pltpu.SemaphoreType.DMA((3,))],
    )(lengths, slot_prompt, slot_span, queries, keys, values)


def widen(v_ref, wide_ref):
    for at in range(0, v_ref.shape[-1], HDIM):
        wide_ref[:, 2 * at : 2 * at + HDIM] = v_ref[:, at : at + HDIM]
        wide_ref[:, 2 * at + HDIM : 2 * at + 2 * HDIM] = jnp.ones(
            (v_ref.shape[0], HDIM), v_ref.dtype
        )


def attend_span(span, q_ref, k_ref, wide_ref, o_ref):
    width = q_ref.shape[-1]
    group = width // k_ref.shape[-1]
    before = span * SPAN
    seen = before + SPAN
    scale = LOG2E / math.sqrt(HDIM)
    row = lax.broadcasted_iota(jnp.int32, (STACK * SPAN, SPAN), 0) % SPAN
    column = lax.broadcasted_iota(jnp.int32, (STACK * SPAN, SPAN), 1)
    visible = column <= row

    def stack(first):
        columns = [pl.ds(pl.multiple_of((first + h) * HDIM, HDIM), HDIM) for h in range(STACK)]
        shared = first // group
        q = jnp.concatenate([q_ref[:, c] for c in columns], axis=0)
        k = k_ref[:seen, pl.ds(pl.multiple_of(shared * HDIM, HDIM), HDIM)]
        wide = wide_ref[:seen, pl.ds(pl.multiple_of(shared * 2 * HDIM, HDIM), 2 * HDIM)]
        scores = lax.dot_general(
            q, k, (((1,), (1,)), ((), ())), preferred_element_type=jnp.float32
        )
        edge = jnp.where(visible, scores[:, before:], -jnp.inf)
        if span:
            scores = jnp.concatenate([scores[:, :before], edge], axis=1)
        else:
            scores = edge
        top = jnp.max(scores, axis=1, keepdims=True)
        weights = jnp.exp2((scores - top) * scale).astype(jnp.bfloat16)
        mixed = jnp.dot(weights, wide, preferred_element_type=jnp.float32)
        mixed = (mixed[:, :HDIM] / mixed[:, HDIM:]).astype(o_ref.dtype)
        for h in range(STACK):
            o_ref[:, columns[h]] = mixed[h * SPAN : (h + 1) * SPAN, :]

    def some_heads(step, carry):
        for n in range(CHAINS):
            stack((step * CHAINS + n) * STACK)
        return carry

    lax.fori_loop(0, width // (CHAINS * STACK * HDIM), some_heads, 0)


def rows_of(span):
    return pl.ds(pl.multiple_of(span * SPAN, SPAN), SPAN)


def local_kernel(meta_ref, q_ref, k_ref, v_ref, o_ref, wide, mixed, zeros, sems):
    live = meta_ref[0]
    zeros[...] = jnp.zeros_like(zeros)
    for span in range(1, MAXC):

        @pl.when(span >= live)
        def _(span=span):
            pltpu.make_async_copy(zeros, o_ref.at[rows_of(span)], sems.at[span]).start()

    widen(v_ref, wide)
    attend_span(0, q_ref.at[:SPAN], k_ref, wide, mixed.at[0])
    first = pltpu.make_async_copy(mixed.at[0], o_ref.at[rows_of(0)], sems.at[0])
    first.start()

    @pl.when(live > 1)
    def _():
        attend_span(1, q_ref.at[SPAN:], k_ref, wide, mixed.at[1])
        second = pltpu.make_async_copy(mixed.at[1], o_ref.at[rows_of(1)], sems.at[MAXC])
        second.start()
        second.wait()

    first.wait()
    for span in range(1, MAXC):

        @pl.when(span >= live)
        def _(span=span):
            pltpu.make_async_copy(zeros, o_ref.at[rows_of(span)], sems.at[span]).wait()


def attend_local(meta, queries, keys, values):
    width = queries.shape[1]
    return pl.pallas_call(
        local_kernel,
        out_shape=jax.ShapeDtypeStruct((MAXC * SPAN, width), queries.dtype),
        in_specs=[SMEM, VMEM, VMEM, VMEM],
        out_specs=ANY,
        scratch_shapes=[
            pltpu.VMEM((SLOTS * SPAN, 2 * keys.shape[1]), keys.dtype),
            pltpu.VMEM((SLOTS, SPAN, width), queries.dtype),
            pltpu.VMEM((SPAN, width), queries.dtype),
            pltpu.SemaphoreType.DMA((MAXC + 1,)),
        ],
        compiler_params=pltpu.CompilerParams(vmem_limit_bytes=VMEM_BYTES),
        cost_estimate=pl.CostEstimate(
            flops=12 * SPAN * SPAN * width, bytes_accessed=12 * SPAN * width, transcendentals=0
        ),
    )(meta, queries, keys, values)


def arrived_kernel(pieces, offsets, meta_ref, *refs):
    count, parts = len(pieces), sum(pieces)
    q_refs, (k_hbm, v_hbm, _, o_ref, k_ref, v_ref, wide, q_buf, mixed, sems) = (
        refs[:parts],
        refs[parts:],
    )
    dests = [meta_ref[offset] for offset in offsets]
    wanted = dests[0] >= 0
    for dest in dests[1:]:
        wanted |= dest >= 0

    @pl.when(wanted)
    def _():
        copy_k = pltpu.make_async_copy(k_hbm, k_ref, sems.at[2 * count])
        copy_v = pltpu.make_async_copy(v_hbm, v_ref, sems.at[2 * count + 1])
        copy_k.start()
        copy_v.start()
        for j in range(count):

            @pl.when(dests[j] >= 0)
            def _(j=j):
                rows = SPAN // pieces[j]
                for n in range(pieces[j]):
                    pltpu.make_async_copy(
                        q_refs[sum(pieces[:j]) + n],
                        q_buf.at[j, n * rows : (n + 1) * rows],
                        sems.at[j],
                    ).start()

        copy_k.wait()
        copy_v.wait()
        widen(v_ref, wide)

        def one(j, carry):
            dest = dests[0]
            for n in range(1, count):
                dest = jnp.where(j == n, dests[n], dest)

            @pl.when(dest >= 0)
            def _():
                pltpu.make_async_copy(q_buf.at[j], q_buf.at[j], sems.at[j]).wait()
                for span in range(1, MAXC):

                    @pl.when(dest == span)
                    def _(span=span):
                        attend_span(span, q_buf.at[j], k_ref, wide, mixed.at[j])

                pltpu.make_async_copy(
                    mixed.at[j], o_ref.at[rows_of(dest)], sems.at[count + j]
                ).start()

            return carry

        lax.fori_loop(0, count, one, 0)
        for j in range(count):

            @pl.when(dests[j] >= 0)
            def _(j=j):
                pltpu.make_async_copy(
                    mixed.at[j], o_ref.at[rows_of(dests[j])], sems.at[count + j]
                ).wait()


def attend_arrived(meta, offsets, blocks, cache_keys, cache_values, attention):
    pieces = [len(block) for block in blocks]
    count, parts = len(pieces), sum(pieces)
    width = attention.shape[1]
    return pl.pallas_call(
        lambda *refs: arrived_kernel(pieces, offsets, *refs),
        out_shape=jax.ShapeDtypeStruct(attention.shape, attention.dtype),
        in_specs=[SMEM] + [ANY] * (parts + 3),
        out_specs=ANY,
        input_output_aliases={parts + 3: 0},
        scratch_shapes=[
            pltpu.VMEM(cache_keys.shape, cache_keys.dtype),
            pltpu.VMEM(cache_values.shape, cache_values.dtype),
            pltpu.VMEM((cache_keys.shape[0], 2 * cache_keys.shape[1]), cache_keys.dtype),
            pltpu.VMEM((count, SPAN, width), attention.dtype),
            pltpu.VMEM((count, SPAN, width), attention.dtype),
            pltpu.SemaphoreType.DMA((2 * count + 2,)),
        ],
        compiler_params=pltpu.CompilerParams(vmem_limit_bytes=VMEM_BYTES),
        cost_estimate=pl.CostEstimate(
            flops=16 * SPAN * SPAN * width * count,
            bytes_accessed=4 * SPAN * width * count,
            transcendentals=0,
        ),
    )(meta, *[part for block in blocks for part in block], cache_keys, cache_values, attention)


def order_kernel(offsets, meta_ref, own_k, own_v, *refs):
    pairs, (o_k, o_v, k_buf, v_buf, in_sems, out_sems) = refs[:-6], refs[-6:]
    live = meta_ref[0]

    def fetches():
        yield None, own_k.at[:SPAN], k_buf.at[rows_of(0)]
        yield None, own_v.at[:SPAN], v_buf.at[rows_of(0)]
        yield live > 1, own_k.at[SPAN:], k_buf.at[rows_of(1)]
        yield live > 1, own_v.at[SPAN:], v_buf.at[rows_of(1)]
        for j, offset in enumerate(offsets):
            there = rows_of(jnp.maximum(meta_ref[offset], 0))
            yield meta_ref[offset] >= 0, pairs[2 * j], k_buf.at[there]
            yield meta_ref[offset] >= 0, pairs[2 * j + 1], v_buf.at[there]

    for span in range(1, MAXC):

        @pl.when(span >= live)
        def _(span=span):
            k_buf[rows_of(span), :] = jnp.zeros((SPAN, k_buf.shape[1]), k_buf.dtype)
            v_buf[rows_of(span), :] = jnp.zeros((SPAN, v_buf.shape[1]), v_buf.dtype)

    for act in ("start", "wait"):
        for n, (needed, here, there) in enumerate(fetches()):
            copy = pltpu.make_async_copy(here, there, in_sems.at[n])
            if needed is None:
                getattr(copy, act)()
            else:
                pl.when(needed)(getattr(copy, act))
    copy_k = pltpu.make_async_copy(k_buf, o_k, out_sems.at[0])
    copy_v = pltpu.make_async_copy(v_buf, o_v, out_sems.at[1])
    copy_k.start()
    copy_v.start()
    copy_k.wait()
    copy_v.wait()


def put_in_order(meta, offsets, keys, values, whole, halves):
    shape = (MAXC * SPAN, keys.shape[1])
    out = jax.ShapeDtypeStruct(shape, keys.dtype)

    def kernel(meta_ref, own_k, own_v, *refs):
        blocks, rest = refs[: len(whole)], refs[len(whole) :]
        pairs = [part for block in blocks for part in (block.at[:SPAN], block.at[SPAN:])]
        order_kernel(offsets, meta_ref, own_k, own_v, *pairs, *rest)

    return pl.pallas_call(
        kernel,
        out_shape=(out, out),
        in_specs=[SMEM] + [ANY] * (4 + len(whole)),
        out_specs=(ANY, ANY),
        scratch_shapes=[
            pltpu.VMEM(shape, keys.dtype),
            pltpu.VMEM(shape, keys.dtype),
            pltpu.SemaphoreType.DMA((6 + 2 * len(whole),)),
            pltpu.SemaphoreType.DMA((2,)),
        ],
        compiler_params=pltpu.CompilerParams(vmem_limit_bytes=VMEM_BYTES),
        cost_estimate=pl.CostEstimate(
            flops=0, bytes_accessed=8 * MAXC * SPAN * keys.shape[1], transcendentals=0
        ),
    )(meta, keys, values, *whole, *halves)


def gathered_kernel(meta_ref, first_ref, later_ref, k_ref, v_ref, o_ref, wide):
    at = pl.program_id(1)
    live = meta_ref[0]
    widen(v_ref, wide)
    for span in range(MAXC):
        q_ref = first_ref if span == 0 else later_ref.at[0]

        @pl.when((at == span) & (span < live))
        def _(span=span, q_ref=q_ref):
            attend_span(span, q_ref, k_ref, wide, o_ref)

    @pl.when(at >= live)
    def _():
        o_ref[...] = jnp.zeros_like(o_ref)


def attend_gathered(live, source, first, later, cache_keys, cache_values):
    home_rows, key_width = cache_keys.shape
    width = first.shape[1]
    groups = key_width // HDIM
    part = width // groups
    meta = jnp.concatenate([live.reshape(1), source]).astype(jnp.int32)
    return pl.pallas_call(
        gathered_kernel,
        out_shape=jax.ShapeDtypeStruct((home_rows, width), first.dtype),
        grid_spec=pltpu.PrefetchScalarGridSpec(
            num_scalar_prefetch=1,
            grid=(groups, MAXC),
            in_specs=[
                pl.BlockSpec((SPAN, part), lambda g, m, meta: (0, g)),
                pl.BlockSpec((1, SPAN, part), lambda g, m, meta: (meta[1 + m], 0, g)),
                pl.BlockSpec((home_rows, HDIM), lambda g, m, meta: (0, g)),
                pl.BlockSpec((home_rows, HDIM), lambda g, m, meta: (0, g)),
            ],
            out_specs=pl.BlockSpec((SPAN, part), lambda g, m, meta: (m, g)),
            scratch_shapes=[pltpu.VMEM((home_rows, 2 * HDIM), cache_keys.dtype)],
        ),
        compiler_params=pltpu.CompilerParams(vmem_limit_bytes=VMEM_BYTES),
    )(meta, first, later, cache_keys, cache_values)


def gather_all(queries, keys, values, lengths, slot_prompt, slot_span):
    mine = lax.axis_index("replica")
    home_rows, key_width = MAXC * SPAN, keys.shape[1]
    live = lengths[mine]
    spans = jnp.arange(MAXC, dtype=jnp.int32)
    matches = (slot_prompt[None, :, 1] == mine) & (slot_span[None, :, 1] == spans[:, None])
    here = jnp.any(matches, axis=1)
    source = jnp.argmax(matches, axis=1).astype(jnp.int32)
    slots_k = lax.all_gather(keys[SPAN:], "replica")
    slots_v = lax.all_gather(values[SPAN:], "replica")
    slots_q = lax.all_gather(queries[SPAN:], "replica")

    def in_order(first, slots):
        picked = jnp.take(slots, source, axis=0)
        kept = jnp.where(here[:, None, None], picked, jnp.zeros((), slots.dtype))
        return jnp.concatenate([first, kept[1:].reshape(home_rows - SPAN, key_width)], axis=0)

    cache_keys = in_order(keys[:SPAN], slots_k)
    cache_values = in_order(values[:SPAN], slots_v)
    attention = attend_gathered(live, source, queries[:SPAN], slots_q, cache_keys, cache_values)
    return (attention, cache_keys, cache_values)


def per_device(queries, keys, values, lengths, slot_prompt, slot_span):
    replicas = lax.axis_size("replica")
    if replicas != 8:
        return gather_all(queries, keys, values, lengths, slot_prompt, slot_span)
    ring = column_ring(replicas)
    farthest = replicas // 2
    together = lax.optimization_barrier

    def shift(block, step):
        pairs = [(r, ring[(n + step) % replicas]) for n, r in enumerate(ring)]
        return lax.ppermute(block, "replica", pairs)

    def go_on(both):
        return [shift(both[0], 1), shift(both[1], -1)]

    def halves(both):
        half = both[0].shape[0] // 2
        return [both[0][:half], both[1][half:]]

    own_q, own_kv, meta = pack(queries, keys, values, lengths, slot_prompt, slot_span)
    q, kv = [[own_q, own_q]], [[own_kv, own_kv]]
    kv.append(go_on(kv[0]))
    q.append(go_on(q[0]))
    attention = attend_local(meta, queries, keys, values)
    kv[1], attention = together((kv[1], attention))
    kv.append(go_on(kv[1]))
    kv.append(go_on(kv[2]))
    q[1], kv[3] = together((q[1], kv[3]))
    q.append(go_on(q[1]))
    kv.append(go_on(halves(kv[3])))
    offsets = [way % replicas for n in range(1, farthest) for way in (n, -n)]
    cache_keys, cache_values = put_in_order(
        meta, offsets + [farthest], keys, values, kv[1] + kv[2] + kv[3], kv[4]
    )
    q[2], cache_keys = together((q[2], cache_keys))
    q.append(go_on(q[2]))

    def attend(first, last, attention):
        blocks = [(block,) for both in q[first : last + 1] for block in both]
        return attend_arrived(
            meta,
            offsets[2 * first - 2 : 2 * last],
            blocks,
            cache_keys,
            cache_values,
            attention,
        )

    attention = attend(1, 2, attention)
    q[3], attention = together((q[3], attention))
    q.append(go_on(halves(q[3])))
    attention = attend(3, 3, attention)
    attention = attend_arrived(
        meta, [farthest], [tuple(q[4])], cache_keys, cache_values, attention
    )
    return (attention, cache_keys, cache_values)


def solution(mesh):
    in_specs = (
        P(("group", "replica"), "tensor"),
        P(("group", "replica"), "tensor"),
        P(("group", "replica"), "tensor"),
        P("group"),
        P("group", None),
        P("group", None),
    )
    out_specs = (
        P(("group", "replica"), "tensor"),
        P(("group", "replica"), "tensor"),
        P(("group", "replica"), "tensor"),
    )
    return jax.shard_map(
        per_device, mesh=mesh, in_specs=in_specs, out_specs=out_specs, check_vma=False
    )
```

```python
import math

import jax
import jax.numpy as jnp
from jax import lax
from jax.experimental import pallas as pl
from jax.experimental.pallas import tpu as pltpu
from jax.sharding import PartitionSpec as P

HDIM = 128
SPAN = 128
SLOTS = 2
MAXC = 8
STACK = 4
LOG2E = 1.0 / math.log(2.0)
VMEM_BYTES = 60 * 1024 * 1024
LEAST_SUM, MOST_SUM = 1e-20, 1e30
ANY = pl.BlockSpec(memory_space=pl.ANY)
SMEM = pl.BlockSpec(memory_space=pltpu.SMEM)
VMEM = pl.BlockSpec(memory_space=pltpu.VMEM)


def column_ring(replicas):
    return list(range(0, replicas, 2)) + list(range(replicas - 1, 0, -2))


def pass_on(fetches, stores):
    for copy in fetches:
        copy.start()
    for copy in fetches:
        copy.wait()
    for copy in stores:
        copy.start()
    for copy in stores:
        copy.wait()


def pack_kv_kernel(k_ref, v_ref, o_ref, buf, sems):
    pass_on(
        [
            pltpu.make_async_copy(k_ref.at[SPAN:], buf.at[:SPAN], sems.at[0]),
            pltpu.make_async_copy(v_ref.at[SPAN:], buf.at[SPAN:], sems.at[1]),
        ],
        [pltpu.make_async_copy(buf, o_ref, sems.at[2])],
    )


def pack_kv(keys, values):
    shape = (2 * SPAN, keys.shape[1])
    return pl.pallas_call(
        pack_kv_kernel,
        out_shape=jax.ShapeDtypeStruct(shape, keys.dtype),
        in_specs=[ANY] * 2,
        out_specs=ANY,
        scratch_shapes=[pltpu.VMEM(shape, keys.dtype), pltpu.SemaphoreType.DMA((3,))],
        compiler_params=pltpu.CompilerParams(vmem_limit_bytes=VMEM_BYTES),
    )(keys, values)


def pack_q_kernel(q_ref, o_top, o_bottom, buf, sems):
    half = SPAN // 2
    pass_on(
        [
            pltpu.make_async_copy(q_ref.at[SPAN : SPAN + half], buf.at[:half], sems.at[0]),
            pltpu.make_async_copy(q_ref.at[SPAN + half :], buf.at[half:], sems.at[1]),
        ],
        [
            pltpu.make_async_copy(buf.at[:half], o_top, sems.at[2]),
            pltpu.make_async_copy(buf.at[half:], o_bottom, sems.at[3]),
        ],
    )


def pack_q(queries):
    width = queries.shape[1]
    half = jax.ShapeDtypeStruct((SPAN // 2, width), queries.dtype)
    return pl.pallas_call(
        pack_q_kernel,
        out_shape=(half, half),
        in_specs=[ANY],
        out_specs=(ANY, ANY),
        scratch_shapes=[
            pltpu.VMEM((SPAN, width), queries.dtype),
            pltpu.SemaphoreType.DMA((4,)),
        ],
        compiler_params=pltpu.CompilerParams(vmem_limit_bytes=VMEM_BYTES),
    )(queries)


def places_kernel(length_ref, prompt_ref, span_ref, meta_ref):
    replicas = length_ref.shape[0]
    mine = lax.axis_index("replica")
    meta_ref[0] = length_ref[mine]
    place = jnp.where(mine % 2 == 0, mine // 2, replicas - 1 - mine // 2)
    for n in range(1, replicas):
        at = (place + replicas - n) % replicas
        other = jnp.where(at < replicas // 2, 2 * at, 2 * (replicas - at) - 1)
        meta_ref[n] = jnp.where(prompt_ref[other, 1] == mine, span_ref[other, 1], -1)


def places(lengths, slot_prompt, slot_span):
    return pl.pallas_call(
        places_kernel,
        out_shape=jax.ShapeDtypeStruct(lengths.shape, jnp.int32),
        in_specs=[SMEM] * 3,
        out_specs=SMEM,
    )(lengths, slot_prompt, slot_span)


def widen(v_ref, wide_ref):
    for at in range(0, v_ref.shape[-1], HDIM):
        wide_ref[:, 2 * at : 2 * at + HDIM] = v_ref[:, at : at + HDIM]
        wide_ref[:, 2 * at + HDIM : 2 * at + 2 * HDIM] = jnp.ones(
            (v_ref.shape[0], HDIM), v_ref.dtype
        )


def attend_span(span, q_ref, k_ref, wide_ref, o_ref):
    width = q_ref.shape[-1]
    group = width // k_ref.shape[-1]
    before = span * SPAN
    seen = before + SPAN
    scale = LOG2E / math.sqrt(HDIM)
    row = lax.broadcasted_iota(jnp.int32, (STACK * SPAN, SPAN), 0) % SPAN
    column = lax.broadcasted_iota(jnp.int32, (STACK * SPAN, SPAN), 1)
    visible = column <= row

    def some_heads(step, shifted):
        columns = [
            pl.ds(pl.multiple_of((step * STACK + h) * HDIM, HDIM), HDIM) for h in range(STACK)
        ]
        shared = step * STACK // group
        q = jnp.concatenate([q_ref[:, c] for c in columns], axis=0)
        k = k_ref[:seen, pl.ds(pl.multiple_of(shared * HDIM, HDIM), HDIM)]
        wide = wide_ref[:seen, pl.ds(pl.multiple_of(shared * 2 * HDIM, HDIM), 2 * HDIM)]
        scores = lax.dot_general(
            q, k, (((1,), (1,)), ((), ())), preferred_element_type=jnp.float32
        )
        edge = jnp.where(visible, scores[:, before:], -jnp.inf)
        if span:
            scores = jnp.concatenate([scores[:, :before], edge], axis=1)
        else:
            scores = edge
        if shifted:
            scores = scores - jnp.max(scores, axis=1, keepdims=True)
        weights = jnp.exp2(scores * scale).astype(jnp.bfloat16)
        mixed = jnp.dot(weights, wide, preferred_element_type=jnp.float32)
        total = mixed[:, HDIM:]
        inverse = pl.reciprocal(total, approx=True)
        inverse = inverse * (2.0 - total * inverse)
        mixed = (mixed[:, :HDIM] * inverse).astype(o_ref.dtype)
        for h in range(STACK):
            o_ref[:, columns[h]] = mixed[h * SPAN : (h + 1) * SPAN, :]
        return total.reshape(-1, 8, HDIM)

    def plain(step, bounds):
        total = some_heads(step, False)
        return (
            jnp.minimum(bounds[0], jnp.min(total, axis=0)),
            jnp.maximum(bounds[1], jnp.max(total, axis=0)),
        )

    def again(step, carry):
        some_heads(step, True)
        return carry

    steps = width // (STACK * HDIM)
    one = jnp.ones((8, HDIM), jnp.float32)
    least, most = lax.fori_loop(0, steps, plain, (one, one))
    safe = (jnp.min(least) > LEAST_SUM) & (jnp.max(most) < MOST_SUM)

    @pl.when(jnp.logical_not(safe))
    def _():
        lax.fori_loop(0, steps, again, 0)


def rows_of(span):
    return pl.ds(pl.multiple_of(span * SPAN, SPAN), SPAN)


def local_kernel(meta_ref, q_hbm, k_hbm, v_hbm, o_ref, q_ref, k_ref, v_ref, wide, mixed, zeros, sems):
    live = meta_ref[0]
    fetches = [
        pltpu.make_async_copy(k_hbm, k_ref, sems.at[MAXC + 1]),
        pltpu.make_async_copy(v_hbm, v_ref, sems.at[MAXC + 2]),
        pltpu.make_async_copy(q_hbm, q_ref, sems.at[MAXC + 3]),
    ]
    for copy in fetches:
        copy.start()
    zeros[...] = jnp.zeros_like(zeros)
    for span in range(1, MAXC):

        @pl.when(span >= live)
        def _(span=span):
            pltpu.make_async_copy(zeros, o_ref.at[rows_of(span)], sems.at[span]).start()

    for copy in fetches:
        copy.wait()
    widen(v_ref, wide)
    attend_span(0, q_ref.at[:SPAN], k_ref, wide, mixed.at[0])
    first = pltpu.make_async_copy(mixed.at[0], o_ref.at[rows_of(0)], sems.at[0])
    first.start()

    @pl.when(live > 1)
    def _():
        attend_span(1, q_ref.at[SPAN:], k_ref, wide, mixed.at[1])
        second = pltpu.make_async_copy(mixed.at[1], o_ref.at[rows_of(1)], sems.at[MAXC])
        second.start()
        second.wait()

    first.wait()
    for span in range(1, MAXC):

        @pl.when(span >= live)
        def _(span=span):
            pltpu.make_async_copy(zeros, o_ref.at[rows_of(span)], sems.at[span]).wait()


def attend_local(meta, queries, keys, values):
    width = queries.shape[1]
    return pl.pallas_call(
        local_kernel,
        out_shape=jax.ShapeDtypeStruct((MAXC * SPAN, width), queries.dtype),
        in_specs=[SMEM, ANY, ANY, ANY],
        out_specs=ANY,
        scratch_shapes=[
            pltpu.VMEM(queries.shape, queries.dtype),
            pltpu.VMEM(keys.shape, keys.dtype),
            pltpu.VMEM(values.shape, values.dtype),
            pltpu.VMEM((SLOTS * SPAN, 2 * keys.shape[1]), keys.dtype),
            pltpu.VMEM((SLOTS, SPAN, width), queries.dtype),
            pltpu.VMEM((SPAN, width), queries.dtype),
            pltpu.SemaphoreType.DMA((MAXC + 4,)),
        ],
        compiler_params=pltpu.CompilerParams(vmem_limit_bytes=VMEM_BYTES),
        cost_estimate=pl.CostEstimate(
            flops=12 * SPAN * SPAN * width, bytes_accessed=12 * SPAN * width, transcendentals=0
        ),
    )(meta, queries, keys, values)


def arrived_kernel(pieces, offsets, meta_ref, *refs):
    count, parts = len(pieces), sum(pieces)
    q_refs, (k_hbm, v_hbm, _, o_ref, k_ref, v_ref, wide, q_buf, mixed, sems) = (
        refs[:parts],
        refs[parts:],
    )
    dests = [meta_ref[offset] for offset in offsets]
    wanted = dests[0] >= 0
    for dest in dests[1:]:
        wanted |= dest >= 0

    @pl.when(wanted)
    def _():
        copy_k = pltpu.make_async_copy(k_hbm, k_ref, sems.at[2 * count])
        copy_v = pltpu.make_async_copy(v_hbm, v_ref, sems.at[2 * count + 1])
        copy_k.start()
        copy_v.start()
        for j in range(count):

            @pl.when(dests[j] >= 0)
            def _(j=j):
                rows = SPAN // pieces[j]
                for n in range(pieces[j]):
                    pltpu.make_async_copy(
                        q_refs[sum(pieces[:j]) + n],
                        q_buf.at[j, n * rows : (n + 1) * rows],
                        sems.at[j],
                    ).start()

        copy_k.wait()
        copy_v.wait()
        widen(v_ref, wide)

        def one(j, carry):
            dest = dests[0]
            for n in range(1, count):
                dest = jnp.where(j == n, dests[n], dest)

            @pl.when(dest >= 0)
            def _():
                pltpu.make_async_copy(q_buf.at[j], q_buf.at[j], sems.at[j]).wait()
                for span in range(1, MAXC):

                    @pl.when(dest == span)
                    def _(span=span):
                        attend_span(span, q_buf.at[j], k_ref, wide, mixed.at[j])

                pltpu.make_async_copy(
                    mixed.at[j], o_ref.at[rows_of(dest)], sems.at[count + j]
                ).start()

            return carry

        lax.fori_loop(0, count, one, 0)
        for j in range(count):

            @pl.when(dests[j] >= 0)
            def _(j=j):
                pltpu.make_async_copy(
                    mixed.at[j], o_ref.at[rows_of(dests[j])], sems.at[count + j]
                ).wait()


def attend_arrived(meta, offsets, blocks, cache_keys, cache_values, attention):
    pieces = [len(block) for block in blocks]
    count, parts = len(pieces), sum(pieces)
    width = attention.shape[1]
    return pl.pallas_call(
        lambda *refs: arrived_kernel(pieces, offsets, *refs),
        out_shape=jax.ShapeDtypeStruct(attention.shape, attention.dtype),
        in_specs=[SMEM] + [ANY] * (parts + 3),
        out_specs=ANY,
        input_output_aliases={parts + 3: 0},
        scratch_shapes=[
            pltpu.VMEM(cache_keys.shape, cache_keys.dtype),
            pltpu.VMEM(cache_values.shape, cache_values.dtype),
            pltpu.VMEM((cache_keys.shape[0], 2 * cache_keys.shape[1]), cache_keys.dtype),
            pltpu.VMEM((count, SPAN, width), attention.dtype),
            pltpu.VMEM((count, SPAN, width), attention.dtype),
            pltpu.SemaphoreType.DMA((2 * count + 2,)),
        ],
        compiler_params=pltpu.CompilerParams(vmem_limit_bytes=VMEM_BYTES),
        cost_estimate=pl.CostEstimate(
            flops=16 * SPAN * SPAN * width * count,
            bytes_accessed=4 * SPAN * width * count,
            transcendentals=0,
        ),
    )(meta, *[part for block in blocks for part in block], cache_keys, cache_values, attention)


def order_kernel(offsets, meta_ref, own_k, own_v, *refs):
    pairs, (o_k, o_v, k_buf, v_buf, in_sems, out_sems) = refs[:-6], refs[-6:]
    live = meta_ref[0]

    def fetches():
        yield None, own_k.at[:SPAN], k_buf.at[rows_of(0)]
        yield None, own_v.at[:SPAN], v_buf.at[rows_of(0)]
        yield live > 1, own_k.at[SPAN:], k_buf.at[rows_of(1)]
        yield live > 1, own_v.at[SPAN:], v_buf.at[rows_of(1)]
        for j, offset in enumerate(offsets):
            there = rows_of(jnp.maximum(meta_ref[offset], 0))
            yield meta_ref[offset] >= 0, pairs[2 * j], k_buf.at[there]
            yield meta_ref[offset] >= 0, pairs[2 * j + 1], v_buf.at[there]

    for span in range(1, MAXC):

        @pl.when(span >= live)
        def _(span=span):
            k_buf[rows_of(span), :] = jnp.zeros((SPAN, k_buf.shape[1]), k_buf.dtype)
            v_buf[rows_of(span), :] = jnp.zeros((SPAN, v_buf.shape[1]), v_buf.dtype)

    for act in ("start", "wait"):
        for n, (needed, here, there) in enumerate(fetches()):
            copy = pltpu.make_async_copy(here, there, in_sems.at[n])
            if needed is None:
                getattr(copy, act)()
            else:
                pl.when(needed)(getattr(copy, act))
    copy_k = pltpu.make_async_copy(k_buf, o_k, out_sems.at[0])
    copy_v = pltpu.make_async_copy(v_buf, o_v, out_sems.at[1])
    copy_k.start()
    copy_v.start()
    copy_k.wait()
    copy_v.wait()


def put_in_order(meta, offsets, keys, values, whole, halves):
    shape = (MAXC * SPAN, keys.shape[1])
    out = jax.ShapeDtypeStruct(shape, keys.dtype)

    def kernel(meta_ref, own_k, own_v, *refs):
        blocks, rest = refs[: len(whole)], refs[len(whole) :]
        pairs = [part for block in blocks for part in (block.at[:SPAN], block.at[SPAN:])]
        order_kernel(offsets, meta_ref, own_k, own_v, *pairs, *rest)

    return pl.pallas_call(
        kernel,
        out_shape=(out, out),
        in_specs=[SMEM] + [ANY] * (4 + len(whole)),
        out_specs=(ANY, ANY),
        scratch_shapes=[
            pltpu.VMEM(shape, keys.dtype),
            pltpu.VMEM(shape, keys.dtype),
            pltpu.SemaphoreType.DMA((6 + 2 * len(whole),)),
            pltpu.SemaphoreType.DMA((2,)),
        ],
        compiler_params=pltpu.CompilerParams(vmem_limit_bytes=VMEM_BYTES),
        cost_estimate=pl.CostEstimate(
            flops=0, bytes_accessed=8 * MAXC * SPAN * keys.shape[1], transcendentals=0
        ),
    )(meta, keys, values, *whole, *halves)


def gathered_kernel(meta_ref, first_ref, later_ref, k_ref, v_ref, o_ref, wide):
    at = pl.program_id(1)
    live = meta_ref[0]
    widen(v_ref, wide)
    for span in range(MAXC):
        q_ref = first_ref if span == 0 else later_ref.at[0]

        @pl.when((at == span) & (span < live))
        def _(span=span, q_ref=q_ref):
            attend_span(span, q_ref, k_ref, wide, o_ref)

    @pl.when(at >= live)
    def _():
        o_ref[...] = jnp.zeros_like(o_ref)


def attend_gathered(live, source, first, later, cache_keys, cache_values):
    home_rows, key_width = cache_keys.shape
    width = first.shape[1]
    groups = key_width // HDIM
    part = width // groups
    meta = jnp.concatenate([live.reshape(1), source]).astype(jnp.int32)
    return pl.pallas_call(
        gathered_kernel,
        out_shape=jax.ShapeDtypeStruct((home_rows, width), first.dtype),
        grid_spec=pltpu.PrefetchScalarGridSpec(
            num_scalar_prefetch=1,
            grid=(groups, MAXC),
            in_specs=[
                pl.BlockSpec((SPAN, part), lambda g, m, meta: (0, g)),
                pl.BlockSpec((1, SPAN, part), lambda g, m, meta: (meta[1 + m], 0, g)),
                pl.BlockSpec((home_rows, HDIM), lambda g, m, meta: (0, g)),
                pl.BlockSpec((home_rows, HDIM), lambda g, m, meta: (0, g)),
            ],
            out_specs=pl.BlockSpec((SPAN, part), lambda g, m, meta: (m, g)),
            scratch_shapes=[pltpu.VMEM((home_rows, 2 * HDIM), cache_keys.dtype)],
        ),
        compiler_params=pltpu.CompilerParams(vmem_limit_bytes=VMEM_BYTES),
    )(meta, first, later, cache_keys, cache_values)


def gather_all(queries, keys, values, lengths, slot_prompt, slot_span):
    mine = lax.axis_index("replica")
    home_rows, key_width = MAXC * SPAN, keys.shape[1]
    live = lengths[mine]
    spans = jnp.arange(MAXC, dtype=jnp.int32)
    matches = (slot_prompt[None, :, 1] == mine) & (slot_span[None, :, 1] == spans[:, None])
    here = jnp.any(matches, axis=1)
    source = jnp.argmax(matches, axis=1).astype(jnp.int32)
    slots_k = lax.all_gather(keys[SPAN:], "replica")
    slots_v = lax.all_gather(values[SPAN:], "replica")
    slots_q = lax.all_gather(queries[SPAN:], "replica")

    def in_order(first, slots):
        picked = jnp.take(slots, source, axis=0)
        kept = jnp.where(here[:, None, None], picked, jnp.zeros((), slots.dtype))
        return jnp.concatenate([first, kept[1:].reshape(home_rows - SPAN, key_width)], axis=0)

    cache_keys = in_order(keys[:SPAN], slots_k)
    cache_values = in_order(values[:SPAN], slots_v)
    attention = attend_gathered(live, source, queries[:SPAN], slots_q, cache_keys, cache_values)
    return (attention, cache_keys, cache_values)


def per_device(queries, keys, values, lengths, slot_prompt, slot_span):
    replicas = lax.axis_size("replica")
    if replicas != 8:
        return gather_all(queries, keys, values, lengths, slot_prompt, slot_span)
    ring = column_ring(replicas)
    farthest = replicas // 2
    together = lax.optimization_barrier

    def shift(block, step):
        pairs = [(r, ring[(n + step) % replicas]) for n, r in enumerate(ring)]
        return lax.ppermute(block, "replica", pairs)

    def go_on(both):
        return [shift(both[0], 1), shift(both[1], -1)]

    own_kv = pack_kv(keys, values)
    kv = [[own_kv, own_kv]]
    kv.append(go_on(kv[0]))
    own_kv, queries = together((own_kv, queries))
    own_top, own_bottom = pack_q(queries)
    top, bottom = [[own_top, own_top]], [[own_bottom, own_bottom]]
    top.append(go_on(top[0]))
    lengths, kv[1] = together((lengths, kv[1]))
    kv.append(go_on(kv[1]))
    meta = places(lengths, slot_prompt, slot_span)
    bottom[0], meta = together((bottom[0], meta))
    bottom.append(go_on(bottom[0]))
    attention = attend_local(meta, queries, keys, values)
    kv[2], attention = together((kv[2], attention))
    kv.append(go_on(kv[2]))
    top[1], kv[2] = together((top[1], kv[2]))
    top.append(go_on(top[1]))
    half = SPAN
    kv.append(go_on([kv[3][0][:half], kv[3][1][half:]]))
    bottom[1], kv[3] = together((bottom[1], kv[3]))
    bottom.append(go_on(bottom[1]))
    offsets = [way % replicas for n in range(1, farthest) for way in (n, -n)]
    cache_keys, cache_values = put_in_order(
        meta, offsets + [farthest], keys, values, kv[1] + kv[2] + kv[3], kv[4]
    )
    top[2], cache_keys = together((top[2], cache_keys))
    top.append(go_on(top[2]))
    bottom.append(go_on(bottom[2]))

    def attend(first, last, attention):
        blocks = [
            pair for n in range(first, last + 1) for pair in zip(top[n], bottom[n], strict=True)
        ]
        return attend_arrived(
            meta,
            offsets[2 * first - 2 : 2 * last],
            blocks,
            cache_keys,
            cache_values,
            attention,
        )

    attention = attend(1, 2, attention)
    top[3], bottom[3], attention = together((top[3], bottom[3], attention))
    last = (shift(top[3][0], 1), shift(bottom[3][1], -1))
    attention = attend(3, 3, attention)
    attention = attend_arrived(meta, [farthest], [last], cache_keys, cache_values, attention)
    return (attention, cache_keys, cache_values)


def solution(mesh):
    in_specs = (
        P(("group", "replica"), "tensor"),
        P(("group", "replica"), "tensor"),
        P(("group", "replica"), "tensor"),
        P("group"),
        P("group", None),
        P("group", None),
    )
    out_specs = (
        P(("group", "replica"), "tensor"),
        P(("group", "replica"), "tensor"),
        P(("group", "replica"), "tensor"),
    )
    return jax.shard_map(
        per_device, mesh=mesh, in_specs=in_specs, out_specs=out_specs, check_vma=False
    )
```

```python
import functools
import math

import jax
import jax.numpy as jnp
from jax import lax
from jax.experimental import pallas as pl
from jax.experimental.pallas import tpu as pltpu
from jax.sharding import PartitionSpec as P

HDIM = 128
SPAN = 128
SLOTS = 2
MAXC = 8
BLOCK = 2 * SPAN
LOG2E = 1.0 / math.log(2.0)
VMEM_BYTES = 60 * 1024 * 1024
LEAST_SUM, MOST_SUM = 1e-20, 1e30
ANY = pl.BlockSpec(memory_space=pl.ANY)
SMEM = pl.BlockSpec(memory_space=pltpu.SMEM)
VMEM = pl.BlockSpec(memory_space=pltpu.VMEM)


def column_ring(replicas):
    return list(range(0, replicas, 2)) + list(range(replicas - 1, 0, -2))


def pass_on(fetches, stores):
    for copy in fetches:
        copy.start()
    for copy in fetches:
        copy.wait()
    for copy in stores:
        copy.start()
    for copy in stores:
        copy.wait()


def pack_kv_kernel(k_ref, v_ref, o_ref, buf, sems):
    pass_on(
        [
            pltpu.make_async_copy(k_ref.at[SPAN:], buf.at[:SPAN], sems.at[0]),
            pltpu.make_async_copy(v_ref.at[SPAN:], buf.at[SPAN:], sems.at[1]),
        ],
        [pltpu.make_async_copy(buf, o_ref, sems.at[2])],
    )


def pack_kv(keys, values):
    shape = (2 * SPAN, keys.shape[1])
    return pl.pallas_call(
        pack_kv_kernel,
        out_shape=jax.ShapeDtypeStruct(shape, keys.dtype),
        in_specs=[ANY] * 2,
        out_specs=ANY,
        scratch_shapes=[pltpu.VMEM(shape, keys.dtype), pltpu.SemaphoreType.DMA((3,))],
        compiler_params=pltpu.CompilerParams(vmem_limit_bytes=VMEM_BYTES),
    )(keys, values)


def pack_q_kernel(q_ref, o_top, o_bottom, buf, sems):
    half = SPAN // 2
    pass_on(
        [
            pltpu.make_async_copy(q_ref.at[SPAN : SPAN + half], buf.at[:half], sems.at[0]),
            pltpu.make_async_copy(q_ref.at[SPAN + half :], buf.at[half:], sems.at[1]),
        ],
        [
            pltpu.make_async_copy(buf.at[:half], o_top, sems.at[2]),
            pltpu.make_async_copy(buf.at[half:], o_bottom, sems.at[3]),
        ],
    )


def pack_q(queries):
    width = queries.shape[1]
    half = jax.ShapeDtypeStruct((SPAN // 2, width), queries.dtype)
    return pl.pallas_call(
        pack_q_kernel,
        out_shape=(half, half),
        in_specs=[ANY],
        out_specs=(ANY, ANY),
        scratch_shapes=[
            pltpu.VMEM((SPAN, width), queries.dtype),
            pltpu.SemaphoreType.DMA((4,)),
        ],
        compiler_params=pltpu.CompilerParams(vmem_limit_bytes=VMEM_BYTES),
    )(queries)


def places(lengths, slot_prompt, slot_span):
    replicas = lengths.shape[0]
    mine = lax.axis_index("replica")
    ring = jnp.arange(replicas, dtype=jnp.int32)
    place = jnp.where(mine % 2 == 0, mine // 2, replicas - 1 - mine // 2)
    at = (place + replicas - ring) % replicas
    other = jnp.where(at < replicas // 2, 2 * at, 2 * (replicas - at) - 1)
    chosen = other[:, None] == ring[None, :]
    wanted = chosen & (slot_prompt[None, :, 1] == mine) & (ring[:, None] > 0)
    spans = jnp.where(wanted, slot_span[None, :, 1] + 1, 0)
    whole = jnp.where(chosen & (ring[:, None] == 0), lengths[None, :] + 1, 0)
    return jnp.sum(spans + whole, axis=1) - 1


def widen(v_ref, wide_ref):
    for at in range(0, v_ref.shape[-1], HDIM):
        wide_ref[:, 2 * at : 2 * at + HDIM] = v_ref[:, at : at + HDIM]
        wide_ref[:, 2 * at + HDIM : 2 * at + 2 * HDIM] = jnp.ones(
            (v_ref.shape[0], HDIM), v_ref.dtype
        )


def attend_span(span, q_ref, k_ref, wide_ref, o_ref, stacked, mixed, top):
    width = q_ref.shape[-1]
    kv_heads = k_ref.shape[-1] // HDIM
    group = width // (kv_heads * HDIM)
    rows = group * SPAN
    scale = LOG2E / math.sqrt(HDIM)
    blocks = span // (BLOCK // SPAN)
    edge = span % (BLOCK // SPAN) * SPAN

    def lanes(at, many=1):
        return pl.ds(pl.multiple_of(at * many * HDIM, HDIM), many * HDIM)

    def scores(shared, block, masked):
        keys = pl.ds(pl.multiple_of(block * BLOCK, BLOCK), BLOCK)
        found = lax.dot_general(
            stacked[...],
            k_ref[keys, lanes(shared)],
            (((1,), (1,)), ((), ())),
            preferred_element_type=jnp.float32,
        )
        if masked:
            row = lax.broadcasted_iota(jnp.int32, (rows, BLOCK), 0) % SPAN
            column = lax.broadcasted_iota(jnp.int32, (rows, BLOCK), 1)
            found = jnp.where(column <= row + edge, found, -jnp.inf)
        return found

    def products(shared, block, masked, shifted):
        keys = pl.ds(pl.multiple_of(block * BLOCK, BLOCK), BLOCK)
        found = scores(shared, block, masked)
        if shifted:
            found = found - jnp.concatenate([top[...]] * (BLOCK // HDIM), axis=1)
        weights = jnp.exp2(found * scale).astype(jnp.bfloat16)
        return jnp.dot(
            weights,
            wide_ref[keys, lanes(shared, 2)],
            preferred_element_type=jnp.float32,
        )

    def widest(found):
        return functools.reduce(
            jnp.maximum, [found[:, at : at + HDIM] for at in range(0, BLOCK, HDIM)]
        )

    def one_head(shared, shifted):
        for h in range(group):
            stacked[h * SPAN : (h + 1) * SPAN, :] = q_ref[:, lanes(shared * group + h)]
        if shifted:
            top[...] = widest(scores(shared, blocks, True))

            def look(block, carry):
                top[...] = jnp.maximum(top[...], widest(scores(shared, block, False)))
                return carry

            lax.fori_loop(0, blocks, look, 0)
            top[...] = jnp.broadcast_to(
                jnp.max(top[...], axis=1, keepdims=True), top.shape
            )
        mixed[...] = products(shared, blocks, True, shifted)

        def add(block, carry):
            mixed[...] += products(shared, block, False, shifted)
            return carry

        lax.fori_loop(0, blocks, add, 0)
        total = mixed[:, HDIM:]
        inverse = pl.reciprocal(total, approx=True)
        inverse = inverse * (2.0 - total * inverse)
        result = (mixed[:, :HDIM] * inverse).astype(o_ref.dtype)
        for h in range(group):
            o_ref[:, lanes(shared * group + h)] = result[h * SPAN : (h + 1) * SPAN, :]
        return total.reshape(-1, 8, HDIM)

    def plain(shared, bounds):
        total = one_head(shared, False)
        return (
            jnp.minimum(bounds[0], jnp.min(total, axis=0)),
            jnp.maximum(bounds[1], jnp.max(total, axis=0)),
        )

    def again(shared, carry):
        one_head(shared, True)
        return carry

    one = jnp.ones((8, HDIM), jnp.float32)
    least, most = lax.fori_loop(0, kv_heads, plain, (one, one))
    safe = (jnp.min(least) > LEAST_SUM) & (jnp.max(most) < MOST_SUM)

    @pl.when(jnp.logical_not(safe))
    def _():
        lax.fori_loop(0, kv_heads, again, 0)


def work_space(width, key_width):
    rows = width // key_width * SPAN
    return [
        pltpu.VMEM((rows, HDIM), jnp.bfloat16),
        pltpu.VMEM((rows, 2 * HDIM), jnp.float32),
        pltpu.VMEM((rows, HDIM), jnp.float32),
    ]


def rows_of(span):
    return pl.ds(pl.multiple_of(span * SPAN, SPAN), SPAN)


def local_kernel(meta_ref, q_hbm, k_hbm, v_hbm, o_ref, q_ref, k_ref, v_ref, wide, mixed, zeros, sems, *work):
    live = meta_ref[0]
    fetches = [
        pltpu.make_async_copy(k_hbm, k_ref, sems.at[MAXC + 1]),
        pltpu.make_async_copy(v_hbm, v_ref, sems.at[MAXC + 2]),
        pltpu.make_async_copy(q_hbm, q_ref, sems.at[MAXC + 3]),
    ]
    for copy in fetches:
        copy.start()
    zeros[...] = jnp.zeros_like(zeros)
    for span in range(1, MAXC):

        @pl.when(span >= live)
        def _(span=span):
            pltpu.make_async_copy(zeros, o_ref.at[rows_of(span)], sems.at[span]).start()

    for copy in fetches:
        copy.wait()
    widen(v_ref, wide)
    attend_span(0, q_ref.at[:SPAN], k_ref, wide, mixed.at[0], *work)
    first = pltpu.make_async_copy(mixed.at[0], o_ref.at[rows_of(0)], sems.at[0])
    first.start()

    @pl.when(live > 1)
    def _():
        attend_span(1, q_ref.at[SPAN:], k_ref, wide, mixed.at[1], *work)
        second = pltpu.make_async_copy(mixed.at[1], o_ref.at[rows_of(1)], sems.at[MAXC])
        second.start()
        second.wait()

    first.wait()
    for span in range(1, MAXC):

        @pl.when(span >= live)
        def _(span=span):
            pltpu.make_async_copy(zeros, o_ref.at[rows_of(span)], sems.at[span]).wait()


def attend_local(meta, queries, keys, values):
    width = queries.shape[1]
    return pl.pallas_call(
        local_kernel,
        out_shape=jax.ShapeDtypeStruct((MAXC * SPAN, width), queries.dtype),
        in_specs=[SMEM, ANY, ANY, ANY],
        out_specs=ANY,
        scratch_shapes=[
            pltpu.VMEM(queries.shape, queries.dtype),
            pltpu.VMEM(keys.shape, keys.dtype),
            pltpu.VMEM(values.shape, values.dtype),
            pltpu.VMEM((SLOTS * SPAN, 2 * keys.shape[1]), keys.dtype),
            pltpu.VMEM((SLOTS, SPAN, width), queries.dtype),
            pltpu.VMEM((SPAN, width), queries.dtype),
            pltpu.SemaphoreType.DMA((MAXC + 4,)),
            *work_space(width, keys.shape[1]),
        ],
        compiler_params=pltpu.CompilerParams(vmem_limit_bytes=VMEM_BYTES),
        cost_estimate=pl.CostEstimate(
            flops=12 * SPAN * SPAN * width, bytes_accessed=12 * SPAN * width, transcendentals=0
        ),
    )(meta, queries, keys, values)


def arrived_kernel(pieces, offsets, meta_ref, *refs):
    count, parts = len(pieces), sum(pieces)
    q_refs, (k_hbm, v_hbm, _, o_ref, k_ref, v_ref, wide, q_buf, mixed, sems, *work) = (
        refs[:parts],
        refs[parts:],
    )
    dests = [meta_ref[offset] for offset in offsets]
    wanted = dests[0] >= 0
    for dest in dests[1:]:
        wanted |= dest >= 0

    @pl.when(wanted)
    def _():
        copy_k = pltpu.make_async_copy(k_hbm, k_ref, sems.at[2 * count])
        copy_v = pltpu.make_async_copy(v_hbm, v_ref, sems.at[2 * count + 1])
        copy_k.start()
        copy_v.start()
        for j in range(count):

            @pl.when(dests[j] >= 0)
            def _(j=j):
                rows = SPAN // pieces[j]
                for n in range(pieces[j]):
                    pltpu.make_async_copy(
                        q_refs[sum(pieces[:j]) + n],
                        q_buf.at[j, n * rows : (n + 1) * rows],
                        sems.at[j],
                    ).start()

        copy_k.wait()
        copy_v.wait()
        widen(v_ref, wide)

        def one(j, carry):
            dest = dests[0]
            for n in range(1, count):
                dest = jnp.where(j == n, dests[n], dest)

            @pl.when(dest >= 0)
            def _():
                pltpu.make_async_copy(q_buf.at[j], q_buf.at[j], sems.at[j]).wait()
                attend_span(dest, q_buf.at[j], k_ref, wide, mixed.at[j], *work)
                pltpu.make_async_copy(
                    mixed.at[j], o_ref.at[rows_of(dest)], sems.at[count + j]
                ).start()

            return carry

        lax.fori_loop(0, count, one, 0)
        for j in range(count):

            @pl.when(dests[j] >= 0)
            def _(j=j):
                pltpu.make_async_copy(
                    mixed.at[j], o_ref.at[rows_of(dests[j])], sems.at[count + j]
                ).wait()


def attend_arrived(meta, offsets, blocks, cache_keys, cache_values, attention):
    pieces = [len(block) for block in blocks]
    count, parts = len(pieces), sum(pieces)
    width = attention.shape[1]
    return pl.pallas_call(
        lambda *refs: arrived_kernel(pieces, offsets, *refs),
        out_shape=jax.ShapeDtypeStruct(attention.shape, attention.dtype),
        in_specs=[SMEM] + [ANY] * (parts + 3),
        out_specs=ANY,
        input_output_aliases={parts + 3: 0},
        scratch_shapes=[
            pltpu.VMEM(cache_keys.shape, cache_keys.dtype),
            pltpu.VMEM(cache_values.shape, cache_values.dtype),
            pltpu.VMEM((cache_keys.shape[0], 2 * cache_keys.shape[1]), cache_keys.dtype),
            pltpu.VMEM((count, SPAN, width), attention.dtype),
            pltpu.VMEM((count, SPAN, width), attention.dtype),
            pltpu.SemaphoreType.DMA((2 * count + 2,)),
            *work_space(width, cache_keys.shape[1]),
        ],
        compiler_params=pltpu.CompilerParams(vmem_limit_bytes=VMEM_BYTES),
        cost_estimate=pl.CostEstimate(
            flops=16 * SPAN * SPAN * width * count,
            bytes_accessed=4 * SPAN * width * count,
            transcendentals=0,
        ),
    )(meta, *[part for block in blocks for part in block], cache_keys, cache_values, attention)


def order_kernel(offsets, meta_ref, own_k, own_v, *refs):
    pairs, (o_k, o_v, k_buf, v_buf, in_sems, out_sems) = refs[:-6], refs[-6:]
    live = meta_ref[0]

    def fetches():
        yield None, own_k.at[:SPAN], k_buf.at[rows_of(0)]
        yield None, own_v.at[:SPAN], v_buf.at[rows_of(0)]
        yield live > 1, own_k.at[SPAN:], k_buf.at[rows_of(1)]
        yield live > 1, own_v.at[SPAN:], v_buf.at[rows_of(1)]
        for j, offset in enumerate(offsets):
            there = rows_of(jnp.maximum(meta_ref[offset], 0))
            yield meta_ref[offset] >= 0, pairs[2 * j], k_buf.at[there]
            yield meta_ref[offset] >= 0, pairs[2 * j + 1], v_buf.at[there]

    for span in range(1, MAXC):

        @pl.when(span >= live)
        def _(span=span):
            k_buf[rows_of(span), :] = jnp.zeros((SPAN, k_buf.shape[1]), k_buf.dtype)
            v_buf[rows_of(span), :] = jnp.zeros((SPAN, v_buf.shape[1]), v_buf.dtype)

    for act in ("start", "wait"):
        for n, (needed, here, there) in enumerate(fetches()):
            copy = pltpu.make_async_copy(here, there, in_sems.at[n])
            if needed is None:
                getattr(copy, act)()
            else:
                pl.when(needed)(getattr(copy, act))
    copy_k = pltpu.make_async_copy(k_buf, o_k, out_sems.at[0])
    copy_v = pltpu.make_async_copy(v_buf, o_v, out_sems.at[1])
    copy_k.start()
    copy_v.start()
    copy_k.wait()
    copy_v.wait()


def put_in_order(meta, offsets, keys, values, blocks):
    shape = (MAXC * SPAN, keys.shape[1])
    out = jax.ShapeDtypeStruct(shape, keys.dtype)

    def kernel(meta_ref, own_k, own_v, *refs):
        blocks_refs, rest = refs[: len(blocks)], refs[len(blocks) :]
        pairs = [part for ref in blocks_refs for part in (ref.at[:SPAN], ref.at[SPAN:])]
        order_kernel(offsets, meta_ref, own_k, own_v, *pairs, *rest)

    return pl.pallas_call(
        kernel,
        out_shape=(out, out),
        in_specs=[SMEM] + [ANY] * (2 + len(blocks)),
        out_specs=(ANY, ANY),
        scratch_shapes=[
            pltpu.VMEM(shape, keys.dtype),
            pltpu.VMEM(shape, keys.dtype),
            pltpu.SemaphoreType.DMA((4 + 2 * len(blocks),)),
            pltpu.SemaphoreType.DMA((2,)),
        ],
        compiler_params=pltpu.CompilerParams(vmem_limit_bytes=VMEM_BYTES),
        cost_estimate=pl.CostEstimate(
            flops=0, bytes_accessed=8 * MAXC * SPAN * keys.shape[1], transcendentals=0
        ),
    )(meta, keys, values, *blocks)


def gathered_kernel(meta_ref, first_ref, later_ref, k_ref, v_ref, o_ref, wide, *work):
    at = pl.program_id(1)
    live = meta_ref[0]
    widen(v_ref, wide)

    @pl.when(at == 0)
    def _():
        attend_span(at, first_ref, k_ref, wide, o_ref, *work)

    @pl.when((at > 0) & (at < live))
    def _():
        attend_span(at, later_ref.at[0], k_ref, wide, o_ref, *work)

    @pl.when(at >= live)
    def _():
        o_ref[...] = jnp.zeros_like(o_ref)


def attend_gathered(live, source, first, later, cache_keys, cache_values):
    home_rows, key_width = cache_keys.shape
    width = first.shape[1]
    groups = key_width // HDIM
    part = width // groups
    meta = jnp.concatenate([live.reshape(1), source]).astype(jnp.int32)
    return pl.pallas_call(
        gathered_kernel,
        out_shape=jax.ShapeDtypeStruct((home_rows, width), first.dtype),
        grid_spec=pltpu.PrefetchScalarGridSpec(
            num_scalar_prefetch=1,
            grid=(groups, MAXC),
            in_specs=[
                pl.BlockSpec((SPAN, part), lambda g, m, meta: (0, g)),
                pl.BlockSpec((1, SPAN, part), lambda g, m, meta: (meta[1 + m], 0, g)),
                pl.BlockSpec((home_rows, HDIM), lambda g, m, meta: (0, g)),
                pl.BlockSpec((home_rows, HDIM), lambda g, m, meta: (0, g)),
            ],
            out_specs=pl.BlockSpec((SPAN, part), lambda g, m, meta: (m, g)),
            scratch_shapes=[
                pltpu.VMEM((home_rows, 2 * HDIM), cache_keys.dtype),
                *work_space(part, HDIM),
            ],
        ),
        compiler_params=pltpu.CompilerParams(vmem_limit_bytes=VMEM_BYTES),
    )(meta, first, later, cache_keys, cache_values)


def gather_all(queries, keys, values, lengths, slot_prompt, slot_span):
    mine = lax.axis_index("replica")
    home_rows, key_width = MAXC * SPAN, keys.shape[1]
    live = lengths[mine]
    spans = jnp.arange(MAXC, dtype=jnp.int32)
    matches = (slot_prompt[None, :, 1] == mine) & (slot_span[None, :, 1] == spans[:, None])
    here = jnp.any(matches, axis=1)
    source = jnp.argmax(matches, axis=1).astype(jnp.int32)
    slots_k = lax.all_gather(keys[SPAN:], "replica")
    slots_v = lax.all_gather(values[SPAN:], "replica")
    slots_q = lax.all_gather(queries[SPAN:], "replica")

    def in_order(first, slots):
        picked = jnp.take(slots, source, axis=0)
        kept = jnp.where(here[:, None, None], picked, jnp.zeros((), slots.dtype))
        return jnp.concatenate([first, kept[1:].reshape(home_rows - SPAN, key_width)], axis=0)

    cache_keys = in_order(keys[:SPAN], slots_k)
    cache_values = in_order(values[:SPAN], slots_v)
    attention = attend_gathered(live, source, queries[:SPAN], slots_q, cache_keys, cache_values)
    return (attention, cache_keys, cache_values)


def per_device(queries, keys, values, lengths, slot_prompt, slot_span):
    replicas = lax.axis_size("replica")
    if replicas != 8:
        return gather_all(queries, keys, values, lengths, slot_prompt, slot_span)
    ring = column_ring(replicas)
    farthest = replicas // 2

    def after(block, *others):
        return lax.optimization_barrier((block, others))[0]

    def shift(block, step):
        pairs = [(r, ring[(n + step) % replicas]) for n, r in enumerate(ring)]
        return lax.ppermute(block, "replica", pairs)

    def go_on(both):
        return [shift(both[0], 1), shift(both[1], -1)]

    own_kv = pack_kv(keys, values)
    kv = [[own_kv, own_kv]]
    kv.append(go_on(kv[0]))
    own_top, own_bottom = pack_q(after(queries, own_kv))
    top, bottom = [[own_top, own_top]], [[own_bottom, own_bottom]]
    top.append(go_on(top[0]))
    kv.append(go_on(kv[1]))
    bottom.append(go_on(after(bottom[0], kv[1])))
    kv.append(go_on(kv[2]))
    top.append(go_on(after(top[1], kv[2])))
    kv.append([shift(kv[3][0], 1)])
    bottom.append(go_on(after(bottom[1], kv[3], kv[4])))
    meta = places(lengths, slot_prompt, slot_span)
    offsets = [way % replicas for n in range(1, farthest) for way in (n, -n)]
    cache_keys, cache_values = put_in_order(
        meta, offsets + [farthest], keys, values, kv[1] + kv[2] + kv[3] + kv[4]
    )
    top.append(go_on(after(top[2], cache_keys)))
    bottom.append(go_on(bottom[2]))

    def attend(first, last, attention):
        blocks = [
            pair for n in range(first, last + 1) for pair in zip(top[n], bottom[n], strict=True)
        ]
        return attend_arrived(
            meta,
            offsets[2 * first - 2 : 2 * last],
            blocks,
            cache_keys,
            cache_values,
            attention,
        )

    attention = attend_local(meta, queries, keys, values)
    attention = attend(1, 2, attention)
    last = (
        shift(after(top[3][0], attention), 1),
        shift(after(bottom[3][1], attention), -1),
    )
    attention = attend(3, 3, attention)
    attention = attend_arrived(meta, [farthest], [last], cache_keys, cache_values, attention)
    return (attention, cache_keys, cache_values)


def solution(mesh):
    in_specs = (
        P(("group", "replica"), "tensor"),
        P(("group", "replica"), "tensor"),
        P(("group", "replica"), "tensor"),
        P("group"),
        P("group", None),
        P("group", None),
    )
    out_specs = (
        P(("group", "replica"), "tensor"),
        P(("group", "replica"), "tensor"),
        P(("group", "replica"), "tensor"),
    )
    return jax.shard_map(
        per_device, mesh=mesh, in_specs=in_specs, out_specs=out_specs, check_vma=False
    )
```

```python
import functools
import math

import jax
import jax.numpy as jnp
from jax import lax
from jax.experimental import pallas as pl
from jax.experimental.pallas import tpu as pltpu
from jax.sharding import PartitionSpec as P

HDIM = 128
SPAN = 128
SLOTS = 2
MAXC = 8
BLOCK = 2 * SPAN
LOG2E = 1.0 / math.log(2.0)
VMEM_BYTES = 40 * 1024 * 1024
MOST_VMEM_BYTES = 60 * 1024 * 1024
LEAST_SUM, MOST_SUM = 1e-20, 1e30
ANY = pl.BlockSpec(memory_space=pl.ANY)
SMEM = pl.BlockSpec(memory_space=pltpu.SMEM)
VMEM = pl.BlockSpec(memory_space=pltpu.VMEM)


def column_ring(replicas):
    return list(range(0, replicas, 2)) + list(range(replicas - 1, 0, -2))


def pass_on(fetches, stores):
    for copy in fetches:
        copy.start()
    for copy in fetches:
        copy.wait()
    for copy in stores:
        copy.start()
    for copy in stores:
        copy.wait()


def pack_kv_kernel(k_ref, v_ref, o_ref, buf, sems):
    pass_on(
        [
            pltpu.make_async_copy(k_ref.at[SPAN:], buf.at[:SPAN], sems.at[0]),
            pltpu.make_async_copy(v_ref.at[SPAN:], buf.at[SPAN:], sems.at[1]),
        ],
        [pltpu.make_async_copy(buf, o_ref, sems.at[2])],
    )


def pack_kv(keys, values):
    shape = (2 * SPAN, keys.shape[1])
    return pl.pallas_call(
        pack_kv_kernel,
        out_shape=jax.ShapeDtypeStruct(shape, keys.dtype),
        in_specs=[ANY] * 2,
        out_specs=ANY,
        scratch_shapes=[pltpu.VMEM(shape, keys.dtype), pltpu.SemaphoreType.DMA((3,))],
        compiler_params=pltpu.CompilerParams(vmem_limit_bytes=MOST_VMEM_BYTES),
    )(keys, values)


def pack_q_kernel(q_ref, o_top, o_bottom, buf, sems):
    half = SPAN // 2
    pass_on(
        [
            pltpu.make_async_copy(q_ref.at[SPAN : SPAN + half], buf.at[:half], sems.at[0]),
            pltpu.make_async_copy(q_ref.at[SPAN + half :], buf.at[half:], sems.at[1]),
        ],
        [
            pltpu.make_async_copy(buf.at[:half], o_top, sems.at[2]),
            pltpu.make_async_copy(buf.at[half:], o_bottom, sems.at[3]),
        ],
    )


def pack_q(queries):
    width = queries.shape[1]
    half = jax.ShapeDtypeStruct((SPAN // 2, width), queries.dtype)
    return pl.pallas_call(
        pack_q_kernel,
        out_shape=(half, half),
        in_specs=[ANY],
        out_specs=(ANY, ANY),
        scratch_shapes=[
            pltpu.VMEM((SPAN, width), queries.dtype),
            pltpu.SemaphoreType.DMA((4,)),
        ],
        compiler_params=pltpu.CompilerParams(vmem_limit_bytes=MOST_VMEM_BYTES),
    )(queries)


def places(lengths, slot_prompt, slot_span):
    replicas = lengths.shape[0]
    mine = lax.axis_index("replica")
    ring = jnp.arange(replicas, dtype=jnp.int32)
    place = jnp.where(mine % 2 == 0, mine // 2, replicas - 1 - mine // 2)
    at = (place + replicas - ring) % replicas
    other = jnp.where(at < replicas // 2, 2 * at, 2 * (replicas - at) - 1)
    chosen = other[:, None] == ring[None, :]
    wanted = chosen & (slot_prompt[None, :, 1] == mine) & (ring[:, None] > 0)
    spans = jnp.where(wanted, slot_span[None, :, 1] + 1, 0)
    whole = jnp.where(chosen & (ring[:, None] == 0), lengths[None, :] + 1, 0)
    return jnp.sum(spans + whole, axis=1) - 1


def widen(v_ref, wide_ref):
    for at in range(0, v_ref.shape[-1], HDIM):
        wide_ref[:, 2 * at : 2 * at + HDIM] = v_ref[:, at : at + HDIM]
        wide_ref[:, 2 * at + HDIM : 2 * at + 2 * HDIM] = jnp.ones(
            (v_ref.shape[0], HDIM), v_ref.dtype
        )


def stack(q_refs, stacked):
    kv_heads, rows, _ = stacked.shape
    group = rows // SPAN
    for shared in range(kv_heads):
        for h in range(group):
            at = (shared * group + h) * HDIM
            row = h * SPAN
            for q_ref in q_refs:
                many = q_ref.shape[0]
                stacked[shared, row : row + many, :] = q_ref[:, at : at + HDIM]
                row += many


def attend_span(span, stacked, k_ref, wide_ref, mixed, top, shifted):
    kv_heads, rows, _ = stacked.shape
    scale = LOG2E / math.sqrt(HDIM)
    blocks = span // (BLOCK // SPAN)
    edge = span % (BLOCK // SPAN) * SPAN

    def scores(shared, block, masked):
        keys = pl.ds(pl.multiple_of(block * BLOCK, BLOCK), BLOCK)
        found = lax.dot_general(
            stacked[shared],
            k_ref[keys, shared * HDIM : (shared + 1) * HDIM],
            (((1,), (1,)), ((), ())),
            preferred_element_type=jnp.float32,
        )
        if masked:
            row = lax.broadcasted_iota(jnp.int32, (rows, BLOCK), 0) % SPAN
            column = lax.broadcasted_iota(jnp.int32, (rows, BLOCK), 1)
            found = jnp.where(column <= row + edge, found, -jnp.inf)
        return found

    def products(shared, block, found):
        keys = pl.ds(pl.multiple_of(block * BLOCK, BLOCK), BLOCK)
        if shifted:
            found = found - jnp.concatenate([top[shared]] * (BLOCK // HDIM), axis=1)
        weights = jnp.exp2(found * scale).astype(jnp.bfloat16)
        return jnp.dot(
            weights,
            wide_ref[keys, 2 * shared * HDIM : 2 * (shared + 1) * HDIM],
            preferred_element_type=jnp.float32,
        )

    def widest(found):
        return functools.reduce(
            jnp.maximum, [found[:, at : at + HDIM] for at in range(0, BLOCK, HDIM)]
        )

    if shifted:
        for shared in range(kv_heads):
            top[shared] = widest(scores(shared, blocks, True))

            def look(block, carry, shared=shared):
                top[shared] = jnp.maximum(top[shared], widest(scores(shared, block, False)))
                return carry

            lax.fori_loop(0, blocks, look, 0)
            top[shared] = jnp.broadcast_to(
                jnp.max(top[shared], axis=1, keepdims=True), top.shape[1:]
            )

    found = [scores(shared, blocks, True) for shared in range(kv_heads)]
    for shared in range(kv_heads):
        mixed[shared] = products(shared, blocks, found[shared])

    def add(block, carry):
        found = [scores(shared, block, False) for shared in range(kv_heads)]
        for shared in range(kv_heads):
            mixed[shared] += products(shared, block, found[shared])
        return carry

    lax.fori_loop(0, blocks, add, 0)


def finish(mixed, o_ref, bounds):
    kv_heads, rows, _ = mixed.shape
    for shared in range(kv_heads):
        total = mixed[shared, :, HDIM:]
        inverse = pl.reciprocal(total, approx=True)
        inverse = inverse * (2.0 - total * inverse)
        result = (mixed[shared, :, :HDIM] * inverse).astype(o_ref.dtype)
        for h in range(rows // SPAN):
            at = (shared * rows // SPAN + h) * HDIM
            o_ref[:, at : at + HDIM] = result[h * SPAN : (h + 1) * SPAN, :]
        total = total.reshape(-1, 8, HDIM)
        bounds[0] = jnp.minimum(bounds[0], jnp.min(total, axis=0))
        bounds[1] = jnp.maximum(bounds[1], jnp.max(total, axis=0))


def twice_if_needed(work, bounds):
    bounds[...] = jnp.ones_like(bounds)
    work(False)
    safe = (jnp.min(bounds[0]) > LEAST_SUM) & (jnp.max(bounds[1]) < MOST_SUM)

    @pl.when(jnp.logical_not(safe))
    def _():
        work(True)


def work_space(count, width, key_width):
    kv_heads = key_width // HDIM
    rows = width // key_width * SPAN
    return [
        pltpu.VMEM((count, kv_heads, rows, HDIM), jnp.bfloat16),
        pltpu.VMEM((kv_heads, rows, 2 * HDIM), jnp.float32),
        pltpu.VMEM((kv_heads, rows, HDIM), jnp.float32),
        pltpu.VMEM((2, 8, HDIM), jnp.float32),
    ]


def rows_of(span):
    return pl.ds(pl.multiple_of(span * SPAN, SPAN), SPAN)


def attend_blocks(dests, q_parts, k_ref, wide_ref, o_ref, out_buf, out_sems, stacked, mixed, top, bounds):
    count = len(dests)
    for j in range(count):

        @pl.when(dests[j] >= 0)
        def _(j=j):
            stack(q_parts[j], stacked.at[j])

    def store(j, dest):
        return pltpu.make_async_copy(out_buf.at[j], o_ref.at[rows_of(dest)], out_sems.at[j])

    def work(shifted):
        def one(j, carry):
            dest = dests[0]
            for n in range(1, count):
                dest = jnp.where(j == n, dests[n], dest)

            @pl.when(dest >= 0)
            def _():
                attend_span(dest, stacked.at[j], k_ref, wide_ref, mixed, top, shifted)
                finish(mixed, out_buf.at[j], bounds)
                store(j, dest).start()

            return carry

        lax.fori_loop(0, count, one, 0)
        for j in range(count):
            pl.when(dests[j] >= 0)(store(j, jnp.maximum(dests[j], 0)).wait)

    twice_if_needed(work, bounds)


def local_kernel(length_ref, q_hbm, k_hbm, v_hbm, o_ref, q_ref, k_ref, v_ref, wide, zeros, sems, *work):
    live = length_ref[lax.axis_index("replica")]
    fetches = [
        pltpu.make_async_copy(k_hbm, k_ref, sems.at[0]),
        pltpu.make_async_copy(v_hbm, v_ref, sems.at[MAXC]),
        pltpu.make_async_copy(q_hbm, q_ref, sems.at[MAXC + 1]),
    ]
    for copy in fetches:
        copy.start()
    zeros[...] = jnp.zeros_like(zeros)

    def clear(span):
        return pltpu.make_async_copy(zeros, o_ref.at[rows_of(span)], sems.at[span])

    for span in range(1, MAXC):
        pl.when(span >= live)(clear(span).start)
    for copy in fetches:
        copy.wait()
    widen(v_ref, wide)
    attend_blocks(
        [jnp.int32(0), jnp.where(live > 1, 1, -1)],
        [(q_ref.at[:SPAN],), (q_ref.at[SPAN:],)],
        k_ref,
        wide,
        o_ref,
        *work,
    )
    for span in range(1, MAXC):
        pl.when(span >= live)(clear(span).wait)


def attend_local(lengths, queries, keys, values):
    width, key_width = queries.shape[1], keys.shape[1]
    return pl.pallas_call(
        local_kernel,
        out_shape=jax.ShapeDtypeStruct((MAXC * SPAN, width), queries.dtype),
        in_specs=[SMEM, ANY, ANY, ANY],
        out_specs=ANY,
        scratch_shapes=[
            pltpu.VMEM(queries.shape, queries.dtype),
            pltpu.VMEM(keys.shape, keys.dtype),
            pltpu.VMEM(values.shape, values.dtype),
            pltpu.VMEM((SLOTS * SPAN, 2 * key_width), keys.dtype),
            pltpu.VMEM((SPAN, width), queries.dtype),
            pltpu.SemaphoreType.DMA((MAXC + 2,)),
            pltpu.VMEM((SLOTS, SPAN, width), queries.dtype),
            pltpu.SemaphoreType.DMA((SLOTS,)),
            *work_space(SLOTS, width, key_width),
        ],
        compiler_params=pltpu.CompilerParams(vmem_limit_bytes=MOST_VMEM_BYTES),
        cost_estimate=pl.CostEstimate(
            flops=12 * SPAN * SPAN * width, bytes_accessed=12 * SPAN * width, transcendentals=0
        ),
    )(lengths, queries, keys, values)


def arrived_kernel(pieces, offsets, meta_ref, *refs):
    parts = sum(pieces)
    q_refs, (k_ref, wide_ref, _, o_ref, *rest) = refs[:parts], refs[parts:]
    dests = [meta_ref[offset] for offset in offsets]
    q_parts = [q_refs[sum(pieces[:j]) : sum(pieces[: j + 1])] for j in range(len(pieces))]
    wanted = functools.reduce(jnp.maximum, dests) >= 0

    @pl.when(wanted)
    def _():
        attend_blocks(dests, q_parts, k_ref, wide_ref, o_ref, *rest)


def attend_arrived(meta, offsets, blocks, ordered_keys, wide_values, attention):
    pieces = [len(block) for block in blocks]
    count, parts = len(pieces), sum(pieces)
    width = attention.shape[1]
    return pl.pallas_call(
        lambda *refs: arrived_kernel(pieces, offsets, *refs),
        out_shape=jax.ShapeDtypeStruct(attention.shape, attention.dtype),
        in_specs=[SMEM] + [VMEM] * (parts + 2) + [ANY],
        out_specs=ANY,
        input_output_aliases={parts + 3: 0},
        scratch_shapes=[
            pltpu.VMEM((count, SPAN, width), attention.dtype),
            pltpu.SemaphoreType.DMA((count,)),
            *work_space(count, width, ordered_keys.shape[1]),
        ],
        compiler_params=pltpu.CompilerParams(vmem_limit_bytes=VMEM_BYTES),
        cost_estimate=pl.CostEstimate(
            flops=16 * SPAN * SPAN * width * count,
            bytes_accessed=4 * SPAN * width * count,
            transcendentals=0,
        ),
    )(meta, *[part for block in blocks for part in block], ordered_keys, wide_values, attention)


def order_kernel(offsets, meta_ref, own_k, own_v, *refs):
    blocks, (o_k, o_v, k_buf, wide, v_buf, in_sems, out_sems) = refs[: len(offsets)], refs[len(offsets) :]
    live = meta_ref[0]

    def fetches():
        yield None, own_k.at[:SPAN], k_buf.at[rows_of(0)]
        yield None, own_v.at[:SPAN], v_buf.at[rows_of(0)]
        yield live > 1, own_k.at[SPAN:], k_buf.at[rows_of(1)]
        yield live > 1, own_v.at[SPAN:], v_buf.at[rows_of(1)]

    def each(act):
        for n, (needed, here, there) in enumerate(fetches()):
            copy = getattr(pltpu.make_async_copy(here, there, in_sems.at[n]), act)
            if needed is None:
                copy()
            else:
                pl.when(needed)(copy)

    each("start")
    for span in range(1, MAXC):

        @pl.when(span >= live)
        def _(span=span):
            k_buf[rows_of(span), :] = jnp.zeros((SPAN, k_buf.shape[1]), k_buf.dtype)
            v_buf[rows_of(span), :] = jnp.zeros((SPAN, v_buf.shape[1]), v_buf.dtype)

    for block, offset in zip(blocks, offsets, strict=True):
        dest = meta_ref[offset]

        @pl.when(dest >= 0)
        def _(block=block, dest=dest):
            k_buf[rows_of(dest), :] = block[:SPAN, :]
            v_buf[rows_of(dest), :] = block[SPAN:, :]

    each("wait")
    copy_k = pltpu.make_async_copy(k_buf, o_k, out_sems.at[0])
    copy_v = pltpu.make_async_copy(v_buf, o_v, out_sems.at[1])
    copy_k.start()
    copy_v.start()

    @pl.when(live > 1)
    def _():
        widen(v_buf, wide)

    copy_k.wait()
    copy_v.wait()


def put_in_order(meta, offsets, keys, values, blocks):
    rows, width = MAXC * SPAN, keys.shape[1]
    out = jax.ShapeDtypeStruct((rows, width), keys.dtype)
    return pl.pallas_call(
        lambda *refs: order_kernel(offsets, *refs),
        out_shape=(out, out, out, jax.ShapeDtypeStruct((rows, 2 * width), keys.dtype)),
        in_specs=[SMEM, ANY, ANY] + [VMEM] * len(blocks),
        out_specs=(ANY, ANY, VMEM, VMEM),
        scratch_shapes=[
            pltpu.VMEM((rows, width), keys.dtype),
            pltpu.SemaphoreType.DMA((4,)),
            pltpu.SemaphoreType.DMA((2,)),
        ],
        compiler_params=pltpu.CompilerParams(vmem_limit_bytes=VMEM_BYTES),
        cost_estimate=pl.CostEstimate(
            flops=0, bytes_accessed=8 * MAXC * SPAN * keys.shape[1], transcendentals=0
        ),
    )(meta, keys, values, *blocks)


def gathered_kernel(meta_ref, first_ref, later_ref, k_ref, v_ref, o_ref, wide, stacked, mixed, top, bounds):
    at = pl.program_id(1)
    live = meta_ref[0]
    widen(v_ref, wide)

    @pl.when(at == 0)
    def _():
        stack((first_ref,), stacked.at[0])

    @pl.when(at > 0)
    def _():
        stack((later_ref.at[0],), stacked.at[0])

    def work(shifted):
        attend_span(at, stacked.at[0], k_ref, wide, mixed, top, shifted)
        finish(mixed, o_ref, bounds)

    @pl.when(at < live)
    def _():
        twice_if_needed(work, bounds)

    @pl.when(at >= live)
    def _():
        o_ref[...] = jnp.zeros_like(o_ref)


def attend_gathered(live, source, first, later, cache_keys, cache_values):
    home_rows, key_width = cache_keys.shape
    width = first.shape[1]
    groups = key_width // HDIM
    part = width // groups
    meta = jnp.concatenate([live.reshape(1), source]).astype(jnp.int32)
    return pl.pallas_call(
        gathered_kernel,
        out_shape=jax.ShapeDtypeStruct((home_rows, width), first.dtype),
        grid_spec=pltpu.PrefetchScalarGridSpec(
            num_scalar_prefetch=1,
            grid=(groups, MAXC),
            in_specs=[
                pl.BlockSpec((SPAN, part), lambda g, m, meta: (0, g)),
                pl.BlockSpec((1, SPAN, part), lambda g, m, meta: (meta[1 + m], 0, g)),
                pl.BlockSpec((home_rows, HDIM), lambda g, m, meta: (0, g)),
                pl.BlockSpec((home_rows, HDIM), lambda g, m, meta: (0, g)),
            ],
            out_specs=pl.BlockSpec((SPAN, part), lambda g, m, meta: (m, g)),
            scratch_shapes=[
                pltpu.VMEM((home_rows, 2 * HDIM), cache_keys.dtype),
                *work_space(1, part, HDIM),
            ],
        ),
        compiler_params=pltpu.CompilerParams(vmem_limit_bytes=VMEM_BYTES),
    )(meta, first, later, cache_keys, cache_values)


def gather_all(queries, keys, values, lengths, slot_prompt, slot_span):
    mine = lax.axis_index("replica")
    home_rows, key_width = MAXC * SPAN, keys.shape[1]
    live = lengths[mine]
    spans = jnp.arange(MAXC, dtype=jnp.int32)
    matches = (slot_prompt[None, :, 1] == mine) & (slot_span[None, :, 1] == spans[:, None])
    here = jnp.any(matches, axis=1)
    source = jnp.argmax(matches, axis=1).astype(jnp.int32)
    slots_k = lax.all_gather(keys[SPAN:], "replica")
    slots_v = lax.all_gather(values[SPAN:], "replica")
    slots_q = lax.all_gather(queries[SPAN:], "replica")

    def in_order(first, slots):
        picked = jnp.take(slots, source, axis=0)
        kept = jnp.where(here[:, None, None], picked, jnp.zeros((), slots.dtype))
        return jnp.concatenate([first, kept[1:].reshape(home_rows - SPAN, key_width)], axis=0)

    cache_keys = in_order(keys[:SPAN], slots_k)
    cache_values = in_order(values[:SPAN], slots_v)
    attention = attend_gathered(live, source, queries[:SPAN], slots_q, cache_keys, cache_values)
    return (attention, cache_keys, cache_values)


def per_device(queries, keys, values, lengths, slot_prompt, slot_span):
    replicas = lax.axis_size("replica")
    if replicas != 8:
        return gather_all(queries, keys, values, lengths, slot_prompt, slot_span)
    ring = column_ring(replicas)
    farthest = replicas // 2

    def after(block, *others):
        return lax.optimization_barrier((block, others))[0]

    def shift(block, step):
        pairs = [(r, ring[(n + step) % replicas]) for n, r in enumerate(ring)]
        return lax.ppermute(block, "replica", pairs)

    def go_on(both):
        return [shift(both[0], 1), shift(both[1], -1)]

    own_kv = pack_kv(keys, values)
    kv = [[own_kv, own_kv]]
    kv.append(go_on(kv[0]))
    own_top, own_bottom = pack_q(after(queries, own_kv))
    top, bottom = [[own_top, own_top]], [[own_bottom, own_bottom]]
    top.append(go_on(top[0]))
    attention = attend_local(lengths, after(queries, own_top), keys, values)
    kv.append(go_on([after(block, attention) for block in kv[1]]))
    bottom.append(go_on(after(bottom[0], kv[1])))
    kv.append(go_on(kv[2]))
    top.append(go_on(after(top[1], kv[2])))
    kv.append([shift(kv[3][0], 1)])
    bottom.append(go_on(after(bottom[1], kv[3], kv[4])))
    meta = places(lengths, slot_prompt, slot_span)
    offsets = [way % replicas for n in range(1, farthest) for way in (n, -n)]
    cache_keys, cache_values, ordered_keys, wide_values = put_in_order(
        meta, offsets + [farthest], keys, values, kv[1] + kv[2] + kv[3] + kv[4]
    )
    top.append(go_on(after(top[2], ordered_keys)))
    bottom.append(go_on(bottom[2]))

    def attend(first, last, attention):
        blocks = [
            pair for n in range(first, last + 1) for pair in zip(top[n], bottom[n], strict=True)
        ]
        return attend_arrived(
            meta,
            offsets[2 * first - 2 : 2 * last],
            blocks,
            ordered_keys,
            wide_values,
            attention,
        )

    attention = attend(1, 2, attention)
    last = (
        shift(after(top[3][0], attention), 1),
        shift(after(bottom[3][1], attention), -1),
    )
    attention = attend(3, 3, attention)
    attention = attend_arrived(meta, [farthest], [last], ordered_keys, wide_values, attention)
    return (attention, cache_keys, cache_values)


def solution(mesh):
    in_specs = (
        P(("group", "replica"), "tensor"),
        P(("group", "replica"), "tensor"),
        P(("group", "replica"), "tensor"),
        P("group"),
        P("group", None),
        P("group", None),
    )
    out_specs = (
        P(("group", "replica"), "tensor"),
        P(("group", "replica"), "tensor"),
        P(("group", "replica"), "tensor"),
    )
    return jax.shard_map(
        per_device, mesh=mesh, in_specs=in_specs, out_specs=out_specs, check_vma=False
    )
```

```python
import functools
import math

import jax
import jax.numpy as jnp
from jax import lax
from jax.experimental import pallas as pl
from jax.experimental.pallas import tpu as pltpu
from jax.sharding import PartitionSpec as P

HDIM = 128
SPAN = 128
SLOTS = 2
MAXC = 8
BLOCK = 2 * SPAN
LOG2E = 1.0 / math.log(2.0)
VMEM_BYTES = 40 * 1024 * 1024
MOST_VMEM_BYTES = 60 * 1024 * 1024
LEAST_SUM, MOST_SUM = 1e-20, 1e30
ANY = pl.BlockSpec(memory_space=pl.ANY)
SMEM = pl.BlockSpec(memory_space=pltpu.SMEM)
VMEM = pl.BlockSpec(memory_space=pltpu.VMEM)


def cost_of(us):
    return pl.CostEstimate(flops=int(us * 1.15e9), bytes_accessed=0, transcendentals=0)


def column_ring(replicas):
    return list(range(0, replicas, 2)) + list(range(replicas - 1, 0, -2))


def pass_on(fetches, stores):
    for copy in fetches:
        copy.start()
    for copy in fetches:
        copy.wait()
    for copy in stores:
        copy.start()
    for copy in stores:
        copy.wait()


def pack_kv_kernel(k_ref, v_ref, o_ref, buf, sems):
    pass_on(
        [
            pltpu.make_async_copy(k_ref.at[SPAN:], buf.at[:SPAN], sems.at[0]),
            pltpu.make_async_copy(v_ref.at[SPAN:], buf.at[SPAN:], sems.at[1]),
        ],
        [pltpu.make_async_copy(buf, o_ref, sems.at[2])],
    )


def pack_kv(keys, values):
    shape = (2 * SPAN, keys.shape[1])
    return pl.pallas_call(
        pack_kv_kernel,
        out_shape=jax.ShapeDtypeStruct(shape, keys.dtype),
        in_specs=[ANY] * 2,
        out_specs=ANY,
        scratch_shapes=[pltpu.VMEM(shape, keys.dtype), pltpu.SemaphoreType.DMA((3,))],
        compiler_params=pltpu.CompilerParams(vmem_limit_bytes=MOST_VMEM_BYTES),
        cost_estimate=cost_of(1.7),
    )(keys, values)


def pack_q_kernel(q_ref, o_top, o_bottom, buf, sems):
    half = SPAN // 2
    pass_on(
        [
            pltpu.make_async_copy(q_ref.at[SPAN : SPAN + half], buf.at[:half], sems.at[0]),
            pltpu.make_async_copy(q_ref.at[SPAN + half :], buf.at[half:], sems.at[1]),
        ],
        [
            pltpu.make_async_copy(buf.at[:half], o_top, sems.at[2]),
            pltpu.make_async_copy(buf.at[half:], o_bottom, sems.at[3]),
        ],
    )


def pack_q(queries):
    width = queries.shape[1]
    half = jax.ShapeDtypeStruct((SPAN // 2, width), queries.dtype)
    return pl.pallas_call(
        pack_q_kernel,
        out_shape=(half, half),
        in_specs=[ANY],
        out_specs=(ANY, ANY),
        scratch_shapes=[
            pltpu.VMEM((SPAN, width), queries.dtype),
            pltpu.SemaphoreType.DMA((4,)),
        ],
        compiler_params=pltpu.CompilerParams(vmem_limit_bytes=MOST_VMEM_BYTES),
        cost_estimate=cost_of(1.7),
    )(queries)


def places(lengths, slot_prompt, slot_span):
    replicas = lengths.shape[0]
    mine = lax.axis_index("replica")
    ring = jnp.arange(replicas, dtype=jnp.int32)
    place = jnp.where(mine % 2 == 0, mine // 2, replicas - 1 - mine // 2)
    at = (place + replicas - ring) % replicas
    other = jnp.where(at < replicas // 2, 2 * at, 2 * (replicas - at) - 1)
    chosen = other[:, None] == ring[None, :]
    wanted = chosen & (slot_prompt[None, :, 1] == mine) & (ring[:, None] > 0)
    spans = jnp.where(wanted, slot_span[None, :, 1] + 1, 0)
    whole = jnp.where(chosen & (ring[:, None] == 0), lengths[None, :] + 1, 0)
    return jnp.sum(spans + whole, axis=1) - 1


def widen(v_ref, wide_ref):
    for at in range(0, v_ref.shape[-1], HDIM):
        wide_ref[:, 2 * at : 2 * at + HDIM] = v_ref[:, at : at + HDIM]
        wide_ref[:, 2 * at + HDIM : 2 * at + 2 * HDIM] = jnp.ones(
            (v_ref.shape[0], HDIM), v_ref.dtype
        )


def stack(q_refs, stacked):
    kv_heads, rows, _ = stacked.shape
    group = rows // SPAN
    for shared in range(kv_heads):
        for h in range(group):
            at = (shared * group + h) * HDIM
            row = h * SPAN
            for q_ref in q_refs:
                many = q_ref.shape[0]
                stacked[shared, row : row + many, :] = q_ref[:, at : at + HDIM]
                row += many


def attend_span(span, stacked, k_ref, wide_ref, mixed, top, shifted):
    kv_heads, rows, _ = stacked.shape
    scale = LOG2E / math.sqrt(HDIM)
    blocks = span // (BLOCK // SPAN)
    edge = span % (BLOCK // SPAN) * SPAN

    def scores(shared, block, masked):
        keys = pl.ds(pl.multiple_of(block * BLOCK, BLOCK), BLOCK)
        found = lax.dot_general(
            stacked[shared],
            k_ref[keys, shared * HDIM : (shared + 1) * HDIM],
            (((1,), (1,)), ((), ())),
            preferred_element_type=jnp.float32,
        )
        if masked:
            row = lax.broadcasted_iota(jnp.int32, (rows, BLOCK), 0) % SPAN
            column = lax.broadcasted_iota(jnp.int32, (rows, BLOCK), 1)
            found = jnp.where(column <= row + edge, found, -jnp.inf)
        return found

    def products(shared, block, found):
        keys = pl.ds(pl.multiple_of(block * BLOCK, BLOCK), BLOCK)
        if shifted:
            found = found - jnp.concatenate([top[shared]] * (BLOCK // HDIM), axis=1)
        weights = jnp.exp2(found * scale).astype(jnp.bfloat16)
        return jnp.dot(
            weights,
            wide_ref[keys, 2 * shared * HDIM : 2 * (shared + 1) * HDIM],
            preferred_element_type=jnp.float32,
        )

    def widest(found):
        return functools.reduce(
            jnp.maximum, [found[:, at : at + HDIM] for at in range(0, BLOCK, HDIM)]
        )

    if shifted:
        for shared in range(kv_heads):
            top[shared] = widest(scores(shared, blocks, True))

            def look(block, carry, shared=shared):
                top[shared] = jnp.maximum(top[shared], widest(scores(shared, block, False)))
                return carry

            lax.fori_loop(0, blocks, look, 0)
            top[shared] = jnp.broadcast_to(
                jnp.max(top[shared], axis=1, keepdims=True), top.shape[1:]
            )

    found = [scores(shared, blocks, True) for shared in range(kv_heads)]
    for shared in range(kv_heads):
        mixed[shared] = products(shared, blocks, found[shared])

    def add(block, carry):
        found = [scores(shared, block, False) for shared in range(kv_heads)]
        for shared in range(kv_heads):
            mixed[shared] += products(shared, block, found[shared])
        return carry

    lax.fori_loop(0, blocks, add, 0)


def finish(mixed, o_ref, bounds):
    kv_heads, rows, _ = mixed.shape
    for shared in range(kv_heads):
        total = mixed[shared, :, HDIM:]
        inverse = pl.reciprocal(total, approx=True)
        inverse = inverse * (2.0 - total * inverse)
        result = (mixed[shared, :, :HDIM] * inverse).astype(o_ref.dtype)
        for h in range(rows // SPAN):
            at = (shared * rows // SPAN + h) * HDIM
            o_ref[:, at : at + HDIM] = result[h * SPAN : (h + 1) * SPAN, :]
        total = total.reshape(-1, 8, HDIM)
        bounds[0] = jnp.minimum(bounds[0], jnp.min(total, axis=0))
        bounds[1] = jnp.maximum(bounds[1], jnp.max(total, axis=0))


def twice_if_needed(work, bounds):
    bounds[...] = jnp.ones_like(bounds)
    work(False)
    safe = (jnp.min(bounds[0]) > LEAST_SUM) & (jnp.max(bounds[1]) < MOST_SUM)

    @pl.when(jnp.logical_not(safe))
    def _():
        work(True)


def work_space(count, width, key_width):
    kv_heads = key_width // HDIM
    rows = width // key_width * SPAN
    return [
        pltpu.VMEM((count, kv_heads, rows, HDIM), jnp.bfloat16),
        pltpu.VMEM((kv_heads, rows, 2 * HDIM), jnp.float32),
        pltpu.VMEM((kv_heads, rows, HDIM), jnp.float32),
        pltpu.VMEM((2, 8, HDIM), jnp.float32),
    ]


def rows_of(span):
    return pl.ds(pl.multiple_of(span * SPAN, SPAN), SPAN)


def attend_blocks(dests, q_parts, k_ref, wide_ref, o_ref, out_buf, out_sems, stacked, mixed, top, bounds):
    count = len(dests)
    for j in range(count):

        @pl.when(dests[j] >= 0)
        def _(j=j):
            stack(q_parts[j], stacked.at[j])

    def store(j, dest):
        return pltpu.make_async_copy(out_buf.at[j], o_ref.at[rows_of(dest)], out_sems.at[j])

    def work(shifted):
        def one(j, carry):
            dest = dests[0]
            for n in range(1, count):
                dest = jnp.where(j == n, dests[n], dest)

            @pl.when(dest >= 0)
            def _():
                attend_span(dest, stacked.at[j], k_ref, wide_ref, mixed, top, shifted)
                finish(mixed, out_buf.at[j], bounds)
                store(j, dest).start()

            return carry

        lax.fori_loop(0, count, one, 0)
        for j in range(count):
            pl.when(dests[j] >= 0)(store(j, jnp.maximum(dests[j], 0)).wait)

    twice_if_needed(work, bounds)


def local_kernel(length_ref, q_hbm, k_hbm, v_hbm, o_ref, q_ref, k_ref, v_ref, wide, zeros, sems, *work):
    live = length_ref[lax.axis_index("replica")]
    fetches = [
        pltpu.make_async_copy(k_hbm, k_ref, sems.at[0]),
        pltpu.make_async_copy(v_hbm, v_ref, sems.at[MAXC]),
        pltpu.make_async_copy(q_hbm, q_ref, sems.at[MAXC + 1]),
    ]
    for copy in fetches:
        copy.start()
    zeros[...] = jnp.zeros_like(zeros)

    def clear(span):
        return pltpu.make_async_copy(zeros, o_ref.at[rows_of(span)], sems.at[span])

    for span in range(1, MAXC):
        pl.when(span >= live)(clear(span).start)
    for copy in fetches:
        copy.wait()
    widen(v_ref, wide)
    attend_blocks(
        [jnp.int32(0), jnp.where(live > 1, 1, -1)],
        [(q_ref.at[:SPAN],), (q_ref.at[SPAN:],)],
        k_ref,
        wide,
        o_ref,
        *work,
    )
    for span in range(1, MAXC):
        pl.when(span >= live)(clear(span).wait)


def attend_local(lengths, queries, keys, values):
    width, key_width = queries.shape[1], keys.shape[1]
    return pl.pallas_call(
        local_kernel,
        out_shape=jax.ShapeDtypeStruct((MAXC * SPAN, width), queries.dtype),
        in_specs=[SMEM, ANY, ANY, ANY],
        out_specs=ANY,
        scratch_shapes=[
            pltpu.VMEM(queries.shape, queries.dtype),
            pltpu.VMEM(keys.shape, keys.dtype),
            pltpu.VMEM(values.shape, values.dtype),
            pltpu.VMEM((SLOTS * SPAN, 2 * key_width), keys.dtype),
            pltpu.VMEM((SPAN, width), queries.dtype),
            pltpu.SemaphoreType.DMA((MAXC + 2,)),
            pltpu.VMEM((SLOTS, SPAN, width), queries.dtype),
            pltpu.SemaphoreType.DMA((SLOTS,)),
            *work_space(SLOTS, width, key_width),
        ],
        compiler_params=pltpu.CompilerParams(vmem_limit_bytes=MOST_VMEM_BYTES),
        cost_estimate=cost_of(6),
    )(lengths, queries, keys, values)


def arrived_kernel(pieces, offsets, meta_ref, *refs):
    parts = sum(pieces)
    q_refs, (k_ref, wide_ref, _, o_ref, *rest) = refs[:parts], refs[parts:]
    dests = [meta_ref[offset] for offset in offsets]
    q_parts = [q_refs[sum(pieces[:j]) : sum(pieces[: j + 1])] for j in range(len(pieces))]
    wanted = functools.reduce(jnp.maximum, dests) >= 0

    @pl.when(wanted)
    def _():
        attend_blocks(dests, q_parts, k_ref, wide_ref, o_ref, *rest)


def attend_arrived(meta, offsets, blocks, ordered_keys, wide_values, attention):
    pieces = [len(block) for block in blocks]
    count, parts = len(pieces), sum(pieces)
    width = attention.shape[1]
    return pl.pallas_call(
        lambda *refs: arrived_kernel(pieces, offsets, *refs),
        out_shape=jax.ShapeDtypeStruct(attention.shape, attention.dtype),
        in_specs=[SMEM] + [VMEM] * (parts + 2) + [ANY],
        out_specs=ANY,
        input_output_aliases={parts + 3: 0},
        scratch_shapes=[
            pltpu.VMEM((count, SPAN, width), attention.dtype),
            pltpu.SemaphoreType.DMA((count,)),
            *work_space(count, width, ordered_keys.shape[1]),
        ],
        compiler_params=pltpu.CompilerParams(vmem_limit_bytes=VMEM_BYTES),
        cost_estimate=cost_of(1 + 2.5 * count),
    )(meta, *[part for block in blocks for part in block], ordered_keys, wide_values, attention)


def order_kernel(offsets, meta_ref, own_k, own_v, *refs):
    blocks, (o_k, o_v, k_buf, wide, v_buf, in_sems, out_sems) = refs[: len(offsets)], refs[len(offsets) :]
    live = meta_ref[0]

    def fetches():
        yield None, own_k.at[:SPAN], k_buf.at[rows_of(0)]
        yield None, own_v.at[:SPAN], v_buf.at[rows_of(0)]
        yield live > 1, own_k.at[SPAN:], k_buf.at[rows_of(1)]
        yield live > 1, own_v.at[SPAN:], v_buf.at[rows_of(1)]

    def each(act):
        for n, (needed, here, there) in enumerate(fetches()):
            copy = getattr(pltpu.make_async_copy(here, there, in_sems.at[n]), act)
            if needed is None:
                copy()
            else:
                pl.when(needed)(copy)

    each("start")
    for span in range(1, MAXC):

        @pl.when(span >= live)
        def _(span=span):
            k_buf[rows_of(span), :] = jnp.zeros((SPAN, k_buf.shape[1]), k_buf.dtype)
            v_buf[rows_of(span), :] = jnp.zeros((SPAN, v_buf.shape[1]), v_buf.dtype)

    for block, offset in zip(blocks, offsets, strict=True):
        dest = meta_ref[offset]

        @pl.when(dest >= 0)
        def _(block=block, dest=dest):
            k_buf[rows_of(dest), :] = block[:SPAN, :]
            v_buf[rows_of(dest), :] = block[SPAN:, :]

    each("wait")
    copy_k = pltpu.make_async_copy(k_buf, o_k, out_sems.at[0])
    copy_v = pltpu.make_async_copy(v_buf, o_v, out_sems.at[1])
    copy_k.start()
    copy_v.start()

    @pl.when(live > 1)
    def _():
        widen(v_buf, wide)

    copy_k.wait()
    copy_v.wait()


def put_in_order(meta, offsets, keys, values, blocks):
    rows, width = MAXC * SPAN, keys.shape[1]
    out = jax.ShapeDtypeStruct((rows, width), keys.dtype)
    return pl.pallas_call(
        lambda *refs: order_kernel(offsets, *refs),
        out_shape=(out, out, out, jax.ShapeDtypeStruct((rows, 2 * width), keys.dtype)),
        in_specs=[SMEM, ANY, ANY] + [VMEM] * len(blocks),
        out_specs=(ANY, ANY, VMEM, VMEM),
        scratch_shapes=[
            pltpu.VMEM((rows, width), keys.dtype),
            pltpu.SemaphoreType.DMA((4,)),
            pltpu.SemaphoreType.DMA((2,)),
        ],
        compiler_params=pltpu.CompilerParams(vmem_limit_bytes=VMEM_BYTES),
        cost_estimate=cost_of(2),
    )(meta, keys, values, *blocks)


def gathered_kernel(meta_ref, first_ref, later_ref, k_ref, v_ref, o_ref, wide, stacked, mixed, top, bounds):
    at = pl.program_id(1)
    live = meta_ref[0]
    widen(v_ref, wide)

    @pl.when(at == 0)
    def _():
        stack((first_ref,), stacked.at[0])

    @pl.when(at > 0)
    def _():
        stack((later_ref.at[0],), stacked.at[0])

    def work(shifted):
        attend_span(at, stacked.at[0], k_ref, wide, mixed, top, shifted)
        finish(mixed, o_ref, bounds)

    @pl.when(at < live)
    def _():
        twice_if_needed(work, bounds)

    @pl.when(at >= live)
    def _():
        o_ref[...] = jnp.zeros_like(o_ref)


def attend_gathered(live, source, first, later, cache_keys, cache_values):
    home_rows, key_width = cache_keys.shape
    width = first.shape[1]
    groups = key_width // HDIM
    part = width // groups
    meta = jnp.concatenate([live.reshape(1), source]).astype(jnp.int32)
    return pl.pallas_call(
        gathered_kernel,
        out_shape=jax.ShapeDtypeStruct((home_rows, width), first.dtype),
        grid_spec=pltpu.PrefetchScalarGridSpec(
            num_scalar_prefetch=1,
            grid=(groups, MAXC),
            in_specs=[
                pl.BlockSpec((SPAN, part), lambda g, m, meta: (0, g)),
                pl.BlockSpec((1, SPAN, part), lambda g, m, meta: (meta[1 + m], 0, g)),
                pl.BlockSpec((home_rows, HDIM), lambda g, m, meta: (0, g)),
                pl.BlockSpec((home_rows, HDIM), lambda g, m, meta: (0, g)),
            ],
            out_specs=pl.BlockSpec((SPAN, part), lambda g, m, meta: (m, g)),
            scratch_shapes=[
                pltpu.VMEM((home_rows, 2 * HDIM), cache_keys.dtype),
                *work_space(1, part, HDIM),
            ],
        ),
        compiler_params=pltpu.CompilerParams(vmem_limit_bytes=VMEM_BYTES),
    )(meta, first, later, cache_keys, cache_values)


def gather_all(queries, keys, values, lengths, slot_prompt, slot_span):
    mine = lax.axis_index("replica")
    home_rows, key_width = MAXC * SPAN, keys.shape[1]
    live = lengths[mine]
    spans = jnp.arange(MAXC, dtype=jnp.int32)
    matches = (slot_prompt[None, :, 1] == mine) & (slot_span[None, :, 1] == spans[:, None])
    here = jnp.any(matches, axis=1)
    source = jnp.argmax(matches, axis=1).astype(jnp.int32)
    slots_k = lax.all_gather(keys[SPAN:], "replica")
    slots_v = lax.all_gather(values[SPAN:], "replica")
    slots_q = lax.all_gather(queries[SPAN:], "replica")

    def in_order(first, slots):
        picked = jnp.take(slots, source, axis=0)
        kept = jnp.where(here[:, None, None], picked, jnp.zeros((), slots.dtype))
        return jnp.concatenate([first, kept[1:].reshape(home_rows - SPAN, key_width)], axis=0)

    cache_keys = in_order(keys[:SPAN], slots_k)
    cache_values = in_order(values[:SPAN], slots_v)
    attention = attend_gathered(live, source, queries[:SPAN], slots_q, cache_keys, cache_values)
    return (attention, cache_keys, cache_values)


def per_device(queries, keys, values, lengths, slot_prompt, slot_span):
    replicas = lax.axis_size("replica")
    if replicas != 8:
        return gather_all(queries, keys, values, lengths, slot_prompt, slot_span)
    ring = column_ring(replicas)
    farthest = replicas // 2

    def after(block, *others):
        return lax.optimization_barrier((block, others))[0]

    def shift(block, step):
        pairs = [(r, ring[(n + step) % replicas]) for n, r in enumerate(ring)]
        return lax.ppermute(block, "replica", pairs)

    def go_on(both):
        return [shift(both[0], 1), shift(both[1], -1)]

    own_kv = pack_kv(keys, values)
    kv = [[own_kv, own_kv]]
    kv.append(go_on(kv[0]))
    own_top, own_bottom = pack_q(after(queries, own_kv))
    top, bottom = [[own_top, own_top]], [[own_bottom, own_bottom]]
    top.append(go_on(top[0]))
    kv.append(go_on(kv[1]))
    bottom.append(go_on(after(bottom[0], kv[1])))
    attention = attend_local(lengths, after(queries, kv[1]), keys, values)
    kv.append(go_on([after(block, attention) for block in kv[2]]))
    top.append(go_on(after(top[1], kv[2])))
    kv.append([shift(kv[3][0], 1)])
    bottom.append(go_on(after(bottom[1], kv[3], kv[4])))
    meta = places(lengths, slot_prompt, slot_span)
    offsets = [way % replicas for n in range(1, farthest) for way in (n, -n)]
    cache_keys, cache_values, ordered_keys, wide_values = put_in_order(
        meta, offsets + [farthest], keys, values, kv[1] + kv[2] + kv[3] + kv[4]
    )
    top.append(go_on(after(top[2], ordered_keys)))

    def attend(n, attention):
        blocks = list(zip(top[n], bottom[n], strict=True))
        return attend_arrived(
            meta, offsets[2 * n - 2 : 2 * n], blocks, ordered_keys, wide_values, attention
        )

    attention = attend(1, attention)
    bottom.append(go_on(after(bottom[2], attention)))
    attention = attend(2, attention)
    last = (
        shift(after(top[3][0], attention), 1),
        shift(after(bottom[3][1], attention), -1),
    )
    attention = attend(3, attention)
    attention = attend_arrived(meta, [farthest], [last], ordered_keys, wide_values, attention)
    return (attention, cache_keys, cache_values)


def solution(mesh):
    in_specs = (
        P(("group", "replica"), "tensor"),
        P(("group", "replica"), "tensor"),
        P(("group", "replica"), "tensor"),
        P("group"),
        P("group", None),
        P("group", None),
    )
    out_specs = (
        P(("group", "replica"), "tensor"),
        P(("group", "replica"), "tensor"),
        P(("group", "replica"), "tensor"),
    )
    return jax.shard_map(
        per_device, mesh=mesh, in_specs=in_specs, out_specs=out_specs, check_vma=False
    )
```

```python
import functools
import math

import jax
import jax.numpy as jnp
from jax import lax
from jax.experimental import pallas as pl
from jax.experimental.pallas import tpu as pltpu
from jax.sharding import PartitionSpec as P

HDIM = 128
SPAN = 128
SLOTS = 2
MAXC = 8
BLOCK = 2 * SPAN
LOG2E = 1.0 / math.log(2.0)
VMEM_BYTES = 40 * 1024 * 1024
MOST_VMEM_BYTES = 60 * 1024 * 1024
LEAST_SUM, MOST_SUM = 1e-20, 1e30
ANY = pl.BlockSpec(memory_space=pl.ANY)
SMEM = pl.BlockSpec(memory_space=pltpu.SMEM)
VMEM = pl.BlockSpec(memory_space=pltpu.VMEM)


def cost_of(us):
    return pl.CostEstimate(flops=int(us * 1.15e9), bytes_accessed=0, transcendentals=0)


def column_ring(replicas):
    return list(range(0, replicas, 2)) + list(range(replicas - 1, 0, -2))


def pass_on(fetches, stores):
    for copy in fetches:
        copy.start()
    for copy in fetches:
        copy.wait()
    for copy in stores:
        copy.start()
    for copy in stores:
        copy.wait()


def pack_kv_kernel(k_ref, v_ref, o_ref, buf, sems):
    pass_on(
        [
            pltpu.make_async_copy(k_ref.at[SPAN:], buf.at[:SPAN], sems.at[0]),
            pltpu.make_async_copy(v_ref.at[SPAN:], buf.at[SPAN:], sems.at[1]),
        ],
        [pltpu.make_async_copy(buf, o_ref, sems.at[2])],
    )


def pack_kv(keys, values):
    shape = (2 * SPAN, keys.shape[1])
    return pl.pallas_call(
        pack_kv_kernel,
        out_shape=jax.ShapeDtypeStruct(shape, keys.dtype),
        in_specs=[ANY] * 2,
        out_specs=ANY,
        scratch_shapes=[pltpu.VMEM(shape, keys.dtype), pltpu.SemaphoreType.DMA((3,))],
        compiler_params=pltpu.CompilerParams(vmem_limit_bytes=MOST_VMEM_BYTES),
        cost_estimate=cost_of(1.7),
    )(keys, values)


def pack_q_kernel(q_ref, o_top, o_bottom, buf, sems):
    half = SPAN // 2
    pass_on(
        [
            pltpu.make_async_copy(q_ref.at[SPAN : SPAN + half], buf.at[:half], sems.at[0]),
            pltpu.make_async_copy(q_ref.at[SPAN + half :], buf.at[half:], sems.at[1]),
        ],
        [
            pltpu.make_async_copy(buf.at[:half], o_top, sems.at[2]),
            pltpu.make_async_copy(buf.at[half:], o_bottom, sems.at[3]),
        ],
    )


def pack_q(queries):
    width = queries.shape[1]
    half = jax.ShapeDtypeStruct((SPAN // 2, width), queries.dtype)
    return pl.pallas_call(
        pack_q_kernel,
        out_shape=(half, half),
        in_specs=[ANY],
        out_specs=(ANY, ANY),
        scratch_shapes=[
            pltpu.VMEM((SPAN, width), queries.dtype),
            pltpu.SemaphoreType.DMA((4,)),
        ],
        compiler_params=pltpu.CompilerParams(vmem_limit_bytes=MOST_VMEM_BYTES),
        cost_estimate=cost_of(1.7),
    )(queries)


def places(lengths, slot_prompt, slot_span):
    replicas = lengths.shape[0]
    mine = lax.axis_index("replica")
    ring = jnp.arange(replicas, dtype=jnp.int32)
    place = jnp.where(mine % 2 == 0, mine // 2, replicas - 1 - mine // 2)
    at = (place + replicas - ring) % replicas
    other = jnp.where(at < replicas // 2, 2 * at, 2 * (replicas - at) - 1)
    chosen = other[:, None] == ring[None, :]
    wanted = chosen & (slot_prompt[None, :, 1] == mine) & (ring[:, None] > 0)
    spans = jnp.where(wanted, slot_span[None, :, 1] + 1, 0)
    whole = jnp.where(chosen & (ring[:, None] == 0), lengths[None, :] + 1, 0)
    return jnp.sum(spans + whole, axis=1) - 1


def widen(v_ref, wide_ref):
    for at in range(0, v_ref.shape[-1], HDIM):
        wide_ref[:, 2 * at : 2 * at + HDIM] = v_ref[:, at : at + HDIM]
        wide_ref[:, 2 * at + HDIM : 2 * at + 2 * HDIM] = jnp.ones(
            (v_ref.shape[0], HDIM), v_ref.dtype
        )


def stack(q_refs, stacked):
    kv_heads, rows, _ = stacked.shape
    group = rows // SPAN
    for shared in range(kv_heads):
        for h in range(group):
            at = (shared * group + h) * HDIM
            row = h * SPAN
            for q_ref in q_refs:
                many = q_ref.shape[0]
                stacked[shared, row : row + many, :] = q_ref[:, at : at + HDIM]
                row += many


def attend_span(span, stacked, k_ref, wide_ref, mixed, top, shifted):
    kv_heads, rows, _ = stacked.shape
    scale = LOG2E / math.sqrt(HDIM)
    blocks = span // (BLOCK // SPAN)
    edge = span % (BLOCK // SPAN) * SPAN

    def scores(shared, block, masked):
        keys = pl.ds(pl.multiple_of(block * BLOCK, BLOCK), BLOCK)
        found = lax.dot_general(
            stacked[shared],
            k_ref[keys, shared * HDIM : (shared + 1) * HDIM],
            (((1,), (1,)), ((), ())),
            preferred_element_type=jnp.float32,
        )
        if masked:
            row = lax.broadcasted_iota(jnp.int32, (rows, BLOCK), 0) % SPAN
            column = lax.broadcasted_iota(jnp.int32, (rows, BLOCK), 1)
            found = jnp.where(column <= row + edge, found, -jnp.inf)
        return found

    def products(shared, block, found):
        keys = pl.ds(pl.multiple_of(block * BLOCK, BLOCK), BLOCK)
        if shifted:
            found = found - jnp.concatenate([top[shared]] * (BLOCK // HDIM), axis=1)
        weights = jnp.exp2(found * scale).astype(jnp.bfloat16)
        return jnp.dot(
            weights,
            wide_ref[keys, 2 * shared * HDIM : 2 * (shared + 1) * HDIM],
            preferred_element_type=jnp.float32,
        )

    def widest(found):
        return functools.reduce(
            jnp.maximum, [found[:, at : at + HDIM] for at in range(0, BLOCK, HDIM)]
        )

    if shifted:
        for shared in range(kv_heads):
            top[shared] = widest(scores(shared, blocks, True))

            def look(block, carry, shared=shared):
                top[shared] = jnp.maximum(top[shared], widest(scores(shared, block, False)))
                return carry

            lax.fori_loop(0, blocks, look, 0)
            top[shared] = jnp.broadcast_to(
                jnp.max(top[shared], axis=1, keepdims=True), top.shape[1:]
            )

    found = [scores(shared, blocks, True) for shared in range(kv_heads)]
    for shared in range(kv_heads):
        mixed[shared] = products(shared, blocks, found[shared])

    def add(block, carry):
        found = [scores(shared, block, False) for shared in range(kv_heads)]
        for shared in range(kv_heads):
            mixed[shared] += products(shared, block, found[shared])
        return carry

    lax.fori_loop(0, blocks, add, 0)


def finish(mixed, o_ref, bounds):
    kv_heads, rows, _ = mixed.shape
    for shared in range(kv_heads):
        total = mixed[shared, :, HDIM:]
        inverse = pl.reciprocal(total, approx=True)
        inverse = inverse * (2.0 - total * inverse)
        result = (mixed[shared, :, :HDIM] * inverse).astype(o_ref.dtype)
        for h in range(rows // SPAN):
            at = (shared * rows // SPAN + h) * HDIM
            o_ref[:, at : at + HDIM] = result[h * SPAN : (h + 1) * SPAN, :]
        total = total.reshape(-1, 8, HDIM)
        bounds[0] = jnp.minimum(bounds[0], jnp.min(total, axis=0))
        bounds[1] = jnp.maximum(bounds[1], jnp.max(total, axis=0))


def twice_if_needed(work, drain, bounds):
    bounds[...] = jnp.ones_like(bounds)
    work(False)
    safe = (jnp.min(bounds[0]) > LEAST_SUM) & (jnp.max(bounds[1]) < MOST_SUM)
    drain()

    @pl.when(jnp.logical_not(safe))
    def _():
        work(True)
        drain()


def work_space(count, width, key_width):
    kv_heads = key_width // HDIM
    rows = width // key_width * SPAN
    return [
        pltpu.VMEM((count, kv_heads, rows, HDIM), jnp.bfloat16),
        pltpu.VMEM((kv_heads, rows, 2 * HDIM), jnp.float32),
        pltpu.VMEM((kv_heads, rows, HDIM), jnp.float32),
        pltpu.VMEM((2, 8, HDIM), jnp.float32),
    ]


def rows_of(span):
    return pl.ds(pl.multiple_of(span * SPAN, SPAN), SPAN)


def attend_blocks(dests, q_parts, k_ref, wide_ref, o_ref, out_buf, out_sems, stacked, mixed, top, bounds):
    count = len(dests)
    for j in range(count):

        @pl.when(dests[j] >= 0)
        def _(j=j):
            stack(q_parts[j], stacked.at[j])

    def store(j, dest):
        return pltpu.make_async_copy(out_buf.at[j], o_ref.at[rows_of(dest)], out_sems.at[j])

    def work(shifted):
        def one(j, carry):
            dest = dests[0]
            for n in range(1, count):
                dest = jnp.where(j == n, dests[n], dest)

            @pl.when(dest >= 0)
            def _():
                attend_span(dest, stacked.at[j], k_ref, wide_ref, mixed, top, shifted)
                finish(mixed, out_buf.at[j], bounds)
                store(j, dest).start()

            return carry

        lax.fori_loop(0, count, one, 0)

    def drain():
        for j in range(count):
            pl.when(dests[j] >= 0)(store(j, jnp.maximum(dests[j], 0)).wait)

    twice_if_needed(work, drain, bounds)


def local_kernel(length_ref, q_hbm, k_hbm, v_hbm, o_ref, q_ref, k_ref, v_ref, wide, zeros, sems, *work):
    live = length_ref[lax.axis_index("replica")]
    fetches = [
        pltpu.make_async_copy(k_hbm, k_ref, sems.at[0]),
        pltpu.make_async_copy(v_hbm, v_ref, sems.at[MAXC]),
        pltpu.make_async_copy(q_hbm, q_ref, sems.at[MAXC + 1]),
    ]
    for copy in fetches:
        copy.start()
    zeros[...] = jnp.zeros_like(zeros)

    def clear(span):
        return pltpu.make_async_copy(zeros, o_ref.at[rows_of(span)], sems.at[span])

    for span in range(1, MAXC):
        pl.when(span >= live)(clear(span).start)
    for copy in fetches:
        copy.wait()
    widen(v_ref, wide)
    attend_blocks(
        [jnp.int32(0), jnp.where(live > 1, 1, -1)],
        [(q_ref.at[:SPAN],), (q_ref.at[SPAN:],)],
        k_ref,
        wide,
        o_ref,
        *work,
    )
    for span in range(1, MAXC):
        pl.when(span >= live)(clear(span).wait)


def attend_local(lengths, queries, keys, values):
    width, key_width = queries.shape[1], keys.shape[1]
    return pl.pallas_call(
        local_kernel,
        out_shape=jax.ShapeDtypeStruct((MAXC * SPAN, width), queries.dtype),
        in_specs=[SMEM, ANY, ANY, ANY],
        out_specs=ANY,
        scratch_shapes=[
            pltpu.VMEM(queries.shape, queries.dtype),
            pltpu.VMEM(keys.shape, keys.dtype),
            pltpu.VMEM(values.shape, values.dtype),
            pltpu.VMEM((SLOTS * SPAN, 2 * key_width), keys.dtype),
            pltpu.VMEM((SPAN, width), queries.dtype),
            pltpu.SemaphoreType.DMA((MAXC + 2,)),
            pltpu.VMEM((SLOTS, SPAN, width), queries.dtype),
            pltpu.SemaphoreType.DMA((SLOTS,)),
            *work_space(SLOTS, width, key_width),
        ],
        compiler_params=pltpu.CompilerParams(vmem_limit_bytes=MOST_VMEM_BYTES),
        cost_estimate=cost_of(0.3),
    )(lengths, queries, keys, values)


def arrived_kernel(pieces, offsets, meta_ref, *refs):
    parts = sum(pieces)
    q_refs, (k_ref, wide_ref, _, o_ref, *rest) = refs[:parts], refs[parts:]
    dests = [meta_ref[offset] for offset in offsets]
    q_parts = [q_refs[sum(pieces[:j]) : sum(pieces[: j + 1])] for j in range(len(pieces))]
    wanted = functools.reduce(jnp.maximum, dests) >= 0

    @pl.when(wanted)
    def _():
        attend_blocks(dests, q_parts, k_ref, wide_ref, o_ref, *rest)


def attend_arrived(meta, offsets, blocks, ordered_keys, wide_values, attention):
    pieces = [len(block) for block in blocks]
    count, parts = len(pieces), sum(pieces)
    width = attention.shape[1]
    return pl.pallas_call(
        lambda *refs: arrived_kernel(pieces, offsets, *refs),
        out_shape=jax.ShapeDtypeStruct(attention.shape, attention.dtype),
        in_specs=[SMEM] + [VMEM] * (parts + 2) + [ANY],
        out_specs=ANY,
        input_output_aliases={parts + 3: 0},
        scratch_shapes=[
            pltpu.VMEM((count, SPAN, width), attention.dtype),
            pltpu.SemaphoreType.DMA((count,)),
            *work_space(count, width, ordered_keys.shape[1]),
        ],
        compiler_params=pltpu.CompilerParams(vmem_limit_bytes=VMEM_BYTES),
        cost_estimate=cost_of(1 + 2.5 * count),
    )(meta, *[part for block in blocks for part in block], ordered_keys, wide_values, attention)


def order_kernel(offsets, meta_ref, own_k, own_v, *refs):
    blocks, (o_k, o_v, k_buf, wide, v_buf, in_sems, out_sems) = refs[: len(offsets)], refs[len(offsets) :]
    live = meta_ref[0]

    def fetches():
        yield None, own_k.at[:SPAN], k_buf.at[rows_of(0)]
        yield None, own_v.at[:SPAN], v_buf.at[rows_of(0)]
        yield live > 1, own_k.at[SPAN:], k_buf.at[rows_of(1)]
        yield live > 1, own_v.at[SPAN:], v_buf.at[rows_of(1)]

    def each(act):
        for n, (needed, here, there) in enumerate(fetches()):
            copy = getattr(pltpu.make_async_copy(here, there, in_sems.at[n]), act)
            if needed is None:
                copy()
            else:
                pl.when(needed)(copy)

    each("start")
    for span in range(1, MAXC):

        @pl.when(span >= live)
        def _(span=span):
            k_buf[rows_of(span), :] = jnp.zeros((SPAN, k_buf.shape[1]), k_buf.dtype)
            v_buf[rows_of(span), :] = jnp.zeros((SPAN, v_buf.shape[1]), v_buf.dtype)

    for block, offset in zip(blocks, offsets, strict=True):
        dest = meta_ref[offset]

        @pl.when(dest >= 0)
        def _(block=block, dest=dest):
            k_buf[rows_of(dest), :] = block[:SPAN, :]
            v_buf[rows_of(dest), :] = block[SPAN:, :]

    each("wait")
    copy_k = pltpu.make_async_copy(k_buf, o_k, out_sems.at[0])
    copy_v = pltpu.make_async_copy(v_buf, o_v, out_sems.at[1])
    copy_k.start()
    copy_v.start()

    @pl.when(live > 1)
    def _():
        widen(v_buf, wide)

    copy_k.wait()
    copy_v.wait()


def put_in_order(meta, offsets, keys, values, blocks):
    rows, width = MAXC * SPAN, keys.shape[1]
    out = jax.ShapeDtypeStruct((rows, width), keys.dtype)
    return pl.pallas_call(
        lambda *refs: order_kernel(offsets, *refs),
        out_shape=(out, out, out, jax.ShapeDtypeStruct((rows, 2 * width), keys.dtype)),
        in_specs=[SMEM, ANY, ANY] + [VMEM] * len(blocks),
        out_specs=(ANY, ANY, VMEM, VMEM),
        scratch_shapes=[
            pltpu.VMEM((rows, width), keys.dtype),
            pltpu.SemaphoreType.DMA((4,)),
            pltpu.SemaphoreType.DMA((2,)),
        ],
        compiler_params=pltpu.CompilerParams(vmem_limit_bytes=VMEM_BYTES),
        cost_estimate=cost_of(2),
    )(meta, keys, values, *blocks)


def gathered_kernel(meta_ref, first_ref, later_ref, k_ref, v_ref, o_ref, wide, stacked, mixed, top, bounds):
    at = pl.program_id(1)
    live = meta_ref[0]
    widen(v_ref, wide)

    @pl.when(at == 0)
    def _():
        stack((first_ref,), stacked.at[0])

    @pl.when(at > 0)
    def _():
        stack((later_ref.at[0],), stacked.at[0])

    def work(shifted):
        attend_span(at, stacked.at[0], k_ref, wide, mixed, top, shifted)
        finish(mixed, o_ref, bounds)

    @pl.when(at < live)
    def _():
        twice_if_needed(work, lambda: None, bounds)

    @pl.when(at >= live)
    def _():
        o_ref[...] = jnp.zeros_like(o_ref)


def attend_gathered(live, source, first, later, cache_keys, cache_values):
    home_rows, key_width = cache_keys.shape
    width = first.shape[1]
    groups = key_width // HDIM
    part = width // groups
    meta = jnp.concatenate([live.reshape(1), source]).astype(jnp.int32)
    return pl.pallas_call(
        gathered_kernel,
        out_shape=jax.ShapeDtypeStruct((home_rows, width), first.dtype),
        grid_spec=pltpu.PrefetchScalarGridSpec(
            num_scalar_prefetch=1,
            grid=(groups, MAXC),
            in_specs=[
                pl.BlockSpec((SPAN, part), lambda g, m, meta: (0, g)),
                pl.BlockSpec((1, SPAN, part), lambda g, m, meta: (meta[1 + m], 0, g)),
                pl.BlockSpec((home_rows, HDIM), lambda g, m, meta: (0, g)),
                pl.BlockSpec((home_rows, HDIM), lambda g, m, meta: (0, g)),
            ],
            out_specs=pl.BlockSpec((SPAN, part), lambda g, m, meta: (m, g)),
            scratch_shapes=[
                pltpu.VMEM((home_rows, 2 * HDIM), cache_keys.dtype),
                *work_space(1, part, HDIM),
            ],
        ),
        compiler_params=pltpu.CompilerParams(vmem_limit_bytes=VMEM_BYTES),
    )(meta, first, later, cache_keys, cache_values)


def gather_all(queries, keys, values, lengths, slot_prompt, slot_span):
    mine = lax.axis_index("replica")
    home_rows, key_width = MAXC * SPAN, keys.shape[1]
    live = lengths[mine]
    spans = jnp.arange(MAXC, dtype=jnp.int32)
    matches = (slot_prompt[None, :, 1] == mine) & (slot_span[None, :, 1] == spans[:, None])
    here = jnp.any(matches, axis=1)
    source = jnp.argmax(matches, axis=1).astype(jnp.int32)
    slots_k = lax.all_gather(keys[SPAN:], "replica")
    slots_v = lax.all_gather(values[SPAN:], "replica")
    slots_q = lax.all_gather(queries[SPAN:], "replica")

    def in_order(first, slots):
        picked = jnp.take(slots, source, axis=0)
        kept = jnp.where(here[:, None, None], picked, jnp.zeros((), slots.dtype))
        return jnp.concatenate([first, kept[1:].reshape(home_rows - SPAN, key_width)], axis=0)

    cache_keys = in_order(keys[:SPAN], slots_k)
    cache_values = in_order(values[:SPAN], slots_v)
    attention = attend_gathered(live, source, queries[:SPAN], slots_q, cache_keys, cache_values)
    return (attention, cache_keys, cache_values)


def per_device(queries, keys, values, lengths, slot_prompt, slot_span):
    replicas = lax.axis_size("replica")
    if replicas != 8:
        return gather_all(queries, keys, values, lengths, slot_prompt, slot_span)
    ring = column_ring(replicas)
    farthest = replicas // 2

    def after(block, *others):
        return lax.optimization_barrier((block, others))[0]

    def shift(block, step):
        pairs = [(r, ring[(n + step) % replicas]) for n, r in enumerate(ring)]
        return lax.ppermute(block, "replica", pairs)

    def go_on(both):
        return [shift(both[0], 1), shift(both[1], -1)]

    own_kv = pack_kv(keys, values)
    kv = [[own_kv, own_kv]]
    kv.append(go_on(kv[0]))
    own_top, own_bottom = pack_q(after(queries, own_kv))
    top, bottom = [[own_top, own_top]], [[own_bottom, own_bottom]]
    top.append(go_on(top[0]))
    kv.append(go_on(kv[1]))
    bottom.append(go_on(after(bottom[0], kv[2])))
    attention = attend_local(lengths, after(queries, kv[1]), keys, values)
    kv.append(go_on([after(block, attention) for block in kv[2]]))
    kv.append([shift(kv[3][0], 1)])
    top.append(go_on(after(top[1], kv[4])))
    bottom.append(go_on(after(bottom[1], kv[3], kv[4])))
    meta = places(lengths, slot_prompt, slot_span)
    offsets = [way % replicas for n in range(1, farthest) for way in (n, -n)]
    cache_keys, cache_values, ordered_keys, wide_values = put_in_order(
        meta, offsets + [farthest], keys, values, kv[1] + kv[2] + kv[3] + kv[4]
    )
    top.append(go_on(after(top[2], ordered_keys)))

    def attend(n, attention):
        blocks = list(zip(top[n], bottom[n], strict=True))
        return attend_arrived(
            meta, offsets[2 * n - 2 : 2 * n], blocks, ordered_keys, wide_values, attention
        )

    attention = attend(1, attention)
    bottom.append(go_on(after(bottom[2], attention)))
    attention = attend(2, attention)
    last = (
        shift(after(top[3][0], attention), 1),
        shift(after(bottom[3][1], attention), -1),
    )
    attention = attend(3, attention)
    attention = attend_arrived(meta, [farthest], [last], ordered_keys, wide_values, attention)
    return (attention, cache_keys, cache_values)


def solution(mesh):
    in_specs = (
        P(("group", "replica"), "tensor"),
        P(("group", "replica"), "tensor"),
        P(("group", "replica"), "tensor"),
        P("group"),
        P("group", None),
        P("group", None),
    )
    out_specs = (
        P(("group", "replica"), "tensor"),
        P(("group", "replica"), "tensor"),
        P(("group", "replica"), "tensor"),
    )
    return jax.shard_map(
        per_device, mesh=mesh, in_specs=in_specs, out_specs=out_specs, check_vma=False
    )
```

```python
import functools
import math

import jax
import jax.numpy as jnp
from jax import lax
from jax.experimental import pallas as pl
from jax.experimental.pallas import tpu as pltpu
from jax.sharding import PartitionSpec as P

HDIM = 128
SPAN = 128
SLOTS = 2
MAXC = 8
BLOCK = 2 * SPAN
LOG2E = 1.0 / math.log(2.0)
VMEM_BYTES = 40 * 1024 * 1024
MOST_VMEM_BYTES = 60 * 1024 * 1024
LEAST_SUM, MOST_SUM = 1e-20, 1e30
ANY = pl.BlockSpec(memory_space=pl.ANY)
SMEM = pl.BlockSpec(memory_space=pltpu.SMEM)
VMEM = pl.BlockSpec(memory_space=pltpu.VMEM)


def cost_of(us):
    return pl.CostEstimate(flops=int(us * 1.15e9), bytes_accessed=0, transcendentals=0)


def column_ring(replicas):
    return list(range(0, replicas, 2)) + list(range(replicas - 1, 0, -2))


def pass_on(fetches, stores):
    for copy in fetches:
        copy.start()
    for copy in fetches:
        copy.wait()
    for copy in stores:
        copy.start()
    for copy in stores:
        copy.wait()


def pack_kv_kernel(k_ref, v_ref, o_ref, buf, sems):
    pass_on(
        [
            pltpu.make_async_copy(k_ref.at[SPAN:], buf.at[:SPAN], sems.at[0]),
            pltpu.make_async_copy(v_ref.at[SPAN:], buf.at[SPAN:], sems.at[1]),
        ],
        [pltpu.make_async_copy(buf, o_ref, sems.at[2])],
    )


def pack_kv(keys, values):
    shape = (2 * SPAN, keys.shape[1])
    return pl.pallas_call(
        pack_kv_kernel,
        out_shape=jax.ShapeDtypeStruct(shape, keys.dtype),
        in_specs=[ANY] * 2,
        out_specs=ANY,
        scratch_shapes=[pltpu.VMEM(shape, keys.dtype), pltpu.SemaphoreType.DMA((3,))],
        compiler_params=pltpu.CompilerParams(vmem_limit_bytes=MOST_VMEM_BYTES),
        cost_estimate=cost_of(1.7),
    )(keys, values)


def pack_q_kernel(q_ref, o_top, o_bottom, buf, sems):
    half = SPAN // 2
    pass_on(
        [
            pltpu.make_async_copy(q_ref.at[SPAN : SPAN + half], buf.at[:half], sems.at[0]),
            pltpu.make_async_copy(q_ref.at[SPAN + half :], buf.at[half:], sems.at[1]),
        ],
        [
            pltpu.make_async_copy(buf.at[:half], o_top, sems.at[2]),
            pltpu.make_async_copy(buf.at[half:], o_bottom, sems.at[3]),
        ],
    )


def pack_q(queries):
    width = queries.shape[1]
    half = jax.ShapeDtypeStruct((SPAN // 2, width), queries.dtype)
    return pl.pallas_call(
        pack_q_kernel,
        out_shape=(half, half),
        in_specs=[ANY],
        out_specs=(ANY, ANY),
        scratch_shapes=[
            pltpu.VMEM((SPAN, width), queries.dtype),
            pltpu.SemaphoreType.DMA((4,)),
        ],
        compiler_params=pltpu.CompilerParams(vmem_limit_bytes=MOST_VMEM_BYTES),
        cost_estimate=cost_of(1.7),
    )(queries)


def places(lengths, slot_prompt, slot_span):
    replicas = lengths.shape[0]
    mine = lax.axis_index("replica")
    ring = jnp.arange(replicas, dtype=jnp.int32)
    place = jnp.where(mine % 2 == 0, mine // 2, replicas - 1 - mine // 2)
    at = (place + replicas - ring) % replicas
    other = jnp.where(at < replicas // 2, 2 * at, 2 * (replicas - at) - 1)
    chosen = other[:, None] == ring[None, :]
    wanted = chosen & (slot_prompt[None, :, 1] == mine) & (ring[:, None] > 0)
    spans = jnp.where(wanted, slot_span[None, :, 1] + 1, 0)
    whole = jnp.where(chosen & (ring[:, None] == 0), lengths[None, :] + 1, 0)
    return jnp.sum(spans + whole, axis=1) - 1


def widen(v_ref, wide_ref):
    for at in range(0, v_ref.shape[-1], HDIM):
        wide_ref[:, 2 * at : 2 * at + HDIM] = v_ref[:, at : at + HDIM]
        wide_ref[:, 2 * at + HDIM : 2 * at + 2 * HDIM] = jnp.ones(
            (v_ref.shape[0], HDIM), v_ref.dtype
        )


def stack(q_refs, stacked):
    kv_heads, rows, _ = stacked.shape
    group = rows // SPAN
    for shared in range(kv_heads):
        for h in range(group):
            at = (shared * group + h) * HDIM
            row = h * SPAN
            for q_ref in q_refs:
                many = q_ref.shape[0]
                stacked[shared, row : row + many, :] = q_ref[:, at : at + HDIM]
                row += many


def attend_span(span, stacked, k_ref, wide_ref, mixed, top, shifted):
    kv_heads, rows, _ = stacked.shape
    scale = LOG2E / math.sqrt(HDIM)
    blocks = span // (BLOCK // SPAN)
    edge = span % (BLOCK // SPAN) * SPAN

    def scores(shared, block, masked):
        keys = pl.ds(pl.multiple_of(block * BLOCK, BLOCK), BLOCK)
        found = lax.dot_general(
            stacked[shared],
            k_ref[keys, shared * HDIM : (shared + 1) * HDIM],
            (((1,), (1,)), ((), ())),
            preferred_element_type=jnp.float32,
        )
        if masked:
            row = lax.broadcasted_iota(jnp.int32, (rows, BLOCK), 0) % SPAN
            column = lax.broadcasted_iota(jnp.int32, (rows, BLOCK), 1)
            found = jnp.where(column <= row + edge, found, -jnp.inf)
        return found

    def products(shared, block, found):
        keys = pl.ds(pl.multiple_of(block * BLOCK, BLOCK), BLOCK)
        if shifted:
            found = found - jnp.concatenate([top[shared]] * (BLOCK // HDIM), axis=1)
        weights = jnp.exp2(found * scale).astype(jnp.bfloat16)
        return jnp.dot(
            weights,
            wide_ref[keys, 2 * shared * HDIM : 2 * (shared + 1) * HDIM],
            preferred_element_type=jnp.float32,
        )

    def widest(found):
        return functools.reduce(
            jnp.maximum, [found[:, at : at + HDIM] for at in range(0, BLOCK, HDIM)]
        )

    if shifted:
        for shared in range(kv_heads):
            top[shared] = widest(scores(shared, blocks, True))

            def look(block, carry, shared=shared):
                top[shared] = jnp.maximum(top[shared], widest(scores(shared, block, False)))
                return carry

            lax.fori_loop(0, blocks, look, 0)
            top[shared] = jnp.broadcast_to(
                jnp.max(top[shared], axis=1, keepdims=True), top.shape[1:]
            )

    found = [scores(shared, blocks, True) for shared in range(kv_heads)]
    for shared in range(kv_heads):
        mixed[shared] = products(shared, blocks, found[shared])

    def add(block, carry):
        found = [scores(shared, block, False) for shared in range(kv_heads)]
        for shared in range(kv_heads):
            mixed[shared] += products(shared, block, found[shared])
        return carry

    lax.fori_loop(0, blocks, add, 0)


def finish(mixed, o_ref, bounds):
    kv_heads, rows, _ = mixed.shape
    for shared in range(kv_heads):
        total = mixed[shared, :, HDIM:]
        inverse = pl.reciprocal(total, approx=True)
        inverse = inverse * (2.0 - total * inverse)
        result = (mixed[shared, :, :HDIM] * inverse).astype(o_ref.dtype)
        for h in range(rows // SPAN):
            at = (shared * rows // SPAN + h) * HDIM
            o_ref[:, at : at + HDIM] = result[h * SPAN : (h + 1) * SPAN, :]
        total = total.reshape(-1, 8, HDIM)
        bounds[0] = jnp.minimum(bounds[0], jnp.min(total, axis=0))
        bounds[1] = jnp.maximum(bounds[1], jnp.max(total, axis=0))


def twice_if_needed(work, drain, bounds):
    bounds[...] = jnp.ones_like(bounds)
    work(False)
    safe = (jnp.min(bounds[0]) > LEAST_SUM) & (jnp.max(bounds[1]) < MOST_SUM)
    drain()

    @pl.when(jnp.logical_not(safe))
    def _():
        work(True)
        drain()


def work_space(count, width, key_width):
    kv_heads = key_width // HDIM
    rows = width // key_width * SPAN
    return [
        pltpu.VMEM((count, kv_heads, rows, HDIM), jnp.bfloat16),
        pltpu.VMEM((kv_heads, rows, 2 * HDIM), jnp.float32),
        pltpu.VMEM((kv_heads, rows, HDIM), jnp.float32),
        pltpu.VMEM((2, 8, HDIM), jnp.float32),
    ]


def rows_of(span):
    return pl.ds(pl.multiple_of(span * SPAN, SPAN), SPAN)


def attend_blocks(dests, q_parts, k_ref, wide_ref, out_buf, store, stacked, mixed, top, bounds):
    count = len(dests)
    for j in range(count):

        @pl.when(dests[j] >= 0)
        def _(j=j):
            stack(q_parts[j], stacked.at[j])

    def work(shifted):
        def one(j, carry):
            dest = dests[0]
            for n in range(1, count):
                dest = jnp.where(j == n, dests[n], dest)

            @pl.when(dest >= 0)
            def _():
                attend_span(dest, stacked.at[j], k_ref, wide_ref, mixed, top, shifted)
                finish(mixed, out_buf.at[j], bounds)
                if store is not None:
                    store(j, dest).start()

            return carry

        lax.fori_loop(0, count, one, 0)

    def drain():
        if store is not None:
            for j in range(count):
                pl.when(dests[j] >= 0)(store(j, jnp.maximum(dests[j], 0)).wait)

    twice_if_needed(work, drain, bounds)


def stores(buf, o_ref, sems):
    return lambda j, span: pltpu.make_async_copy(buf.at[j], o_ref.at[rows_of(span)], sems.at[j])


def local_kernel(length_ref, q_hbm, k_hbm, v_hbm, o_ref, q_ref, k_ref, v_ref, wide, zeros, sems, out_buf, out_sems, *work):
    live = length_ref[lax.axis_index("replica")]
    fetches = [
        pltpu.make_async_copy(k_hbm, k_ref, sems.at[0]),
        pltpu.make_async_copy(v_hbm, v_ref, sems.at[MAXC]),
        pltpu.make_async_copy(q_hbm, q_ref, sems.at[MAXC + 1]),
    ]
    for copy in fetches:
        copy.start()
    zeros[...] = jnp.zeros_like(zeros)

    def clear(span):
        return pltpu.make_async_copy(zeros, o_ref.at[rows_of(span)], sems.at[span])

    for span in range(1, MAXC):
        pl.when(span >= live)(clear(span).start)
    for copy in fetches:
        copy.wait()
    widen(v_ref, wide)
    attend_blocks(
        [jnp.int32(0), jnp.where(live > 1, 1, -1)],
        [(q_ref.at[:SPAN],), (q_ref.at[SPAN:],)],
        k_ref,
        wide,
        out_buf,
        stores(out_buf, o_ref, out_sems),
        *work,
    )
    for span in range(1, MAXC):
        pl.when(span >= live)(clear(span).wait)


def attend_local(lengths, queries, keys, values):
    width, key_width = queries.shape[1], keys.shape[1]
    return pl.pallas_call(
        local_kernel,
        out_shape=jax.ShapeDtypeStruct((MAXC * SPAN, width), queries.dtype),
        in_specs=[SMEM, ANY, ANY, ANY],
        out_specs=ANY,
        scratch_shapes=[
            pltpu.VMEM(queries.shape, queries.dtype),
            pltpu.VMEM(keys.shape, keys.dtype),
            pltpu.VMEM(values.shape, values.dtype),
            pltpu.VMEM((SLOTS * SPAN, 2 * key_width), keys.dtype),
            pltpu.VMEM((SPAN, width), queries.dtype),
            pltpu.SemaphoreType.DMA((MAXC + 2,)),
            pltpu.VMEM((SLOTS, SPAN, width), queries.dtype),
            pltpu.SemaphoreType.DMA((SLOTS,)),
            *work_space(SLOTS, width, key_width),
        ],
        compiler_params=pltpu.CompilerParams(vmem_limit_bytes=MOST_VMEM_BYTES),
        cost_estimate=cost_of(0.3),
    )(lengths, queries, keys, values)


def parts_of(refs, pieces):
    return [refs[sum(pieces[:j]) : sum(pieces[: j + 1])] for j in range(len(pieces))]


def any_of(dests):
    return functools.reduce(jnp.maximum, dests) >= 0


def first_kernel(kv_offsets, offsets, pieces, meta_ref, own_k, own_v, *refs):
    parts = sum(pieces)
    blocks, refs = refs[: len(kv_offsets)], refs[len(kv_offsets) :]
    q_refs, refs = refs[:parts], refs[parts:]
    o_k, o_v, k_buf, wide, out_buf, v_buf, in_sems, out_sems, *work = refs
    live = meta_ref[0]

    def fetches():
        yield None, own_k.at[:SPAN], k_buf.at[rows_of(0)]
        yield None, own_v.at[:SPAN], v_buf.at[rows_of(0)]
        yield live > 1, own_k.at[SPAN:], k_buf.at[rows_of(1)]
        yield live > 1, own_v.at[SPAN:], v_buf.at[rows_of(1)]

    def each(act):
        for n, (needed, here, there) in enumerate(fetches()):
            copy = getattr(pltpu.make_async_copy(here, there, in_sems.at[n]), act)
            if needed is None:
                copy()
            else:
                pl.when(needed)(copy)

    each("start")
    for span in range(1, MAXC):

        @pl.when(span >= live)
        def _(span=span):
            k_buf[rows_of(span), :] = jnp.zeros((SPAN, k_buf.shape[1]), k_buf.dtype)
            v_buf[rows_of(span), :] = jnp.zeros((SPAN, v_buf.shape[1]), v_buf.dtype)

    for block, offset in zip(blocks, kv_offsets, strict=True):
        dest = meta_ref[offset]

        @pl.when(dest >= 0)
        def _(block=block, dest=dest):
            k_buf[rows_of(dest), :] = block[:SPAN, :]
            v_buf[rows_of(dest), :] = block[SPAN:, :]

    each("wait")
    copy_k = pltpu.make_async_copy(k_buf, o_k, out_sems.at[0])
    copy_v = pltpu.make_async_copy(v_buf, o_v, out_sems.at[1])
    copy_k.start()
    copy_v.start()
    dests = [meta_ref[offset] for offset in offsets]

    @pl.when(live > 1)
    def _():
        widen(v_buf, wide)

    @pl.when(any_of(dests))
    def _():
        attend_blocks(dests, parts_of(q_refs, pieces), k_buf, wide, out_buf, None, *work)

    copy_k.wait()
    copy_v.wait()


def attend_first(meta, keys, values, kv_offsets, kv_blocks, offsets, blocks):
    rows, key_width = MAXC * SPAN, keys.shape[1]
    pieces = [len(block) for block in blocks]
    count, width = len(pieces), blocks[0][0].shape[1]
    out = jax.ShapeDtypeStruct((rows, key_width), keys.dtype)
    return pl.pallas_call(
        lambda *refs: first_kernel(kv_offsets, offsets, pieces, *refs),
        out_shape=(
            out,
            out,
            out,
            jax.ShapeDtypeStruct((rows, 2 * key_width), keys.dtype),
            jax.ShapeDtypeStruct((count, SPAN, width), keys.dtype),
        ),
        in_specs=[SMEM, ANY, ANY] + [VMEM] * (len(kv_blocks) + sum(pieces)),
        out_specs=(ANY, ANY, VMEM, VMEM, VMEM),
        scratch_shapes=[
            pltpu.VMEM((rows, key_width), keys.dtype),
            pltpu.SemaphoreType.DMA((4,)),
            pltpu.SemaphoreType.DMA((2,)),
            *work_space(count, width, key_width),
        ],
        compiler_params=pltpu.CompilerParams(vmem_limit_bytes=VMEM_BYTES),
        cost_estimate=cost_of(2 + 2.5 * count),
    )(meta, keys, values, *kv_blocks, *[part for block in blocks for part in block])


def later_kernel(offsets, pieces, meta_ref, *refs):
    parts = sum(pieces)
    q_refs, (k_ref, wide_ref, out_buf, *work) = refs[:parts], refs[parts:]
    dests = [meta_ref[offset] for offset in offsets]

    @pl.when(any_of(dests))
    def _():
        attend_blocks(dests, parts_of(q_refs, pieces), k_ref, wide_ref, out_buf, None, *work)


def attend_later(meta, offsets, blocks, ordered_keys, wide_values):
    pieces = [len(block) for block in blocks]
    count, width = len(pieces), blocks[0][0].shape[1]
    return pl.pallas_call(
        lambda *refs: later_kernel(offsets, pieces, *refs),
        out_shape=jax.ShapeDtypeStruct((count, SPAN, width), ordered_keys.dtype),
        in_specs=[SMEM] + [VMEM] * (sum(pieces) + 2),
        out_specs=VMEM,
        scratch_shapes=work_space(count, width, ordered_keys.shape[1]),
        compiler_params=pltpu.CompilerParams(vmem_limit_bytes=VMEM_BYTES),
        cost_estimate=cost_of(1 + 2.5 * count),
    )(meta, *[part for block in blocks for part in block], ordered_keys, wide_values)


def last_kernel(before, offsets, pieces, meta_ref, *refs):
    parts = sum(pieces)
    results, refs = refs[: len(before)], refs[len(before) :]
    q_refs, (k_ref, wide_ref, _, o_ref, out_buf, sems, out_sems, *work) = refs[:parts], refs[parts:]
    earlier = [
        (meta_ref[offset], result, j, n)
        for n, (result, its_offsets) in enumerate(zip(results, before, strict=True))
        for j, offset in enumerate(its_offsets)
    ]

    def each(act):
        for dest, result, j, n in earlier:
            copy = pltpu.make_async_copy(
                result.at[j], o_ref.at[rows_of(jnp.maximum(dest, 0))], sems.at[n, j]
            )
            pl.when(dest >= 0)(getattr(copy, act))

    each("start")
    dests = [meta_ref[offset] for offset in offsets]

    @pl.when(any_of(dests))
    def _():
        attend_blocks(
            dests,
            parts_of(q_refs, pieces),
            k_ref,
            wide_ref,
            out_buf,
            stores(out_buf, o_ref, out_sems),
            *work,
        )

    each("wait")


def attend_last(meta, before, results, offsets, blocks, ordered_keys, wide_values, attention):
    pieces = [len(block) for block in blocks]
    count, parts = len(pieces), sum(pieces)
    width = attention.shape[1]
    most = max(len(its_offsets) for its_offsets in before)
    return pl.pallas_call(
        lambda *refs: last_kernel(before, offsets, pieces, *refs),
        out_shape=jax.ShapeDtypeStruct(attention.shape, attention.dtype),
        in_specs=[SMEM] + [VMEM] * (len(results) + parts + 2) + [ANY],
        out_specs=ANY,
        input_output_aliases={len(results) + parts + 3: 0},
        scratch_shapes=[
            pltpu.VMEM((count, SPAN, width), attention.dtype),
            pltpu.SemaphoreType.DMA((len(before), most)),
            pltpu.SemaphoreType.DMA((count,)),
            *work_space(count, width, ordered_keys.shape[1]),
        ],
        compiler_params=pltpu.CompilerParams(vmem_limit_bytes=VMEM_BYTES),
        cost_estimate=cost_of(4),
    )(
        meta,
        *results,
        *[part for block in blocks for part in block],
        ordered_keys,
        wide_values,
        attention,
    )


def gathered_kernel(meta_ref, first_ref, later_ref, k_ref, v_ref, o_ref, wide, stacked, mixed, top, bounds):
    at = pl.program_id(1)
    live = meta_ref[0]
    widen(v_ref, wide)

    @pl.when(at == 0)
    def _():
        stack((first_ref,), stacked.at[0])

    @pl.when(at > 0)
    def _():
        stack((later_ref.at[0],), stacked.at[0])

    def work(shifted):
        attend_span(at, stacked.at[0], k_ref, wide, mixed, top, shifted)
        finish(mixed, o_ref, bounds)

    @pl.when(at < live)
    def _():
        twice_if_needed(work, lambda: None, bounds)

    @pl.when(at >= live)
    def _():
        o_ref[...] = jnp.zeros_like(o_ref)


def attend_gathered(live, source, first, later, cache_keys, cache_values):
    home_rows, key_width = cache_keys.shape
    width = first.shape[1]
    groups = key_width // HDIM
    part = width // groups
    meta = jnp.concatenate([live.reshape(1), source]).astype(jnp.int32)
    return pl.pallas_call(
        gathered_kernel,
        out_shape=jax.ShapeDtypeStruct((home_rows, width), first.dtype),
        grid_spec=pltpu.PrefetchScalarGridSpec(
            num_scalar_prefetch=1,
            grid=(groups, MAXC),
            in_specs=[
                pl.BlockSpec((SPAN, part), lambda g, m, meta: (0, g)),
                pl.BlockSpec((1, SPAN, part), lambda g, m, meta: (meta[1 + m], 0, g)),
                pl.BlockSpec((home_rows, HDIM), lambda g, m, meta: (0, g)),
                pl.BlockSpec((home_rows, HDIM), lambda g, m, meta: (0, g)),
            ],
            out_specs=pl.BlockSpec((SPAN, part), lambda g, m, meta: (m, g)),
            scratch_shapes=[
                pltpu.VMEM((home_rows, 2 * HDIM), cache_keys.dtype),
                *work_space(1, part, HDIM),
            ],
        ),
        compiler_params=pltpu.CompilerParams(vmem_limit_bytes=VMEM_BYTES),
    )(meta, first, later, cache_keys, cache_values)


def gather_all(queries, keys, values, lengths, slot_prompt, slot_span):
    mine = lax.axis_index("replica")
    home_rows, key_width = MAXC * SPAN, keys.shape[1]
    live = lengths[mine]
    spans = jnp.arange(MAXC, dtype=jnp.int32)
    matches = (slot_prompt[None, :, 1] == mine) & (slot_span[None, :, 1] == spans[:, None])
    here = jnp.any(matches, axis=1)
    source = jnp.argmax(matches, axis=1).astype(jnp.int32)
    slots_k = lax.all_gather(keys[SPAN:], "replica")
    slots_v = lax.all_gather(values[SPAN:], "replica")
    slots_q = lax.all_gather(queries[SPAN:], "replica")

    def in_order(first, slots):
        picked = jnp.take(slots, source, axis=0)
        kept = jnp.where(here[:, None, None], picked, jnp.zeros((), slots.dtype))
        return jnp.concatenate([first, kept[1:].reshape(home_rows - SPAN, key_width)], axis=0)

    cache_keys = in_order(keys[:SPAN], slots_k)
    cache_values = in_order(values[:SPAN], slots_v)
    attention = attend_gathered(live, source, queries[:SPAN], slots_q, cache_keys, cache_values)
    return (attention, cache_keys, cache_values)


def per_device(queries, keys, values, lengths, slot_prompt, slot_span):
    replicas = lax.axis_size("replica")
    if replicas != 8:
        return gather_all(queries, keys, values, lengths, slot_prompt, slot_span)
    ring = column_ring(replicas)
    farthest = replicas // 2

    def after(block, *others):
        return lax.optimization_barrier((block, others))[0]

    def shift(block, step):
        pairs = [(r, ring[(n + step) % replicas]) for n, r in enumerate(ring)]
        return lax.ppermute(block, "replica", pairs)

    def go_on(both):
        return [shift(both[0], 1), shift(both[1], -1)]

    own_kv = pack_kv(keys, values)
    kv = [[own_kv, own_kv]]
    kv.append(go_on(kv[0]))
    own_top, own_bottom = pack_q(after(queries, own_kv))
    top, bottom = [[own_top, own_top]], [[own_bottom, own_bottom]]
    top.append(go_on(top[0]))
    kv.append(go_on(kv[1]))
    bottom.append(go_on([after(block, kv[1]) for block in bottom[0]]))
    attention = attend_local(lengths, after(queries, kv[1]), keys, values)
    kv.append(go_on([after(block, attention) for block in kv[2]]))
    top.append(go_on([after(block, kv[2]) for block in top[1]]))
    kv.append([shift(kv[3][0], 1)])
    bottom.append(go_on([after(block, kv[3]) for block in bottom[1]]))
    meta = places(lengths, slot_prompt, slot_span)
    offsets = [[n, replicas - n] for n in range(1, farthest)]

    def blocks(n):
        return list(zip(top[n], bottom[n], strict=True))

    cache_keys, cache_values, ordered_keys, wide_values, result = attend_first(
        meta, keys, values, sum(offsets, []) + [farthest], sum(kv[1:], []), offsets[0], blocks(1)
    )
    results = [result]
    top.append(go_on(top[2]))
    bottom.append(go_on([after(block, results[0]) for block in bottom[2]]))
    results.append(attend_later(meta, offsets[1], blocks(2), ordered_keys, wide_values))
    last = (
        shift(after(top[3][0], results[1]), 1),
        shift(after(bottom[3][1], results[1]), -1),
    )
    results.append(attend_later(meta, offsets[2], blocks(3), ordered_keys, wide_values))
    attention = attend_last(
        meta, offsets, results, [farthest], [last], ordered_keys, wide_values, attention
    )
    return (attention, cache_keys, cache_values)


def solution(mesh):
    in_specs = (
        P(("group", "replica"), "tensor"),
        P(("group", "replica"), "tensor"),
        P(("group", "replica"), "tensor"),
        P("group"),
        P("group", None),
        P("group", None),
    )
    out_specs = (
        P(("group", "replica"), "tensor"),
        P(("group", "replica"), "tensor"),
        P(("group", "replica"), "tensor"),
    )
    return jax.shard_map(
        per_device, mesh=mesh, in_specs=in_specs, out_specs=out_specs, check_vma=False
    )
```

```python
import functools
import math

import jax
import jax.numpy as jnp
from jax import lax
from jax.experimental import pallas as pl
from jax.experimental.pallas import tpu as pltpu
from jax.sharding import PartitionSpec as P

HDIM = 128
SPAN = 128
SLOTS = 2
MAXC = 8
BLOCK = 4
LOG2E = 1.0 / math.log(2.0)
VMEM_BYTES = 40 * 1024 * 1024
MOST_VMEM_BYTES = 60 * 1024 * 1024
LEAST_SUM, MOST_SUM = 1e-20, 1e30
ANY = pl.BlockSpec(memory_space=pl.ANY)
SMEM = pl.BlockSpec(memory_space=pltpu.SMEM)
VMEM = pl.BlockSpec(memory_space=pltpu.VMEM)


def cost_of(us):
    return pl.CostEstimate(flops=int(us * 1.15e9), bytes_accessed=0, transcendentals=0)


def column_ring(replicas):
    return list(range(0, replicas, 2)) + list(range(replicas - 1, 0, -2))


def pass_on(fetches, stores):
    for copy in fetches:
        copy.start()
    for copy in fetches:
        copy.wait()
    for copy in stores:
        copy.start()
    for copy in stores:
        copy.wait()


def pack_kv_kernel(k_ref, v_ref, o_ref, buf, sems):
    pass_on(
        [
            pltpu.make_async_copy(k_ref.at[SPAN:], buf.at[:SPAN], sems.at[0]),
            pltpu.make_async_copy(v_ref.at[SPAN:], buf.at[SPAN:], sems.at[1]),
        ],
        [pltpu.make_async_copy(buf, o_ref, sems.at[2])],
    )


def pack_kv(keys, values):
    shape = (2 * SPAN, keys.shape[1])
    return pl.pallas_call(
        pack_kv_kernel,
        out_shape=jax.ShapeDtypeStruct(shape, keys.dtype),
        in_specs=[ANY] * 2,
        out_specs=ANY,
        scratch_shapes=[pltpu.VMEM(shape, keys.dtype), pltpu.SemaphoreType.DMA((3,))],
        compiler_params=pltpu.CompilerParams(vmem_limit_bytes=MOST_VMEM_BYTES),
        cost_estimate=cost_of(1.7),
    )(keys, values)


def pack_q_kernel(q_ref, o_top, o_bottom, buf, sems):
    half = SPAN // 2
    pass_on(
        [
            pltpu.make_async_copy(q_ref.at[SPAN : SPAN + half], buf.at[:half], sems.at[0]),
            pltpu.make_async_copy(q_ref.at[SPAN + half :], buf.at[half:], sems.at[1]),
        ],
        [
            pltpu.make_async_copy(buf.at[:half], o_top, sems.at[2]),
            pltpu.make_async_copy(buf.at[half:], o_bottom, sems.at[3]),
        ],
    )


def pack_q(queries):
    width = queries.shape[1]
    half = jax.ShapeDtypeStruct((SPAN // 2, width), queries.dtype)
    return pl.pallas_call(
        pack_q_kernel,
        out_shape=(half, half),
        in_specs=[ANY],
        out_specs=(ANY, ANY),
        scratch_shapes=[
            pltpu.VMEM((SPAN, width), queries.dtype),
            pltpu.SemaphoreType.DMA((4,)),
        ],
        compiler_params=pltpu.CompilerParams(vmem_limit_bytes=MOST_VMEM_BYTES),
        cost_estimate=cost_of(1.7),
    )(queries)


def places(lengths, slot_prompt, slot_span):
    replicas = lengths.shape[0]
    mine = lax.axis_index("replica")
    ring = jnp.arange(replicas, dtype=jnp.int32)
    place = jnp.where(mine % 2 == 0, mine // 2, replicas - 1 - mine // 2)
    at = (place + replicas - ring) % replicas
    other = jnp.where(at < replicas // 2, 2 * at, 2 * (replicas - at) - 1)
    chosen = other[:, None] == ring[None, :]
    wanted = chosen & (slot_prompt[None, :, 1] == mine) & (ring[:, None] > 0)
    spans = jnp.where(wanted, slot_span[None, :, 1] + 1, 0)
    whole = jnp.where(chosen & (ring[:, None] == 0), lengths[None, :] + 1, 0)
    return jnp.sum(spans + whole, axis=1) - 1


def widen(v_ref, wide_ref):
    for at in range(0, v_ref.shape[-1], HDIM):
        wide_ref[:, 2 * at : 2 * at + HDIM] = v_ref[:, at : at + HDIM]
        wide_ref[:, 2 * at + HDIM : 2 * at + 2 * HDIM] = jnp.ones(
            (v_ref.shape[0], HDIM), v_ref.dtype
        )


def stack(q_refs, stacked):
    kv_heads, rows, _ = stacked.shape
    group = rows // SPAN
    for shared in range(kv_heads):
        for h in range(group):
            at = (shared * group + h) * HDIM
            row = h * SPAN
            for q_ref in q_refs:
                many = q_ref.shape[0]
                stacked[shared, row : row + many, :] = q_ref[:, at : at + HDIM]
                row += many


def attend_span(span, stacked, k_ref, wide_ref, mixed, top, shifted):
    kv_heads, rows, _ = stacked.shape
    heads = range(kv_heads)
    scale = LOG2E / math.sqrt(HDIM)
    blocks = span // BLOCK

    def keys_of(block, spans):
        return pl.ds(pl.multiple_of(block * BLOCK * SPAN, BLOCK * SPAN), spans * SPAN)

    def scores(shared, block, spans, masked):
        found = lax.dot_general(
            stacked[shared],
            k_ref[keys_of(block, spans), shared * HDIM : (shared + 1) * HDIM],
            (((1,), (1,)), ((), ())),
            preferred_element_type=jnp.float32,
        )
        if masked:
            row = lax.broadcasted_iota(jnp.int32, (rows, SPAN), 0) % SPAN
            column = lax.broadcasted_iota(jnp.int32, (rows, SPAN), 1)
            edge = jnp.where(column <= row, found[:, -SPAN:], -jnp.inf)
            found = jnp.concatenate([found[:, :-SPAN], edge], axis=1) if spans > 1 else edge
        return found

    def products(shared, block, spans, found):
        if shifted:
            found = found - jnp.concatenate([top[shared]] * spans, axis=1)
        weights = jnp.exp2(found * scale).astype(jnp.bfloat16)
        return jnp.dot(
            weights,
            wide_ref[keys_of(block, spans), 2 * shared * HDIM : 2 * (shared + 1) * HDIM],
            preferred_element_type=jnp.float32,
        )

    def widest(found):
        columns = [found[:, at : at + HDIM] for at in range(0, found.shape[1], HDIM)]
        return functools.reduce(jnp.maximum, columns)

    def remainder(act):
        for spans in range(1, BLOCK + 1):
            pl.when(span % BLOCK == spans - 1)(functools.partial(act, spans))

    if shifted:

        def look_first(spans):
            for shared in heads:
                top[shared] = widest(scores(shared, blocks, spans, True))

        def look(block, carry):
            for shared in heads:
                found = widest(scores(shared, block, BLOCK, False))
                top[shared] = jnp.maximum(top[shared], found)
            return carry

        remainder(look_first)
        lax.fori_loop(0, blocks, look, 0)
        for shared in heads:
            most = jnp.max(top[shared], axis=1, keepdims=True)
            top[shared] = jnp.broadcast_to(most, top.shape[1:])

    def first(spans):
        found = [scores(shared, blocks, spans, True) for shared in heads]
        for shared in heads:
            mixed[shared] = products(shared, blocks, spans, found[shared])

    def add(block, carry):
        found = [scores(shared, block, BLOCK, False) for shared in heads]
        for shared in heads:
            mixed[shared] += products(shared, block, BLOCK, found[shared])
        return carry

    remainder(first)
    lax.fori_loop(0, blocks, add, 0)


def finish(mixed, o_ref, bounds):
    kv_heads, rows, _ = mixed.shape
    for shared in range(kv_heads):
        total = mixed[shared, :, HDIM:]
        inverse = pl.reciprocal(total, approx=True)
        inverse = inverse * (2.0 - total * inverse)
        result = (mixed[shared, :, :HDIM] * inverse).astype(o_ref.dtype)
        for h in range(rows // SPAN):
            at = (shared * rows // SPAN + h) * HDIM
            o_ref[:, at : at + HDIM] = result[h * SPAN : (h + 1) * SPAN, :]
        total = total.reshape(-1, 8, HDIM)
        bounds[0] = jnp.minimum(bounds[0], jnp.min(total, axis=0))
        bounds[1] = jnp.maximum(bounds[1], jnp.max(total, axis=0))


def twice_if_needed(work, drain, bounds):
    bounds[...] = jnp.ones_like(bounds)
    work(False)
    safe = (jnp.min(bounds[0]) > LEAST_SUM) & (jnp.max(bounds[1]) < MOST_SUM)
    drain()

    @pl.when(jnp.logical_not(safe))
    def _():
        work(True)
        drain()


def work_space(count, width, key_width):
    kv_heads = key_width // HDIM
    rows = width // key_width * SPAN
    return [
        pltpu.VMEM((count, kv_heads, rows, HDIM), jnp.bfloat16),
        pltpu.VMEM((kv_heads, rows, 2 * HDIM), jnp.float32),
        pltpu.VMEM((kv_heads, rows, HDIM), jnp.float32),
        pltpu.VMEM((2, 8, HDIM), jnp.float32),
    ]


def rows_of(span):
    return pl.ds(pl.multiple_of(span * SPAN, SPAN), SPAN)


def attend_blocks(dests, q_parts, k_ref, wide_ref, out_buf, store, stacked, mixed, top, bounds):
    count = len(dests)
    for j in range(count):

        @pl.when(dests[j] >= 0)
        def _(j=j):
            stack(q_parts[j], stacked.at[j])

    def work(shifted):
        def one(j, carry):
            dest = dests[0]
            for n in range(1, count):
                dest = jnp.where(j == n, dests[n], dest)

            @pl.when(dest >= 0)
            def _():
                attend_span(dest, stacked.at[j], k_ref, wide_ref, mixed, top, shifted)
                finish(mixed, out_buf.at[j], bounds)
                if store is not None:
                    store(j, dest).start()

            return carry

        lax.fori_loop(0, count, one, 0)

    def drain():
        if store is not None:
            for j in range(count):
                pl.when(dests[j] >= 0)(store(j, jnp.maximum(dests[j], 0)).wait)

    twice_if_needed(work, drain, bounds)


def stores(buf, o_ref, sems):
    return lambda j, span: pltpu.make_async_copy(buf.at[j], o_ref.at[rows_of(span)], sems.at[j])


def local_kernel(length_ref, q_hbm, k_hbm, v_hbm, o_ref, q_ref, k_ref, v_ref, wide, zeros, sems, out_buf, out_sems, *work):
    live = length_ref[lax.axis_index("replica")]
    fetches = [
        pltpu.make_async_copy(k_hbm, k_ref, sems.at[0]),
        pltpu.make_async_copy(v_hbm, v_ref, sems.at[MAXC]),
        pltpu.make_async_copy(q_hbm, q_ref, sems.at[MAXC + 1]),
    ]
    for copy in fetches:
        copy.start()
    zeros[...] = jnp.zeros_like(zeros)

    def clear(span):
        return pltpu.make_async_copy(zeros, o_ref.at[rows_of(span)], sems.at[span])

    for span in range(1, MAXC):
        pl.when(span >= live)(clear(span).start)
    for copy in fetches:
        copy.wait()
    widen(v_ref, wide)
    attend_blocks(
        [jnp.int32(0), jnp.where(live > 1, 1, -1)],
        [(q_ref.at[:SPAN],), (q_ref.at[SPAN:],)],
        k_ref,
        wide,
        out_buf,
        stores(out_buf, o_ref, out_sems),
        *work,
    )
    for span in range(1, MAXC):
        pl.when(span >= live)(clear(span).wait)


def attend_local(lengths, queries, keys, values):
    width, key_width = queries.shape[1], keys.shape[1]
    return pl.pallas_call(
        local_kernel,
        out_shape=jax.ShapeDtypeStruct((MAXC * SPAN, width), queries.dtype),
        in_specs=[SMEM, ANY, ANY, ANY],
        out_specs=ANY,
        scratch_shapes=[
            pltpu.VMEM(queries.shape, queries.dtype),
            pltpu.VMEM(keys.shape, keys.dtype),
            pltpu.VMEM(values.shape, values.dtype),
            pltpu.VMEM((SLOTS * SPAN, 2 * key_width), keys.dtype),
            pltpu.VMEM((SPAN, width), queries.dtype),
            pltpu.SemaphoreType.DMA((MAXC + 2,)),
            pltpu.VMEM((SLOTS, SPAN, width), queries.dtype),
            pltpu.SemaphoreType.DMA((SLOTS,)),
            *work_space(SLOTS, width, key_width),
        ],
        compiler_params=pltpu.CompilerParams(vmem_limit_bytes=MOST_VMEM_BYTES),
        cost_estimate=cost_of(5),
    )(lengths, queries, keys, values)


def parts_of(refs, pieces):
    return [refs[sum(pieces[:j]) : sum(pieces[: j + 1])] for j in range(len(pieces))]


def any_of(dests):
    return functools.reduce(jnp.maximum, dests) >= 0


def first_kernel(kv_offsets, offsets, pieces, meta_ref, own_k, own_v, *refs):
    parts = sum(pieces)
    blocks, refs = refs[: len(kv_offsets)], refs[len(kv_offsets) :]
    q_refs, refs = refs[:parts], refs[parts:]
    o_k, o_v, k_buf, wide, out_buf, v_buf, in_sems, out_sems, *work = refs
    live = meta_ref[0]

    def fetches():
        yield None, own_k.at[:SPAN], k_buf.at[rows_of(0)]
        yield None, own_v.at[:SPAN], v_buf.at[rows_of(0)]
        yield live > 1, own_k.at[SPAN:], k_buf.at[rows_of(1)]
        yield live > 1, own_v.at[SPAN:], v_buf.at[rows_of(1)]

    def each(act):
        for n, (needed, here, there) in enumerate(fetches()):
            copy = getattr(pltpu.make_async_copy(here, there, in_sems.at[n]), act)
            if needed is None:
                copy()
            else:
                pl.when(needed)(copy)

    each("start")
    for span in range(1, MAXC):

        @pl.when(span >= live)
        def _(span=span):
            k_buf[rows_of(span), :] = jnp.zeros((SPAN, k_buf.shape[1]), k_buf.dtype)
            v_buf[rows_of(span), :] = jnp.zeros((SPAN, v_buf.shape[1]), v_buf.dtype)

    for block, offset in zip(blocks, kv_offsets, strict=True):
        dest = meta_ref[offset]

        @pl.when(dest >= 0)
        def _(block=block, dest=dest):
            k_buf[rows_of(dest), :] = block[:SPAN, :]
            v_buf[rows_of(dest), :] = block[SPAN:, :]

    each("wait")
    copy_k = pltpu.make_async_copy(k_buf, o_k, out_sems.at[0])
    copy_v = pltpu.make_async_copy(v_buf, o_v, out_sems.at[1])
    copy_k.start()
    copy_v.start()
    dests = [meta_ref[offset] for offset in offsets]

    @pl.when(live > 1)
    def _():
        widen(v_buf, wide)

    @pl.when(any_of(dests))
    def _():
        attend_blocks(dests, parts_of(q_refs, pieces), k_buf, wide, out_buf, None, *work)

    copy_k.wait()
    copy_v.wait()


def attend_first(meta, keys, values, kv_offsets, kv_blocks, offsets, blocks):
    rows, key_width = MAXC * SPAN, keys.shape[1]
    pieces = [len(block) for block in blocks]
    count, width = len(pieces), blocks[0][0].shape[1]
    out = jax.ShapeDtypeStruct((rows, key_width), keys.dtype)
    return pl.pallas_call(
        lambda *refs: first_kernel(kv_offsets, offsets, pieces, *refs),
        out_shape=(
            out,
            out,
            out,
            jax.ShapeDtypeStruct((rows, 2 * key_width), keys.dtype),
            jax.ShapeDtypeStruct((count, SPAN, width), keys.dtype),
        ),
        in_specs=[SMEM, ANY, ANY] + [VMEM] * (len(kv_blocks) + sum(pieces)),
        out_specs=(ANY, ANY, VMEM, VMEM, VMEM),
        scratch_shapes=[
            pltpu.VMEM((rows, key_width), keys.dtype),
            pltpu.SemaphoreType.DMA((4,)),
            pltpu.SemaphoreType.DMA((2,)),
            *work_space(count, width, key_width),
        ],
        compiler_params=pltpu.CompilerParams(vmem_limit_bytes=VMEM_BYTES),
        cost_estimate=cost_of(1 * (2 + 2.5 * count)),
    )(meta, keys, values, *kv_blocks, *[part for block in blocks for part in block])


def later_kernel(offsets, pieces, meta_ref, *refs):
    parts = sum(pieces)
    q_refs, (k_ref, wide_ref, out_buf, *work) = refs[:parts], refs[parts:]
    dests = [meta_ref[offset] for offset in offsets]

    @pl.when(any_of(dests))
    def _():
        attend_blocks(dests, parts_of(q_refs, pieces), k_ref, wide_ref, out_buf, None, *work)


def attend_later(meta, offsets, blocks, ordered_keys, wide_values):
    pieces = [len(block) for block in blocks]
    count, width = len(pieces), blocks[0][0].shape[1]
    return pl.pallas_call(
        lambda *refs: later_kernel(offsets, pieces, *refs),
        out_shape=jax.ShapeDtypeStruct((count, SPAN, width), ordered_keys.dtype),
        in_specs=[SMEM] + [VMEM] * (sum(pieces) + 2),
        out_specs=VMEM,
        scratch_shapes=work_space(count, width, ordered_keys.shape[1]),
        compiler_params=pltpu.CompilerParams(vmem_limit_bytes=VMEM_BYTES),
        cost_estimate=cost_of(1 * (1 + 2.5 * count)),
    )(meta, *[part for block in blocks for part in block], ordered_keys, wide_values)


def last_kernel(before, offsets, pieces, meta_ref, *refs):
    parts = sum(pieces)
    results, refs = refs[: len(before)], refs[len(before) :]
    q_refs, (k_ref, wide_ref, _, o_ref, out_buf, sems, out_sems, *work) = refs[:parts], refs[parts:]
    earlier = [
        (meta_ref[offset], result, j, n)
        for n, (result, its_offsets) in enumerate(zip(results, before, strict=True))
        for j, offset in enumerate(its_offsets)
    ]

    def each(act):
        for dest, result, j, n in earlier:
            copy = pltpu.make_async_copy(
                result.at[j], o_ref.at[rows_of(jnp.maximum(dest, 0))], sems.at[n, j]
            )
            pl.when(dest >= 0)(getattr(copy, act))

    each("start")
    dests = [meta_ref[offset] for offset in offsets]

    @pl.when(any_of(dests))
    def _():
        attend_blocks(
            dests,
            parts_of(q_refs, pieces),
            k_ref,
            wide_ref,
            out_buf,
            stores(out_buf, o_ref, out_sems),
            *work,
        )

    each("wait")


def attend_last(meta, before, results, offsets, blocks, ordered_keys, wide_values, attention):
    pieces = [len(block) for block in blocks]
    count, parts = len(pieces), sum(pieces)
    width = attention.shape[1]
    most = max(len(its_offsets) for its_offsets in before)
    return pl.pallas_call(
        lambda *refs: last_kernel(before, offsets, pieces, *refs),
        out_shape=jax.ShapeDtypeStruct(attention.shape, attention.dtype),
        in_specs=[SMEM] + [VMEM] * (len(results) + parts + 2) + [ANY],
        out_specs=ANY,
        input_output_aliases={len(results) + parts + 3: 0},
        scratch_shapes=[
            pltpu.VMEM((count, SPAN, width), attention.dtype),
            pltpu.SemaphoreType.DMA((len(before), most)),
            pltpu.SemaphoreType.DMA((count,)),
            *work_space(count, width, ordered_keys.shape[1]),
        ],
        compiler_params=pltpu.CompilerParams(vmem_limit_bytes=VMEM_BYTES),
        cost_estimate=cost_of(4),
    )(
        meta,
        *results,
        *[part for block in blocks for part in block],
        ordered_keys,
        wide_values,
        attention,
    )


def gathered_kernel(meta_ref, first_ref, later_ref, k_ref, v_ref, o_ref, wide, stacked, mixed, top, bounds):
    at = pl.program_id(1)
    live = meta_ref[0]
    widen(v_ref, wide)

    @pl.when(at == 0)
    def _():
        stack((first_ref,), stacked.at[0])

    @pl.when(at > 0)
    def _():
        stack((later_ref.at[0],), stacked.at[0])

    def work(shifted):
        attend_span(at, stacked.at[0], k_ref, wide, mixed, top, shifted)
        finish(mixed, o_ref, bounds)

    @pl.when(at < live)
    def _():
        twice_if_needed(work, lambda: None, bounds)

    @pl.when(at >= live)
    def _():
        o_ref[...] = jnp.zeros_like(o_ref)


def attend_gathered(live, source, first, later, cache_keys, cache_values):
    home_rows, key_width = cache_keys.shape
    width = first.shape[1]
    groups = key_width // HDIM
    part = width // groups
    meta = jnp.concatenate([live.reshape(1), source]).astype(jnp.int32)
    return pl.pallas_call(
        gathered_kernel,
        out_shape=jax.ShapeDtypeStruct((home_rows, width), first.dtype),
        grid_spec=pltpu.PrefetchScalarGridSpec(
            num_scalar_prefetch=1,
            grid=(groups, MAXC),
            in_specs=[
                pl.BlockSpec((SPAN, part), lambda g, m, meta: (0, g)),
                pl.BlockSpec((1, SPAN, part), lambda g, m, meta: (meta[1 + m], 0, g)),
                pl.BlockSpec((home_rows, HDIM), lambda g, m, meta: (0, g)),
                pl.BlockSpec((home_rows, HDIM), lambda g, m, meta: (0, g)),
            ],
            out_specs=pl.BlockSpec((SPAN, part), lambda g, m, meta: (m, g)),
            scratch_shapes=[
                pltpu.VMEM((home_rows, 2 * HDIM), cache_keys.dtype),
                *work_space(1, part, HDIM),
            ],
        ),
        compiler_params=pltpu.CompilerParams(vmem_limit_bytes=VMEM_BYTES),
    )(meta, first, later, cache_keys, cache_values)


def gather_all(queries, keys, values, lengths, slot_prompt, slot_span):
    mine = lax.axis_index("replica")
    home_rows, key_width = MAXC * SPAN, keys.shape[1]
    live = lengths[mine]
    spans = jnp.arange(MAXC, dtype=jnp.int32)
    matches = (slot_prompt[None, :, 1] == mine) & (slot_span[None, :, 1] == spans[:, None])
    here = jnp.any(matches, axis=1)
    source = jnp.argmax(matches, axis=1).astype(jnp.int32)
    slots_k = lax.all_gather(keys[SPAN:], "replica")
    slots_v = lax.all_gather(values[SPAN:], "replica")
    slots_q = lax.all_gather(queries[SPAN:], "replica")

    def in_order(first, slots):
        picked = jnp.take(slots, source, axis=0)
        kept = jnp.where(here[:, None, None], picked, jnp.zeros((), slots.dtype))
        return jnp.concatenate([first, kept[1:].reshape(home_rows - SPAN, key_width)], axis=0)

    cache_keys = in_order(keys[:SPAN], slots_k)
    cache_values = in_order(values[:SPAN], slots_v)
    attention = attend_gathered(live, source, queries[:SPAN], slots_q, cache_keys, cache_values)
    return (attention, cache_keys, cache_values)


def per_device(queries, keys, values, lengths, slot_prompt, slot_span):
    replicas = lax.axis_size("replica")
    if replicas != 8:
        return gather_all(queries, keys, values, lengths, slot_prompt, slot_span)
    ring = column_ring(replicas)
    farthest = replicas // 2

    def after(block, *others):
        return lax.optimization_barrier((block, others))[0]

    def joined(both):
        return list(lax.optimization_barrier(tuple(both)))

    def shift(block, step):
        pairs = [(r, ring[(n + step) % replicas]) for n, r in enumerate(ring)]
        return lax.ppermute(block, "replica", pairs)

    def go_on(both):
        return [shift(both[0], 1), shift(both[1], -1)]

    own_kv = pack_kv(keys, values)
    kv = [[own_kv, own_kv]]
    kv.append(go_on(kv[0]))
    own_top, own_bottom = pack_q(after(queries, own_kv))
    top, bottom = [[own_top, own_top]], [[own_bottom, own_bottom]]
    top.append(joined(go_on(top[0])))
    kv[1] = joined(kv[1])
    kv.append(joined(go_on(kv[1])))
    attention = attend_local(lengths, after(queries, kv[1]), keys, values)
    bottom.append(joined(go_on([after(block, top[1]) for block in bottom[0]])))
    kv.append(joined(go_on([after(block, attention) for block in kv[2]])))
    top.append(joined(go_on([after(block, kv[3]) for block in top[1]])))
    kv.append([shift(kv[3][0], 1)])
    bottom.append(joined(go_on([after(block, kv[3]) for block in bottom[1]])))
    meta = places(lengths, slot_prompt, slot_span)
    offsets = [[n, replicas - n] for n in range(1, farthest)]

    def blocks(n):
        return list(zip(top[n], bottom[n], strict=True))

    cache_keys, cache_values, ordered_keys, wide_values, result = attend_first(
        meta, keys, values, sum(offsets, []) + [farthest], sum(kv[1:], []), offsets[0], blocks(1)
    )
    results = [result]
    top.append(joined(go_on(top[2])))
    bottom.append(joined(go_on([after(block, results[0]) for block in bottom[2]])))
    results.append(attend_later(meta, offsets[1], blocks(2), ordered_keys, wide_values))
    last = (
        shift(after(top[3][0], results[1]), 1),
        shift(after(bottom[3][1], results[1]), -1),
    )
    results.append(attend_later(meta, offsets[2], blocks(3), ordered_keys, wide_values))
    attention = attend_last(
        meta, offsets, results, [farthest], [last], ordered_keys, wide_values, attention
    )
    return (attention, cache_keys, cache_values)


def solution(mesh):
    in_specs = (
        P(("group", "replica"), "tensor"),
        P(("group", "replica"), "tensor"),
        P(("group", "replica"), "tensor"),
        P("group"),
        P("group", None),
        P("group", None),
    )
    out_specs = (
        P(("group", "replica"), "tensor"),
        P(("group", "replica"), "tensor"),
        P(("group", "replica"), "tensor"),
    )
    return jax.shard_map(
        per_device, mesh=mesh, in_specs=in_specs, out_specs=out_specs, check_vma=False
    )
```

```python
import functools
import math

import jax
import jax.numpy as jnp
from jax import lax
from jax.experimental import pallas as pl
from jax.experimental.pallas import tpu as pltpu
from jax.sharding import PartitionSpec as P

HDIM = 128
SPAN = 128
SLOTS = 2
MAXC = 8
BLOCK = 4
PART = 2
LOG2E = 1.0 / math.log(2.0)
VMEM_BYTES = 40 * 1024 * 1024
MOST_VMEM_BYTES = 60 * 1024 * 1024
LEAST_SUM, MOST_SUM = 1e-20, 1e30
ANY = pl.BlockSpec(memory_space=pl.ANY)
SMEM = pl.BlockSpec(memory_space=pltpu.SMEM)
VMEM = pl.BlockSpec(memory_space=pltpu.VMEM)


def cost_of(us):
    return pl.CostEstimate(flops=int(us * 1.15e9), bytes_accessed=0, transcendentals=0)


def column_ring(replicas):
    return list(range(0, replicas, 2)) + list(range(replicas - 1, 0, -2))


def pass_on(fetches, stores):
    for copy in fetches:
        copy.start()
    for copy in fetches:
        copy.wait()
    for copy in stores:
        copy.start()
    for copy in stores:
        copy.wait()


def pack_kv_kernel(k_ref, v_ref, o_ref, buf, sems):
    pass_on(
        [
            pltpu.make_async_copy(k_ref.at[SPAN:], buf.at[:SPAN], sems.at[0]),
            pltpu.make_async_copy(v_ref.at[SPAN:], buf.at[SPAN:], sems.at[1]),
        ],
        [pltpu.make_async_copy(buf, o_ref, sems.at[2])],
    )


def pack_kv(keys, values):
    shape = (2 * SPAN, keys.shape[1])
    return pl.pallas_call(
        pack_kv_kernel,
        out_shape=jax.ShapeDtypeStruct(shape, keys.dtype),
        in_specs=[ANY] * 2,
        out_specs=ANY,
        scratch_shapes=[pltpu.VMEM(shape, keys.dtype), pltpu.SemaphoreType.DMA((3,))],
        compiler_params=pltpu.CompilerParams(vmem_limit_bytes=MOST_VMEM_BYTES),
        cost_estimate=cost_of(1.7),
    )(keys, values)


def pack_q_kernel(q_ref, o_top, o_bottom, buf, sems):
    half = SPAN // 2
    pass_on(
        [
            pltpu.make_async_copy(q_ref.at[SPAN : SPAN + half], buf.at[:half], sems.at[0]),
            pltpu.make_async_copy(q_ref.at[SPAN + half :], buf.at[half:], sems.at[1]),
        ],
        [
            pltpu.make_async_copy(buf.at[:half], o_top, sems.at[2]),
            pltpu.make_async_copy(buf.at[half:], o_bottom, sems.at[3]),
        ],
    )


def pack_q(queries):
    width = queries.shape[1]
    half = jax.ShapeDtypeStruct((SPAN // 2, width), queries.dtype)
    return pl.pallas_call(
        pack_q_kernel,
        out_shape=(half, half),
        in_specs=[ANY],
        out_specs=(ANY, ANY),
        scratch_shapes=[
            pltpu.VMEM((SPAN, width), queries.dtype),
            pltpu.SemaphoreType.DMA((4,)),
        ],
        compiler_params=pltpu.CompilerParams(vmem_limit_bytes=MOST_VMEM_BYTES),
        cost_estimate=cost_of(1.7),
    )(queries)


def places(lengths, slot_prompt, slot_span):
    replicas = lengths.shape[0]
    mine = lax.axis_index("replica")
    ring = jnp.arange(replicas, dtype=jnp.int32)
    place = jnp.where(mine % 2 == 0, mine // 2, replicas - 1 - mine // 2)
    at = (place + replicas - ring) % replicas
    other = jnp.where(at < replicas // 2, 2 * at, 2 * (replicas - at) - 1)
    chosen = other[:, None] == ring[None, :]
    wanted = chosen & (slot_prompt[None, :, 1] == mine) & (ring[:, None] > 0)
    spans = jnp.where(wanted, slot_span[None, :, 1] + 1, 0)
    whole = jnp.where(chosen & (ring[:, None] == 0), lengths[None, :] + 1, 0)
    return jnp.sum(spans + whole, axis=1) - 1


def widen(v_ref, wide_ref):
    for at in range(0, v_ref.shape[-1], HDIM):
        wide_ref[:, 2 * at : 2 * at + HDIM] = v_ref[:, at : at + HDIM]
        wide_ref[:, 2 * at + HDIM : 2 * at + 2 * HDIM] = jnp.ones(
            (v_ref.shape[0], HDIM), v_ref.dtype
        )


def stack(q_refs, stacked):
    kv_heads, rows, _ = stacked.shape
    group = rows // SPAN
    for shared in range(kv_heads):
        for h in range(group):
            at = (shared * group + h) * HDIM
            row = h * SPAN
            for q_ref in q_refs:
                many = q_ref.shape[0]
                stacked[shared, row : row + many, :] = q_ref[:, at : at + HDIM]
                row += many


def attend_span(span, stacked, k_ref, wide_ref, mixed):
    kv_heads, rows, _ = stacked.shape
    heads = range(kv_heads)
    scale = LOG2E / math.sqrt(HDIM)
    blocks = span // BLOCK
    edge = span % PART * SPAN

    def keys_of(block, spans):
        return pl.ds(pl.multiple_of(block * BLOCK * SPAN, BLOCK * SPAN), spans * SPAN)

    def scores(shared, block, spans, masked):
        found = lax.dot_general(
            stacked[shared],
            k_ref[keys_of(block, spans), shared * HDIM : (shared + 1) * HDIM],
            (((1,), (1,)), ((), ())),
            preferred_element_type=jnp.float32,
        )
        if masked:
            seen = (spans - PART) * SPAN
            row = lax.broadcasted_iota(jnp.int32, (rows, PART * SPAN), 0) % SPAN
            column = lax.broadcasted_iota(jnp.int32, (rows, PART * SPAN), 1)
            last = jnp.where(column <= row + edge, found[:, seen:], -jnp.inf)
            found = jnp.concatenate([found[:, :seen], last], axis=1) if seen else last
        return found

    def products(shared, block, spans, found):
        return jnp.dot(
            jnp.exp2(found * scale).astype(jnp.bfloat16),
            wide_ref[keys_of(block, spans), 2 * shared * HDIM : 2 * (shared + 1) * HDIM],
            preferred_element_type=jnp.float32,
        )

    most = k_ref.shape[0] // SPAN
    for spans in range(PART, min(BLOCK, most) + 1, PART):

        @pl.when(span % BLOCK // PART == spans // PART - 1)
        def _(spans=spans):
            found = [scores(shared, blocks, spans, True) for shared in heads]
            for shared in heads:
                mixed[shared] = products(shared, blocks, spans, found[shared])

    def add(block, carry):
        found = [scores(shared, block, BLOCK, False) for shared in heads]
        for shared in heads:
            mixed[shared] += products(shared, block, BLOCK, found[shared])
        return carry

    if most > BLOCK:
        lax.fori_loop(0, blocks, add, 0)


def attend_span_shifted(span, stacked, k_ref, wide_ref, mixed, top):
    kv_heads, rows, _ = stacked.shape
    scale = LOG2E / math.sqrt(HDIM)

    def one_head(shared, carry):
        def scores(block):
            found = lax.dot_general(
                stacked[shared],
                k_ref[rows_of(block), pl.ds(pl.multiple_of(shared * HDIM, HDIM), HDIM)],
                (((1,), (1,)), ((), ())),
                preferred_element_type=jnp.float32,
            )
            row = lax.broadcasted_iota(jnp.int32, (rows, SPAN), 0) % SPAN
            column = lax.broadcasted_iota(jnp.int32, (rows, SPAN), 1)
            return jnp.where(column <= row + (span - block) * SPAN, found, -jnp.inf)

        def look(block, carry):
            top[...] = jnp.maximum(top[...], scores(block))
            return carry

        def add(block, carry):
            weights = jnp.exp2((scores(block) - top[...]) * scale).astype(jnp.bfloat16)
            mixed[shared] += jnp.dot(
                weights,
                wide_ref[
                    rows_of(block), pl.ds(pl.multiple_of(2 * shared * HDIM, 2 * HDIM), 2 * HDIM)
                ],
                preferred_element_type=jnp.float32,
            )
            return carry

        top[...] = jnp.full_like(top, -jnp.inf)
        lax.fori_loop(0, span + 1, look, 0)
        top[...] = jnp.broadcast_to(jnp.max(top[...], axis=1, keepdims=True), top.shape)
        mixed[shared] = jnp.zeros(mixed.shape[1:], mixed.dtype)
        lax.fori_loop(0, span + 1, add, 0)
        return carry

    lax.fori_loop(0, kv_heads, one_head, 0)


def finish(mixed, o_ref, bounds):
    kv_heads, rows, _ = mixed.shape
    for shared in range(kv_heads):
        total = mixed[shared, :, HDIM:]
        inverse = pl.reciprocal(total, approx=True)
        inverse = inverse * (2.0 - total * inverse)
        result = (mixed[shared, :, :HDIM] * inverse).astype(o_ref.dtype)
        for h in range(rows // SPAN):
            at = (shared * rows // SPAN + h) * HDIM
            o_ref[:, at : at + HDIM] = result[h * SPAN : (h + 1) * SPAN, :]
        total = total.reshape(-1, 8, HDIM)
        bounds[0] = jnp.minimum(bounds[0], jnp.min(total, axis=0))
        bounds[1] = jnp.maximum(bounds[1], jnp.max(total, axis=0))


def twice_if_needed(work, drain, bounds):
    bounds[...] = jnp.ones_like(bounds)
    work(False)
    safe = (jnp.min(bounds[0]) > LEAST_SUM) & (jnp.max(bounds[1]) < MOST_SUM)
    drain()

    @pl.when(jnp.logical_not(safe))
    def _():
        work(True)
        drain()


def work_space(count, width, key_width):
    kv_heads = key_width // HDIM
    rows = width // key_width * SPAN
    return [
        pltpu.VMEM((count, kv_heads, rows, HDIM), jnp.bfloat16),
        pltpu.VMEM((kv_heads, rows, 2 * HDIM), jnp.float32),
        pltpu.VMEM((rows, HDIM), jnp.float32),
        pltpu.VMEM((2, 8, HDIM), jnp.float32),
    ]


def rows_of(span):
    return pl.ds(pl.multiple_of(span * SPAN, SPAN), SPAN)


def attend_blocks(dests, q_parts, k_ref, wide_ref, out_buf, store, stacked, mixed, top, bounds):
    count = len(dests)
    for j in range(count):

        @pl.when(dests[j] >= 0)
        def _(j=j):
            stack(q_parts[j], stacked.at[j])

    def work(shifted):
        def one(j, carry):
            dest = dests[0]
            for n in range(1, count):
                dest = jnp.where(j == n, dests[n], dest)

            @pl.when(dest >= 0)
            def _():
                if shifted:
                    attend_span_shifted(dest, stacked.at[j], k_ref, wide_ref, mixed, top)
                else:
                    attend_span(dest, stacked.at[j], k_ref, wide_ref, mixed)
                finish(mixed, out_buf.at[j], bounds)
                if store is not None:
                    store(j, dest).start()

            return carry

        lax.fori_loop(0, count, one, 0)

    def drain():
        if store is not None:
            for j in range(count):
                pl.when(dests[j] >= 0)(store(j, jnp.maximum(dests[j], 0)).wait)

    twice_if_needed(work, drain, bounds)


def stores(buf, o_ref, sems):
    return lambda j, span: pltpu.make_async_copy(buf.at[j], o_ref.at[rows_of(span)], sems.at[j])


def local_kernel(length_ref, q_hbm, k_hbm, v_hbm, o_ref, q_ref, k_ref, v_ref, wide, zeros, sems, out_buf, out_sems, *work):
    live = length_ref[lax.axis_index("replica")]
    fetches = [
        pltpu.make_async_copy(k_hbm, k_ref, sems.at[0]),
        pltpu.make_async_copy(v_hbm, v_ref, sems.at[MAXC]),
        pltpu.make_async_copy(q_hbm, q_ref, sems.at[MAXC + 1]),
    ]
    for copy in fetches:
        copy.start()
    zeros[...] = jnp.zeros_like(zeros)

    def clear(span):
        return pltpu.make_async_copy(zeros, o_ref.at[rows_of(span)], sems.at[span])

    for span in range(1, MAXC):
        pl.when(span >= live)(clear(span).start)
    for copy in fetches:
        copy.wait()
    widen(v_ref, wide)
    attend_blocks(
        [jnp.int32(0), jnp.where(live > 1, 1, -1)],
        [(q_ref.at[:SPAN],), (q_ref.at[SPAN:],)],
        k_ref,
        wide,
        out_buf,
        stores(out_buf, o_ref, out_sems),
        *work,
    )
    for span in range(1, MAXC):
        pl.when(span >= live)(clear(span).wait)


def attend_local(lengths, queries, keys, values):
    width, key_width = queries.shape[1], keys.shape[1]
    return pl.pallas_call(
        local_kernel,
        out_shape=jax.ShapeDtypeStruct((MAXC * SPAN, width), queries.dtype),
        in_specs=[SMEM, ANY, ANY, ANY],
        out_specs=ANY,
        scratch_shapes=[
            pltpu.VMEM(queries.shape, queries.dtype),
            pltpu.VMEM(keys.shape, keys.dtype),
            pltpu.VMEM(values.shape, values.dtype),
            pltpu.VMEM((SLOTS * SPAN, 2 * key_width), keys.dtype),
            pltpu.VMEM((SPAN, width), queries.dtype),
            pltpu.SemaphoreType.DMA((MAXC + 2,)),
            pltpu.VMEM((SLOTS, SPAN, width), queries.dtype),
            pltpu.SemaphoreType.DMA((SLOTS,)),
            *work_space(SLOTS, width, key_width),
        ],
        compiler_params=pltpu.CompilerParams(vmem_limit_bytes=MOST_VMEM_BYTES),
        cost_estimate=cost_of(5),
    )(lengths, queries, keys, values)


def parts_of(refs, pieces):
    return [refs[sum(pieces[:j]) : sum(pieces[: j + 1])] for j in range(len(pieces))]


def any_of(dests):
    return functools.reduce(jnp.maximum, dests) >= 0


def first_kernel(kv_offsets, offsets, pieces, meta_ref, own_k, own_v, *refs):
    parts = sum(pieces)
    blocks, refs = refs[: len(kv_offsets)], refs[len(kv_offsets) :]
    q_refs, refs = refs[:parts], refs[parts:]
    o_k, o_v, k_buf, wide, out_buf, v_buf, in_sems, out_sems, *work = refs
    live = meta_ref[0]

    def fetches():
        yield None, own_k.at[:SPAN], k_buf.at[rows_of(0)]
        yield None, own_v.at[:SPAN], v_buf.at[rows_of(0)]
        yield live > 1, own_k.at[SPAN:], k_buf.at[rows_of(1)]
        yield live > 1, own_v.at[SPAN:], v_buf.at[rows_of(1)]

    def each(act):
        for n, (needed, here, there) in enumerate(fetches()):
            copy = getattr(pltpu.make_async_copy(here, there, in_sems.at[n]), act)
            if needed is None:
                copy()
            else:
                pl.when(needed)(copy)

    each("start")
    for span in range(1, MAXC):

        @pl.when(span >= live)
        def _(span=span):
            k_buf[rows_of(span), :] = jnp.zeros((SPAN, k_buf.shape[1]), k_buf.dtype)
            v_buf[rows_of(span), :] = jnp.zeros((SPAN, v_buf.shape[1]), v_buf.dtype)

    for block, offset in zip(blocks, kv_offsets, strict=True):
        dest = meta_ref[offset]

        @pl.when(dest >= 0)
        def _(block=block, dest=dest):
            k_buf[rows_of(dest), :] = block[:SPAN, :]
            v_buf[rows_of(dest), :] = block[SPAN:, :]

    each("wait")
    copy_k = pltpu.make_async_copy(k_buf, o_k, out_sems.at[0])
    copy_v = pltpu.make_async_copy(v_buf, o_v, out_sems.at[1])
    copy_k.start()
    copy_v.start()
    dests = [meta_ref[offset] for offset in offsets]

    @pl.when(live > 1)
    def _():
        widen(v_buf, wide)

    @pl.when(any_of(dests))
    def _():
        attend_blocks(dests, parts_of(q_refs, pieces), k_buf, wide, out_buf, None, *work)

    copy_k.wait()
    copy_v.wait()


def attend_first(meta, keys, values, kv_offsets, kv_blocks, offsets, blocks):
    rows, key_width = MAXC * SPAN, keys.shape[1]
    pieces = [len(block) for block in blocks]
    count, width = len(pieces), blocks[0][0].shape[1]
    out = jax.ShapeDtypeStruct((rows, key_width), keys.dtype)
    return pl.pallas_call(
        lambda *refs: first_kernel(kv_offsets, offsets, pieces, *refs),
        out_shape=(
            out,
            out,
            out,
            jax.ShapeDtypeStruct((rows, 2 * key_width), keys.dtype),
            jax.ShapeDtypeStruct((count, SPAN, width), keys.dtype),
        ),
        in_specs=[SMEM, ANY, ANY] + [VMEM] * (len(kv_blocks) + sum(pieces)),
        out_specs=(ANY, ANY, VMEM, VMEM, VMEM),
        scratch_shapes=[
            pltpu.VMEM((rows, key_width), keys.dtype),
            pltpu.SemaphoreType.DMA((4,)),
            pltpu.SemaphoreType.DMA((2,)),
            *work_space(count, width, key_width),
        ],
        compiler_params=pltpu.CompilerParams(vmem_limit_bytes=VMEM_BYTES),
        cost_estimate=cost_of(1 * (2 + 2.5 * count)),
    )(meta, keys, values, *kv_blocks, *[part for block in blocks for part in block])


def later_kernel(offsets, pieces, meta_ref, *refs):
    parts = sum(pieces)
    q_refs, (k_ref, wide_ref, out_buf, *work) = refs[:parts], refs[parts:]
    dests = [meta_ref[offset] for offset in offsets]

    @pl.when(any_of(dests))
    def _():
        attend_blocks(dests, parts_of(q_refs, pieces), k_ref, wide_ref, out_buf, None, *work)


def attend_later(meta, offsets, blocks, ordered_keys, wide_values):
    pieces = [len(block) for block in blocks]
    count, width = len(pieces), blocks[0][0].shape[1]
    return pl.pallas_call(
        lambda *refs: later_kernel(offsets, pieces, *refs),
        out_shape=jax.ShapeDtypeStruct((count, SPAN, width), ordered_keys.dtype),
        in_specs=[SMEM] + [VMEM] * (sum(pieces) + 2),
        out_specs=VMEM,
        scratch_shapes=work_space(count, width, ordered_keys.shape[1]),
        compiler_params=pltpu.CompilerParams(vmem_limit_bytes=VMEM_BYTES),
        cost_estimate=cost_of(1 * (1 + 2.5 * count)),
    )(meta, *[part for block in blocks for part in block], ordered_keys, wide_values)


def last_kernel(before, offsets, pieces, meta_ref, *refs):
    parts = sum(pieces)
    results, refs = refs[: len(before)], refs[len(before) :]
    q_refs, (k_ref, wide_ref, _, o_ref, out_buf, sems, out_sems, *work) = refs[:parts], refs[parts:]
    earlier = [
        (meta_ref[offset], result, j, n)
        for n, (result, its_offsets) in enumerate(zip(results, before, strict=True))
        for j, offset in enumerate(its_offsets)
    ]

    def each(act):
        for dest, result, j, n in earlier:
            copy = pltpu.make_async_copy(
                result.at[j], o_ref.at[rows_of(jnp.maximum(dest, 0))], sems.at[n, j]
            )
            pl.when(dest >= 0)(getattr(copy, act))

    each("start")
    dests = [meta_ref[offset] for offset in offsets]

    @pl.when(any_of(dests))
    def _():
        attend_blocks(
            dests,
            parts_of(q_refs, pieces),
            k_ref,
            wide_ref,
            out_buf,
            stores(out_buf, o_ref, out_sems),
            *work,
        )

    each("wait")


def attend_last(meta, before, results, offsets, blocks, ordered_keys, wide_values, attention):
    pieces = [len(block) for block in blocks]
    count, parts = len(pieces), sum(pieces)
    width = attention.shape[1]
    most = max(len(its_offsets) for its_offsets in before)
    return pl.pallas_call(
        lambda *refs: last_kernel(before, offsets, pieces, *refs),
        out_shape=jax.ShapeDtypeStruct(attention.shape, attention.dtype),
        in_specs=[SMEM] + [VMEM] * (len(results) + parts + 2) + [ANY],
        out_specs=ANY,
        input_output_aliases={len(results) + parts + 3: 0},
        scratch_shapes=[
            pltpu.VMEM((count, SPAN, width), attention.dtype),
            pltpu.SemaphoreType.DMA((len(before), most)),
            pltpu.SemaphoreType.DMA((count,)),
            *work_space(count, width, ordered_keys.shape[1]),
        ],
        compiler_params=pltpu.CompilerParams(vmem_limit_bytes=VMEM_BYTES),
        cost_estimate=cost_of(4),
    )(
        meta,
        *results,
        *[part for block in blocks for part in block],
        ordered_keys,
        wide_values,
        attention,
    )


def gathered_kernel(meta_ref, first_ref, later_ref, k_ref, v_ref, o_ref, wide, stacked, mixed, top, bounds):
    at = pl.program_id(1)
    live = meta_ref[0]
    widen(v_ref, wide)

    @pl.when(at == 0)
    def _():
        stack((first_ref,), stacked.at[0])

    @pl.when(at > 0)
    def _():
        stack((later_ref.at[0],), stacked.at[0])

    def work(shifted):
        if shifted:
            attend_span_shifted(at, stacked.at[0], k_ref, wide, mixed, top)
        else:
            attend_span(at, stacked.at[0], k_ref, wide, mixed)
        finish(mixed, o_ref, bounds)

    @pl.when(at < live)
    def _():
        twice_if_needed(work, lambda: None, bounds)

    @pl.when(at >= live)
    def _():
        o_ref[...] = jnp.zeros_like(o_ref)


def attend_gathered(live, source, first, later, cache_keys, cache_values):
    home_rows, key_width = cache_keys.shape
    width = first.shape[1]
    groups = key_width // HDIM
    part = width // groups
    meta = jnp.concatenate([live.reshape(1), source]).astype(jnp.int32)
    return pl.pallas_call(
        gathered_kernel,
        out_shape=jax.ShapeDtypeStruct((home_rows, width), first.dtype),
        grid_spec=pltpu.PrefetchScalarGridSpec(
            num_scalar_prefetch=1,
            grid=(groups, MAXC),
            in_specs=[
                pl.BlockSpec((SPAN, part), lambda g, m, meta: (0, g)),
                pl.BlockSpec((1, SPAN, part), lambda g, m, meta: (meta[1 + m], 0, g)),
                pl.BlockSpec((home_rows, HDIM), lambda g, m, meta: (0, g)),
                pl.BlockSpec((home_rows, HDIM), lambda g, m, meta: (0, g)),
            ],
            out_specs=pl.BlockSpec((SPAN, part), lambda g, m, meta: (m, g)),
            scratch_shapes=[
                pltpu.VMEM((home_rows, 2 * HDIM), cache_keys.dtype),
                *work_space(1, part, HDIM),
            ],
        ),
        compiler_params=pltpu.CompilerParams(vmem_limit_bytes=VMEM_BYTES),
    )(meta, first, later, cache_keys, cache_values)


def gather_all(queries, keys, values, lengths, slot_prompt, slot_span):
    mine = lax.axis_index("replica")
    home_rows, key_width = MAXC * SPAN, keys.shape[1]
    live = lengths[mine]
    spans = jnp.arange(MAXC, dtype=jnp.int32)
    matches = (slot_prompt[None, :, 1] == mine) & (slot_span[None, :, 1] == spans[:, None])
    here = jnp.any(matches, axis=1)
    source = jnp.argmax(matches, axis=1).astype(jnp.int32)
    slots_k = lax.all_gather(keys[SPAN:], "replica")
    slots_v = lax.all_gather(values[SPAN:], "replica")
    slots_q = lax.all_gather(queries[SPAN:], "replica")

    def in_order(first, slots):
        picked = jnp.take(slots, source, axis=0)
        kept = jnp.where(here[:, None, None], picked, jnp.zeros((), slots.dtype))
        return jnp.concatenate([first, kept[1:].reshape(home_rows - SPAN, key_width)], axis=0)

    cache_keys = in_order(keys[:SPAN], slots_k)
    cache_values = in_order(values[:SPAN], slots_v)
    attention = attend_gathered(live, source, queries[:SPAN], slots_q, cache_keys, cache_values)
    return (attention, cache_keys, cache_values)


def per_device(queries, keys, values, lengths, slot_prompt, slot_span):
    replicas = lax.axis_size("replica")
    if replicas != 8:
        return gather_all(queries, keys, values, lengths, slot_prompt, slot_span)
    ring = column_ring(replicas)
    farthest = replicas // 2

    def after(block, *others):
        return lax.optimization_barrier((block, others))[0]

    def joined(both):
        return list(lax.optimization_barrier(tuple(both)))

    def shift(block, step):
        pairs = [(r, ring[(n + step) % replicas]) for n, r in enumerate(ring)]
        return lax.ppermute(block, "replica", pairs)

    def go_on(both):
        return [shift(both[0], 1), shift(both[1], -1)]

    own_kv = pack_kv(keys, values)
    kv = [[own_kv, own_kv]]
    kv.append(go_on(kv[0]))
    own_top, own_bottom = pack_q(after(queries, own_kv))
    top, bottom = [[own_top, own_top]], [[own_bottom, own_bottom]]
    top.append(joined(go_on(top[0])))
    kv[1] = joined(kv[1])
    kv.append(joined(go_on(kv[1])))
    attention = attend_local(lengths, after(queries, kv[1]), keys, values)
    bottom.append(joined(go_on([after(block, top[1]) for block in bottom[0]])))
    kv.append(joined(go_on([after(block, attention) for block in kv[2]])))
    top.append(joined(go_on([after(block, kv[3]) for block in top[1]])))
    kv.append([shift(kv[3][0], 1)])
    bottom.append(joined(go_on([after(block, kv[3]) for block in bottom[1]])))
    meta = places(lengths, slot_prompt, slot_span)
    offsets = [[n, replicas - n] for n in range(1, farthest)]

    def blocks(n):
        return list(zip(top[n], bottom[n], strict=True))

    cache_keys, cache_values, ordered_keys, wide_values, result = attend_first(
        meta, keys, values, sum(offsets, []) + [farthest], sum(kv[1:], []), offsets[0], blocks(1)
    )
    results = [result]
    top.append(joined(go_on(top[2])))
    bottom.append(joined(go_on([after(block, results[0]) for block in bottom[2]])))
    results.append(attend_later(meta, offsets[1], blocks(2), ordered_keys, wide_values))
    last = (
        shift(after(top[3][0], results[1]), 1),
        shift(after(bottom[3][1], results[1]), -1),
    )
    results.append(attend_later(meta, offsets[2], blocks(3), ordered_keys, wide_values))
    attention = attend_last(
        meta, offsets, results, [farthest], [last], ordered_keys, wide_values, attention
    )
    return (attention, cache_keys, cache_values)


def solution(mesh):
    in_specs = (
        P(("group", "replica"), "tensor"),
        P(("group", "replica"), "tensor"),
        P(("group", "replica"), "tensor"),
        P("group"),
        P("group", None),
        P("group", None),
    )
    out_specs = (
        P(("group", "replica"), "tensor"),
        P(("group", "replica"), "tensor"),
        P(("group", "replica"), "tensor"),
    )
    return jax.shard_map(
        per_device, mesh=mesh, in_specs=in_specs, out_specs=out_specs, check_vma=False
    )
```

```python
import functools
import math

import jax
import jax.numpy as jnp
from jax import lax
from jax.experimental import pallas as pl
from jax.experimental.pallas import tpu as pltpu
from jax.sharding import PartitionSpec as P

HDIM = 128
SPAN = 128
SLOTS = 2
MAXC = 8
BLOCK = 4
PART = 2
LOG2E = 1.0 / math.log(2.0)
VMEM_BYTES = 40 * 1024 * 1024
MOST_VMEM_BYTES = 60 * 1024 * 1024
LOCAL_VMEM_BYTES = 56 * 1024 * 1024
LEAST_SUM, MOST_SUM = 1e-20, 1e30
ANY = pl.BlockSpec(memory_space=pl.ANY)
SMEM = pl.BlockSpec(memory_space=pltpu.SMEM)
VMEM = pl.BlockSpec(memory_space=pltpu.VMEM)


def cost_of(us):
    return pl.CostEstimate(flops=int(us * 1.15e9), bytes_accessed=0, transcendentals=0)


def column_ring(replicas):
    return list(range(0, replicas, 2)) + list(range(replicas - 1, 0, -2))


def copy_all(copies):
    for copy in copies:
        copy.start()
    for copy in copies:
        copy.wait()


def pack_kv_kernel(k_ref, v_ref, o_ref, sems):
    copy_all(
        [
            pltpu.make_async_copy(k_ref.at[SPAN:], o_ref.at[:SPAN], sems.at[0]),
            pltpu.make_async_copy(v_ref.at[SPAN:], o_ref.at[SPAN:], sems.at[1]),
        ]
    )


def pack_kv(keys, values):
    return pl.pallas_call(
        pack_kv_kernel,
        out_shape=jax.ShapeDtypeStruct((2 * SPAN, keys.shape[1]), keys.dtype),
        in_specs=[ANY] * 2,
        out_specs=VMEM,
        scratch_shapes=[pltpu.SemaphoreType.DMA((2,))],
        compiler_params=pltpu.CompilerParams(vmem_limit_bytes=MOST_VMEM_BYTES),
        cost_estimate=cost_of(1),
    )(keys, values)


def pack_q_kernel(q_ref, o_top, o_bottom, sems):
    half = SPAN // 2
    copy_all(
        [
            pltpu.make_async_copy(q_ref.at[SPAN : SPAN + half], o_top, sems.at[0]),
            pltpu.make_async_copy(q_ref.at[SPAN + half :], o_bottom, sems.at[1]),
        ]
    )


def pack_q(queries):
    half = jax.ShapeDtypeStruct((SPAN // 2, queries.shape[1]), queries.dtype)
    return pl.pallas_call(
        pack_q_kernel,
        out_shape=(half, half),
        in_specs=[ANY],
        out_specs=(VMEM, VMEM),
        scratch_shapes=[pltpu.SemaphoreType.DMA((2,))],
        compiler_params=pltpu.CompilerParams(vmem_limit_bytes=MOST_VMEM_BYTES),
        cost_estimate=cost_of(1),
    )(queries)


def places(lengths, slot_prompt, slot_span):
    replicas = lengths.shape[0]
    mine = lax.axis_index("replica")
    ring = jnp.arange(replicas, dtype=jnp.int32)
    place = jnp.where(mine % 2 == 0, mine // 2, replicas - 1 - mine // 2)
    at = (place + replicas - ring) % replicas
    other = jnp.where(at < replicas // 2, 2 * at, 2 * (replicas - at) - 1)
    chosen = other[:, None] == ring[None, :]
    wanted = chosen & (slot_prompt[None, :, 1] == mine) & (ring[:, None] > 0)
    spans = jnp.where(wanted, slot_span[None, :, 1] + 1, 0)
    whole = jnp.where(chosen & (ring[:, None] == 0), lengths[None, :] + 1, 0)
    return jnp.sum(spans + whole, axis=1) - 1


def widen(v_ref, wide_ref):
    for at in range(0, v_ref.shape[-1], HDIM):
        wide_ref[:, 2 * at : 2 * at + HDIM] = v_ref[:, at : at + HDIM]
        wide_ref[:, 2 * at + HDIM : 2 * at + 2 * HDIM] = jnp.ones(
            (v_ref.shape[0], HDIM), v_ref.dtype
        )


def stack(q_refs, stacked):
    kv_heads, rows, _ = stacked.shape
    group = rows // SPAN
    for shared in range(kv_heads):
        for h in range(group):
            at = (shared * group + h) * HDIM
            row = h * SPAN
            for q_ref in q_refs:
                many = q_ref.shape[0]
                stacked[shared, row : row + many, :] = q_ref[:, at : at + HDIM]
                row += many


def attend_span(span, stacked, k_ref, wide_ref, mixed):
    kv_heads, rows, _ = stacked.shape
    heads = range(kv_heads)
    scale = LOG2E / math.sqrt(HDIM)
    blocks = span // BLOCK
    edge = span % PART * SPAN

    def keys_of(block, spans):
        return pl.ds(pl.multiple_of(block * BLOCK * SPAN, BLOCK * SPAN), spans * SPAN)

    def scores(shared, block, spans, masked):
        found = lax.dot_general(
            stacked[shared],
            k_ref[keys_of(block, spans), shared * HDIM : (shared + 1) * HDIM],
            (((1,), (1,)), ((), ())),
            preferred_element_type=jnp.float32,
        )
        if masked:
            seen = (spans - PART) * SPAN
            row = lax.broadcasted_iota(jnp.int32, (rows, PART * SPAN), 0) % SPAN
            column = lax.broadcasted_iota(jnp.int32, (rows, PART * SPAN), 1)
            last = jnp.where(column <= row + edge, found[:, seen:], -jnp.inf)
            found = jnp.concatenate([found[:, :seen], last], axis=1) if seen else last
        return found

    def products(shared, block, spans, found):
        return jnp.dot(
            jnp.exp2(found * scale).astype(jnp.bfloat16),
            wide_ref[keys_of(block, spans), 2 * shared * HDIM : 2 * (shared + 1) * HDIM],
            preferred_element_type=jnp.float32,
        )

    most = k_ref.shape[0] // SPAN
    for spans in range(PART, min(BLOCK, most) + 1, PART):

        @pl.when(span % BLOCK // PART == spans // PART - 1)
        def _(spans=spans):
            found = [scores(shared, blocks, spans, True) for shared in heads]
            for shared in heads:
                mixed[shared] = products(shared, blocks, spans, found[shared])

    def add(block, carry):
        found = [scores(shared, block, BLOCK, False) for shared in heads]
        for shared in heads:
            mixed[shared] += products(shared, block, BLOCK, found[shared])
        return carry

    if most > BLOCK:
        lax.fori_loop(0, blocks, add, 0)


def attend_span_shifted(span, stacked, k_ref, wide_ref, mixed, top):
    kv_heads, rows, _ = stacked.shape
    scale = LOG2E / math.sqrt(HDIM)

    def one_head(shared, carry):
        def scores(block):
            found = lax.dot_general(
                stacked[shared],
                k_ref[rows_of(block), pl.ds(pl.multiple_of(shared * HDIM, HDIM), HDIM)],
                (((1,), (1,)), ((), ())),
                preferred_element_type=jnp.float32,
            )
            row = lax.broadcasted_iota(jnp.int32, (rows, SPAN), 0) % SPAN
            column = lax.broadcasted_iota(jnp.int32, (rows, SPAN), 1)
            return jnp.where(column <= row + (span - block) * SPAN, found, -jnp.inf)

        def look(block, carry):
            top[...] = jnp.maximum(top[...], scores(block))
            return carry

        def add(block, carry):
            weights = jnp.exp2((scores(block) - top[...]) * scale).astype(jnp.bfloat16)
            mixed[shared] += jnp.dot(
                weights,
                wide_ref[
                    rows_of(block), pl.ds(pl.multiple_of(2 * shared * HDIM, 2 * HDIM), 2 * HDIM)
                ],
                preferred_element_type=jnp.float32,
            )
            return carry

        top[...] = jnp.full_like(top, -jnp.inf)
        lax.fori_loop(0, span + 1, look, 0)
        top[...] = jnp.broadcast_to(jnp.max(top[...], axis=1, keepdims=True), top.shape)
        mixed[shared] = jnp.zeros(mixed.shape[1:], mixed.dtype)
        lax.fori_loop(0, span + 1, add, 0)
        return carry

    lax.fori_loop(0, kv_heads, one_head, 0)


def finish(mixed, o_ref, bounds):
    kv_heads, rows, _ = mixed.shape
    for shared in range(kv_heads):
        total = mixed[shared, :, HDIM:]
        inverse = pl.reciprocal(total, approx=True)
        inverse = inverse * (2.0 - total * inverse)
        result = (mixed[shared, :, :HDIM] * inverse).astype(o_ref.dtype)
        for h in range(rows // SPAN):
            at = (shared * rows // SPAN + h) * HDIM
            o_ref[:, at : at + HDIM] = result[h * SPAN : (h + 1) * SPAN, :]
        total = total.reshape(-1, 8, HDIM)
        bounds[0] = jnp.minimum(bounds[0], jnp.min(total, axis=0))
        bounds[1] = jnp.maximum(bounds[1], jnp.max(total, axis=0))


def twice_if_needed(work, drain, bounds):
    bounds[...] = jnp.ones_like(bounds)
    work(False)
    safe = (jnp.min(bounds[0]) > LEAST_SUM) & (jnp.max(bounds[1]) < MOST_SUM)
    drain()

    @pl.when(jnp.logical_not(safe))
    def _():
        work(True)
        drain()


def work_space(count, width, key_width):
    kv_heads = key_width // HDIM
    rows = width // key_width * SPAN
    return [
        pltpu.VMEM((count, kv_heads, rows, HDIM), jnp.bfloat16),
        pltpu.VMEM((kv_heads, rows, 2 * HDIM), jnp.float32),
        pltpu.VMEM((rows, HDIM), jnp.float32),
        pltpu.VMEM((2, 8, HDIM), jnp.float32),
    ]


def rows_of(span):
    return pl.ds(pl.multiple_of(span * SPAN, SPAN), SPAN)


def attend_blocks(dests, q_parts, k_ref, wide_ref, out_buf, store, stacked, mixed, top, bounds):
    count = len(dests)
    for j in range(count):

        @pl.when(dests[j] >= 0)
        def _(j=j):
            stack(q_parts[j], stacked.at[j])

    def work(shifted):
        def one(j, carry):
            dest = dests[0]
            for n in range(1, count):
                dest = jnp.where(j == n, dests[n], dest)

            @pl.when(dest >= 0)
            def _():
                if shifted:
                    attend_span_shifted(dest, stacked.at[j], k_ref, wide_ref, mixed, top)
                else:
                    attend_span(dest, stacked.at[j], k_ref, wide_ref, mixed)
                finish(mixed, out_buf.at[j], bounds)
                if store is not None:
                    store(j, dest).start()

            return carry

        lax.fori_loop(0, count, one, 0)

    def drain():
        if store is not None:
            for j in range(count):
                pl.when(dests[j] >= 0)(store(j, jnp.maximum(dests[j], 0)).wait)

    twice_if_needed(work, drain, bounds)


def stores(buf, o_ref, sems):
    return lambda j, span: pltpu.make_async_copy(buf.at[j], o_ref.at[rows_of(span)], sems.at[j])


def local_kernel(length_ref, q_hbm, k_hbm, v_hbm, out_buf, q_ref, k_ref, v_ref, wide, sems, *work):
    live = length_ref[lax.axis_index("replica")]

    def fetch(slot):
        rows = slice(slot * SPAN, (slot + 1) * SPAN)
        return pltpu.make_async_copy(q_hbm.at[rows], q_ref.at[rows], sems.at[2 + slot])

    fetches = [
        pltpu.make_async_copy(k_hbm, k_ref, sems.at[0]),
        pltpu.make_async_copy(v_hbm, v_ref, sems.at[1]),
        fetch(0),
    ]
    for copy in fetches:
        copy.start()
    pl.when(live > 1)(fetch(1).start)
    for copy in fetches:
        copy.wait()
    widen(v_ref, wide)
    pl.when(live > 1)(fetch(1).wait)
    attend_blocks(
        [jnp.int32(0), jnp.where(live > 1, 1, -1)],
        [(q_ref.at[:SPAN],), (q_ref.at[SPAN:],)],
        k_ref,
        wide,
        out_buf,
        None,
        *work,
    )


def attend_local(lengths, queries, keys, values):
    width, key_width = queries.shape[1], keys.shape[1]
    return pl.pallas_call(
        local_kernel,
        out_shape=jax.ShapeDtypeStruct((SLOTS, SPAN, width), queries.dtype),
        in_specs=[SMEM, ANY, ANY, ANY],
        out_specs=VMEM,
        scratch_shapes=[
            pltpu.VMEM(queries.shape, queries.dtype),
            pltpu.VMEM(keys.shape, keys.dtype),
            pltpu.VMEM(values.shape, values.dtype),
            pltpu.VMEM((SLOTS * SPAN, 2 * key_width), keys.dtype),
            pltpu.SemaphoreType.DMA((2 + SLOTS,)),
            *work_space(SLOTS, width, key_width),
        ],
        compiler_params=pltpu.CompilerParams(vmem_limit_bytes=LOCAL_VMEM_BYTES),
        cost_estimate=cost_of(5),
    )(lengths, queries, keys, values)


def parts_of(refs, pieces):
    return [refs[sum(pieces[:j]) : sum(pieces[: j + 1])] for j in range(len(pieces))]


def any_of(dests):
    return functools.reduce(jnp.maximum, dests) >= 0


def first_kernel(kv_offsets, offsets, pieces, meta_ref, own_k, own_v, *refs):
    parts = sum(pieces)
    blocks, refs = refs[: len(kv_offsets)], refs[len(kv_offsets) :]
    q_refs, refs = refs[:parts], refs[parts:]
    local, o_k, o_v, k_buf, wide, out_buf, o_ref, v_buf, zeros, in_sems, out_sems, span_sems, *work = refs
    live = meta_ref[0]

    def fetches():
        yield None, own_k.at[:SPAN], k_buf.at[rows_of(0)]
        yield None, own_v.at[:SPAN], v_buf.at[rows_of(0)]
        yield live > 1, own_k.at[SPAN:], k_buf.at[rows_of(1)]
        yield live > 1, own_v.at[SPAN:], v_buf.at[rows_of(1)]

    def each(act):
        for n, (needed, here, there) in enumerate(fetches()):
            copy = getattr(pltpu.make_async_copy(here, there, in_sems.at[n]), act)
            if needed is None:
                copy()
            else:
                pl.when(needed)(copy)

    def each_span(act):
        for span in range(MAXC):
            there, sem = o_ref.at[rows_of(span)], span_sems.at[span]
            if span < SLOTS:
                copy = pltpu.make_async_copy(local.at[span], there, sem)
                pl.when(span < live)(getattr(copy, act))
            if span > 0:
                pl.when(span >= live)(getattr(pltpu.make_async_copy(zeros, there, sem), act))

    each("start")
    zeros[...] = jnp.zeros_like(zeros)
    each_span("start")
    for span in range(1, MAXC):

        @pl.when(span >= live)
        def _(span=span):
            k_buf[rows_of(span), :] = jnp.zeros((SPAN, k_buf.shape[1]), k_buf.dtype)
            v_buf[rows_of(span), :] = jnp.zeros((SPAN, v_buf.shape[1]), v_buf.dtype)

    for block, offset in zip(blocks, kv_offsets, strict=True):
        dest = meta_ref[offset]

        @pl.when(dest >= 0)
        def _(block=block, dest=dest):
            k_buf[rows_of(dest), :] = block[:SPAN, :]
            v_buf[rows_of(dest), :] = block[SPAN:, :]

    each("wait")
    copy_k = pltpu.make_async_copy(k_buf, o_k, out_sems.at[0])
    copy_v = pltpu.make_async_copy(v_buf, o_v, out_sems.at[1])
    copy_k.start()
    copy_v.start()
    dests = [meta_ref[offset] for offset in offsets]

    @pl.when(live > 1)
    def _():
        widen(v_buf, wide)

    @pl.when(any_of(dests))
    def _():
        attend_blocks(dests, parts_of(q_refs, pieces), k_buf, wide, out_buf, None, *work)

    copy_k.wait()
    copy_v.wait()
    each_span("wait")


def attend_first(meta, keys, values, kv_offsets, kv_blocks, offsets, blocks, local):
    rows, key_width = MAXC * SPAN, keys.shape[1]
    pieces = [len(block) for block in blocks]
    count, width = len(pieces), blocks[0][0].shape[1]
    out = jax.ShapeDtypeStruct((rows, key_width), keys.dtype)
    return pl.pallas_call(
        lambda *refs: first_kernel(kv_offsets, offsets, pieces, *refs),
        out_shape=(
            out,
            out,
            out,
            jax.ShapeDtypeStruct((rows, 2 * key_width), keys.dtype),
            jax.ShapeDtypeStruct((count, SPAN, width), keys.dtype),
            jax.ShapeDtypeStruct((rows, width), keys.dtype),
        ),
        in_specs=[SMEM, ANY, ANY] + [VMEM] * (len(kv_blocks) + sum(pieces) + 1),
        out_specs=(ANY, ANY, VMEM, VMEM, VMEM, ANY),
        scratch_shapes=[
            pltpu.VMEM((rows, key_width), keys.dtype),
            pltpu.VMEM((SPAN, width), keys.dtype),
            pltpu.SemaphoreType.DMA((4,)),
            pltpu.SemaphoreType.DMA((2,)),
            pltpu.SemaphoreType.DMA((MAXC,)),
            *work_space(count, width, key_width),
        ],
        compiler_params=pltpu.CompilerParams(vmem_limit_bytes=VMEM_BYTES),
        cost_estimate=cost_of(1 * (2 + 2.5 * count)),
    )(meta, keys, values, *kv_blocks, *[part for block in blocks for part in block], local)


def later_kernel(offsets, pieces, meta_ref, *refs):
    parts = sum(pieces)
    q_refs, (k_ref, wide_ref, out_buf, *work) = refs[:parts], refs[parts:]
    dests = [meta_ref[offset] for offset in offsets]

    @pl.when(any_of(dests))
    def _():
        attend_blocks(dests, parts_of(q_refs, pieces), k_ref, wide_ref, out_buf, None, *work)


def attend_later(meta, offsets, blocks, ordered_keys, wide_values):
    pieces = [len(block) for block in blocks]
    count, width = len(pieces), blocks[0][0].shape[1]
    return pl.pallas_call(
        lambda *refs: later_kernel(offsets, pieces, *refs),
        out_shape=jax.ShapeDtypeStruct((count, SPAN, width), ordered_keys.dtype),
        in_specs=[SMEM] + [VMEM] * (sum(pieces) + 2),
        out_specs=VMEM,
        scratch_shapes=work_space(count, width, ordered_keys.shape[1]),
        compiler_params=pltpu.CompilerParams(vmem_limit_bytes=VMEM_BYTES),
        cost_estimate=cost_of(1 * (1 + 2.5 * count)),
    )(meta, *[part for block in blocks for part in block], ordered_keys, wide_values)


def last_kernel(before, offsets, pieces, meta_ref, *refs):
    parts = sum(pieces)
    results, refs = refs[: len(before)], refs[len(before) :]
    q_refs, (k_ref, wide_ref, _, o_ref, out_buf, sems, out_sems, *work) = refs[:parts], refs[parts:]
    earlier = [
        (meta_ref[offset], result, j, n)
        for n, (result, its_offsets) in enumerate(zip(results, before, strict=True))
        for j, offset in enumerate(its_offsets)
    ]

    def each(act):
        for dest, result, j, n in earlier:
            copy = pltpu.make_async_copy(
                result.at[j], o_ref.at[rows_of(jnp.maximum(dest, 0))], sems.at[n, j]
            )
            pl.when(dest >= 0)(getattr(copy, act))

    each("start")
    dests = [meta_ref[offset] for offset in offsets]

    @pl.when(any_of(dests))
    def _():
        attend_blocks(
            dests,
            parts_of(q_refs, pieces),
            k_ref,
            wide_ref,
            out_buf,
            stores(out_buf, o_ref, out_sems),
            *work,
        )

    each("wait")


def attend_last(meta, before, results, offsets, blocks, ordered_keys, wide_values, attention):
    pieces = [len(block) for block in blocks]
    count, parts = len(pieces), sum(pieces)
    width = attention.shape[1]
    most = max(len(its_offsets) for its_offsets in before)
    return pl.pallas_call(
        lambda *refs: last_kernel(before, offsets, pieces, *refs),
        out_shape=jax.ShapeDtypeStruct(attention.shape, attention.dtype),
        in_specs=[SMEM] + [VMEM] * (len(results) + parts + 2) + [ANY],
        out_specs=ANY,
        input_output_aliases={len(results) + parts + 3: 0},
        scratch_shapes=[
            pltpu.VMEM((count, SPAN, width), attention.dtype),
            pltpu.SemaphoreType.DMA((len(before), most)),
            pltpu.SemaphoreType.DMA((count,)),
            *work_space(count, width, ordered_keys.shape[1]),
        ],
        compiler_params=pltpu.CompilerParams(vmem_limit_bytes=VMEM_BYTES),
        cost_estimate=cost_of(4),
    )(
        meta,
        *results,
        *[part for block in blocks for part in block],
        ordered_keys,
        wide_values,
        attention,
    )


def gathered_kernel(meta_ref, first_ref, later_ref, k_ref, v_ref, o_ref, wide, stacked, mixed, top, bounds):
    at = pl.program_id(1)
    live = meta_ref[0]
    widen(v_ref, wide)

    @pl.when(at == 0)
    def _():
        stack((first_ref,), stacked.at[0])

    @pl.when(at > 0)
    def _():
        stack((later_ref.at[0],), stacked.at[0])

    def work(shifted):
        if shifted:
            attend_span_shifted(at, stacked.at[0], k_ref, wide, mixed, top)
        else:
            attend_span(at, stacked.at[0], k_ref, wide, mixed)
        finish(mixed, o_ref, bounds)

    @pl.when(at < live)
    def _():
        twice_if_needed(work, lambda: None, bounds)

    @pl.when(at >= live)
    def _():
        o_ref[...] = jnp.zeros_like(o_ref)


def attend_gathered(live, source, first, later, cache_keys, cache_values):
    home_rows, key_width = cache_keys.shape
    width = first.shape[1]
    groups = key_width // HDIM
    part = width // groups
    meta = jnp.concatenate([live.reshape(1), source]).astype(jnp.int32)
    return pl.pallas_call(
        gathered_kernel,
        out_shape=jax.ShapeDtypeStruct((home_rows, width), first.dtype),
        grid_spec=pltpu.PrefetchScalarGridSpec(
            num_scalar_prefetch=1,
            grid=(groups, MAXC),
            in_specs=[
                pl.BlockSpec((SPAN, part), lambda g, m, meta: (0, g)),
                pl.BlockSpec((1, SPAN, part), lambda g, m, meta: (meta[1 + m], 0, g)),
                pl.BlockSpec((home_rows, HDIM), lambda g, m, meta: (0, g)),
                pl.BlockSpec((home_rows, HDIM), lambda g, m, meta: (0, g)),
            ],
            out_specs=pl.BlockSpec((SPAN, part), lambda g, m, meta: (m, g)),
            scratch_shapes=[
                pltpu.VMEM((home_rows, 2 * HDIM), cache_keys.dtype),
                *work_space(1, part, HDIM),
            ],
        ),
        compiler_params=pltpu.CompilerParams(vmem_limit_bytes=VMEM_BYTES),
    )(meta, first, later, cache_keys, cache_values)


def gather_all(queries, keys, values, lengths, slot_prompt, slot_span):
    mine = lax.axis_index("replica")
    home_rows, key_width = MAXC * SPAN, keys.shape[1]
    live = lengths[mine]
    spans = jnp.arange(MAXC, dtype=jnp.int32)
    matches = (slot_prompt[None, :, 1] == mine) & (slot_span[None, :, 1] == spans[:, None])
    here = jnp.any(matches, axis=1)
    source = jnp.argmax(matches, axis=1).astype(jnp.int32)
    slots_k = lax.all_gather(keys[SPAN:], "replica")
    slots_v = lax.all_gather(values[SPAN:], "replica")
    slots_q = lax.all_gather(queries[SPAN:], "replica")

    def in_order(first, slots):
        picked = jnp.take(slots, source, axis=0)
        kept = jnp.where(here[:, None, None], picked, jnp.zeros((), slots.dtype))
        return jnp.concatenate([first, kept[1:].reshape(home_rows - SPAN, key_width)], axis=0)

    cache_keys = in_order(keys[:SPAN], slots_k)
    cache_values = in_order(values[:SPAN], slots_v)
    attention = attend_gathered(live, source, queries[:SPAN], slots_q, cache_keys, cache_values)
    return (attention, cache_keys, cache_values)


def per_device(queries, keys, values, lengths, slot_prompt, slot_span):
    replicas = lax.axis_size("replica")
    if replicas != 8:
        return gather_all(queries, keys, values, lengths, slot_prompt, slot_span)
    ring = column_ring(replicas)
    farthest = replicas // 2

    def after(block, *others):
        return lax.optimization_barrier((block, others))[0]

    def joined(both):
        return list(lax.optimization_barrier(tuple(both)))

    def shift(block, step):
        pairs = [(r, ring[(n + step) % replicas]) for n, r in enumerate(ring)]
        return lax.ppermute(block, "replica", pairs)

    def go_on(both):
        return [shift(both[0], 1), shift(both[1], -1)]

    own_kv = pack_kv(keys, values)
    kv = [[own_kv, own_kv]]
    kv.append(go_on(kv[0]))
    own_top, own_bottom = pack_q(after(queries, own_kv))
    top, bottom = [[own_top, own_top]], [[own_bottom, own_bottom]]
    top.append(joined(go_on(top[0])))
    kv[1] = joined(kv[1])
    kv.append(joined(go_on(kv[1])))
    local = attend_local(lengths, after(queries, kv[1]), keys, values)
    bottom.append(joined(go_on([after(block, top[1]) for block in bottom[0]])))
    kv.append(joined(go_on([after(block, local) for block in kv[2]])))
    top.append(joined(go_on([after(block, kv[3]) for block in top[1]])))
    kv.append([shift(kv[3][0], 1)])
    bottom.append(joined(go_on([after(block, kv[3]) for block in bottom[1]])))
    meta = places(lengths, slot_prompt, slot_span)
    offsets = [[n, replicas - n] for n in range(1, farthest)]

    def blocks(n):
        return list(zip(top[n], bottom[n], strict=True))

    cache_keys, cache_values, ordered_keys, wide_values, result, attention = attend_first(
        meta,
        keys,
        values,
        sum(offsets, []) + [farthest],
        sum(kv[1:], []),
        offsets[0],
        blocks(1),
        local,
    )
    results = [result]
    top.append(joined(go_on(top[2])))
    bottom.append(joined(go_on([after(block, results[0]) for block in bottom[2]])))
    results.append(attend_later(meta, offsets[1], blocks(2), ordered_keys, wide_values))
    last = (
        shift(after(top[3][0], results[1]), 1),
        shift(after(bottom[3][1], results[1]), -1),
    )
    results.append(attend_later(meta, offsets[2], blocks(3), ordered_keys, wide_values))
    attention = attend_last(
        meta, offsets, results, [farthest], [last], ordered_keys, wide_values, attention
    )
    return (attention, cache_keys, cache_values)


def solution(mesh):
    in_specs = (
        P(("group", "replica"), "tensor"),
        P(("group", "replica"), "tensor"),
        P(("group", "replica"), "tensor"),
        P("group"),
        P("group", None),
        P("group", None),
    )
    out_specs = (
        P(("group", "replica"), "tensor"),
        P(("group", "replica"), "tensor"),
        P(("group", "replica"), "tensor"),
    )
    return jax.shard_map(
        per_device, mesh=mesh, in_specs=in_specs, out_specs=out_specs, check_vma=False
    )
```

```python
import functools
import math

import jax
import jax.numpy as jnp
from jax import lax
from jax.experimental import pallas as pl
from jax.experimental.pallas import tpu as pltpu
from jax.sharding import PartitionSpec as P

HDIM = 128
SPAN = 128
SLOTS = 2
MAXC = 8
BLOCK = 4
PART = 2
LOG2E = 1.0 / math.log(2.0)
VMEM_BYTES = 40 * 1024 * 1024
MOST_VMEM_BYTES = 60 * 1024 * 1024
LEAST_SUM, MOST_SUM = 1e-20, 1e30
ANY = pl.BlockSpec(memory_space=pl.ANY)
SMEM = pl.BlockSpec(memory_space=pltpu.SMEM)
VMEM = pl.BlockSpec(memory_space=pltpu.VMEM)


def cost_of(us):
    return pl.CostEstimate(flops=int(us * 1.15e9), bytes_accessed=0, transcendentals=0)


def column_ring(replicas):
    return list(range(0, replicas, 2)) + list(range(replicas - 1, 0, -2))


def copy_all(copies):
    for copy in copies:
        copy.start()
    for copy in copies:
        copy.wait()


def pack_kv_kernel(k_ref, v_ref, o_ref, sems):
    copy_all(
        [
            pltpu.make_async_copy(k_ref.at[SPAN:], o_ref.at[:SPAN], sems.at[0]),
            pltpu.make_async_copy(v_ref.at[SPAN:], o_ref.at[SPAN:], sems.at[1]),
        ]
    )


def pack_kv(keys, values):
    return pl.pallas_call(
        pack_kv_kernel,
        out_shape=jax.ShapeDtypeStruct((2 * SPAN, keys.shape[1]), keys.dtype),
        in_specs=[ANY] * 2,
        out_specs=VMEM,
        scratch_shapes=[pltpu.SemaphoreType.DMA((2,))],
        compiler_params=pltpu.CompilerParams(vmem_limit_bytes=MOST_VMEM_BYTES),
        cost_estimate=cost_of(1),
    )(keys, values)


def pack_q_kernel(q_ref, o_top, o_bottom, sems):
    half = SPAN // 2
    copy_all(
        [
            pltpu.make_async_copy(q_ref.at[SPAN : SPAN + half], o_top, sems.at[0]),
            pltpu.make_async_copy(q_ref.at[SPAN + half :], o_bottom, sems.at[1]),
        ]
    )


def pack_q(queries):
    half = jax.ShapeDtypeStruct((SPAN // 2, queries.shape[1]), queries.dtype)
    return pl.pallas_call(
        pack_q_kernel,
        out_shape=(half, half),
        in_specs=[ANY],
        out_specs=(VMEM, VMEM),
        scratch_shapes=[pltpu.SemaphoreType.DMA((2,))],
        compiler_params=pltpu.CompilerParams(vmem_limit_bytes=VMEM_BYTES),
        cost_estimate=cost_of(1),
    )(queries)


def places(lengths, slot_prompt, slot_span):
    replicas = lengths.shape[0]
    mine = lax.axis_index("replica")
    ring = jnp.arange(replicas, dtype=jnp.int32)
    place = jnp.where(mine % 2 == 0, mine // 2, replicas - 1 - mine // 2)
    at = (place + replicas - ring) % replicas
    other = jnp.where(at < replicas // 2, 2 * at, 2 * (replicas - at) - 1)
    chosen = other[:, None] == ring[None, :]
    wanted = chosen & (slot_prompt[None, :, 1] == mine) & (ring[:, None] > 0)
    spans = jnp.where(wanted, slot_span[None, :, 1] + 1, 0)
    whole = jnp.where(chosen & (ring[:, None] == 0), lengths[None, :] + 1, 0)
    return jnp.sum(spans + whole, axis=1) - 1


def widen(v_ref, wide_ref):
    for at in range(0, v_ref.shape[-1], HDIM):
        wide_ref[:, 2 * at : 2 * at + HDIM] = v_ref[:, at : at + HDIM]
        wide_ref[:, 2 * at + HDIM : 2 * at + 2 * HDIM] = jnp.ones(
            (v_ref.shape[0], HDIM), v_ref.dtype
        )


def stack(q_refs, stacked):
    kv_heads, rows, _ = stacked.shape
    group = rows // SPAN
    for shared in range(kv_heads):
        for h in range(group):
            at = (shared * group + h) * HDIM
            row = h * SPAN
            for q_ref in q_refs:
                many = q_ref.shape[0]
                stacked[shared, row : row + many, :] = q_ref[:, at : at + HDIM]
                row += many


def attend_span(span, stacked, k_ref, wide_ref, mixed):
    kv_heads, rows, _ = stacked.shape
    heads = range(kv_heads)
    scale = LOG2E / math.sqrt(HDIM)
    blocks = span // BLOCK
    edge = span % PART * SPAN

    def keys_of(block, spans):
        return pl.ds(pl.multiple_of(block * BLOCK * SPAN, BLOCK * SPAN), spans * SPAN)

    def scores(shared, block, spans, masked):
        found = lax.dot_general(
            stacked[shared],
            k_ref[keys_of(block, spans), shared * HDIM : (shared + 1) * HDIM],
            (((1,), (1,)), ((), ())),
            preferred_element_type=jnp.float32,
        )
        if masked:
            seen = (spans - PART) * SPAN
            row = lax.broadcasted_iota(jnp.int32, (rows, PART * SPAN), 0) % SPAN
            column = lax.broadcasted_iota(jnp.int32, (rows, PART * SPAN), 1)
            last = jnp.where(column <= row + edge, found[:, seen:], -jnp.inf)
            found = jnp.concatenate([found[:, :seen], last], axis=1) if seen else last
        return found

    def products(shared, block, spans, found):
        return jnp.dot(
            jnp.exp2(found * scale).astype(jnp.bfloat16),
            wide_ref[keys_of(block, spans), 2 * shared * HDIM : 2 * (shared + 1) * HDIM],
            preferred_element_type=jnp.float32,
        )

    most = k_ref.shape[0] // SPAN
    for spans in range(PART, min(BLOCK, most) + 1, PART):

        @pl.when(span % BLOCK // PART == spans // PART - 1)
        def _(spans=spans):
            found = [scores(shared, blocks, spans, True) for shared in heads]
            for shared in heads:
                mixed[shared] = products(shared, blocks, spans, found[shared])

    def add(block, carry):
        found = [scores(shared, block, BLOCK, False) for shared in heads]
        for shared in heads:
            mixed[shared] += products(shared, block, BLOCK, found[shared])
        return carry

    if most > BLOCK:
        lax.fori_loop(0, blocks, add, 0)


def attend_span_shifted(span, stacked, k_ref, wide_ref, mixed, top):
    kv_heads, rows, _ = stacked.shape
    scale = LOG2E / math.sqrt(HDIM)

    def one_head(shared, carry):
        def scores(block):
            found = lax.dot_general(
                stacked[shared],
                k_ref[rows_of(block), pl.ds(pl.multiple_of(shared * HDIM, HDIM), HDIM)],
                (((1,), (1,)), ((), ())),
                preferred_element_type=jnp.float32,
            )
            row = lax.broadcasted_iota(jnp.int32, (rows, SPAN), 0) % SPAN
            column = lax.broadcasted_iota(jnp.int32, (rows, SPAN), 1)
            return jnp.where(column <= row + (span - block) * SPAN, found, -jnp.inf)

        def look(block, carry):
            top[...] = jnp.maximum(top[...], scores(block))
            return carry

        def add(block, carry):
            weights = jnp.exp2((scores(block) - top[...]) * scale).astype(jnp.bfloat16)
            mixed[shared] += jnp.dot(
                weights,
                wide_ref[
                    rows_of(block), pl.ds(pl.multiple_of(2 * shared * HDIM, 2 * HDIM), 2 * HDIM)
                ],
                preferred_element_type=jnp.float32,
            )
            return carry

        top[...] = jnp.full_like(top, -jnp.inf)
        lax.fori_loop(0, span + 1, look, 0)
        top[...] = jnp.broadcast_to(jnp.max(top[...], axis=1, keepdims=True), top.shape)
        mixed[shared] = jnp.zeros(mixed.shape[1:], mixed.dtype)
        lax.fori_loop(0, span + 1, add, 0)
        return carry

    lax.fori_loop(0, kv_heads, one_head, 0)


def finish(mixed, o_ref, bounds):
    kv_heads, rows, _ = mixed.shape
    for shared in range(kv_heads):
        total = mixed[shared, :, HDIM:]
        inverse = pl.reciprocal(total, approx=True)
        inverse = inverse * (2.0 - total * inverse)
        result = (mixed[shared, :, :HDIM] * inverse).astype(o_ref.dtype)
        for h in range(rows // SPAN):
            at = (shared * rows // SPAN + h) * HDIM
            o_ref[:, at : at + HDIM] = result[h * SPAN : (h + 1) * SPAN, :]
        total = total.reshape(-1, 8, HDIM)
        bounds[0] = jnp.minimum(bounds[0], jnp.min(total, axis=0))
        bounds[1] = jnp.maximum(bounds[1], jnp.max(total, axis=0))


def twice_if_needed(work, drain, bounds):
    bounds[...] = jnp.ones_like(bounds)
    work(False)
    safe = (jnp.min(bounds[0]) > LEAST_SUM) & (jnp.max(bounds[1]) < MOST_SUM)
    drain()

    @pl.when(jnp.logical_not(safe))
    def _():
        work(True)
        drain()


def work_space(count, width, key_width):
    kv_heads = key_width // HDIM
    rows = width // key_width * SPAN
    return [
        pltpu.VMEM((count, kv_heads, rows, HDIM), jnp.bfloat16),
        pltpu.VMEM((kv_heads, rows, 2 * HDIM), jnp.float32),
        pltpu.VMEM((rows, HDIM), jnp.float32),
        pltpu.VMEM((2, 8, HDIM), jnp.float32),
    ]


def rows_of(span):
    return pl.ds(pl.multiple_of(span * SPAN, SPAN), SPAN)


def attend_blocks(dests, q_parts, k_ref, wide_ref, out_buf, store, stacked, mixed, top, bounds):
    count = len(dests)
    for j in range(count):

        @pl.when(dests[j] >= 0)
        def _(j=j):
            stack(q_parts[j], stacked.at[j])

    def work(shifted):
        def one(j, carry):
            dest = dests[0]
            for n in range(1, count):
                dest = jnp.where(j == n, dests[n], dest)

            @pl.when(dest >= 0)
            def _():
                if shifted:
                    attend_span_shifted(dest, stacked.at[j], k_ref, wide_ref, mixed, top)
                else:
                    attend_span(dest, stacked.at[j], k_ref, wide_ref, mixed)
                finish(mixed, out_buf.at[j], bounds)
                if store is not None:
                    store(j, dest).start()

            return carry

        lax.fori_loop(0, count, one, 0)

    def drain():
        if store is not None:
            for j in range(count):
                pl.when(dests[j] >= 0)(store(j, jnp.maximum(dests[j], 0)).wait)

    twice_if_needed(work, drain, bounds)


def stores(buf, o_ref, sems):
    return lambda j, span: pltpu.make_async_copy(buf.at[j], o_ref.at[rows_of(span)], sems.at[j])


def local_kernel(length_ref, q_hbm, k_hbm, v_hbm, out_buf, q_ref, k_ref, v_ref, wide, sems, *work):
    live = length_ref[lax.axis_index("replica")]

    def fetch(slot):
        rows = slice(slot * SPAN, (slot + 1) * SPAN)
        return pltpu.make_async_copy(q_hbm.at[rows], q_ref.at[rows], sems.at[2 + slot])

    fetches = [
        pltpu.make_async_copy(k_hbm, k_ref, sems.at[0]),
        pltpu.make_async_copy(v_hbm, v_ref, sems.at[1]),
        fetch(0),
    ]
    for copy in fetches:
        copy.start()
    pl.when(live > 1)(fetch(1).start)
    for copy in fetches:
        copy.wait()
    widen(v_ref, wide)
    pl.when(live > 1)(fetch(1).wait)
    attend_blocks(
        [jnp.int32(0), jnp.where(live > 1, 1, -1)],
        [(q_ref.at[:SPAN],), (q_ref.at[SPAN:],)],
        k_ref,
        wide,
        out_buf,
        None,
        *work,
    )


def attend_local(lengths, queries, keys, values):
    width, key_width = queries.shape[1], keys.shape[1]
    return pl.pallas_call(
        local_kernel,
        out_shape=jax.ShapeDtypeStruct((SLOTS, SPAN, width), queries.dtype),
        in_specs=[SMEM, ANY, ANY, ANY],
        out_specs=VMEM,
        scratch_shapes=[
            pltpu.VMEM(queries.shape, queries.dtype),
            pltpu.VMEM(keys.shape, keys.dtype),
            pltpu.VMEM(values.shape, values.dtype),
            pltpu.VMEM((SLOTS * SPAN, 2 * key_width), keys.dtype),
            pltpu.SemaphoreType.DMA((2 + SLOTS,)),
            *work_space(SLOTS, width, key_width),
        ],
        compiler_params=pltpu.CompilerParams(vmem_limit_bytes=VMEM_BYTES),
        cost_estimate=cost_of(3.5),
    )(lengths, queries, keys, values)


def parts_of(refs, pieces):
    return [refs[sum(pieces[:j]) : sum(pieces[: j + 1])] for j in range(len(pieces))]


def any_of(dests):
    return functools.reduce(jnp.maximum, dests) >= 0


def first_kernel(kv_offsets, offsets, pieces, meta_ref, own_k, own_v, *refs):
    parts = sum(pieces)
    blocks, refs = refs[: len(kv_offsets)], refs[len(kv_offsets) :]
    q_refs, refs = refs[:parts], refs[parts:]
    local, o_k, o_v, k_buf, wide, out_buf, o_ref, v_buf, zeros, in_sems, out_sems, span_sems, *work = refs
    live = meta_ref[0]

    def fetches():
        yield None, own_k.at[:SPAN], k_buf.at[rows_of(0)]
        yield None, own_v.at[:SPAN], v_buf.at[rows_of(0)]
        yield live > 1, own_k.at[SPAN:], k_buf.at[rows_of(1)]
        yield live > 1, own_v.at[SPAN:], v_buf.at[rows_of(1)]

    def each(act):
        for n, (needed, here, there) in enumerate(fetches()):
            copy = getattr(pltpu.make_async_copy(here, there, in_sems.at[n]), act)
            if needed is None:
                copy()
            else:
                pl.when(needed)(copy)

    def each_span(act):
        for span in range(MAXC):
            there, sem = o_ref.at[rows_of(span)], span_sems.at[span]
            if span < SLOTS:
                copy = pltpu.make_async_copy(local.at[span], there, sem)
                pl.when(span < live)(getattr(copy, act))
            if span > 0:
                pl.when(span >= live)(getattr(pltpu.make_async_copy(zeros, there, sem), act))

    each("start")
    zeros[...] = jnp.zeros_like(zeros)
    each_span("start")
    for span in range(1, MAXC):

        @pl.when(span >= live)
        def _(span=span):
            k_buf[rows_of(span), :] = jnp.zeros((SPAN, k_buf.shape[1]), k_buf.dtype)
            v_buf[rows_of(span), :] = jnp.zeros((SPAN, v_buf.shape[1]), v_buf.dtype)

    for block, offset in zip(blocks, kv_offsets, strict=True):
        dest = meta_ref[offset]

        @pl.when(dest >= 0)
        def _(block=block, dest=dest):
            k_buf[rows_of(dest), :] = block[:SPAN, :]
            v_buf[rows_of(dest), :] = block[SPAN:, :]

    each("wait")
    copy_k = pltpu.make_async_copy(k_buf, o_k, out_sems.at[0])
    copy_v = pltpu.make_async_copy(v_buf, o_v, out_sems.at[1])
    copy_k.start()
    copy_v.start()
    dests = [meta_ref[offset] for offset in offsets]

    @pl.when(live > 1)
    def _():
        widen(v_buf, wide)

    @pl.when(any_of(dests))
    def _():
        attend_blocks(dests, parts_of(q_refs, pieces), k_buf, wide, out_buf, None, *work)

    copy_k.wait()
    copy_v.wait()
    each_span("wait")


def attend_first(meta, keys, values, kv_offsets, kv_blocks, offsets, blocks, local):
    rows, key_width = MAXC * SPAN, keys.shape[1]
    pieces = [len(block) for block in blocks]
    count, width = len(pieces), blocks[0][0].shape[1]
    out = jax.ShapeDtypeStruct((rows, key_width), keys.dtype)
    return pl.pallas_call(
        lambda *refs: first_kernel(kv_offsets, offsets, pieces, *refs),
        out_shape=(
            out,
            out,
            out,
            jax.ShapeDtypeStruct((rows, 2 * key_width), keys.dtype),
            jax.ShapeDtypeStruct((count, SPAN, width), keys.dtype),
            jax.ShapeDtypeStruct((rows, width), keys.dtype),
        ),
        in_specs=[SMEM, ANY, ANY] + [VMEM] * (len(kv_blocks) + sum(pieces) + 1),
        out_specs=(ANY, ANY, VMEM, VMEM, VMEM, ANY),
        scratch_shapes=[
            pltpu.VMEM((rows, key_width), keys.dtype),
            pltpu.VMEM((SPAN, width), keys.dtype),
            pltpu.SemaphoreType.DMA((4,)),
            pltpu.SemaphoreType.DMA((2,)),
            pltpu.SemaphoreType.DMA((MAXC,)),
            *work_space(count, width, key_width),
        ],
        compiler_params=pltpu.CompilerParams(vmem_limit_bytes=VMEM_BYTES),
        cost_estimate=cost_of(2 + 2.5 * count),
    )(meta, keys, values, *kv_blocks, *[part for block in blocks for part in block], local)


def later_kernel(offsets, pieces, meta_ref, *refs):
    parts = sum(pieces)
    q_refs, (k_ref, wide_ref, out_buf, *work) = refs[:parts], refs[parts:]
    dests = [meta_ref[offset] for offset in offsets]

    @pl.when(any_of(dests))
    def _():
        attend_blocks(dests, parts_of(q_refs, pieces), k_ref, wide_ref, out_buf, None, *work)


def attend_later(meta, offsets, blocks, ordered_keys, wide_values):
    pieces = [len(block) for block in blocks]
    count, width = len(pieces), blocks[0][0].shape[1]
    return pl.pallas_call(
        lambda *refs: later_kernel(offsets, pieces, *refs),
        out_shape=jax.ShapeDtypeStruct((count, SPAN, width), ordered_keys.dtype),
        in_specs=[SMEM] + [VMEM] * (sum(pieces) + 2),
        out_specs=VMEM,
        scratch_shapes=work_space(count, width, ordered_keys.shape[1]),
        compiler_params=pltpu.CompilerParams(vmem_limit_bytes=VMEM_BYTES),
        cost_estimate=cost_of(1 + 2.5 * count),
    )(meta, *[part for block in blocks for part in block], ordered_keys, wide_values)


def last_kernel(before, offsets, pieces, meta_ref, *refs):
    parts = sum(pieces)
    results, refs = refs[: len(before)], refs[len(before) :]
    q_refs, (k_ref, wide_ref, _, o_ref, out_buf, sems, out_sems, *work) = refs[:parts], refs[parts:]
    earlier = [
        (meta_ref[offset], result, j, n)
        for n, (result, its_offsets) in enumerate(zip(results, before, strict=True))
        for j, offset in enumerate(its_offsets)
    ]

    def each(act):
        for dest, result, j, n in earlier:
            copy = pltpu.make_async_copy(
                result.at[j], o_ref.at[rows_of(jnp.maximum(dest, 0))], sems.at[n, j]
            )
            pl.when(dest >= 0)(getattr(copy, act))

    each("start")
    dests = [meta_ref[offset] for offset in offsets]

    @pl.when(any_of(dests))
    def _():
        attend_blocks(
            dests,
            parts_of(q_refs, pieces),
            k_ref,
            wide_ref,
            out_buf,
            stores(out_buf, o_ref, out_sems),
            *work,
        )

    each("wait")


def attend_last(meta, before, results, offsets, blocks, ordered_keys, wide_values, attention):
    pieces = [len(block) for block in blocks]
    count, parts = len(pieces), sum(pieces)
    width = attention.shape[1]
    most = max(len(its_offsets) for its_offsets in before)
    return pl.pallas_call(
        lambda *refs: last_kernel(before, offsets, pieces, *refs),
        out_shape=jax.ShapeDtypeStruct(attention.shape, attention.dtype),
        in_specs=[SMEM] + [VMEM] * (len(results) + parts + 2) + [ANY],
        out_specs=ANY,
        input_output_aliases={len(results) + parts + 3: 0},
        scratch_shapes=[
            pltpu.VMEM((count, SPAN, width), attention.dtype),
            pltpu.SemaphoreType.DMA((len(before), most)),
            pltpu.SemaphoreType.DMA((count,)),
            *work_space(count, width, ordered_keys.shape[1]),
        ],
        compiler_params=pltpu.CompilerParams(vmem_limit_bytes=VMEM_BYTES),
        cost_estimate=cost_of(4),
    )(
        meta,
        *results,
        *[part for block in blocks for part in block],
        ordered_keys,
        wide_values,
        attention,
    )


def gathered_kernel(meta_ref, first_ref, later_ref, k_ref, v_ref, o_ref, wide, stacked, mixed, top, bounds):
    at = pl.program_id(1)
    live = meta_ref[0]
    widen(v_ref, wide)

    @pl.when(at == 0)
    def _():
        stack((first_ref,), stacked.at[0])

    @pl.when(at > 0)
    def _():
        stack((later_ref.at[0],), stacked.at[0])

    def work(shifted):
        if shifted:
            attend_span_shifted(at, stacked.at[0], k_ref, wide, mixed, top)
        else:
            attend_span(at, stacked.at[0], k_ref, wide, mixed)
        finish(mixed, o_ref, bounds)

    @pl.when(at < live)
    def _():
        twice_if_needed(work, lambda: None, bounds)

    @pl.when(at >= live)
    def _():
        o_ref[...] = jnp.zeros_like(o_ref)


def attend_gathered(live, source, first, later, cache_keys, cache_values):
    home_rows, key_width = cache_keys.shape
    width = first.shape[1]
    groups = key_width // HDIM
    part = width // groups
    meta = jnp.concatenate([live.reshape(1), source]).astype(jnp.int32)
    return pl.pallas_call(
        gathered_kernel,
        out_shape=jax.ShapeDtypeStruct((home_rows, width), first.dtype),
        grid_spec=pltpu.PrefetchScalarGridSpec(
            num_scalar_prefetch=1,
            grid=(groups, MAXC),
            in_specs=[
                pl.BlockSpec((SPAN, part), lambda g, m, meta: (0, g)),
                pl.BlockSpec((1, SPAN, part), lambda g, m, meta: (meta[1 + m], 0, g)),
                pl.BlockSpec((home_rows, HDIM), lambda g, m, meta: (0, g)),
                pl.BlockSpec((home_rows, HDIM), lambda g, m, meta: (0, g)),
            ],
            out_specs=pl.BlockSpec((SPAN, part), lambda g, m, meta: (m, g)),
            scratch_shapes=[
                pltpu.VMEM((home_rows, 2 * HDIM), cache_keys.dtype),
                *work_space(1, part, HDIM),
            ],
        ),
        compiler_params=pltpu.CompilerParams(vmem_limit_bytes=VMEM_BYTES),
    )(meta, first, later, cache_keys, cache_values)


def gather_all(queries, keys, values, lengths, slot_prompt, slot_span):
    mine = lax.axis_index("replica")
    home_rows, key_width = MAXC * SPAN, keys.shape[1]
    live = lengths[mine]
    spans = jnp.arange(MAXC, dtype=jnp.int32)
    matches = (slot_prompt[None, :, 1] == mine) & (slot_span[None, :, 1] == spans[:, None])
    here = jnp.any(matches, axis=1)
    source = jnp.argmax(matches, axis=1).astype(jnp.int32)
    slots_k = lax.all_gather(keys[SPAN:], "replica")
    slots_v = lax.all_gather(values[SPAN:], "replica")
    slots_q = lax.all_gather(queries[SPAN:], "replica")

    def in_order(first, slots):
        picked = jnp.take(slots, source, axis=0)
        kept = jnp.where(here[:, None, None], picked, jnp.zeros((), slots.dtype))
        return jnp.concatenate([first, kept[1:].reshape(home_rows - SPAN, key_width)], axis=0)

    cache_keys = in_order(keys[:SPAN], slots_k)
    cache_values = in_order(values[:SPAN], slots_v)
    attention = attend_gathered(live, source, queries[:SPAN], slots_q, cache_keys, cache_values)
    return (attention, cache_keys, cache_values)


def per_device(queries, keys, values, lengths, slot_prompt, slot_span):
    replicas = lax.axis_size("replica")
    if replicas != 8:
        return gather_all(queries, keys, values, lengths, slot_prompt, slot_span)
    ring = column_ring(replicas)
    farthest = replicas // 2

    def after(block, *others):
        return lax.optimization_barrier((block, others))[0]

    def joined(both):
        return list(lax.optimization_barrier(tuple(both)))

    def shift(block, step):
        pairs = [(r, ring[(n + step) % replicas]) for n, r in enumerate(ring)]
        return lax.ppermute(block, "replica", pairs)

    def go_on(both):
        return [shift(both[0], 1), shift(both[1], -1)]

    own_kv = pack_kv(keys, values)
    kv = [[own_kv, own_kv]]
    kv.append(go_on(kv[0]))
    own_top, own_bottom = pack_q(after(queries, own_kv))
    first, second = [[own_top, own_bottom]], [[own_bottom, own_top]]
    first.append(joined(go_on(first[0])))
    kv[1] = joined(kv[1])
    kv.append(joined(go_on(kv[1])))
    local = attend_local(lengths, after(queries, kv[1]), keys, values)
    second.append(joined(go_on([after(block, first[1]) for block in second[0]])))
    kv.append(joined(go_on([after(block, local) for block in kv[2]])))
    first.append(joined(go_on([after(block, kv[3]) for block in first[1]])))
    kv.append([shift(kv[3][0], 1)])
    second.append(joined(go_on([after(block, kv[3]) for block in second[1]])))
    meta = places(lengths, slot_prompt, slot_span)
    offsets = [[n, replicas - n] for n in range(1, farthest)]

    def blocks(n):
        return [(first[n][0], second[n][0]), (second[n][1], first[n][1])]

    cache_keys, cache_values, ordered_keys, wide_values, result, attention = attend_first(
        meta,
        keys,
        values,
        sum(offsets, []) + [farthest],
        sum(kv[1:], []),
        offsets[0],
        blocks(1),
        local,
    )
    results = [result]
    first.append(joined(go_on(first[2])))
    second.append(joined(go_on([after(block, results[0]) for block in second[2]])))
    results.append(attend_later(meta, offsets[1], blocks(2), ordered_keys, wide_values))
    last = (
        shift(after(first[3][0], results[1]), 1),
        shift(after(first[3][1], results[1]), -1),
    )
    results.append(attend_later(meta, offsets[2], blocks(3), ordered_keys, wide_values))
    attention = attend_last(
        meta, offsets, results, [farthest], [last], ordered_keys, wide_values, attention
    )
    return (attention, cache_keys, cache_values)


def solution(mesh):
    in_specs = (
        P(("group", "replica"), "tensor"),
        P(("group", "replica"), "tensor"),
        P(("group", "replica"), "tensor"),
        P("group"),
        P("group", None),
        P("group", None),
    )
    out_specs = (
        P(("group", "replica"), "tensor"),
        P(("group", "replica"), "tensor"),
        P(("group", "replica"), "tensor"),
    )
    return jax.shard_map(
        per_device, mesh=mesh, in_specs=in_specs, out_specs=out_specs, check_vma=False
    )
```

```python
import functools
import math

import jax
import jax.numpy as jnp
from jax import lax
from jax.experimental import pallas as pl
from jax.experimental.pallas import tpu as pltpu
from jax.sharding import PartitionSpec as P

HDIM = 128
SPAN = 128
SLOTS = 2
MAXC = 8
BLOCK = 4
PART = 2
LOG2E = 1.0 / math.log(2.0)
VMEM_BYTES = 40 * 1024 * 1024
MOST_VMEM_BYTES = 60 * 1024 * 1024
LEAST_SUM, MOST_SUM = 1e-20, 1e30
ANY = pl.BlockSpec(memory_space=pl.ANY)
SMEM = pl.BlockSpec(memory_space=pltpu.SMEM)
VMEM = pl.BlockSpec(memory_space=pltpu.VMEM)


def cost_of(us):
    return pl.CostEstimate(flops=int(us * 1.15e9), bytes_accessed=0, transcendentals=0)


def column_ring(replicas):
    return list(range(0, replicas, 2)) + list(range(replicas - 1, 0, -2))


def copy_all(copies):
    for copy in copies:
        copy.start()
    for copy in copies:
        copy.wait()


def pack_kv_kernel(k_ref, v_ref, o_ref, sems):
    copy_all(
        [
            pltpu.make_async_copy(k_ref.at[SPAN:], o_ref.at[:SPAN], sems.at[0]),
            pltpu.make_async_copy(v_ref.at[SPAN:], o_ref.at[SPAN:], sems.at[1]),
        ]
    )


def pack_kv(keys, values):
    return pl.pallas_call(
        pack_kv_kernel,
        out_shape=jax.ShapeDtypeStruct((2 * SPAN, keys.shape[1]), keys.dtype),
        in_specs=[ANY] * 2,
        out_specs=VMEM,
        scratch_shapes=[pltpu.SemaphoreType.DMA((2,))],
        compiler_params=pltpu.CompilerParams(vmem_limit_bytes=MOST_VMEM_BYTES),
        cost_estimate=cost_of(1),
    )(keys, values)


def pack_q_kernel(q_ref, o_top, o_bottom, sems):
    half = SPAN // 2
    copy_all(
        [
            pltpu.make_async_copy(q_ref.at[SPAN : SPAN + half], o_top, sems.at[0]),
            pltpu.make_async_copy(q_ref.at[SPAN + half :], o_bottom, sems.at[1]),
        ]
    )


def pack_q(queries):
    half = jax.ShapeDtypeStruct((SPAN // 2, queries.shape[1]), queries.dtype)
    return pl.pallas_call(
        pack_q_kernel,
        out_shape=(half, half),
        in_specs=[ANY],
        out_specs=(VMEM, VMEM),
        scratch_shapes=[pltpu.SemaphoreType.DMA((2,))],
        compiler_params=pltpu.CompilerParams(vmem_limit_bytes=VMEM_BYTES),
        cost_estimate=cost_of(1),
    )(queries)


def places(lengths, slot_prompt, slot_span):
    replicas = lengths.shape[0]
    mine = lax.axis_index("replica")
    ring = jnp.arange(replicas, dtype=jnp.int32)
    place = jnp.where(mine % 2 == 0, mine // 2, replicas - 1 - mine // 2)
    at = (place + replicas - ring) % replicas
    other = jnp.where(at < replicas // 2, 2 * at, 2 * (replicas - at) - 1)
    chosen = other[:, None] == ring[None, :]
    wanted = chosen & (slot_prompt[None, :, 1] == mine) & (ring[:, None] > 0)
    spans = jnp.where(wanted, slot_span[None, :, 1] + 1, 0)
    whole = jnp.where(chosen & (ring[:, None] == 0), lengths[None, :] + 1, 0)
    return jnp.sum(spans + whole, axis=1) - 1


def widen(v_ref, wide_ref):
    for at in range(0, v_ref.shape[-1], HDIM):
        wide_ref[:, 2 * at : 2 * at + HDIM] = v_ref[:, at : at + HDIM]
        wide_ref[:, 2 * at + HDIM : 2 * at + 2 * HDIM] = jnp.ones(
            (v_ref.shape[0], HDIM), v_ref.dtype
        )


def stack(q_ref, stacked):
    kv_heads, rows, _ = stacked.shape
    tall = q_ref.shape[0]
    group = rows // tall
    for shared in range(kv_heads):
        for h in range(group):
            at = (shared * group + h) * HDIM
            stacked[shared, h * tall : (h + 1) * tall, :] = q_ref[:, at : at + HDIM]


def divide(mixed, shared, o_ref, bounds):
    tall = o_ref.shape[0]
    group = mixed.shape[0] // tall
    total = mixed[:, HDIM:]
    inverse = pl.reciprocal(total, approx=True)
    inverse = inverse * (2.0 - total * inverse)
    result = (mixed[:, :HDIM] * inverse).astype(o_ref.dtype)
    for h in range(group):
        at = (shared * group + h) * HDIM
        o_ref[:, at : at + HDIM] = result[h * tall : (h + 1) * tall, :]
    total = total.reshape(-1, 8, HDIM)
    bounds[0] = jnp.minimum(bounds[0], jnp.min(total, axis=0))
    bounds[1] = jnp.maximum(bounds[1], jnp.max(total, axis=0))


def attend_piece(span, start, stacked, k_ref, wide_ref, mixed, o_ref, bounds):
    kv_heads, rows, _ = stacked.shape
    heads = range(kv_heads)
    tall = o_ref.shape[0]
    scale = LOG2E / math.sqrt(HDIM)
    blocks = span // BLOCK
    edge = span % PART * SPAN + start

    def keys_of(block, spans):
        return pl.ds(pl.multiple_of(block * BLOCK * SPAN, BLOCK * SPAN), spans * SPAN)

    def scores(shared, block, spans, masked):
        found = lax.dot_general(
            stacked[shared],
            k_ref[keys_of(block, spans), shared * HDIM : (shared + 1) * HDIM],
            (((1,), (1,)), ((), ())),
            preferred_element_type=jnp.float32,
        )
        if masked:
            seen = (spans - PART) * SPAN
            row = lax.broadcasted_iota(jnp.int32, (rows, PART * SPAN), 0) % tall
            column = lax.broadcasted_iota(jnp.int32, (rows, PART * SPAN), 1)
            last = jnp.where(column <= row + edge, found[:, seen:], -jnp.inf)
            found = jnp.concatenate([found[:, :seen], last], axis=1) if seen else last
        return found

    def products(shared, block, spans, found):
        return jnp.dot(
            jnp.exp2(found * scale).astype(jnp.bfloat16),
            wide_ref[keys_of(block, spans), 2 * shared * HDIM : 2 * (shared + 1) * HDIM],
            preferred_element_type=jnp.float32,
        )

    def add(block, carry):
        found = [scores(shared, block, BLOCK, False) for shared in heads]
        for shared in heads:
            mixed[shared] += products(shared, block, BLOCK, found[shared])
        return carry

    mixed[...] = jnp.zeros_like(mixed)
    most = k_ref.shape[0] // SPAN
    if most > BLOCK:
        lax.fori_loop(0, blocks, add, 0)
    for spans in range(PART, min(BLOCK, most) + 1, PART):

        @pl.when(span % BLOCK // PART == spans // PART - 1)
        def _(spans=spans):
            found = [scores(shared, blocks, spans, True) for shared in heads]
            for shared in heads:
                whole = mixed[shared] + products(shared, blocks, spans, found[shared])
                divide(whole, shared, o_ref, bounds)


def attend_piece_shifted(span, start, stacked, k_ref, wide_ref, mixed, o_ref, bounds, top):
    kv_heads, rows, _ = stacked.shape
    tall = o_ref.shape[0]
    scale = LOG2E / math.sqrt(HDIM)

    def one_head(shared, carry):
        def scores(block):
            found = lax.dot_general(
                stacked[shared],
                k_ref[rows_of(block), pl.ds(pl.multiple_of(shared * HDIM, HDIM), HDIM)],
                (((1,), (1,)), ((), ())),
                preferred_element_type=jnp.float32,
            )
            row = lax.broadcasted_iota(jnp.int32, (rows, SPAN), 0) % tall
            column = lax.broadcasted_iota(jnp.int32, (rows, SPAN), 1)
            return jnp.where(column <= row + (span - block) * SPAN + start, found, -jnp.inf)

        def look(block, carry):
            top[...] = jnp.maximum(top[...], scores(block))
            return carry

        def add(block, carry):
            weights = jnp.exp2((scores(block) - top[...]) * scale).astype(jnp.bfloat16)
            mixed[shared] += jnp.dot(
                weights,
                wide_ref[
                    rows_of(block), pl.ds(pl.multiple_of(2 * shared * HDIM, 2 * HDIM), 2 * HDIM)
                ],
                preferred_element_type=jnp.float32,
            )
            return carry

        top[...] = jnp.full_like(top, -jnp.inf)
        lax.fori_loop(0, span + 1, look, 0)
        top[...] = jnp.broadcast_to(jnp.max(top[...], axis=1, keepdims=True), top.shape)
        mixed[shared] = jnp.zeros(mixed.shape[1:], mixed.dtype)
        lax.fori_loop(0, span + 1, add, 0)
        return carry

    lax.fori_loop(0, kv_heads, one_head, 0)
    for shared in range(kv_heads):
        divide(mixed[shared], shared, o_ref, bounds)


def twice_if_needed(work, drain, bounds):
    bounds[...] = jnp.ones_like(bounds)
    work(False)
    safe = (jnp.min(bounds[0]) > LEAST_SUM) & (jnp.max(bounds[1]) < MOST_SUM)
    drain()

    @pl.when(jnp.logical_not(safe))
    def _():
        work(True)
        drain()


def work_space(count, tall, width, key_width):
    kv_heads = key_width // HDIM
    rows = width // key_width * tall
    return [
        pltpu.VMEM((count, kv_heads, rows, HDIM), jnp.bfloat16),
        pltpu.VMEM((kv_heads, rows, 2 * HDIM), jnp.float32),
        pltpu.VMEM((rows, HDIM), jnp.float32),
        pltpu.VMEM((2, 8, HDIM), jnp.float32),
    ]


def rows_of(span):
    return pl.ds(pl.multiple_of(span * SPAN, SPAN), SPAN)


def half_of(span, start):
    return pl.ds(pl.multiple_of(span * SPAN + start, SPAN // 2), SPAN // 2)


def pick(j, options):
    chosen = options[0]
    for n in range(1, len(options)):
        chosen = jnp.where(j == n, options[n], chosen)
    return chosen


def attend_pieces(dests, starts, q_refs, k_ref, wide_ref, out_buf, store, stacked, mixed, top, bounds):
    count = len(dests)
    for j in range(count):

        @pl.when(dests[j] >= 0)
        def _(j=j):
            stack(q_refs[j], stacked.at[j])

    def work(shifted):
        def one(j, carry):
            dest, start = pick(j, dests), pick(j, starts)

            @pl.when(dest >= 0)
            def _():
                args = (dest, start, stacked.at[j], k_ref, wide_ref, mixed, out_buf.at[j], bounds)
                if shifted:
                    attend_piece_shifted(*args, top)
                else:
                    attend_piece(*args)
                if store is not None:
                    store(j, dest, start).start()

            return carry

        lax.fori_loop(0, count, one, 0)

    def drain():
        if store is not None:
            for j in range(count):
                pl.when(dests[j] >= 0)(store(j, jnp.maximum(dests[j], 0), starts[j]).wait)

    twice_if_needed(work, drain, bounds)


def stores(buf, o_ref, sems):
    return lambda j, span, start: pltpu.make_async_copy(
        buf.at[j], o_ref.at[half_of(span, start)], sems.at[j]
    )


def local_kernel(length_ref, q_hbm, k_hbm, v_hbm, out_buf, q_ref, k_ref, v_ref, wide, sems, *work):
    live = length_ref[lax.axis_index("replica")]

    def fetch(slot):
        rows = slice(slot * SPAN, (slot + 1) * SPAN)
        return pltpu.make_async_copy(q_hbm.at[rows], q_ref.at[rows], sems.at[2 + slot])

    fetches = [
        pltpu.make_async_copy(k_hbm, k_ref, sems.at[0]),
        pltpu.make_async_copy(v_hbm, v_ref, sems.at[1]),
        fetch(0),
    ]
    for copy in fetches:
        copy.start()
    pl.when(live > 1)(fetch(1).start)
    for copy in fetches:
        copy.wait()
    widen(v_ref, wide)
    pl.when(live > 1)(fetch(1).wait)
    half = SPAN // 2
    second = jnp.where(live > 1, 1, -1)
    attend_pieces(
        [jnp.int32(0), jnp.int32(0), second, second],
        [0, half, 0, half],
        [q_ref.at[n * half : (n + 1) * half] for n in range(2 * SLOTS)],
        k_ref,
        wide,
        out_buf,
        None,
        *work,
    )


def attend_local(lengths, queries, keys, values):
    width, key_width = queries.shape[1], keys.shape[1]
    return pl.pallas_call(
        local_kernel,
        out_shape=jax.ShapeDtypeStruct((2 * SLOTS, SPAN // 2, width), queries.dtype),
        in_specs=[SMEM, ANY, ANY, ANY],
        out_specs=VMEM,
        scratch_shapes=[
            pltpu.VMEM(queries.shape, queries.dtype),
            pltpu.VMEM(keys.shape, keys.dtype),
            pltpu.VMEM(values.shape, values.dtype),
            pltpu.VMEM((SLOTS * SPAN, 2 * key_width), keys.dtype),
            pltpu.SemaphoreType.DMA((2 + SLOTS,)),
            *work_space(2 * SLOTS, SPAN // 2, width, key_width),
        ],
        compiler_params=pltpu.CompilerParams(vmem_limit_bytes=VMEM_BYTES),
        cost_estimate=cost_of(3.5),
    )(lengths, queries, keys, values)


def any_of(dests):
    return functools.reduce(jnp.maximum, dests) >= 0


def first_kernel(kv_offsets, places, meta_ref, own_k, own_v, *refs):
    blocks, refs = refs[: len(kv_offsets)], refs[len(kv_offsets) :]
    q_refs, refs = refs[: len(places)], refs[len(places) :]
    local, o_k, o_v, k_buf, wide, out_buf, o_ref, v_buf, zeros, in_sems, out_sems, span_sems, *work = refs
    live = meta_ref[0]
    half = SPAN // 2

    def fetches():
        yield None, own_k.at[:SPAN], k_buf.at[rows_of(0)]
        yield None, own_v.at[:SPAN], v_buf.at[rows_of(0)]
        yield live > 1, own_k.at[SPAN:], k_buf.at[rows_of(1)]
        yield live > 1, own_v.at[SPAN:], v_buf.at[rows_of(1)]

    def each(act):
        for n, (needed, here, there) in enumerate(fetches()):
            copy = getattr(pltpu.make_async_copy(here, there, in_sems.at[n]), act)
            if needed is None:
                copy()
            else:
                pl.when(needed)(copy)

    def each_span(act):
        for span in range(MAXC):
            if span < SLOTS:
                for n in range(2):
                    copy = pltpu.make_async_copy(
                        local.at[2 * span + n],
                        o_ref.at[half_of(span, n * half)],
                        span_sems.at[span, n],
                    )
                    pl.when(span < live)(getattr(copy, act))
            if span > 0:
                copy = pltpu.make_async_copy(zeros, o_ref.at[rows_of(span)], span_sems.at[span, 0])
                pl.when(span >= live)(getattr(copy, act))

    each("start")
    zeros[...] = jnp.zeros_like(zeros)
    each_span("start")
    for span in range(1, MAXC):

        @pl.when(span >= live)
        def _(span=span):
            k_buf[rows_of(span), :] = jnp.zeros((SPAN, k_buf.shape[1]), k_buf.dtype)
            v_buf[rows_of(span), :] = jnp.zeros((SPAN, v_buf.shape[1]), v_buf.dtype)

    for block, offset in zip(blocks, kv_offsets, strict=True):
        dest = meta_ref[offset]

        @pl.when(dest >= 0)
        def _(block=block, dest=dest):
            k_buf[rows_of(dest), :] = block[:SPAN, :]
            v_buf[rows_of(dest), :] = block[SPAN:, :]

    each("wait")
    copy_k = pltpu.make_async_copy(k_buf, o_k, out_sems.at[0])
    copy_v = pltpu.make_async_copy(v_buf, o_v, out_sems.at[1])
    copy_k.start()
    copy_v.start()
    dests = [meta_ref[offset] for offset, _ in places]

    @pl.when(live > 1)
    def _():
        widen(v_buf, wide)

    @pl.when(any_of(dests))
    def _():
        starts = [start for _, start in places]
        attend_pieces(dests, starts, q_refs, k_buf, wide, out_buf, None, *work)

    copy_k.wait()
    copy_v.wait()
    each_span("wait")


def attend_first(meta, keys, values, kv_offsets, kv_blocks, pieces, local):
    rows, key_width = MAXC * SPAN, keys.shape[1]
    queries = [piece[0] for piece in pieces]
    places = [piece[1:] for piece in pieces]
    count, (tall, width) = len(pieces), queries[0].shape
    out = jax.ShapeDtypeStruct((rows, key_width), keys.dtype)
    return pl.pallas_call(
        lambda *refs: first_kernel(kv_offsets, places, *refs),
        out_shape=(
            out,
            out,
            out,
            jax.ShapeDtypeStruct((rows, 2 * key_width), keys.dtype),
            jax.ShapeDtypeStruct((count, tall, width), keys.dtype),
            jax.ShapeDtypeStruct((rows, width), keys.dtype),
        ),
        in_specs=[SMEM, ANY, ANY] + [VMEM] * (len(kv_blocks) + count + 1),
        out_specs=(ANY, ANY, VMEM, VMEM, VMEM, ANY),
        scratch_shapes=[
            pltpu.VMEM((rows, key_width), keys.dtype),
            pltpu.VMEM((SPAN, width), keys.dtype),
            pltpu.SemaphoreType.DMA((4,)),
            pltpu.SemaphoreType.DMA((2,)),
            pltpu.SemaphoreType.DMA((MAXC, 2)),
            *work_space(count, tall, width, key_width),
        ],
        compiler_params=pltpu.CompilerParams(vmem_limit_bytes=VMEM_BYTES),
        cost_estimate=cost_of(2 + 1.3 * count),
    )(meta, keys, values, *kv_blocks, *queries, local)


def later_kernel(places, meta_ref, *refs):
    q_refs, (k_ref, wide_ref, out_buf, *work) = refs[: len(places)], refs[len(places) :]
    dests = [meta_ref[offset] for offset, _ in places]

    @pl.when(any_of(dests))
    def _():
        starts = [start for _, start in places]
        attend_pieces(dests, starts, q_refs, k_ref, wide_ref, out_buf, None, *work)


def attend_later(meta, pieces, ordered_keys, wide_values):
    queries = [piece[0] for piece in pieces]
    places = [piece[1:] for piece in pieces]
    count, (tall, width) = len(pieces), queries[0].shape
    return pl.pallas_call(
        lambda *refs: later_kernel(places, *refs),
        out_shape=jax.ShapeDtypeStruct((count, tall, width), ordered_keys.dtype),
        in_specs=[SMEM] + [VMEM] * (count + 2),
        out_specs=VMEM,
        scratch_shapes=work_space(count, tall, width, ordered_keys.shape[1]),
        compiler_params=pltpu.CompilerParams(vmem_limit_bytes=VMEM_BYTES),
        cost_estimate=cost_of(1 + 1.3 * count),
    )(meta, *queries, ordered_keys, wide_values)


def last_kernel(before, places, meta_ref, *refs):
    results, refs = refs[: len(before)], refs[len(before) :]
    q_refs, refs = refs[: len(places)], refs[len(places) :]
    k_ref, wide_ref, _, o_ref, out_buf, sems, out_sems, *work = refs

    def each(act):
        for n, (result, its_places) in enumerate(zip(results, before, strict=True)):
            for j, (offset, start) in enumerate(its_places):
                dest = meta_ref[offset]
                copy = pltpu.make_async_copy(
                    result.at[j], o_ref.at[half_of(jnp.maximum(dest, 0), start)], sems.at[n, j]
                )
                pl.when(dest >= 0)(getattr(copy, act))

    each("start")
    dests = [meta_ref[offset] for offset, _ in places]

    @pl.when(any_of(dests))
    def _():
        starts = [start for _, start in places]
        store = stores(out_buf, o_ref, out_sems)
        attend_pieces(dests, starts, q_refs, k_ref, wide_ref, out_buf, store, *work)

    each("wait")


def attend_last(meta, before, results, pieces, ordered_keys, wide_values, attention):
    queries = [piece[0] for piece in pieces]
    places = [piece[1:] for piece in pieces]
    count, (tall, width) = len(pieces), queries[0].shape
    most = max(len(its_places) for its_places in before)
    return pl.pallas_call(
        lambda *refs: last_kernel(before, places, *refs),
        out_shape=jax.ShapeDtypeStruct(attention.shape, attention.dtype),
        in_specs=[SMEM] + [VMEM] * (len(results) + count + 2) + [ANY],
        out_specs=ANY,
        input_output_aliases={len(results) + count + 3: 0},
        scratch_shapes=[
            pltpu.VMEM((count, tall, width), attention.dtype),
            pltpu.SemaphoreType.DMA((len(before), most)),
            pltpu.SemaphoreType.DMA((count,)),
            *work_space(count, tall, width, ordered_keys.shape[1]),
        ],
        compiler_params=pltpu.CompilerParams(vmem_limit_bytes=VMEM_BYTES),
        cost_estimate=cost_of(4),
    )(meta, *results, *queries, ordered_keys, wide_values, attention)


def gathered_kernel(meta_ref, first_ref, later_ref, k_ref, v_ref, o_ref, wide, stacked, mixed, top, bounds):
    at = pl.program_id(1)
    live = meta_ref[0]
    widen(v_ref, wide)

    @pl.when(at == 0)
    def _():
        stack(first_ref, stacked.at[0])

    @pl.when(at > 0)
    def _():
        stack(later_ref.at[0], stacked.at[0])

    def work(shifted):
        args = (at, 0, stacked.at[0], k_ref, wide, mixed, o_ref, bounds)
        if shifted:
            attend_piece_shifted(*args, top)
        else:
            attend_piece(*args)

    @pl.when(at < live)
    def _():
        twice_if_needed(work, lambda: None, bounds)

    @pl.when(at >= live)
    def _():
        o_ref[...] = jnp.zeros_like(o_ref)


def attend_gathered(live, source, first, later, cache_keys, cache_values):
    home_rows, key_width = cache_keys.shape
    width = first.shape[1]
    groups = key_width // HDIM
    part = width // groups
    meta = jnp.concatenate([live.reshape(1), source]).astype(jnp.int32)
    return pl.pallas_call(
        gathered_kernel,
        out_shape=jax.ShapeDtypeStruct((home_rows, width), first.dtype),
        grid_spec=pltpu.PrefetchScalarGridSpec(
            num_scalar_prefetch=1,
            grid=(groups, MAXC),
            in_specs=[
                pl.BlockSpec((SPAN, part), lambda g, m, meta: (0, g)),
                pl.BlockSpec((1, SPAN, part), lambda g, m, meta: (meta[1 + m], 0, g)),
                pl.BlockSpec((home_rows, HDIM), lambda g, m, meta: (0, g)),
                pl.BlockSpec((home_rows, HDIM), lambda g, m, meta: (0, g)),
            ],
            out_specs=pl.BlockSpec((SPAN, part), lambda g, m, meta: (m, g)),
            scratch_shapes=[
                pltpu.VMEM((home_rows, 2 * HDIM), cache_keys.dtype),
                *work_space(1, SPAN, part, HDIM),
            ],
        ),
        compiler_params=pltpu.CompilerParams(vmem_limit_bytes=VMEM_BYTES),
    )(meta, first, later, cache_keys, cache_values)


def gather_all(queries, keys, values, lengths, slot_prompt, slot_span):
    mine = lax.axis_index("replica")
    home_rows, key_width = MAXC * SPAN, keys.shape[1]
    live = lengths[mine]
    spans = jnp.arange(MAXC, dtype=jnp.int32)
    matches = (slot_prompt[None, :, 1] == mine) & (slot_span[None, :, 1] == spans[:, None])
    here = jnp.any(matches, axis=1)
    source = jnp.argmax(matches, axis=1).astype(jnp.int32)
    slots_k = lax.all_gather(keys[SPAN:], "replica")
    slots_v = lax.all_gather(values[SPAN:], "replica")
    slots_q = lax.all_gather(queries[SPAN:], "replica")

    def in_order(first, slots):
        picked = jnp.take(slots, source, axis=0)
        kept = jnp.where(here[:, None, None], picked, jnp.zeros((), slots.dtype))
        return jnp.concatenate([first, kept[1:].reshape(home_rows - SPAN, key_width)], axis=0)

    cache_keys = in_order(keys[:SPAN], slots_k)
    cache_values = in_order(values[:SPAN], slots_v)
    attention = attend_gathered(live, source, queries[:SPAN], slots_q, cache_keys, cache_values)
    return (attention, cache_keys, cache_values)


def per_device(queries, keys, values, lengths, slot_prompt, slot_span):
    replicas = lax.axis_size("replica")
    if replicas != 8:
        return gather_all(queries, keys, values, lengths, slot_prompt, slot_span)
    ring = column_ring(replicas)
    farthest = replicas // 2

    def after(block, *others):
        return lax.optimization_barrier((block, others))[0]

    def joined(both):
        return list(lax.optimization_barrier(tuple(both)))

    def shift(block, step):
        pairs = [(r, ring[(n + step) % replicas]) for n, r in enumerate(ring)]
        return lax.ppermute(block, "replica", pairs)

    def go_on(both):
        return [shift(both[0], 1), shift(both[1], -1)]

    own_kv = pack_kv(keys, values)
    kv = [[own_kv, own_kv]]
    kv.append(go_on(kv[0]))
    own_top, own_bottom = pack_q(after(queries, own_kv))
    first, second = [[own_top, own_bottom]], [[own_bottom, own_top]]
    first.append(joined(go_on(first[0])))
    kv[1] = joined(kv[1])
    kv.append(joined(go_on(kv[1])))
    local = attend_local(lengths, after(queries, kv[1]), keys, values)
    second.append(joined(go_on([after(block, first[1]) for block in second[0]])))
    kv.append(joined(go_on([after(block, local) for block in kv[2]])))
    first.append(joined(go_on([after(block, kv[3]) for block in first[1]])))
    kv.append([shift(kv[3][0], 1)])
    second.append(joined(go_on([after(block, kv[3]) for block in second[1]])))
    meta = places(lengths, slot_prompt, slot_span)
    offsets = [[n, replicas - n] for n in range(1, farthest)]

    def wave(n, which):
        up, down = offsets[n - 1]
        if which is first:
            return [(first[n][0], up, 0), (first[n][1], down, half)]
        return [(second[n][0], up, half), (second[n][1], down, 0)]

    half = SPAN // 2
    cache_keys, cache_values, ordered_keys, wide_values, result, attention = attend_first(
        meta,
        keys,
        values,
        sum(offsets, []) + [farthest],
        sum(kv[1:], []),
        wave(1, first) + wave(1, second),
        local,
    )
    results, before = [result], [wave(1, first) + wave(1, second)]

    def attend(n, which):
        results.append(attend_later(meta, wave(n, which), ordered_keys, wide_values))
        before.append(wave(n, which))

    first.append(joined(go_on(first[2])))
    attend(2, first)
    second.append(joined(go_on([after(block, results[-1]) for block in second[2]])))
    attend(2, second)
    last = [
        (shift(after(first[3][0], results[-1]), 1), farthest, 0),
        (shift(after(first[3][1], results[-1]), -1), farthest, half),
    ]
    attend(3, first)
    attend(3, second)
    before = [[piece[1:] for piece in pieces] for pieces in before]
    attention = attend_last(
        meta, before, results, last, ordered_keys, wide_values, attention
    )
    return (attention, cache_keys, cache_values)


def solution(mesh):
    in_specs = (
        P(("group", "replica"), "tensor"),
        P(("group", "replica"), "tensor"),
        P(("group", "replica"), "tensor"),
        P("group"),
        P("group", None),
        P("group", None),
    )
    out_specs = (
        P(("group", "replica"), "tensor"),
        P(("group", "replica"), "tensor"),
        P(("group", "replica"), "tensor"),
    )
    return jax.shard_map(
        per_device, mesh=mesh, in_specs=in_specs, out_specs=out_specs, check_vma=False
    )
```

```python
import functools
import math

import jax
import jax.numpy as jnp
from jax import lax
from jax.experimental import pallas as pl
from jax.experimental.pallas import tpu as pltpu
from jax.sharding import PartitionSpec as P

HDIM = 128
SPAN = 128
SLOTS = 2
LANES = 128
MAXC = 8
BLOCK = 4
PART = 2
LOG2E = 1.0 / math.log(2.0)
VMEM_BYTES = 40 * 1024 * 1024
MOST_VMEM_BYTES = 60 * 1024 * 1024
LEAST_SUM, MOST_SUM = 1e-20, 1e30
ANY = pl.BlockSpec(memory_space=pl.ANY)
SMEM = pl.BlockSpec(memory_space=pltpu.SMEM)
VMEM = pl.BlockSpec(memory_space=pltpu.VMEM)


def cost_of(us):
    return pl.CostEstimate(flops=int(us * 1.15e9), bytes_accessed=0, transcendentals=0)


def column_ring(replicas):
    return list(range(0, replicas, 2)) + list(range(replicas - 1, 0, -2))


def copy_all(copies):
    for copy in copies:
        copy.start()
    for copy in copies:
        copy.wait()


def pack_kv_kernel(k_ref, v_ref, o_ref, sems):
    copy_all(
        [
            pltpu.make_async_copy(k_ref.at[SPAN:], o_ref.at[:SPAN], sems.at[0]),
            pltpu.make_async_copy(v_ref.at[SPAN:], o_ref.at[SPAN:], sems.at[1]),
        ]
    )


def pack_kv(keys, values):
    return pl.pallas_call(
        pack_kv_kernel,
        out_shape=jax.ShapeDtypeStruct((2 * SPAN, keys.shape[1]), keys.dtype),
        in_specs=[ANY] * 2,
        out_specs=VMEM,
        scratch_shapes=[pltpu.SemaphoreType.DMA((2,))],
        compiler_params=pltpu.CompilerParams(vmem_limit_bytes=MOST_VMEM_BYTES),
        cost_estimate=cost_of(1),
    )(keys, values)


def pack_q_kernel(q_ref, o_top, o_bottom, sems):
    half = SPAN // 2
    copy_all(
        [
            pltpu.make_async_copy(q_ref.at[SPAN : SPAN + half], o_top, sems.at[0]),
            pltpu.make_async_copy(q_ref.at[SPAN + half :], o_bottom, sems.at[1]),
        ]
    )


def pack_q(queries):
    half = jax.ShapeDtypeStruct((SPAN // 2, queries.shape[1]), queries.dtype)
    return pl.pallas_call(
        pack_q_kernel,
        out_shape=(half, half),
        in_specs=[ANY],
        out_specs=(VMEM, VMEM),
        scratch_shapes=[pltpu.SemaphoreType.DMA((2,))],
        compiler_params=pltpu.CompilerParams(vmem_limit_bytes=VMEM_BYTES),
        cost_estimate=cost_of(1),
    )(queries)


def places(lengths, slot_prompt, slot_span):
    replicas = lengths.shape[0]
    mine = lax.axis_index("replica")
    ring = jnp.arange(replicas, dtype=jnp.int32)
    place = jnp.where(mine % 2 == 0, mine // 2, replicas - 1 - mine // 2)
    at = (place + replicas - ring) % replicas
    other = jnp.where(at < replicas // 2, 2 * at, 2 * (replicas - at) - 1)
    chosen = other[:, None] == ring[None, :]
    wanted = chosen & (slot_prompt[None, :, 1] == mine) & (ring[:, None] > 0)
    spans = jnp.where(wanted, slot_span[None, :, 1] + 1, 0)
    whole = jnp.where(chosen & (ring[:, None] == 0), lengths[None, :] + 1, 0)
    table = jnp.sum(spans + whole, axis=1, keepdims=True) - 1
    return jnp.broadcast_to(table, (replicas, LANES))


def entry(meta_ref, n):
    return jnp.max(meta_ref[n : n + 1, :])


def entries(meta_ref, offsets):
    found = {offset: entry(meta_ref, offset) for offset in dict.fromkeys(offsets)}
    return [found[offset] for offset in offsets]


def widen(v_ref, wide_ref):
    for at in range(0, v_ref.shape[-1], HDIM):
        wide_ref[:, 2 * at : 2 * at + HDIM] = v_ref[:, at : at + HDIM]
        wide_ref[:, 2 * at + HDIM : 2 * at + 2 * HDIM] = jnp.ones(
            (v_ref.shape[0], HDIM), v_ref.dtype
        )


def stack(q_ref, stacked):
    kv_heads, rows, _ = stacked.shape
    tall = q_ref.shape[0]
    group = rows // tall
    for shared in range(kv_heads):
        for h in range(group):
            at = (shared * group + h) * HDIM
            stacked[shared, h * tall : (h + 1) * tall, :] = q_ref[:, at : at + HDIM]


def divide(mixed, shared, o_ref, bounds):
    tall = o_ref.shape[0]
    group = mixed.shape[0] // tall
    total = mixed[:, HDIM:]
    inverse = pl.reciprocal(total, approx=True)
    inverse = inverse * (2.0 - total * inverse)
    result = (mixed[:, :HDIM] * inverse).astype(o_ref.dtype)
    for h in range(group):
        at = (shared * group + h) * HDIM
        o_ref[:, at : at + HDIM] = result[h * tall : (h + 1) * tall, :]
    total = total.reshape(-1, 8, HDIM)
    bounds[0] = jnp.minimum(bounds[0], jnp.min(total, axis=0))
    bounds[1] = jnp.maximum(bounds[1], jnp.max(total, axis=0))


def attend_piece(span, start, stacked, k_ref, wide_ref, mixed, o_ref, bounds):
    kv_heads, rows, _ = stacked.shape
    heads = range(kv_heads)
    tall = o_ref.shape[0]
    scale = LOG2E / math.sqrt(HDIM)
    blocks = span // BLOCK
    edge = span % PART * SPAN + start

    def keys_of(block, spans):
        return pl.ds(pl.multiple_of(block * BLOCK * SPAN, BLOCK * SPAN), spans * SPAN)

    def scores(shared, block, spans, masked):
        found = lax.dot_general(
            stacked[shared],
            k_ref[keys_of(block, spans), shared * HDIM : (shared + 1) * HDIM],
            (((1,), (1,)), ((), ())),
            preferred_element_type=jnp.float32,
        )
        if masked:
            seen = (spans - PART) * SPAN
            row = lax.broadcasted_iota(jnp.int32, (rows, PART * SPAN), 0) % tall
            column = lax.broadcasted_iota(jnp.int32, (rows, PART * SPAN), 1)
            last = jnp.where(column <= row + edge, found[:, seen:], -jnp.inf)
            found = jnp.concatenate([found[:, :seen], last], axis=1) if seen else last
        return found

    def products(shared, block, spans, found):
        return jnp.dot(
            jnp.exp2(found * scale).astype(jnp.bfloat16),
            wide_ref[keys_of(block, spans), 2 * shared * HDIM : 2 * (shared + 1) * HDIM],
            preferred_element_type=jnp.float32,
        )

    def add(block, carry):
        found = [scores(shared, block, BLOCK, False) for shared in heads]
        for shared in heads:
            before = jnp.where(block > 0, mixed[shared], 0.0)
            mixed[shared] = before + products(shared, block, BLOCK, found[shared])
        return carry

    most = k_ref.shape[0] // SPAN
    if most > BLOCK:
        lax.fori_loop(0, blocks, add, 0)
    for spans in range(PART, min(BLOCK, most) + 1, PART):

        @pl.when(span % BLOCK // PART == spans // PART - 1)
        def _(spans=spans):
            found = [scores(shared, blocks, spans, True) for shared in heads]
            for shared in heads:
                before = jnp.where(blocks > 0, mixed[shared], 0.0)
                whole = before + products(shared, blocks, spans, found[shared])
                divide(whole, shared, o_ref, bounds)


def attend_piece_shifted(span, start, stacked, k_ref, wide_ref, mixed, o_ref, bounds, top):
    kv_heads, rows, _ = stacked.shape
    tall = o_ref.shape[0]
    scale = LOG2E / math.sqrt(HDIM)

    def one_head(shared, carry):
        def scores(block):
            found = lax.dot_general(
                stacked[shared],
                k_ref[rows_of(block), pl.ds(pl.multiple_of(shared * HDIM, HDIM), HDIM)],
                (((1,), (1,)), ((), ())),
                preferred_element_type=jnp.float32,
            )
            row = lax.broadcasted_iota(jnp.int32, (rows, SPAN), 0) % tall
            column = lax.broadcasted_iota(jnp.int32, (rows, SPAN), 1)
            return jnp.where(column <= row + (span - block) * SPAN + start, found, -jnp.inf)

        def look(block, carry):
            top[...] = jnp.maximum(top[...], scores(block))
            return carry

        def add(block, carry):
            weights = jnp.exp2((scores(block) - top[...]) * scale).astype(jnp.bfloat16)
            mixed[shared] += jnp.dot(
                weights,
                wide_ref[
                    rows_of(block), pl.ds(pl.multiple_of(2 * shared * HDIM, 2 * HDIM), 2 * HDIM)
                ],
                preferred_element_type=jnp.float32,
            )
            return carry

        top[...] = jnp.full_like(top, -jnp.inf)
        lax.fori_loop(0, span + 1, look, 0)
        top[...] = jnp.broadcast_to(jnp.max(top[...], axis=1, keepdims=True), top.shape)
        mixed[shared] = jnp.zeros(mixed.shape[1:], mixed.dtype)
        lax.fori_loop(0, span + 1, add, 0)
        return carry

    lax.fori_loop(0, kv_heads, one_head, 0)
    for shared in range(kv_heads):
        divide(mixed[shared], shared, o_ref, bounds)


def twice_if_needed(work, drain, bounds):
    bounds[...] = jnp.ones_like(bounds)
    work(False)
    safe = (jnp.min(bounds[0]) > LEAST_SUM) & (jnp.max(bounds[1]) < MOST_SUM)
    drain()

    @pl.when(jnp.logical_not(safe))
    def _():
        work(True)
        drain()


def work_space(count, tall, width, key_width):
    kv_heads = key_width // HDIM
    rows = width // key_width * tall
    return [
        pltpu.VMEM((count, kv_heads, rows, HDIM), jnp.bfloat16),
        pltpu.VMEM((kv_heads, rows, 2 * HDIM), jnp.float32),
        pltpu.VMEM((rows, HDIM), jnp.float32),
        pltpu.VMEM((2, 8, HDIM), jnp.float32),
    ]


def rows_of(span):
    return pl.ds(pl.multiple_of(span * SPAN, SPAN), SPAN)


def half_of(span, start):
    return pl.ds(pl.multiple_of(span * SPAN + start, SPAN // 2), SPAN // 2)


def pick(j, options):
    chosen = options[0]
    for n in range(1, len(options)):
        chosen = jnp.where(j == n, options[n], chosen)
    return chosen


def attend_pieces(dests, starts, q_refs, k_ref, wide_ref, out_buf, store, stacked, mixed, top, bounds):
    count = len(dests)
    for j in range(count):

        @pl.when(dests[j] >= 0)
        def _(j=j):
            stack(q_refs[j], stacked.at[j])

    def work(shifted):
        def one(j, carry):
            dest, start = pick(j, dests), pick(j, starts)

            @pl.when(dest >= 0)
            def _():
                args = (dest, start, stacked.at[j], k_ref, wide_ref, mixed, out_buf.at[j], bounds)
                if shifted:
                    attend_piece_shifted(*args, top)
                else:
                    attend_piece(*args)
                if store is not None:
                    store(j, dest, start).start()

            return carry

        lax.fori_loop(0, count, one, 0)

    def drain():
        if store is not None:
            for j in range(count):
                pl.when(dests[j] >= 0)(store(j, jnp.maximum(dests[j], 0), starts[j]).wait)

    twice_if_needed(work, drain, bounds)


def stores(buf, o_ref, sems):
    return lambda j, span, start: pltpu.make_async_copy(
        buf.at[j], o_ref.at[half_of(span, start)], sems.at[j]
    )


def local_kernel(length_ref, q_hbm, k_hbm, v_hbm, out_buf, q_ref, k_ref, v_ref, wide, sems, *work):
    live = length_ref[lax.axis_index("replica")]

    def fetch(slot):
        rows = slice(slot * SPAN, (slot + 1) * SPAN)
        return pltpu.make_async_copy(q_hbm.at[rows], q_ref.at[rows], sems.at[2 + slot])

    fetches = [
        pltpu.make_async_copy(k_hbm, k_ref, sems.at[0]),
        pltpu.make_async_copy(v_hbm, v_ref, sems.at[1]),
        fetch(0),
    ]
    for copy in fetches:
        copy.start()
    pl.when(live > 1)(fetch(1).start)
    for copy in fetches:
        copy.wait()
    widen(v_ref, wide)
    pl.when(live > 1)(fetch(1).wait)
    half = SPAN // 2
    second = jnp.where(live > 1, 1, -1)
    attend_pieces(
        [jnp.int32(0), jnp.int32(0), second, second],
        [0, half, 0, half],
        [q_ref.at[n * half : (n + 1) * half] for n in range(2 * SLOTS)],
        k_ref,
        wide,
        out_buf,
        None,
        *work,
    )


def attend_local(lengths, queries, keys, values):
    width, key_width = queries.shape[1], keys.shape[1]
    return pl.pallas_call(
        local_kernel,
        out_shape=jax.ShapeDtypeStruct((2 * SLOTS, SPAN // 2, width), queries.dtype),
        in_specs=[SMEM, ANY, ANY, ANY],
        out_specs=VMEM,
        scratch_shapes=[
            pltpu.VMEM(queries.shape, queries.dtype),
            pltpu.VMEM(keys.shape, keys.dtype),
            pltpu.VMEM(values.shape, values.dtype),
            pltpu.VMEM((SLOTS * SPAN, 2 * key_width), keys.dtype),
            pltpu.SemaphoreType.DMA((2 + SLOTS,)),
            *work_space(2 * SLOTS, SPAN // 2, width, key_width),
        ],
        compiler_params=pltpu.CompilerParams(vmem_limit_bytes=VMEM_BYTES),
        cost_estimate=cost_of(3.5),
    )(lengths, queries, keys, values)


def any_of(dests):
    return functools.reduce(jnp.maximum, dests) >= 0


def first_kernel(kv_offsets, places, meta_ref, own_k, own_v, *refs):
    blocks, refs = refs[: len(kv_offsets)], refs[len(kv_offsets) :]
    q_refs, refs = refs[: len(places)], refs[len(places) :]
    local, o_k, o_v, k_buf, wide, out_buf, o_ref, v_buf, zeros, in_sems, out_sems, span_sems, *work = refs
    live = entry(meta_ref, 0)
    half = SPAN // 2
    kv_dests = entries(meta_ref, kv_offsets)

    def fetches():
        yield None, own_k.at[:SPAN], k_buf.at[rows_of(0)]
        yield None, own_v.at[:SPAN], v_buf.at[rows_of(0)]
        yield live > 1, own_k.at[SPAN:], k_buf.at[rows_of(1)]
        yield live > 1, own_v.at[SPAN:], v_buf.at[rows_of(1)]

    def each(act):
        for n, (needed, here, there) in enumerate(fetches()):
            copy = getattr(pltpu.make_async_copy(here, there, in_sems.at[n]), act)
            if needed is None:
                copy()
            else:
                pl.when(needed)(copy)

    def each_span(act):
        for span in range(MAXC):
            if span < SLOTS:
                for n in range(2):
                    copy = pltpu.make_async_copy(
                        local.at[2 * span + n],
                        o_ref.at[half_of(span, n * half)],
                        span_sems.at[span, n],
                    )
                    pl.when(span < live)(getattr(copy, act))
            if span > 0:
                copy = pltpu.make_async_copy(zeros, o_ref.at[rows_of(span)], span_sems.at[span, 0])
                pl.when(span >= live)(getattr(copy, act))

    each("start")
    zeros[...] = jnp.zeros_like(zeros)
    each_span("start")
    for span in range(1, MAXC):

        @pl.when(span >= live)
        def _(span=span):
            k_buf[rows_of(span), :] = jnp.zeros((SPAN, k_buf.shape[1]), k_buf.dtype)
            v_buf[rows_of(span), :] = jnp.zeros((SPAN, v_buf.shape[1]), v_buf.dtype)

    for block, dest in zip(blocks, kv_dests, strict=True):

        @pl.when(dest >= 0)
        def _(block=block, dest=dest):
            k_buf[rows_of(dest), :] = block[:SPAN, :]
            v_buf[rows_of(dest), :] = block[SPAN:, :]

    each("wait")
    copy_k = pltpu.make_async_copy(k_buf, o_k, out_sems.at[0])
    copy_v = pltpu.make_async_copy(v_buf, o_v, out_sems.at[1])
    copy_k.start()
    copy_v.start()
    dests = entries(meta_ref, [offset for offset, _ in places])

    @pl.when(live > 1)
    def _():
        widen(v_buf, wide)

    @pl.when(any_of(dests))
    def _():
        starts = [start for _, start in places]
        attend_pieces(dests, starts, q_refs, k_buf, wide, out_buf, None, *work)

    copy_k.wait()
    copy_v.wait()
    each_span("wait")


def attend_first(meta, keys, values, kv_offsets, kv_blocks, pieces, local):
    rows, key_width = MAXC * SPAN, keys.shape[1]
    queries = [piece[0] for piece in pieces]
    places = [piece[1:] for piece in pieces]
    count, (tall, width) = len(pieces), queries[0].shape
    out = jax.ShapeDtypeStruct((rows, key_width), keys.dtype)
    return pl.pallas_call(
        lambda *refs: first_kernel(kv_offsets, places, *refs),
        out_shape=(
            out,
            out,
            out,
            jax.ShapeDtypeStruct((rows, 2 * key_width), keys.dtype),
            jax.ShapeDtypeStruct((count, tall, width), keys.dtype),
            jax.ShapeDtypeStruct((rows, width), keys.dtype),
        ),
        in_specs=[VMEM, ANY, ANY] + [VMEM] * (len(kv_blocks) + count + 1),
        out_specs=(ANY, ANY, VMEM, VMEM, VMEM, ANY),
        scratch_shapes=[
            pltpu.VMEM((rows, key_width), keys.dtype),
            pltpu.VMEM((SPAN, width), keys.dtype),
            pltpu.SemaphoreType.DMA((4,)),
            pltpu.SemaphoreType.DMA((2,)),
            pltpu.SemaphoreType.DMA((MAXC, 2)),
            *work_space(count, tall, width, key_width),
        ],
        compiler_params=pltpu.CompilerParams(vmem_limit_bytes=VMEM_BYTES),
        cost_estimate=cost_of(2 + 1.3 * count),
    )(meta, keys, values, *kv_blocks, *queries, local)


def later_kernel(places, meta_ref, *refs):
    q_refs, (k_ref, wide_ref, out_buf, *work) = refs[: len(places)], refs[len(places) :]
    dests = entries(meta_ref, [offset for offset, _ in places])

    @pl.when(any_of(dests))
    def _():
        starts = [start for _, start in places]
        attend_pieces(dests, starts, q_refs, k_ref, wide_ref, out_buf, None, *work)


def attend_later(meta, pieces, ordered_keys, wide_values):
    queries = [piece[0] for piece in pieces]
    places = [piece[1:] for piece in pieces]
    count, (tall, width) = len(pieces), queries[0].shape
    return pl.pallas_call(
        lambda *refs: later_kernel(places, *refs),
        out_shape=jax.ShapeDtypeStruct((count, tall, width), ordered_keys.dtype),
        in_specs=[VMEM] * (count + 3),
        out_specs=VMEM,
        scratch_shapes=work_space(count, tall, width, ordered_keys.shape[1]),
        compiler_params=pltpu.CompilerParams(vmem_limit_bytes=VMEM_BYTES),
        cost_estimate=cost_of(1 + 1.3 * count),
    )(meta, *queries, ordered_keys, wide_values)


def last_kernel(before, places, meta_ref, *refs):
    results, refs = refs[: len(before)], refs[len(before) :]
    q_refs, refs = refs[: len(places)], refs[len(places) :]
    k_ref, wide_ref, _, o_ref, out_buf, sems, out_sems, *work = refs
    known = {
        offset: entry(meta_ref, offset) for its_places in before for offset, _ in its_places
    }

    def each(act):
        for n, (result, its_places) in enumerate(zip(results, before, strict=True)):
            for j, (offset, start) in enumerate(its_places):
                dest = known[offset]
                copy = pltpu.make_async_copy(
                    result.at[j], o_ref.at[half_of(jnp.maximum(dest, 0), start)], sems.at[n, j]
                )
                pl.when(dest >= 0)(getattr(copy, act))

    each("start")
    dests = entries(meta_ref, [offset for offset, _ in places])

    @pl.when(any_of(dests))
    def _():
        starts = [start for _, start in places]
        store = stores(out_buf, o_ref, out_sems)
        attend_pieces(dests, starts, q_refs, k_ref, wide_ref, out_buf, store, *work)

    each("wait")


def attend_last(meta, before, results, pieces, ordered_keys, wide_values, attention):
    queries = [piece[0] for piece in pieces]
    places = [piece[1:] for piece in pieces]
    count, (tall, width) = len(pieces), queries[0].shape
    most = max(len(its_places) for its_places in before)
    return pl.pallas_call(
        lambda *refs: last_kernel(before, places, *refs),
        out_shape=jax.ShapeDtypeStruct(attention.shape, attention.dtype),
        in_specs=[VMEM] * (len(results) + count + 3) + [ANY],
        out_specs=ANY,
        input_output_aliases={len(results) + count + 3: 0},
        scratch_shapes=[
            pltpu.VMEM((count, tall, width), attention.dtype),
            pltpu.SemaphoreType.DMA((len(before), most)),
            pltpu.SemaphoreType.DMA((count,)),
            *work_space(count, tall, width, ordered_keys.shape[1]),
        ],
        compiler_params=pltpu.CompilerParams(vmem_limit_bytes=VMEM_BYTES),
        cost_estimate=cost_of(4),
    )(meta, *results, *queries, ordered_keys, wide_values, attention)


def gathered_kernel(meta_ref, first_ref, later_ref, k_ref, v_ref, o_ref, wide, stacked, mixed, top, bounds):
    at = pl.program_id(1)
    live = meta_ref[0]
    widen(v_ref, wide)

    @pl.when(at == 0)
    def _():
        stack(first_ref, stacked.at[0])

    @pl.when(at > 0)
    def _():
        stack(later_ref.at[0], stacked.at[0])

    def work(shifted):
        args = (at, 0, stacked.at[0], k_ref, wide, mixed, o_ref, bounds)
        if shifted:
            attend_piece_shifted(*args, top)
        else:
            attend_piece(*args)

    @pl.when(at < live)
    def _():
        twice_if_needed(work, lambda: None, bounds)

    @pl.when(at >= live)
    def _():
        o_ref[...] = jnp.zeros_like(o_ref)


def attend_gathered(live, source, first, later, cache_keys, cache_values):
    home_rows, key_width = cache_keys.shape
    width = first.shape[1]
    groups = key_width // HDIM
    part = width // groups
    meta = jnp.concatenate([live.reshape(1), source]).astype(jnp.int32)
    return pl.pallas_call(
        gathered_kernel,
        out_shape=jax.ShapeDtypeStruct((home_rows, width), first.dtype),
        grid_spec=pltpu.PrefetchScalarGridSpec(
            num_scalar_prefetch=1,
            grid=(groups, MAXC),
            in_specs=[
                pl.BlockSpec((SPAN, part), lambda g, m, meta: (0, g)),
                pl.BlockSpec((1, SPAN, part), lambda g, m, meta: (meta[1 + m], 0, g)),
                pl.BlockSpec((home_rows, HDIM), lambda g, m, meta: (0, g)),
                pl.BlockSpec((home_rows, HDIM), lambda g, m, meta: (0, g)),
            ],
            out_specs=pl.BlockSpec((SPAN, part), lambda g, m, meta: (m, g)),
            scratch_shapes=[
                pltpu.VMEM((home_rows, 2 * HDIM), cache_keys.dtype),
                *work_space(1, SPAN, part, HDIM),
            ],
        ),
        compiler_params=pltpu.CompilerParams(vmem_limit_bytes=VMEM_BYTES),
    )(meta, first, later, cache_keys, cache_values)


def gather_all(queries, keys, values, lengths, slot_prompt, slot_span):
    mine = lax.axis_index("replica")
    home_rows, key_width = MAXC * SPAN, keys.shape[1]
    live = lengths[mine]
    spans = jnp.arange(MAXC, dtype=jnp.int32)
    matches = (slot_prompt[None, :, 1] == mine) & (slot_span[None, :, 1] == spans[:, None])
    here = jnp.any(matches, axis=1)
    source = jnp.argmax(matches, axis=1).astype(jnp.int32)
    slots_k = lax.all_gather(keys[SPAN:], "replica")
    slots_v = lax.all_gather(values[SPAN:], "replica")
    slots_q = lax.all_gather(queries[SPAN:], "replica")

    def in_order(first, slots):
        picked = jnp.take(slots, source, axis=0)
        kept = jnp.where(here[:, None, None], picked, jnp.zeros((), slots.dtype))
        return jnp.concatenate([first, kept[1:].reshape(home_rows - SPAN, key_width)], axis=0)

    cache_keys = in_order(keys[:SPAN], slots_k)
    cache_values = in_order(values[:SPAN], slots_v)
    attention = attend_gathered(live, source, queries[:SPAN], slots_q, cache_keys, cache_values)
    return (attention, cache_keys, cache_values)


def per_device(queries, keys, values, lengths, slot_prompt, slot_span):
    replicas = lax.axis_size("replica")
    if replicas != 8:
        return gather_all(queries, keys, values, lengths, slot_prompt, slot_span)
    ring = column_ring(replicas)
    farthest = replicas // 2

    def after(block, *others):
        return lax.optimization_barrier((block, others))[0]

    def joined(both):
        return list(lax.optimization_barrier(tuple(both)))

    def shift(block, step):
        pairs = [(r, ring[(n + step) % replicas]) for n, r in enumerate(ring)]
        return lax.ppermute(block, "replica", pairs)

    def go_on(both):
        return [shift(both[0], 1), shift(both[1], -1)]

    own_kv = pack_kv(keys, values)
    kv = [[own_kv, own_kv]]
    kv.append(go_on(kv[0]))
    own_top, own_bottom = pack_q(after(queries, own_kv))
    first, second = [[own_top, own_bottom]], [[own_bottom, own_top]]
    first.append(joined(go_on(first[0])))
    kv[1] = joined(kv[1])
    kv.append(joined(go_on(kv[1])))
    local = attend_local(lengths, after(queries, kv[1]), keys, values)
    second.append(joined(go_on([after(block, first[1]) for block in second[0]])))
    kv.append(joined(go_on([after(block, local) for block in kv[2]])))
    first.append(joined(go_on([after(block, kv[3]) for block in first[1]])))
    kv.append([shift(kv[3][0], 1)])
    second.append(joined(go_on([after(block, kv[3]) for block in second[1]])))
    meta = places(lengths, slot_prompt, slot_span)
    offsets = [[n, replicas - n] for n in range(1, farthest)]

    def wave(n, which):
        up, down = offsets[n - 1]
        if which is first:
            return [(first[n][0], up, 0), (first[n][1], down, half)]
        return [(second[n][0], up, half), (second[n][1], down, 0)]

    half = SPAN // 2
    cache_keys, cache_values, ordered_keys, wide_values, result, attention = attend_first(
        meta,
        keys,
        values,
        sum(offsets, []) + [farthest],
        sum(kv[1:], []),
        wave(1, first) + wave(1, second),
        local,
    )
    results, before = [result], [wave(1, first) + wave(1, second)]

    def attend(n, which):
        results.append(attend_later(meta, wave(n, which), ordered_keys, wide_values))
        before.append(wave(n, which))

    first.append(joined(go_on(first[2])))
    attend(2, first)
    second.append(joined(go_on([after(block, results[-1]) for block in second[2]])))
    attend(2, second)
    last = [
        (shift(after(first[3][0], results[-1]), 1), farthest, 0),
        (shift(after(first[3][1], results[-1]), -1), farthest, half),
    ]
    attend(3, first)
    attend(3, second)
    before = [[piece[1:] for piece in pieces] for pieces in before]
    attention = attend_last(
        meta, before, results, last, ordered_keys, wide_values, attention
    )
    return (attention, cache_keys, cache_values)


def solution(mesh):
    in_specs = (
        P(("group", "replica"), "tensor"),
        P(("group", "replica"), "tensor"),
        P(("group", "replica"), "tensor"),
        P("group"),
        P("group", None),
        P("group", None),
    )
    out_specs = (
        P(("group", "replica"), "tensor"),
        P(("group", "replica"), "tensor"),
        P(("group", "replica"), "tensor"),
    )
    return jax.shard_map(
        per_device, mesh=mesh, in_specs=in_specs, out_specs=out_specs, check_vma=False
    )
```

```python
import functools
import math

import jax
import jax.numpy as jnp
from jax import lax
from jax.experimental import pallas as pl
from jax.experimental.pallas import tpu as pltpu
from jax.sharding import PartitionSpec as P

HDIM = 128
SPAN = 128
SLOTS = 2
LANES = 128
MAXC = 8
BLOCK = 4
PART = 2
LOG2E = 1.0 / math.log(2.0)
VMEM_BYTES = 40 * 1024 * 1024
MOST_VMEM_BYTES = 60 * 1024 * 1024
LEAST_SUM, MOST_SUM = 1e-20, 1e30
ANY = pl.BlockSpec(memory_space=pl.ANY)
SMEM = pl.BlockSpec(memory_space=pltpu.SMEM)
VMEM = pl.BlockSpec(memory_space=pltpu.VMEM)


def cost_of(us):
    return pl.CostEstimate(flops=int(us * 1.15e9), bytes_accessed=0, transcendentals=0)


def column_ring(replicas):
    return list(range(0, replicas, 2)) + list(range(replicas - 1, 0, -2))


def copy_all(copies):
    for copy in copies:
        copy.start()
    for copy in copies:
        copy.wait()


def pack_kv_kernel(k_ref, v_ref, o_ref, sems):
    copy_all(
        [
            pltpu.make_async_copy(k_ref.at[SPAN:], o_ref.at[:SPAN], sems.at[0]),
            pltpu.make_async_copy(v_ref.at[SPAN:], o_ref.at[SPAN:], sems.at[1]),
        ]
    )


def pack_kv(keys, values):
    return pl.pallas_call(
        pack_kv_kernel,
        out_shape=jax.ShapeDtypeStruct((2 * SPAN, keys.shape[1]), keys.dtype),
        in_specs=[ANY] * 2,
        out_specs=VMEM,
        scratch_shapes=[pltpu.SemaphoreType.DMA((2,))],
        compiler_params=pltpu.CompilerParams(vmem_limit_bytes=MOST_VMEM_BYTES),
        cost_estimate=cost_of(1),
    )(keys, values)


def pack_q_kernel(q_ref, o_top, o_bottom, sems):
    half = SPAN // 2
    copy_all(
        [
            pltpu.make_async_copy(q_ref.at[SPAN : SPAN + half], o_top, sems.at[0]),
            pltpu.make_async_copy(q_ref.at[SPAN + half :], o_bottom, sems.at[1]),
        ]
    )


def pack_q(queries):
    half = jax.ShapeDtypeStruct((SPAN // 2, queries.shape[1]), queries.dtype)
    return pl.pallas_call(
        pack_q_kernel,
        out_shape=(half, half),
        in_specs=[ANY],
        out_specs=(VMEM, VMEM),
        scratch_shapes=[pltpu.SemaphoreType.DMA((2,))],
        compiler_params=pltpu.CompilerParams(vmem_limit_bytes=VMEM_BYTES),
        cost_estimate=cost_of(1),
    )(queries)


def places(lengths, slot_prompt, slot_span):
    replicas = lengths.shape[0]
    mine = lax.axis_index("replica")
    ring = jnp.arange(replicas, dtype=jnp.int32)
    place = jnp.where(mine % 2 == 0, mine // 2, replicas - 1 - mine // 2)
    at = (place + replicas - ring) % replicas
    other = jnp.where(at < replicas // 2, 2 * at, 2 * (replicas - at) - 1)
    chosen = other[:, None] == ring[None, :]
    wanted = chosen & (slot_prompt[None, :, 1] == mine) & (ring[:, None] > 0)
    spans = jnp.where(wanted, slot_span[None, :, 1] + 1, 0)
    whole = jnp.where(chosen & (ring[:, None] == 0), lengths[None, :] + 1, 0)
    table = jnp.sum(spans + whole, axis=1, keepdims=True) - 1
    return jnp.broadcast_to(table, (replicas, LANES))


def entry(meta_ref, n):
    return jnp.max(meta_ref[n : n + 1, :])


def entries(meta_ref, offsets):
    found = {offset: entry(meta_ref, offset) for offset in dict.fromkeys(offsets)}
    return [found[offset] for offset in offsets]


def widen(v_ref, wide_ref):
    for at in range(0, v_ref.shape[-1], HDIM):
        wide_ref[:, 2 * at : 2 * at + HDIM] = v_ref[:, at : at + HDIM]
        wide_ref[:, 2 * at + HDIM : 2 * at + 2 * HDIM] = jnp.ones(
            (v_ref.shape[0], HDIM), v_ref.dtype
        )


def stack(q_ref, stacked):
    kv_heads, rows, _ = stacked.shape
    tall = q_ref.shape[0]
    group = rows // tall
    for shared in range(kv_heads):
        for h in range(group):
            at = (shared * group + h) * HDIM
            stacked[shared, h * tall : (h + 1) * tall, :] = q_ref[:, at : at + HDIM]


def divide(mixed, shared, o_ref, bounds):
    tall = o_ref.shape[0]
    group = mixed.shape[0] // tall
    total = mixed[:, HDIM:]
    inverse = pl.reciprocal(total, approx=True)
    inverse = inverse * (2.0 - total * inverse)
    result = (mixed[:, :HDIM] * inverse).astype(o_ref.dtype)
    for h in range(group):
        at = (shared * group + h) * HDIM
        o_ref[:, at : at + HDIM] = result[h * tall : (h + 1) * tall, :]
    total = total.reshape(-1, 8, HDIM)
    bounds[0] = jnp.minimum(bounds[0], jnp.min(total, axis=0))
    bounds[1] = jnp.maximum(bounds[1], jnp.max(total, axis=0))


def attend_piece(span, start, stacked, k_ref, wide_ref, mixed, o_ref, bounds):
    kv_heads, rows, _ = stacked.shape
    heads = range(kv_heads)
    tall = o_ref.shape[0]
    scale = LOG2E / math.sqrt(HDIM)
    blocks = span // BLOCK
    edge = span % PART * SPAN + start

    def keys_of(block, spans):
        return pl.ds(pl.multiple_of(block * BLOCK * SPAN, BLOCK * SPAN), spans * SPAN)

    def scores(shared, block, spans, masked):
        found = lax.dot_general(
            stacked[shared],
            k_ref[keys_of(block, spans), shared * HDIM : (shared + 1) * HDIM],
            (((1,), (1,)), ((), ())),
            preferred_element_type=jnp.float32,
        )
        if masked:
            seen = (spans - PART) * SPAN
            row = lax.broadcasted_iota(jnp.int32, (rows, PART * SPAN), 0) % tall
            column = lax.broadcasted_iota(jnp.int32, (rows, PART * SPAN), 1)
            last = jnp.where(column <= row + edge, found[:, seen:], -jnp.inf)
            found = jnp.concatenate([found[:, :seen], last], axis=1) if seen else last
        return found

    def products(shared, block, spans, found):
        return jnp.dot(
            jnp.exp2(found * scale).astype(jnp.bfloat16),
            wide_ref[keys_of(block, spans), 2 * shared * HDIM : 2 * (shared + 1) * HDIM],
            preferred_element_type=jnp.float32,
        )

    def add(block, carry):
        found = [scores(shared, block, BLOCK, False) for shared in heads]
        for shared in heads:
            before = jnp.where(block > 0, mixed[shared], 0.0)
            mixed[shared] = before + products(shared, block, BLOCK, found[shared])
        return carry

    most = k_ref.shape[0] // SPAN
    if most > BLOCK:
        lax.fori_loop(0, blocks, add, 0)
    for spans in range(PART, min(BLOCK, most) + 1, PART):

        @pl.when(span % BLOCK // PART == spans // PART - 1)
        def _(spans=spans):
            found = [scores(shared, blocks, spans, True) for shared in heads]
            for shared in heads:
                before = jnp.where(blocks > 0, mixed[shared], 0.0)
                whole = before + products(shared, blocks, spans, found[shared])
                divide(whole, shared, o_ref, bounds)


def attend_piece_shifted(span, start, stacked, k_ref, wide_ref, mixed, o_ref, bounds, top):
    kv_heads, rows, _ = stacked.shape
    tall = o_ref.shape[0]
    scale = LOG2E / math.sqrt(HDIM)

    def one_head(shared, carry):
        def scores(block):
            found = lax.dot_general(
                stacked[shared],
                k_ref[rows_of(block), pl.ds(pl.multiple_of(shared * HDIM, HDIM), HDIM)],
                (((1,), (1,)), ((), ())),
                preferred_element_type=jnp.float32,
            )
            row = lax.broadcasted_iota(jnp.int32, (rows, SPAN), 0) % tall
            column = lax.broadcasted_iota(jnp.int32, (rows, SPAN), 1)
            return jnp.where(column <= row + (span - block) * SPAN + start, found, -jnp.inf)

        def look(block, carry):
            top[...] = jnp.maximum(top[...], scores(block))
            return carry

        def add(block, carry):
            weights = jnp.exp2((scores(block) - top[...]) * scale).astype(jnp.bfloat16)
            mixed[shared] += jnp.dot(
                weights,
                wide_ref[
                    rows_of(block), pl.ds(pl.multiple_of(2 * shared * HDIM, 2 * HDIM), 2 * HDIM)
                ],
                preferred_element_type=jnp.float32,
            )
            return carry

        top[...] = jnp.full_like(top, -jnp.inf)
        lax.fori_loop(0, span + 1, look, 0)
        top[...] = jnp.broadcast_to(jnp.max(top[...], axis=1, keepdims=True), top.shape)
        mixed[shared] = jnp.zeros(mixed.shape[1:], mixed.dtype)
        lax.fori_loop(0, span + 1, add, 0)
        return carry

    lax.fori_loop(0, kv_heads, one_head, 0)
    for shared in range(kv_heads):
        divide(mixed[shared], shared, o_ref, bounds)


def twice_if_needed(work, drain, bounds):
    bounds[...] = jnp.ones_like(bounds)
    work(False)
    safe = (jnp.min(bounds[0]) > LEAST_SUM) & (jnp.max(bounds[1]) < MOST_SUM)
    drain()

    @pl.when(jnp.logical_not(safe))
    def _():
        work(True)
        drain()


def work_space(count, tall, width, key_width):
    kv_heads = key_width // HDIM
    rows = width // key_width * tall
    return [
        pltpu.VMEM((count, kv_heads, rows, HDIM), jnp.bfloat16),
        pltpu.VMEM((kv_heads, rows, 2 * HDIM), jnp.float32),
        pltpu.VMEM((rows, HDIM), jnp.float32),
        pltpu.VMEM((2, 8, HDIM), jnp.float32),
    ]


def rows_of(span):
    return pl.ds(pl.multiple_of(span * SPAN, SPAN), SPAN)


def half_of(span, start):
    return pl.ds(pl.multiple_of(span * SPAN + start, SPAN // 2), SPAN // 2)


def pick(j, options):
    chosen = options[0]
    for n in range(1, len(options)):
        chosen = jnp.where(j == n, options[n], chosen)
    return chosen


def attend_pieces(dests, starts, q_refs, k_ref, wide_ref, out_buf, store, stacked, mixed, top, bounds):
    count = len(dests)
    for j in range(count):

        @pl.when(dests[j] >= 0)
        def _(j=j):
            stack(q_refs[j], stacked.at[j])

    def work(shifted):
        def one(j, carry):
            dest, start = pick(j, dests), pick(j, starts)

            @pl.when(dest >= 0)
            def _():
                args = (dest, start, stacked.at[j], k_ref, wide_ref, mixed, out_buf.at[j], bounds)
                if shifted:
                    attend_piece_shifted(*args, top)
                else:
                    attend_piece(*args)
                if store is not None:
                    store(j, dest, start).start()

            return carry

        lax.fori_loop(0, count, one, 0)

    def drain():
        if store is not None:
            for j in range(count):
                pl.when(dests[j] >= 0)(store(j, jnp.maximum(dests[j], 0), starts[j]).wait)

    twice_if_needed(work, drain, bounds)


def stores(buf, o_ref, sems):
    return lambda j, span, start: pltpu.make_async_copy(
        buf.at[j], o_ref.at[half_of(span, start)], sems.at[j]
    )


def local_kernel(length_ref, q_hbm, k_hbm, v_hbm, out_buf, q_ref, k_ref, v_ref, wide, sems, *work):
    live = length_ref[lax.axis_index("replica")]

    def fetch(slot):
        rows = slice(slot * SPAN, (slot + 1) * SPAN)
        return pltpu.make_async_copy(q_hbm.at[rows], q_ref.at[rows], sems.at[2 + slot])

    fetches = [
        pltpu.make_async_copy(k_hbm, k_ref, sems.at[0]),
        pltpu.make_async_copy(v_hbm, v_ref, sems.at[1]),
        fetch(0),
    ]
    for copy in fetches:
        copy.start()
    pl.when(live > 1)(fetch(1).start)
    for copy in fetches:
        copy.wait()
    widen(v_ref, wide)
    pl.when(live > 1)(fetch(1).wait)
    half = SPAN // 2
    second = jnp.where(live > 1, 1, -1)
    attend_pieces(
        [jnp.int32(0), jnp.int32(0), second, second],
        [0, half, 0, half],
        [q_ref.at[n * half : (n + 1) * half] for n in range(2 * SLOTS)],
        k_ref,
        wide,
        out_buf,
        None,
        *work,
    )


def attend_local(lengths, queries, keys, values):
    width, key_width = queries.shape[1], keys.shape[1]
    return pl.pallas_call(
        local_kernel,
        out_shape=jax.ShapeDtypeStruct((2 * SLOTS, SPAN // 2, width), queries.dtype),
        in_specs=[SMEM, ANY, ANY, ANY],
        out_specs=VMEM,
        scratch_shapes=[
            pltpu.VMEM(queries.shape, queries.dtype),
            pltpu.VMEM(keys.shape, keys.dtype),
            pltpu.VMEM(values.shape, values.dtype),
            pltpu.VMEM((SLOTS * SPAN, 2 * key_width), keys.dtype),
            pltpu.SemaphoreType.DMA((2 + SLOTS,)),
            *work_space(2 * SLOTS, SPAN // 2, width, key_width),
        ],
        compiler_params=pltpu.CompilerParams(vmem_limit_bytes=VMEM_BYTES),
        cost_estimate=cost_of(3.5),
    )(lengths, queries, keys, values)


def any_of(dests):
    return functools.reduce(jnp.maximum, dests) >= 0


def first_kernel(kv_offsets, places, meta_ref, own_k, own_v, *refs):
    blocks, refs = refs[: len(kv_offsets)], refs[len(kv_offsets) :]
    q_refs, refs = refs[: len(places)], refs[len(places) :]
    local, o_k, o_v, k_buf, wide, out_buf, o_ref, v_buf, zeros, in_sems, out_sems, span_sems, *work = refs
    live = entry(meta_ref, 0)
    half = SPAN // 2
    kv_dests = entries(meta_ref, kv_offsets)

    def fetches():
        yield None, own_k.at[:SPAN], k_buf.at[rows_of(0)]
        yield None, own_v.at[:SPAN], v_buf.at[rows_of(0)]
        yield live > 1, own_k.at[SPAN:], k_buf.at[rows_of(1)]
        yield live > 1, own_v.at[SPAN:], v_buf.at[rows_of(1)]

    def each(act):
        for n, (needed, here, there) in enumerate(fetches()):
            copy = getattr(pltpu.make_async_copy(here, there, in_sems.at[n]), act)
            if needed is None:
                copy()
            else:
                pl.when(needed)(copy)

    def each_span(act):
        for span in range(MAXC):
            if span < SLOTS:
                for n in range(2):
                    copy = pltpu.make_async_copy(
                        local.at[2 * span + n],
                        o_ref.at[half_of(span, n * half)],
                        span_sems.at[span, n],
                    )
                    pl.when(span < live)(getattr(copy, act))
            if span > 0:
                copy = pltpu.make_async_copy(zeros, o_ref.at[rows_of(span)], span_sems.at[span, 0])
                pl.when(span >= live)(getattr(copy, act))

    each("start")
    zeros[...] = jnp.zeros_like(zeros)
    each_span("start")
    for span in range(1, MAXC):

        @pl.when(span >= live)
        def _(span=span):
            k_buf[rows_of(span), :] = jnp.zeros((SPAN, k_buf.shape[1]), k_buf.dtype)
            v_buf[rows_of(span), :] = jnp.zeros((SPAN, v_buf.shape[1]), v_buf.dtype)

    for block, dest in zip(blocks, kv_dests, strict=True):

        @pl.when(dest >= 0)
        def _(block=block, dest=dest):
            k_buf[rows_of(dest), :] = block[:SPAN, :]
            v_buf[rows_of(dest), :] = block[SPAN:, :]

    each("wait")
    copy_k = pltpu.make_async_copy(k_buf, o_k, out_sems.at[0])
    copy_v = pltpu.make_async_copy(v_buf, o_v, out_sems.at[1])
    copy_k.start()
    copy_v.start()
    dests = entries(meta_ref, [offset for offset, _ in places])

    @pl.when(live > 1)
    def _():
        widen(v_buf, wide)

    @pl.when(any_of(dests))
    def _():
        starts = [start for _, start in places]
        attend_pieces(dests, starts, q_refs, k_buf, wide, out_buf, None, *work)

    copy_k.wait()
    copy_v.wait()
    each_span("wait")


def attend_first(meta, keys, values, kv_offsets, kv_blocks, pieces, local):
    rows, key_width = MAXC * SPAN, keys.shape[1]
    queries = [piece[0] for piece in pieces]
    places = [piece[1:] for piece in pieces]
    count, (tall, width) = len(pieces), queries[0].shape
    out = jax.ShapeDtypeStruct((rows, key_width), keys.dtype)
    return pl.pallas_call(
        lambda *refs: first_kernel(kv_offsets, places, *refs),
        out_shape=(
            out,
            out,
            out,
            jax.ShapeDtypeStruct((rows, 2 * key_width), keys.dtype),
            jax.ShapeDtypeStruct((count, tall, width), keys.dtype),
            jax.ShapeDtypeStruct((rows, width), keys.dtype),
        ),
        in_specs=[VMEM, ANY, ANY] + [VMEM] * (len(kv_blocks) + count + 1),
        out_specs=(ANY, ANY, VMEM, VMEM, VMEM, ANY),
        scratch_shapes=[
            pltpu.VMEM((rows, key_width), keys.dtype),
            pltpu.VMEM((SPAN, width), keys.dtype),
            pltpu.SemaphoreType.DMA((4,)),
            pltpu.SemaphoreType.DMA((2,)),
            pltpu.SemaphoreType.DMA((MAXC, 2)),
            *work_space(count, tall, width, key_width),
        ],
        compiler_params=pltpu.CompilerParams(vmem_limit_bytes=VMEM_BYTES),
        cost_estimate=cost_of(2 + 1.3 * count),
    )(meta, keys, values, *kv_blocks, *queries, local)


def later_kernel(places, meta_ref, *refs):
    q_refs, (k_ref, wide_ref, out_buf, *work) = refs[: len(places)], refs[len(places) :]
    dests = entries(meta_ref, [offset for offset, _ in places])

    @pl.when(any_of(dests))
    def _():
        starts = [start for _, start in places]
        attend_pieces(dests, starts, q_refs, k_ref, wide_ref, out_buf, None, *work)


def attend_later(meta, pieces, ordered_keys, wide_values):
    queries = [piece[0] for piece in pieces]
    places = [piece[1:] for piece in pieces]
    count, (tall, width) = len(pieces), queries[0].shape
    return pl.pallas_call(
        lambda *refs: later_kernel(places, *refs),
        out_shape=jax.ShapeDtypeStruct((count, tall, width), ordered_keys.dtype),
        in_specs=[VMEM] * (count + 3),
        out_specs=VMEM,
        scratch_shapes=work_space(count, tall, width, ordered_keys.shape[1]),
        compiler_params=pltpu.CompilerParams(vmem_limit_bytes=VMEM_BYTES),
        cost_estimate=cost_of(1 + 1.3 * count),
    )(meta, *queries, ordered_keys, wide_values)


def last_kernel(before, places, meta_ref, *refs):
    results, refs = refs[: len(before)], refs[len(before) :]
    q_refs, refs = refs[: len(places)], refs[len(places) :]
    k_ref, wide_ref, _, o_ref, out_buf, sems, out_sems, *work = refs
    known = {
        offset: entry(meta_ref, offset) for its_places in before for offset, _ in its_places
    }

    def each(act):
        for n, (result, its_places) in enumerate(zip(results, before, strict=True)):
            for j, (offset, start) in enumerate(its_places):
                dest = known[offset]
                copy = pltpu.make_async_copy(
                    result.at[j], o_ref.at[half_of(jnp.maximum(dest, 0), start)], sems.at[n, j]
                )
                pl.when(dest >= 0)(getattr(copy, act))

    each("start")
    dests = entries(meta_ref, [offset for offset, _ in places])

    @pl.when(any_of(dests))
    def _():
        starts = [start for _, start in places]
        store = stores(out_buf, o_ref, out_sems)
        attend_pieces(dests, starts, q_refs, k_ref, wide_ref, out_buf, store, *work)

    each("wait")


def attend_last(meta, before, results, pieces, ordered_keys, wide_values, attention):
    queries = [piece[0] for piece in pieces]
    places = [piece[1:] for piece in pieces]
    count, (tall, width) = len(pieces), queries[0].shape
    most = max([1, *(len(its_places) for its_places in before)])
    return pl.pallas_call(
        lambda *refs: last_kernel(before, places, *refs),
        out_shape=jax.ShapeDtypeStruct(attention.shape, attention.dtype),
        in_specs=[VMEM] * (len(results) + count + 3) + [ANY],
        out_specs=ANY,
        input_output_aliases={len(results) + count + 3: 0},
        scratch_shapes=[
            pltpu.VMEM((count, tall, width), attention.dtype),
            pltpu.SemaphoreType.DMA((max(1, len(before)), most)),
            pltpu.SemaphoreType.DMA((count,)),
            *work_space(count, tall, width, ordered_keys.shape[1]),
        ],
        compiler_params=pltpu.CompilerParams(vmem_limit_bytes=VMEM_BYTES),
        cost_estimate=cost_of(2.5),
    )(meta, *results, *queries, ordered_keys, wide_values, attention)


def gathered_kernel(meta_ref, first_ref, later_ref, k_ref, v_ref, o_ref, wide, stacked, mixed, top, bounds):
    at = pl.program_id(1)
    live = meta_ref[0]
    widen(v_ref, wide)

    @pl.when(at == 0)
    def _():
        stack(first_ref, stacked.at[0])

    @pl.when(at > 0)
    def _():
        stack(later_ref.at[0], stacked.at[0])

    def work(shifted):
        args = (at, 0, stacked.at[0], k_ref, wide, mixed, o_ref, bounds)
        if shifted:
            attend_piece_shifted(*args, top)
        else:
            attend_piece(*args)

    @pl.when(at < live)
    def _():
        twice_if_needed(work, lambda: None, bounds)

    @pl.when(at >= live)
    def _():
        o_ref[...] = jnp.zeros_like(o_ref)


def attend_gathered(live, source, first, later, cache_keys, cache_values):
    home_rows, key_width = cache_keys.shape
    width = first.shape[1]
    groups = key_width // HDIM
    part = width // groups
    meta = jnp.concatenate([live.reshape(1), source]).astype(jnp.int32)
    return pl.pallas_call(
        gathered_kernel,
        out_shape=jax.ShapeDtypeStruct((home_rows, width), first.dtype),
        grid_spec=pltpu.PrefetchScalarGridSpec(
            num_scalar_prefetch=1,
            grid=(groups, MAXC),
            in_specs=[
                pl.BlockSpec((SPAN, part), lambda g, m, meta: (0, g)),
                pl.BlockSpec((1, SPAN, part), lambda g, m, meta: (meta[1 + m], 0, g)),
                pl.BlockSpec((home_rows, HDIM), lambda g, m, meta: (0, g)),
                pl.BlockSpec((home_rows, HDIM), lambda g, m, meta: (0, g)),
            ],
            out_specs=pl.BlockSpec((SPAN, part), lambda g, m, meta: (m, g)),
            scratch_shapes=[
                pltpu.VMEM((home_rows, 2 * HDIM), cache_keys.dtype),
                *work_space(1, SPAN, part, HDIM),
            ],
        ),
        compiler_params=pltpu.CompilerParams(vmem_limit_bytes=VMEM_BYTES),
    )(meta, first, later, cache_keys, cache_values)


def gather_all(queries, keys, values, lengths, slot_prompt, slot_span):
    mine = lax.axis_index("replica")
    home_rows, key_width = MAXC * SPAN, keys.shape[1]
    live = lengths[mine]
    spans = jnp.arange(MAXC, dtype=jnp.int32)
    matches = (slot_prompt[None, :, 1] == mine) & (slot_span[None, :, 1] == spans[:, None])
    here = jnp.any(matches, axis=1)
    source = jnp.argmax(matches, axis=1).astype(jnp.int32)
    slots_k = lax.all_gather(keys[SPAN:], "replica")
    slots_v = lax.all_gather(values[SPAN:], "replica")
    slots_q = lax.all_gather(queries[SPAN:], "replica")

    def in_order(first, slots):
        picked = jnp.take(slots, source, axis=0)
        kept = jnp.where(here[:, None, None], picked, jnp.zeros((), slots.dtype))
        return jnp.concatenate([first, kept[1:].reshape(home_rows - SPAN, key_width)], axis=0)

    cache_keys = in_order(keys[:SPAN], slots_k)
    cache_values = in_order(values[:SPAN], slots_v)
    attention = attend_gathered(live, source, queries[:SPAN], slots_q, cache_keys, cache_values)
    return (attention, cache_keys, cache_values)


def per_device(queries, keys, values, lengths, slot_prompt, slot_span):
    replicas = lax.axis_size("replica")
    if replicas != 8:
        return gather_all(queries, keys, values, lengths, slot_prompt, slot_span)
    ring = column_ring(replicas)
    farthest = replicas // 2

    def after(block, *others):
        return lax.optimization_barrier((block, others))[0]

    def joined(both):
        return list(lax.optimization_barrier(tuple(both)))

    def shift(block, step):
        pairs = [(r, ring[(n + step) % replicas]) for n, r in enumerate(ring)]
        return lax.ppermute(block, "replica", pairs)

    def go_on(both):
        return [shift(both[0], 1), shift(both[1], -1)]

    own_kv = pack_kv(keys, values)
    kv = [[own_kv, own_kv]]
    kv.append(go_on(kv[0]))
    own_top, own_bottom = pack_q(after(queries, own_kv))
    first, second = [[own_top, own_bottom]], [[own_bottom, own_top]]
    first.append(joined(go_on(first[0])))
    kv[1] = joined(kv[1])
    kv.append(joined(go_on(kv[1])))
    local = attend_local(lengths, after(queries, kv[1]), keys, values)
    second.append(joined(go_on([after(block, first[1]) for block in second[0]])))
    kv.append(joined(go_on([after(block, local) for block in kv[2]])))
    first.append(joined(go_on([after(block, kv[3]) for block in first[1]])))
    kv.append([shift(kv[3][0], 1)])
    second.append(joined(go_on([after(block, kv[3]) for block in second[1]])))
    meta = places(lengths, slot_prompt, slot_span)
    offsets = [[n, replicas - n] for n in range(1, farthest)]

    def wave(n, which):
        up, down = offsets[n - 1]
        if which is first:
            return [(first[n][0], up, 0), (first[n][1], down, half)]
        return [(second[n][0], up, half), (second[n][1], down, 0)]

    half = SPAN // 2
    cache_keys, cache_values, ordered_keys, wide_values, result, attention = attend_first(
        meta,
        keys,
        values,
        sum(offsets, []) + [farthest],
        sum(kv[1:], []),
        wave(1, first) + wave(1, second),
        local,
    )
    results, before = [result], [wave(1, first) + wave(1, second)]

    def attend(n, which):
        results.append(attend_later(meta, wave(n, which), ordered_keys, wide_values))
        before.append(wave(n, which))

    first.append(joined(go_on(first[2])))
    attend(2, first)
    second.append(joined(go_on([after(block, results[-1]) for block in second[2]])))
    attend(2, second)
    last = [
        (shift(after(first[3][0], results[-1]), 1), farthest, 0),
        (shift(after(first[3][1], results[-1]), -1), farthest, half),
    ]
    attend(3, first)
    attend(3, second)
    before = [[piece[1:] for piece in pieces] for pieces in before]
    attention = attend_last(
        meta, before, results, last[1:], ordered_keys, wide_values, attention
    )
    attention = attend_last(meta, [], [], last[:1], ordered_keys, wide_values, attention)
    return (attention, cache_keys, cache_values)


def solution(mesh):
    in_specs = (
        P(("group", "replica"), "tensor"),
        P(("group", "replica"), "tensor"),
        P(("group", "replica"), "tensor"),
        P("group"),
        P("group", None),
        P("group", None),
    )
    out_specs = (
        P(("group", "replica"), "tensor"),
        P(("group", "replica"), "tensor"),
        P(("group", "replica"), "tensor"),
    )
    return jax.shard_map(
        per_device, mesh=mesh, in_specs=in_specs, out_specs=out_specs, check_vma=False
    )
```

```python
import functools
import math

import jax
import jax.numpy as jnp
from jax import lax
from jax.experimental import pallas as pl
from jax.experimental.pallas import tpu as pltpu
from jax.sharding import PartitionSpec as P

HDIM = 128
SPAN = 128
SLOTS = 2
LANES = 128
MAXC = 8
BLOCK = 4
PART = 2
LOG2E = 1.0 / math.log(2.0)
VMEM_BYTES = 40 * 1024 * 1024
MOST_VMEM_BYTES = 60 * 1024 * 1024
LEAST_SUM, MOST_SUM = 1e-20, 1e30
ANY = pl.BlockSpec(memory_space=pl.ANY)
SMEM = pl.BlockSpec(memory_space=pltpu.SMEM)
VMEM = pl.BlockSpec(memory_space=pltpu.VMEM)


def cost_of(us):
    return pl.CostEstimate(flops=int(us * 1.15e9), bytes_accessed=0, transcendentals=0)


def column_ring(replicas):
    return list(range(0, replicas, 2)) + list(range(replicas - 1, 0, -2))


def copy_all(copies):
    for copy in copies:
        copy.start()
    for copy in copies:
        copy.wait()


def pack_kv_kernel(k_ref, v_ref, o_ref, sems):
    copy_all(
        [
            pltpu.make_async_copy(k_ref.at[SPAN:], o_ref.at[:SPAN], sems.at[0]),
            pltpu.make_async_copy(v_ref.at[SPAN:], o_ref.at[SPAN:], sems.at[1]),
        ]
    )


def pack_kv(keys, values):
    return pl.pallas_call(
        pack_kv_kernel,
        out_shape=jax.ShapeDtypeStruct((2 * SPAN, keys.shape[1]), keys.dtype),
        in_specs=[ANY] * 2,
        out_specs=VMEM,
        scratch_shapes=[pltpu.SemaphoreType.DMA((2,))],
        compiler_params=pltpu.CompilerParams(vmem_limit_bytes=MOST_VMEM_BYTES),
        cost_estimate=cost_of(1),
    )(keys, values)


def pack_q_kernel(q_ref, o_top, o_bottom, sems):
    half = SPAN // 2
    copy_all(
        [
            pltpu.make_async_copy(q_ref.at[SPAN : SPAN + half], o_top, sems.at[0]),
            pltpu.make_async_copy(q_ref.at[SPAN + half :], o_bottom, sems.at[1]),
        ]
    )


def pack_q(queries):
    half = jax.ShapeDtypeStruct((SPAN // 2, queries.shape[1]), queries.dtype)
    return pl.pallas_call(
        pack_q_kernel,
        out_shape=(half, half),
        in_specs=[ANY],
        out_specs=(VMEM, VMEM),
        scratch_shapes=[pltpu.SemaphoreType.DMA((2,))],
        compiler_params=pltpu.CompilerParams(vmem_limit_bytes=VMEM_BYTES),
        cost_estimate=cost_of(1),
    )(queries)


def places(lengths, slot_prompt, slot_span):
    replicas = lengths.shape[0]
    mine = lax.axis_index("replica")
    ring = jnp.arange(replicas, dtype=jnp.int32)
    place = jnp.where(mine % 2 == 0, mine // 2, replicas - 1 - mine // 2)
    at = (place + replicas - ring) % replicas
    other = jnp.where(at < replicas // 2, 2 * at, 2 * (replicas - at) - 1)
    chosen = other[:, None] == ring[None, :]
    wanted = chosen & (slot_prompt[None, :, 1] == mine) & (ring[:, None] > 0)
    spans = jnp.where(wanted, slot_span[None, :, 1] + 1, 0)
    whole = jnp.where(chosen & (ring[:, None] == 0), lengths[None, :] + 1, 0)
    table = jnp.sum(spans + whole, axis=1, keepdims=True) - 1
    return jnp.broadcast_to(table, (replicas, LANES))


def entry(meta_ref, n):
    return jnp.max(meta_ref[n : n + 1, :])


def entries(meta_ref, offsets):
    found = {offset: entry(meta_ref, offset) for offset in dict.fromkeys(offsets)}
    return [found[offset] for offset in offsets]


def widen(v_ref, wide_ref):
    for at in range(0, v_ref.shape[-1], HDIM):
        wide_ref[:, 2 * at : 2 * at + HDIM] = v_ref[:, at : at + HDIM]
        wide_ref[:, 2 * at + HDIM : 2 * at + 2 * HDIM] = jnp.ones(
            (v_ref.shape[0], HDIM), v_ref.dtype
        )


def stack(q_ref, stacked):
    kv_heads, rows, _ = stacked.shape
    tall = q_ref.shape[0]
    group = rows // tall
    for shared in range(kv_heads):
        for h in range(group):
            at = (shared * group + h) * HDIM
            stacked[shared, h * tall : (h + 1) * tall, :] = q_ref[:, at : at + HDIM]


def divide(mixed, shared, o_ref, bounds):
    tall = o_ref.shape[0]
    group = mixed.shape[0] // tall
    total = mixed[:, HDIM:]
    inverse = pl.reciprocal(total, approx=True)
    inverse = inverse * (2.0 - total * inverse)
    result = (mixed[:, :HDIM] * inverse).astype(o_ref.dtype)
    for h in range(group):
        at = (shared * group + h) * HDIM
        o_ref[:, at : at + HDIM] = result[h * tall : (h + 1) * tall, :]
    total = total.reshape(-1, 8, HDIM)
    bounds[0] = jnp.minimum(bounds[0], jnp.min(total, axis=0))
    bounds[1] = jnp.maximum(bounds[1], jnp.max(total, axis=0))


def attend_piece(span, start, stacked, k_ref, wide_ref, mixed, o_ref, bounds):
    kv_heads, rows, _ = stacked.shape
    heads = range(kv_heads)
    tall = o_ref.shape[0]
    scale = LOG2E / math.sqrt(HDIM)
    blocks = span // BLOCK
    edge = span % PART * SPAN + start

    def keys_of(block, spans):
        return pl.ds(pl.multiple_of(block * BLOCK * SPAN, BLOCK * SPAN), spans * SPAN)

    def scores(shared, block, spans, masked):
        found = lax.dot_general(
            stacked[shared],
            k_ref[keys_of(block, spans), shared * HDIM : (shared + 1) * HDIM],
            (((1,), (1,)), ((), ())),
            preferred_element_type=jnp.float32,
        )
        if masked:
            seen = (spans - PART) * SPAN
            row = lax.broadcasted_iota(jnp.int32, (rows, PART * SPAN), 0) % tall
            column = lax.broadcasted_iota(jnp.int32, (rows, PART * SPAN), 1)
            last = jnp.where(column <= row + edge, found[:, seen:], -jnp.inf)
            found = jnp.concatenate([found[:, :seen], last], axis=1) if seen else last
        return found

    def products(shared, block, spans, found):
        return jnp.dot(
            jnp.exp2(found * scale).astype(jnp.bfloat16),
            wide_ref[keys_of(block, spans), 2 * shared * HDIM : 2 * (shared + 1) * HDIM],
            preferred_element_type=jnp.float32,
        )

    def add(block, carry):
        found = [scores(shared, block, BLOCK, False) for shared in heads]
        for shared in heads:
            before = jnp.where(block > 0, mixed[shared], 0.0)
            mixed[shared] = before + products(shared, block, BLOCK, found[shared])
        return carry

    most = k_ref.shape[0] // SPAN
    if most > BLOCK:
        lax.fori_loop(0, blocks, add, 0)
    for spans in range(PART, min(BLOCK, most) + 1, PART):

        @pl.when(span % BLOCK // PART == spans // PART - 1)
        def _(spans=spans):
            found = [scores(shared, blocks, spans, True) for shared in heads]
            for shared in heads:
                before = jnp.where(blocks > 0, mixed[shared], 0.0)
                whole = before + products(shared, blocks, spans, found[shared])
                divide(whole, shared, o_ref, bounds)


def attend_piece_shifted(span, start, stacked, k_ref, wide_ref, mixed, o_ref, bounds, top):
    kv_heads, rows, _ = stacked.shape
    tall = o_ref.shape[0]
    scale = LOG2E / math.sqrt(HDIM)

    def one_head(shared, carry):
        def scores(block):
            found = lax.dot_general(
                stacked[shared],
                k_ref[rows_of(block), pl.ds(pl.multiple_of(shared * HDIM, HDIM), HDIM)],
                (((1,), (1,)), ((), ())),
                preferred_element_type=jnp.float32,
            )
            row = lax.broadcasted_iota(jnp.int32, (rows, SPAN), 0) % tall
            column = lax.broadcasted_iota(jnp.int32, (rows, SPAN), 1)
            return jnp.where(column <= row + (span - block) * SPAN + start, found, -jnp.inf)

        def look(block, carry):
            top[...] = jnp.maximum(top[...], scores(block))
            return carry

        def add(block, carry):
            weights = jnp.exp2((scores(block) - top[...]) * scale).astype(jnp.bfloat16)
            mixed[shared] += jnp.dot(
                weights,
                wide_ref[
                    rows_of(block), pl.ds(pl.multiple_of(2 * shared * HDIM, 2 * HDIM), 2 * HDIM)
                ],
                preferred_element_type=jnp.float32,
            )
            return carry

        top[...] = jnp.full_like(top, -jnp.inf)
        lax.fori_loop(0, span + 1, look, 0)
        top[...] = jnp.broadcast_to(jnp.max(top[...], axis=1, keepdims=True), top.shape)
        mixed[shared] = jnp.zeros(mixed.shape[1:], mixed.dtype)
        lax.fori_loop(0, span + 1, add, 0)
        return carry

    lax.fori_loop(0, kv_heads, one_head, 0)
    for shared in range(kv_heads):
        divide(mixed[shared], shared, o_ref, bounds)


def twice_if_needed(work, drain, bounds):
    bounds[...] = jnp.ones_like(bounds)
    work(False)
    safe = (bounds[0] > LEAST_SUM) & (bounds[1] < MOST_SUM)
    unsafe = jnp.max(jnp.where(safe, 0.0, 1.0)) > 0.5
    drain()

    @pl.when(unsafe)
    def _():
        work(True)
        drain()


def work_space(count, tall, width, key_width):
    kv_heads = key_width // HDIM
    rows = width // key_width * tall
    return [
        pltpu.VMEM((count, kv_heads, rows, HDIM), jnp.bfloat16),
        pltpu.VMEM((kv_heads, rows, 2 * HDIM), jnp.float32),
        pltpu.VMEM((rows, HDIM), jnp.float32),
        pltpu.VMEM((2, 8, HDIM), jnp.float32),
    ]


def rows_of(span):
    return pl.ds(pl.multiple_of(span * SPAN, SPAN), SPAN)


def half_of(span, start):
    return pl.ds(pl.multiple_of(span * SPAN + start, SPAN // 2), SPAN // 2)


def pick(j, options):
    chosen = options[0]
    for n in range(1, len(options)):
        chosen = jnp.where(j == n, options[n], chosen)
    return chosen


def attend_pieces(dests, starts, q_refs, k_ref, wide_ref, out_buf, store, stacked, mixed, top, bounds):
    count = len(dests)
    for j in range(count):

        @pl.when(dests[j] >= 0)
        def _(j=j):
            stack(q_refs[j], stacked.at[j])

    def work(shifted):
        def one(j, carry):
            dest, start = pick(j, dests), pick(j, starts)

            @pl.when(dest >= 0)
            def _():
                args = (dest, start, stacked.at[j], k_ref, wide_ref, mixed, out_buf.at[j], bounds)
                if shifted:
                    attend_piece_shifted(*args, top)
                else:
                    attend_piece(*args)
                if store is not None:
                    store(j, dest, start).start()

            return carry

        lax.fori_loop(0, count, one, 0)

    def drain():
        if store is not None:
            for j in range(count):
                pl.when(dests[j] >= 0)(store(j, jnp.maximum(dests[j], 0), starts[j]).wait)

    twice_if_needed(work, drain, bounds)


def stores(buf, o_ref, sems):
    return lambda j, span, start: pltpu.make_async_copy(
        buf.at[j], o_ref.at[half_of(span, start)], sems.at[j]
    )


def local_kernel(length_ref, q_ref, k_ref, v_ref, out_buf, wide, *work):
    live = length_ref[lax.axis_index("replica")]
    widen(v_ref, wide)
    half = SPAN // 2
    second = jnp.where(live > 1, 1, -1)
    attend_pieces(
        [jnp.int32(0), jnp.int32(0), second, second],
        [0, half, 0, half],
        [q_ref.at[n * half : (n + 1) * half] for n in range(2 * SLOTS)],
        k_ref,
        wide,
        out_buf,
        None,
        *work,
    )


def attend_local(lengths, queries, keys, values):
    width, key_width = queries.shape[1], keys.shape[1]
    return pl.pallas_call(
        local_kernel,
        out_shape=jax.ShapeDtypeStruct((2 * SLOTS, SPAN // 2, width), queries.dtype),
        in_specs=[SMEM, VMEM, VMEM, VMEM],
        out_specs=VMEM,
        scratch_shapes=[
            pltpu.VMEM((SLOTS * SPAN, 2 * key_width), keys.dtype),
            *work_space(2 * SLOTS, SPAN // 2, width, key_width),
        ],
        compiler_params=pltpu.CompilerParams(vmem_limit_bytes=VMEM_BYTES),
        cost_estimate=cost_of(3.5),
    )(lengths, queries, keys, values)


def any_of(dests):
    return functools.reduce(jnp.maximum, dests) >= 0


def first_kernel(kv_offsets, places, meta_ref, own_k, own_v, *refs):
    blocks, refs = refs[: len(kv_offsets)], refs[len(kv_offsets) :]
    q_refs, refs = refs[: len(places)], refs[len(places) :]
    local, o_k, o_v, k_buf, wide, out_buf, o_ref, v_buf, zeros, out_sems, span_sems, *work = refs
    live = entry(meta_ref, 0)
    half = SPAN // 2
    kv_dests = entries(meta_ref, kv_offsets)

    def each_span(act):
        for span in range(MAXC):
            if span < SLOTS:
                for n in range(2):
                    copy = pltpu.make_async_copy(
                        local.at[2 * span + n],
                        o_ref.at[half_of(span, n * half)],
                        span_sems.at[span, n],
                    )
                    pl.when(span < live)(getattr(copy, act))
            if span > 0:
                copy = pltpu.make_async_copy(zeros, o_ref.at[rows_of(span)], span_sems.at[span, 0])
                pl.when(span >= live)(getattr(copy, act))

    zeros[...] = jnp.zeros_like(zeros)
    each_span("start")
    k_buf[rows_of(0), :] = own_k[:SPAN, :]
    v_buf[rows_of(0), :] = own_v[:SPAN, :]

    @pl.when(live > 1)
    def _():
        k_buf[rows_of(1), :] = own_k[SPAN:, :]
        v_buf[rows_of(1), :] = own_v[SPAN:, :]

    for span in range(1, MAXC):

        @pl.when(span >= live)
        def _(span=span):
            k_buf[rows_of(span), :] = jnp.zeros((SPAN, k_buf.shape[1]), k_buf.dtype)
            v_buf[rows_of(span), :] = jnp.zeros((SPAN, v_buf.shape[1]), v_buf.dtype)

    for block, dest in zip(blocks, kv_dests, strict=True):

        @pl.when(dest >= 0)
        def _(block=block, dest=dest):
            k_buf[rows_of(dest), :] = block[:SPAN, :]
            v_buf[rows_of(dest), :] = block[SPAN:, :]

    copy_k = pltpu.make_async_copy(k_buf, o_k, out_sems.at[0])
    copy_v = pltpu.make_async_copy(v_buf, o_v, out_sems.at[1])
    copy_k.start()
    copy_v.start()
    dests = entries(meta_ref, [offset for offset, _ in places])

    @pl.when(live > 1)
    def _():
        widen(v_buf, wide)

    @pl.when(any_of(dests))
    def _():
        starts = [start for _, start in places]
        attend_pieces(dests, starts, q_refs, k_buf, wide, out_buf, None, *work)

    copy_k.wait()
    copy_v.wait()
    each_span("wait")


def attend_first(meta, keys, values, kv_offsets, kv_blocks, pieces, local):
    rows, key_width = MAXC * SPAN, keys.shape[1]
    queries = [piece[0] for piece in pieces]
    places = [piece[1:] for piece in pieces]
    count, (tall, width) = len(pieces), queries[0].shape
    out = jax.ShapeDtypeStruct((rows, key_width), keys.dtype)
    return pl.pallas_call(
        lambda *refs: first_kernel(kv_offsets, places, *refs),
        out_shape=(
            out,
            out,
            out,
            jax.ShapeDtypeStruct((rows, 2 * key_width), keys.dtype),
            jax.ShapeDtypeStruct((count, tall, width), keys.dtype),
            jax.ShapeDtypeStruct((rows, width), keys.dtype),
        ),
        in_specs=[VMEM] * (len(kv_blocks) + count + 4),
        out_specs=(ANY, ANY, VMEM, VMEM, VMEM, ANY),
        scratch_shapes=[
            pltpu.VMEM((rows, key_width), keys.dtype),
            pltpu.VMEM((SPAN, width), keys.dtype),
            pltpu.SemaphoreType.DMA((2,)),
            pltpu.SemaphoreType.DMA((MAXC, 2)),
            *work_space(count, tall, width, key_width),
        ],
        compiler_params=pltpu.CompilerParams(vmem_limit_bytes=VMEM_BYTES),
        cost_estimate=cost_of(2 + 1.3 * count),
    )(meta, keys, values, *kv_blocks, *queries, local)


def later_kernel(places, meta_ref, *refs):
    q_refs, (k_ref, wide_ref, out_buf, *work) = refs[: len(places)], refs[len(places) :]
    dests = entries(meta_ref, [offset for offset, _ in places])

    @pl.when(any_of(dests))
    def _():
        starts = [start for _, start in places]
        attend_pieces(dests, starts, q_refs, k_ref, wide_ref, out_buf, None, *work)


def attend_later(meta, pieces, ordered_keys, wide_values):
    queries = [piece[0] for piece in pieces]
    places = [piece[1:] for piece in pieces]
    count, (tall, width) = len(pieces), queries[0].shape
    return pl.pallas_call(
        lambda *refs: later_kernel(places, *refs),
        out_shape=jax.ShapeDtypeStruct((count, tall, width), ordered_keys.dtype),
        in_specs=[VMEM] * (count + 3),
        out_specs=VMEM,
        scratch_shapes=work_space(count, tall, width, ordered_keys.shape[1]),
        compiler_params=pltpu.CompilerParams(vmem_limit_bytes=VMEM_BYTES),
        cost_estimate=cost_of(1 + 1.3 * count),
    )(meta, *queries, ordered_keys, wide_values)


def last_kernel(before, places, meta_ref, *refs):
    results, refs = refs[: len(before)], refs[len(before) :]
    q_refs, refs = refs[: len(places)], refs[len(places) :]
    k_ref, wide_ref, _, o_ref, out_buf, sems, out_sems, *work = refs
    known = {
        offset: entry(meta_ref, offset) for its_places in before for offset, _ in its_places
    }

    def each(act):
        for n, (result, its_places) in enumerate(zip(results, before, strict=True)):
            for j, (offset, start) in enumerate(its_places):
                dest = known[offset]
                copy = pltpu.make_async_copy(
                    result.at[j], o_ref.at[half_of(jnp.maximum(dest, 0), start)], sems.at[n, j]
                )
                pl.when(dest >= 0)(getattr(copy, act))

    each("start")
    dests = entries(meta_ref, [offset for offset, _ in places])

    @pl.when(any_of(dests))
    def _():
        starts = [start for _, start in places]
        store = stores(out_buf, o_ref, out_sems)
        attend_pieces(dests, starts, q_refs, k_ref, wide_ref, out_buf, store, *work)

    each("wait")


def attend_last(meta, before, results, pieces, ordered_keys, wide_values, attention):
    queries = [piece[0] for piece in pieces]
    places = [piece[1:] for piece in pieces]
    count, (tall, width) = len(pieces), queries[0].shape
    most = max([1, *(len(its_places) for its_places in before)])
    return pl.pallas_call(
        lambda *refs: last_kernel(before, places, *refs),
        out_shape=jax.ShapeDtypeStruct(attention.shape, attention.dtype),
        in_specs=[VMEM] * (len(results) + count + 3) + [ANY],
        out_specs=ANY,
        input_output_aliases={len(results) + count + 3: 0},
        scratch_shapes=[
            pltpu.VMEM((count, tall, width), attention.dtype),
            pltpu.SemaphoreType.DMA((max(1, len(before)), most)),
            pltpu.SemaphoreType.DMA((count,)),
            *work_space(count, tall, width, ordered_keys.shape[1]),
        ],
        compiler_params=pltpu.CompilerParams(vmem_limit_bytes=VMEM_BYTES),
        cost_estimate=cost_of(2.5),
    )(meta, *results, *queries, ordered_keys, wide_values, attention)


def gathered_kernel(meta_ref, first_ref, later_ref, k_ref, v_ref, o_ref, wide, stacked, mixed, top, bounds):
    at = pl.program_id(1)
    live = meta_ref[0]
    widen(v_ref, wide)

    @pl.when(at == 0)
    def _():
        stack(first_ref, stacked.at[0])

    @pl.when(at > 0)
    def _():
        stack(later_ref.at[0], stacked.at[0])

    def work(shifted):
        args = (at, 0, stacked.at[0], k_ref, wide, mixed, o_ref, bounds)
        if shifted:
            attend_piece_shifted(*args, top)
        else:
            attend_piece(*args)

    @pl.when(at < live)
    def _():
        twice_if_needed(work, lambda: None, bounds)

    @pl.when(at >= live)
    def _():
        o_ref[...] = jnp.zeros_like(o_ref)


def attend_gathered(live, source, first, later, cache_keys, cache_values):
    home_rows, key_width = cache_keys.shape
    width = first.shape[1]
    groups = key_width // HDIM
    part = width // groups
    meta = jnp.concatenate([live.reshape(1), source]).astype(jnp.int32)
    return pl.pallas_call(
        gathered_kernel,
        out_shape=jax.ShapeDtypeStruct((home_rows, width), first.dtype),
        grid_spec=pltpu.PrefetchScalarGridSpec(
            num_scalar_prefetch=1,
            grid=(groups, MAXC),
            in_specs=[
                pl.BlockSpec((SPAN, part), lambda g, m, meta: (0, g)),
                pl.BlockSpec((1, SPAN, part), lambda g, m, meta: (meta[1 + m], 0, g)),
                pl.BlockSpec((home_rows, HDIM), lambda g, m, meta: (0, g)),
                pl.BlockSpec((home_rows, HDIM), lambda g, m, meta: (0, g)),
            ],
            out_specs=pl.BlockSpec((SPAN, part), lambda g, m, meta: (m, g)),
            scratch_shapes=[
                pltpu.VMEM((home_rows, 2 * HDIM), cache_keys.dtype),
                *work_space(1, SPAN, part, HDIM),
            ],
        ),
        compiler_params=pltpu.CompilerParams(vmem_limit_bytes=VMEM_BYTES),
    )(meta, first, later, cache_keys, cache_values)


def gather_all(queries, keys, values, lengths, slot_prompt, slot_span):
    mine = lax.axis_index("replica")
    home_rows, key_width = MAXC * SPAN, keys.shape[1]
    live = lengths[mine]
    spans = jnp.arange(MAXC, dtype=jnp.int32)
    matches = (slot_prompt[None, :, 1] == mine) & (slot_span[None, :, 1] == spans[:, None])
    here = jnp.any(matches, axis=1)
    source = jnp.argmax(matches, axis=1).astype(jnp.int32)
    slots_k = lax.all_gather(keys[SPAN:], "replica")
    slots_v = lax.all_gather(values[SPAN:], "replica")
    slots_q = lax.all_gather(queries[SPAN:], "replica")

    def in_order(first, slots):
        picked = jnp.take(slots, source, axis=0)
        kept = jnp.where(here[:, None, None], picked, jnp.zeros((), slots.dtype))
        return jnp.concatenate([first, kept[1:].reshape(home_rows - SPAN, key_width)], axis=0)

    cache_keys = in_order(keys[:SPAN], slots_k)
    cache_values = in_order(values[:SPAN], slots_v)
    attention = attend_gathered(live, source, queries[:SPAN], slots_q, cache_keys, cache_values)
    return (attention, cache_keys, cache_values)


def per_device(queries, keys, values, lengths, slot_prompt, slot_span):
    replicas = lax.axis_size("replica")
    if replicas != 8:
        return gather_all(queries, keys, values, lengths, slot_prompt, slot_span)
    ring = column_ring(replicas)
    farthest = replicas // 2

    def after(block, *others):
        return lax.optimization_barrier((block, others))[0]

    def joined(both):
        return list(lax.optimization_barrier(tuple(both)))

    def shift(block, step):
        pairs = [(r, ring[(n + step) % replicas]) for n, r in enumerate(ring)]
        return lax.ppermute(block, "replica", pairs)

    def go_on(both):
        return [shift(both[0], 1), shift(both[1], -1)]

    own_kv = pack_kv(keys, values)
    kv = [[own_kv, own_kv]]
    kv.append(go_on(kv[0]))
    own_top, own_bottom = pack_q(after(queries, own_kv))
    first, second = [[own_top, own_bottom]], [[own_bottom, own_top]]
    first.append(joined(go_on(first[0])))
    kv[1] = joined(kv[1])
    kv.append(joined(go_on(kv[1])))
    local = attend_local(lengths, after(queries, kv[1]), keys, values)
    second.append(joined(go_on([after(block, first[1]) for block in second[0]])))
    kv.append(joined(go_on([after(block, local) for block in kv[2]])))
    first.append(joined(go_on([after(block, kv[3]) for block in first[1]])))
    kv.append([shift(kv[3][0], 1)])
    second.append(joined(go_on([after(block, kv[3]) for block in second[1]])))
    meta = places(lengths, slot_prompt, slot_span)
    offsets = [[n, replicas - n] for n in range(1, farthest)]

    def wave(n, which):
        up, down = offsets[n - 1]
        if which is first:
            return [(first[n][0], up, 0), (first[n][1], down, half)]
        return [(second[n][0], up, half), (second[n][1], down, 0)]

    half = SPAN // 2
    cache_keys, cache_values, ordered_keys, wide_values, result, attention = attend_first(
        meta,
        keys,
        values,
        sum(offsets, []) + [farthest],
        sum(kv[1:], []),
        wave(1, first) + wave(1, second),
        local,
    )
    results, before = [result], [wave(1, first) + wave(1, second)]

    def attend(n, which):
        results.append(attend_later(meta, wave(n, which), ordered_keys, wide_values))
        before.append(wave(n, which))

    first.append(joined(go_on(first[2])))
    attend(2, first)
    second.append(joined(go_on([after(block, results[-1]) for block in second[2]])))
    attend(2, second)
    last = [
        (shift(after(first[3][0], results[-1]), 1), farthest, 0),
        (shift(after(first[3][1], results[-1]), -1), farthest, half),
    ]
    attend(3, first)
    attend(3, second)
    before = [[piece[1:] for piece in pieces] for pieces in before]
    attention = attend_last(
        meta, before, results, last[1:], ordered_keys, wide_values, attention
    )
    attention = attend_last(meta, [], [], last[:1], ordered_keys, wide_values, attention)
    return (attention, cache_keys, cache_values)


def solution(mesh):
    in_specs = (
        P(("group", "replica"), "tensor"),
        P(("group", "replica"), "tensor"),
        P(("group", "replica"), "tensor"),
        P("group"),
        P("group", None),
        P("group", None),
    )
    out_specs = (
        P(("group", "replica"), "tensor"),
        P(("group", "replica"), "tensor"),
        P(("group", "replica"), "tensor"),
    )
    return jax.shard_map(
        per_device, mesh=mesh, in_specs=in_specs, out_specs=out_specs, check_vma=False
    )
```

```python
import functools
import math

import jax
import jax.numpy as jnp
from jax import lax
from jax.experimental import pallas as pl
from jax.experimental.pallas import tpu as pltpu
from jax.sharding import PartitionSpec as P

HDIM = 128
SPAN = 128
SLOTS = 2
LANES = 128
MAXC = 8
BLOCK = 4
PART = 2
LOG2E = 1.0 / math.log(2.0)
VMEM_BYTES = 40 * 1024 * 1024
MOST_VMEM_BYTES = 60 * 1024 * 1024
LEAST_SUM, MOST_SUM = 1e-20, 1e30
ANY = pl.BlockSpec(memory_space=pl.ANY)
SMEM = pl.BlockSpec(memory_space=pltpu.SMEM)
VMEM = pl.BlockSpec(memory_space=pltpu.VMEM)


def cost_of(us):
    return pl.CostEstimate(flops=int(us * 1.15e9), bytes_accessed=0, transcendentals=0)


def column_ring(replicas):
    return list(range(0, replicas, 2)) + list(range(replicas - 1, 0, -2))


def copy_all(copies):
    for copy in copies:
        copy.start()
    for copy in copies:
        copy.wait()


def pack_kv_kernel(k_ref, v_ref, o_ref, sems):
    copy_all(
        [
            pltpu.make_async_copy(k_ref.at[SPAN:], o_ref.at[:SPAN], sems.at[0]),
            pltpu.make_async_copy(v_ref.at[SPAN:], o_ref.at[SPAN:], sems.at[1]),
        ]
    )


def pack_kv(keys, values):
    return pl.pallas_call(
        pack_kv_kernel,
        out_shape=jax.ShapeDtypeStruct((2 * SPAN, keys.shape[1]), keys.dtype),
        in_specs=[ANY] * 2,
        out_specs=VMEM,
        scratch_shapes=[pltpu.SemaphoreType.DMA((2,))],
        compiler_params=pltpu.CompilerParams(vmem_limit_bytes=MOST_VMEM_BYTES),
        cost_estimate=cost_of(1),
    )(keys, values)


def pack_q_kernel(q_ref, o_top, o_bottom, sems):
    half = SPAN // 2
    copy_all(
        [
            pltpu.make_async_copy(q_ref.at[SPAN : SPAN + half], o_top, sems.at[0]),
            pltpu.make_async_copy(q_ref.at[SPAN + half :], o_bottom, sems.at[1]),
        ]
    )


def pack_q(queries):
    half = jax.ShapeDtypeStruct((SPAN // 2, queries.shape[1]), queries.dtype)
    return pl.pallas_call(
        pack_q_kernel,
        out_shape=(half, half),
        in_specs=[ANY],
        out_specs=(VMEM, VMEM),
        scratch_shapes=[pltpu.SemaphoreType.DMA((2,))],
        compiler_params=pltpu.CompilerParams(vmem_limit_bytes=VMEM_BYTES),
        cost_estimate=cost_of(1),
    )(queries)


def places(lengths, slot_prompt, slot_span):
    replicas = lengths.shape[0]
    mine = lax.axis_index("replica")
    ring = jnp.arange(replicas, dtype=jnp.int32)
    place = jnp.where(mine % 2 == 0, mine // 2, replicas - 1 - mine // 2)
    at = (place + replicas - ring) % replicas
    other = jnp.where(at < replicas // 2, 2 * at, 2 * (replicas - at) - 1)
    chosen = other[:, None] == ring[None, :]
    wanted = chosen & (slot_prompt[None, :, 1] == mine) & (ring[:, None] > 0)
    spans = jnp.where(wanted, slot_span[None, :, 1] + 1, 0)
    whole = jnp.where(chosen & (ring[:, None] == 0), lengths[None, :] + 1, 0)
    table = jnp.sum(spans + whole, axis=1, keepdims=True) - 1
    return jnp.broadcast_to(table, (replicas, LANES))


def entry(meta_ref, n):
    return jnp.max(meta_ref[n : n + 1, :])


def entries(meta_ref, offsets):
    found = {offset: entry(meta_ref, offset) for offset in dict.fromkeys(offsets)}
    return [found[offset] for offset in offsets]


def widen(v_ref, wide_ref):
    for at in range(0, v_ref.shape[-1], HDIM):
        wide_ref[:, 2 * at : 2 * at + HDIM] = v_ref[:, at : at + HDIM]
        wide_ref[:, 2 * at + HDIM : 2 * at + 2 * HDIM] = jnp.ones(
            (v_ref.shape[0], HDIM), v_ref.dtype
        )


def stack(q_ref, stacked):
    kv_heads, rows, _ = stacked.shape
    tall = q_ref.shape[0]
    group = rows // tall
    for shared in range(kv_heads):
        for h in range(group):
            at = (shared * group + h) * HDIM
            stacked[shared, h * tall : (h + 1) * tall, :] = q_ref[:, at : at + HDIM]


def divide(mixed, shared, o_ref, bounds):
    tall = o_ref.shape[0]
    group = mixed.shape[0] // tall
    total = mixed[:, HDIM:]
    inverse = pl.reciprocal(total, approx=True)
    inverse = inverse * (2.0 - total * inverse)
    result = (mixed[:, :HDIM] * inverse).astype(o_ref.dtype)
    for h in range(group):
        at = (shared * group + h) * HDIM
        o_ref[:, at : at + HDIM] = result[h * tall : (h + 1) * tall, :]
    total = total.reshape(-1, 8, HDIM)
    bounds[0] = jnp.minimum(bounds[0], jnp.min(total, axis=0))
    bounds[1] = jnp.maximum(bounds[1], jnp.max(total, axis=0))


def attend_piece(span, start, stacked, k_ref, wide_ref, mixed, o_ref, bounds):
    kv_heads, rows, _ = stacked.shape
    heads = range(kv_heads)
    tall = o_ref.shape[0]
    scale = LOG2E / math.sqrt(HDIM)
    blocks = span // BLOCK
    edge = span % PART * SPAN + start

    def keys_of(block, spans):
        return pl.ds(pl.multiple_of(block * BLOCK * SPAN, BLOCK * SPAN), spans * SPAN)

    def scores(shared, block, spans, masked):
        found = lax.dot_general(
            stacked[shared],
            k_ref[keys_of(block, spans), shared * HDIM : (shared + 1) * HDIM],
            (((1,), (1,)), ((), ())),
            preferred_element_type=jnp.float32,
        )
        if masked:
            seen = (spans - PART) * SPAN
            row = lax.broadcasted_iota(jnp.int32, (rows, PART * SPAN), 0) % tall
            column = lax.broadcasted_iota(jnp.int32, (rows, PART * SPAN), 1)
            last = jnp.where(column <= row + edge, found[:, seen:], -jnp.inf)
            found = jnp.concatenate([found[:, :seen], last], axis=1) if seen else last
        return found

    def products(shared, block, spans, found):
        return jnp.dot(
            jnp.exp2(found * scale).astype(jnp.bfloat16),
            wide_ref[keys_of(block, spans), 2 * shared * HDIM : 2 * (shared + 1) * HDIM],
            preferred_element_type=jnp.float32,
        )

    def add(block, carry):
        found = [scores(shared, block, BLOCK, False) for shared in heads]
        for shared in heads:
            before = jnp.where(block > 0, mixed[shared], 0.0)
            mixed[shared] = before + products(shared, block, BLOCK, found[shared])
        return carry

    most = k_ref.shape[0] // SPAN
    if most > BLOCK:
        lax.fori_loop(0, blocks, add, 0)
    for spans in range(PART, min(BLOCK, most) + 1, PART):

        @pl.when(span % BLOCK // PART == spans // PART - 1)
        def _(spans=spans):
            found = [scores(shared, blocks, spans, True) for shared in heads]
            for shared in heads:
                before = jnp.where(blocks > 0, mixed[shared], 0.0)
                whole = before + products(shared, blocks, spans, found[shared])
                divide(whole, shared, o_ref, bounds)


def attend_piece_shifted(span, start, stacked, k_ref, wide_ref, mixed, o_ref, bounds, top):
    kv_heads, rows, _ = stacked.shape
    tall = o_ref.shape[0]
    scale = LOG2E / math.sqrt(HDIM)

    def one_head(shared, carry):
        def scores(block):
            found = lax.dot_general(
                stacked[shared],
                k_ref[rows_of(block), pl.ds(pl.multiple_of(shared * HDIM, HDIM), HDIM)],
                (((1,), (1,)), ((), ())),
                preferred_element_type=jnp.float32,
            )
            row = lax.broadcasted_iota(jnp.int32, (rows, SPAN), 0) % tall
            column = lax.broadcasted_iota(jnp.int32, (rows, SPAN), 1)
            return jnp.where(column <= row + (span - block) * SPAN + start, found, -jnp.inf)

        def look(block, carry):
            top[...] = jnp.maximum(top[...], scores(block))
            return carry

        def add(block, carry):
            weights = jnp.exp2((scores(block) - top[...]) * scale).astype(jnp.bfloat16)
            mixed[shared] += jnp.dot(
                weights,
                wide_ref[
                    rows_of(block), pl.ds(pl.multiple_of(2 * shared * HDIM, 2 * HDIM), 2 * HDIM)
                ],
                preferred_element_type=jnp.float32,
            )
            return carry

        top[...] = jnp.full_like(top, -jnp.inf)
        lax.fori_loop(0, span + 1, look, 0)
        top[...] = jnp.broadcast_to(jnp.max(top[...], axis=1, keepdims=True), top.shape)
        mixed[shared] = jnp.zeros(mixed.shape[1:], mixed.dtype)
        lax.fori_loop(0, span + 1, add, 0)
        return carry

    lax.fori_loop(0, kv_heads, one_head, 0)
    for shared in range(kv_heads):
        divide(mixed[shared], shared, o_ref, bounds)


def twice_if_needed(work, drain, bounds):
    bounds[...] = jnp.ones_like(bounds)
    work(False)
    safe = (bounds[0] > LEAST_SUM) & (bounds[1] < MOST_SUM)
    unsafe = jnp.max(jnp.where(safe, 0.0, 1.0)) > 0.5
    drain()

    @pl.when(unsafe)
    def _():
        work(True)
        drain()


def work_space(count, tall, width, key_width):
    kv_heads = key_width // HDIM
    rows = width // key_width * tall
    return [
        pltpu.VMEM((count, kv_heads, rows, HDIM), jnp.bfloat16),
        pltpu.VMEM((kv_heads, rows, 2 * HDIM), jnp.float32),
        pltpu.VMEM((rows, HDIM), jnp.float32),
        pltpu.VMEM((2, 8, HDIM), jnp.float32),
    ]


def rows_of(span):
    return pl.ds(pl.multiple_of(span * SPAN, SPAN), SPAN)


def half_of(span, start):
    return pl.ds(pl.multiple_of(span * SPAN + start, SPAN // 2), SPAN // 2)


def pick(j, options):
    chosen = options[0]
    for n in range(1, len(options)):
        chosen = jnp.where(j == n, options[n], chosen)
    return chosen


def attend_pieces(dests, starts, q_refs, k_ref, wide_ref, out_buf, store, stacked, mixed, top, bounds):
    count = len(dests)
    for j in range(count):

        @pl.when(dests[j] >= 0)
        def _(j=j):
            stack(q_refs[j], stacked.at[j])

    def work(shifted):
        def one(j, carry):
            dest, start = pick(j, dests), pick(j, starts)

            @pl.when(dest >= 0)
            def _():
                args = (dest, start, stacked.at[j], k_ref, wide_ref, mixed, out_buf.at[j], bounds)
                if shifted:
                    attend_piece_shifted(*args, top)
                else:
                    attend_piece(*args)
                if store is not None:
                    store(j, dest, start).start()

            return carry

        lax.fori_loop(0, count, one, 0)

    def drain():
        if store is not None:
            for j in range(count):
                pl.when(dests[j] >= 0)(store(j, jnp.maximum(dests[j], 0), starts[j]).wait)

    twice_if_needed(work, drain, bounds)


def stores(buf, o_ref, sems):
    return lambda j, span, start: pltpu.make_async_copy(
        buf.at[j], o_ref.at[half_of(span, start)], sems.at[j]
    )


def local_kernel(length_ref, q_ref, k_ref, v_ref, out_buf, wide, *work):
    live = length_ref[lax.axis_index("replica")]
    widen(v_ref, wide)
    half = SPAN // 2
    second = jnp.where(live > 1, 1, -1)
    attend_pieces(
        [jnp.int32(0), jnp.int32(0), second, second],
        [0, half, 0, half],
        [q_ref.at[n * half : (n + 1) * half] for n in range(2 * SLOTS)],
        k_ref,
        wide,
        out_buf,
        None,
        *work,
    )


def attend_local(lengths, queries, keys, values):
    width, key_width = queries.shape[1], keys.shape[1]
    return pl.pallas_call(
        local_kernel,
        out_shape=jax.ShapeDtypeStruct((2 * SLOTS, SPAN // 2, width), queries.dtype),
        in_specs=[SMEM, VMEM, VMEM, VMEM],
        out_specs=VMEM,
        scratch_shapes=[
            pltpu.VMEM((SLOTS * SPAN, 2 * key_width), keys.dtype),
            *work_space(2 * SLOTS, SPAN // 2, width, key_width),
        ],
        compiler_params=pltpu.CompilerParams(vmem_limit_bytes=VMEM_BYTES),
        cost_estimate=cost_of(3.5),
    )(lengths, queries, keys, values)


def any_of(dests):
    return functools.reduce(jnp.maximum, dests) >= 0


def first_kernel(kv_offsets, places, meta_ref, own_k, own_v, *refs):
    blocks, refs = refs[: len(kv_offsets)], refs[len(kv_offsets) :]
    q_refs, refs = refs[: len(places)], refs[len(places) :]
    local, o_k, o_v, k_buf, wide, out_buf, o_ref, v_buf, zeros, out_sems, span_sems, *work = refs
    live = entry(meta_ref, 0)
    half = SPAN // 2
    kv_dests = entries(meta_ref, kv_offsets)

    def each_span(act):
        for span in range(MAXC):
            if span < SLOTS:
                for n in range(2):
                    copy = pltpu.make_async_copy(
                        local.at[2 * span + n],
                        o_ref.at[half_of(span, n * half)],
                        span_sems.at[span, n],
                    )
                    pl.when(span < live)(getattr(copy, act))
            if span > 0:
                copy = pltpu.make_async_copy(zeros, o_ref.at[rows_of(span)], span_sems.at[span, 0])
                pl.when(span >= live)(getattr(copy, act))

    zeros[...] = jnp.zeros_like(zeros)
    each_span("start")
    k_buf[rows_of(0), :] = own_k[:SPAN, :]
    v_buf[rows_of(0), :] = own_v[:SPAN, :]

    @pl.when(live > 1)
    def _():
        k_buf[rows_of(1), :] = own_k[SPAN:, :]
        v_buf[rows_of(1), :] = own_v[SPAN:, :]

    for span in range(1, MAXC):

        @pl.when(span >= live)
        def _(span=span):
            k_buf[rows_of(span), :] = jnp.zeros((SPAN, k_buf.shape[1]), k_buf.dtype)
            v_buf[rows_of(span), :] = jnp.zeros((SPAN, v_buf.shape[1]), v_buf.dtype)

    for block, dest in zip(blocks, kv_dests, strict=True):

        @pl.when(dest >= 0)
        def _(block=block, dest=dest):
            k_buf[rows_of(dest), :] = block[:SPAN, :]
            v_buf[rows_of(dest), :] = block[SPAN:, :]

    copy_k = pltpu.make_async_copy(k_buf, o_k, out_sems.at[0])
    copy_v = pltpu.make_async_copy(v_buf, o_v, out_sems.at[1])
    copy_k.start()
    copy_v.start()
    dests = entries(meta_ref, [offset for offset, _ in places])

    @pl.when(live > 1)
    def _():
        widen(v_buf, wide)

    @pl.when(any_of(dests))
    def _():
        starts = [start for _, start in places]
        attend_pieces(dests, starts, q_refs, k_buf, wide, out_buf, None, *work)

    copy_k.wait()
    copy_v.wait()
    each_span("wait")


def attend_first(meta, keys, values, kv_offsets, kv_blocks, pieces, local):
    rows, key_width = MAXC * SPAN, keys.shape[1]
    queries = [piece[0] for piece in pieces]
    places = [piece[1:] for piece in pieces]
    count, (tall, width) = len(pieces), queries[0].shape
    out = jax.ShapeDtypeStruct((rows, key_width), keys.dtype)
    return pl.pallas_call(
        lambda *refs: first_kernel(kv_offsets, places, *refs),
        out_shape=(
            out,
            out,
            out,
            jax.ShapeDtypeStruct((rows, 2 * key_width), keys.dtype),
            jax.ShapeDtypeStruct((count, tall, width), keys.dtype),
            jax.ShapeDtypeStruct((rows, width), keys.dtype),
        ),
        in_specs=[VMEM] * (len(kv_blocks) + count + 4),
        out_specs=(ANY, ANY, VMEM, VMEM, VMEM, ANY),
        scratch_shapes=[
            pltpu.VMEM((rows, key_width), keys.dtype),
            pltpu.VMEM((SPAN, width), keys.dtype),
            pltpu.SemaphoreType.DMA((2,)),
            pltpu.SemaphoreType.DMA((MAXC, 2)),
            *work_space(count, tall, width, key_width),
        ],
        compiler_params=pltpu.CompilerParams(vmem_limit_bytes=VMEM_BYTES),
        cost_estimate=cost_of(2 + 1.3 * count),
    )(meta, keys, values, *kv_blocks, *queries, local)


def later_kernel(places, meta_ref, *refs):
    q_refs, (k_ref, wide_ref, out_buf, *work) = refs[: len(places)], refs[len(places) :]
    dests = entries(meta_ref, [offset for offset, _ in places])

    @pl.when(any_of(dests))
    def _():
        starts = [start for _, start in places]
        attend_pieces(dests, starts, q_refs, k_ref, wide_ref, out_buf, None, *work)


def attend_later(meta, pieces, ordered_keys, wide_values):
    queries = [piece[0] for piece in pieces]
    places = [piece[1:] for piece in pieces]
    count, (tall, width) = len(pieces), queries[0].shape
    return pl.pallas_call(
        lambda *refs: later_kernel(places, *refs),
        out_shape=jax.ShapeDtypeStruct((count, tall, width), ordered_keys.dtype),
        in_specs=[VMEM] * (count + 3),
        out_specs=VMEM,
        scratch_shapes=work_space(count, tall, width, ordered_keys.shape[1]),
        compiler_params=pltpu.CompilerParams(vmem_limit_bytes=VMEM_BYTES),
        cost_estimate=cost_of(1 + 1.3 * count),
    )(meta, *queries, ordered_keys, wide_values)


def last_kernel(before, places, meta_ref, *refs):
    results, refs = refs[: len(before)], refs[len(before) :]
    q_refs, refs = refs[: len(places)], refs[len(places) :]
    k_ref, wide_ref, _, o_ref, out_buf, sems, out_sems, *work = refs
    known = {
        offset: entry(meta_ref, offset) for its_places in before for offset, _ in its_places
    }

    def each(act):
        for n, (result, its_places) in enumerate(zip(results, before, strict=True)):
            for j, (offset, start) in enumerate(its_places):
                dest = known[offset]
                copy = pltpu.make_async_copy(
                    result.at[j], o_ref.at[half_of(jnp.maximum(dest, 0), start)], sems.at[n, j]
                )
                pl.when(dest >= 0)(getattr(copy, act))

    each("start")
    dests = entries(meta_ref, [offset for offset, _ in places])

    @pl.when(any_of(dests))
    def _():
        starts = [start for _, start in places]
        store = stores(out_buf, o_ref, out_sems)
        attend_pieces(dests, starts, q_refs, k_ref, wide_ref, out_buf, store, *work)

    each("wait")


def attend_last(meta, before, results, pieces, ordered_keys, wide_values, attention):
    queries = [piece[0] for piece in pieces]
    places = [piece[1:] for piece in pieces]
    count, (tall, width) = len(pieces), queries[0].shape
    most = max([1, *(len(its_places) for its_places in before)])
    return pl.pallas_call(
        lambda *refs: last_kernel(before, places, *refs),
        out_shape=jax.ShapeDtypeStruct(attention.shape, attention.dtype),
        in_specs=[VMEM] * (len(results) + count + 3) + [ANY],
        out_specs=ANY,
        input_output_aliases={len(results) + count + 3: 0},
        scratch_shapes=[
            pltpu.VMEM((count, tall, width), attention.dtype),
            pltpu.SemaphoreType.DMA((max(1, len(before)), most)),
            pltpu.SemaphoreType.DMA((count,)),
            *work_space(count, tall, width, ordered_keys.shape[1]),
        ],
        compiler_params=pltpu.CompilerParams(vmem_limit_bytes=VMEM_BYTES),
        cost_estimate=cost_of(2.5),
    )(meta, *results, *queries, ordered_keys, wide_values, attention)


def gathered_kernel(meta_ref, first_ref, later_ref, k_ref, v_ref, o_ref, wide, stacked, mixed, top, bounds):
    at = pl.program_id(1)
    live = meta_ref[0]
    widen(v_ref, wide)

    @pl.when(at == 0)
    def _():
        stack(first_ref, stacked.at[0])

    @pl.when(at > 0)
    def _():
        stack(later_ref.at[0], stacked.at[0])

    def work(shifted):
        args = (at, 0, stacked.at[0], k_ref, wide, mixed, o_ref, bounds)
        if shifted:
            attend_piece_shifted(*args, top)
        else:
            attend_piece(*args)

    @pl.when(at < live)
    def _():
        twice_if_needed(work, lambda: None, bounds)

    @pl.when(at >= live)
    def _():
        o_ref[...] = jnp.zeros_like(o_ref)


def attend_gathered(live, source, first, later, cache_keys, cache_values):
    home_rows, key_width = cache_keys.shape
    width = first.shape[1]
    groups = key_width // HDIM
    part = width // groups
    meta = jnp.concatenate([live.reshape(1), source]).astype(jnp.int32)
    return pl.pallas_call(
        gathered_kernel,
        out_shape=jax.ShapeDtypeStruct((home_rows, width), first.dtype),
        grid_spec=pltpu.PrefetchScalarGridSpec(
            num_scalar_prefetch=1,
            grid=(groups, MAXC),
            in_specs=[
                pl.BlockSpec((SPAN, part), lambda g, m, meta: (0, g)),
                pl.BlockSpec((1, SPAN, part), lambda g, m, meta: (meta[1 + m], 0, g)),
                pl.BlockSpec((home_rows, HDIM), lambda g, m, meta: (0, g)),
                pl.BlockSpec((home_rows, HDIM), lambda g, m, meta: (0, g)),
            ],
            out_specs=pl.BlockSpec((SPAN, part), lambda g, m, meta: (m, g)),
            scratch_shapes=[
                pltpu.VMEM((home_rows, 2 * HDIM), cache_keys.dtype),
                *work_space(1, SPAN, part, HDIM),
            ],
        ),
        compiler_params=pltpu.CompilerParams(vmem_limit_bytes=VMEM_BYTES),
    )(meta, first, later, cache_keys, cache_values)


def gather_all(queries, keys, values, lengths, slot_prompt, slot_span):
    mine = lax.axis_index("replica")
    home_rows, key_width = MAXC * SPAN, keys.shape[1]
    live = lengths[mine]
    spans = jnp.arange(MAXC, dtype=jnp.int32)
    matches = (slot_prompt[None, :, 1] == mine) & (slot_span[None, :, 1] == spans[:, None])
    here = jnp.any(matches, axis=1)
    source = jnp.argmax(matches, axis=1).astype(jnp.int32)
    slots_k = lax.all_gather(keys[SPAN:], "replica")
    slots_v = lax.all_gather(values[SPAN:], "replica")
    slots_q = lax.all_gather(queries[SPAN:], "replica")

    def in_order(first, slots):
        picked = jnp.take(slots, source, axis=0)
        kept = jnp.where(here[:, None, None], picked, jnp.zeros((), slots.dtype))
        return jnp.concatenate([first, kept[1:].reshape(home_rows - SPAN, key_width)], axis=0)

    cache_keys = in_order(keys[:SPAN], slots_k)
    cache_values = in_order(values[:SPAN], slots_v)
    attention = attend_gathered(live, source, queries[:SPAN], slots_q, cache_keys, cache_values)
    return (attention, cache_keys, cache_values)


def per_device(queries, keys, values, lengths, slot_prompt, slot_span):
    replicas = lax.axis_size("replica")
    if replicas != 8:
        return gather_all(queries, keys, values, lengths, slot_prompt, slot_span)
    ring = column_ring(replicas)
    farthest = replicas // 2

    def after(block, *others):
        return lax.optimization_barrier((block, others))[0]

    def joined(both):
        return list(lax.optimization_barrier(tuple(both)))

    def shift(block, step):
        pairs = [(r, ring[(n + step) % replicas]) for n, r in enumerate(ring)]
        return lax.ppermute(block, "replica", pairs)

    def go_on(both):
        return [shift(both[0], 1), shift(both[1], -1)]

    own_kv = pack_kv(keys, values)
    kv = [[own_kv, own_kv]]
    kv.append(go_on(kv[0]))
    own_top, own_bottom = pack_q(after(queries, own_kv))
    first, second = [[own_top, own_bottom]], [[own_bottom, own_top]]
    first.append(joined(go_on(first[0])))
    kv[1] = joined(kv[1])
    kv.append(joined(go_on(kv[1])))
    local = attend_local(lengths, after(queries, kv[1]), keys, values)
    second.append(joined(go_on([after(block, first[1]) for block in second[0]])))
    kv.append(joined(go_on([after(block, local) for block in kv[2]])))
    first.append(joined(go_on([after(block, kv[3]) for block in first[1]])))
    kv.append([shift(kv[3][0], 1)])
    second.append(joined(go_on([after(block, kv[3]) for block in second[1]])))
    meta = places(lengths, slot_prompt, slot_span)
    offsets = [[n, replicas - n] for n in range(1, farthest)]

    def wave(n, which):
        up, down = offsets[n - 1]
        if which is first:
            return [(first[n][0], up, 0), (first[n][1], down, half)]
        return [(second[n][0], up, half), (second[n][1], down, 0)]

    half = SPAN // 2
    cache_keys, cache_values, ordered_keys, wide_values, result, attention = attend_first(
        meta,
        keys,
        values,
        sum(offsets, []) + [farthest],
        sum(kv[1:], []),
        wave(1, first) + wave(1, second),
        local,
    )
    results, before = [result], [wave(1, first) + wave(1, second)]

    def attend(n, which):
        results.append(attend_later(meta, wave(n, which), ordered_keys, wide_values))
        before.append(wave(n, which))

    first.append(joined(go_on(first[2])))
    attend(2, first)
    second.append(joined(go_on([after(block, results[-1]) for block in second[2]])))
    attend(2, second)
    last = [
        (shift(after(first[3][0], results[-1]), 1), farthest, 0),
        (shift(after(first[3][1], results[-1]), -1), farthest, half),
    ]

    def attend_and_store(done, pieces, attention):
        places = [[piece[1:] for piece in its_pieces] for its_pieces in before[done]]
        return attend_last(
            meta, places, results[done], pieces, ordered_keys, wide_values, attention
        )

    attention = attend_and_store(slice(0, 3), wave(3, first), attention)
    attend(3, second)
    attention = attend_and_store(slice(3, 4), last[1:], attention)
    attention = attend_and_store(slice(0, 0), last[:1], attention)
    return (attention, cache_keys, cache_values)


def solution(mesh):
    in_specs = (
        P(("group", "replica"), "tensor"),
        P(("group", "replica"), "tensor"),
        P(("group", "replica"), "tensor"),
        P("group"),
        P("group", None),
        P("group", None),
    )
    out_specs = (
        P(("group", "replica"), "tensor"),
        P(("group", "replica"), "tensor"),
        P(("group", "replica"), "tensor"),
    )
    return jax.shard_map(
        per_device, mesh=mesh, in_specs=in_specs, out_specs=out_specs, check_vma=False
    )
```

```python
import functools
import math

import jax
import jax.numpy as jnp
from jax import lax
from jax.experimental import pallas as pl
from jax.experimental.pallas import tpu as pltpu
from jax.sharding import PartitionSpec as P

HDIM = 128
SPAN = 128
SLOTS = 2
LANES = 128
MAXC = 8
BLOCK = 4
PART = 1
LOG2E = 1.0 / math.log(2.0)
VMEM_BYTES = 40 * 1024 * 1024
MOST_VMEM_BYTES = 60 * 1024 * 1024
LEAST_SUM, MOST_SUM = 1e-20, 1e30
ANY = pl.BlockSpec(memory_space=pl.ANY)
SMEM = pl.BlockSpec(memory_space=pltpu.SMEM)
VMEM = pl.BlockSpec(memory_space=pltpu.VMEM)


def cost_of(us):
    return pl.CostEstimate(flops=int(us * 1.15e9), bytes_accessed=0, transcendentals=0)


def column_ring(replicas):
    return list(range(0, replicas, 2)) + list(range(replicas - 1, 0, -2))


def copy_all(copies):
    for copy in copies:
        copy.start()
    for copy in copies:
        copy.wait()


def pack_kv_kernel(k_ref, v_ref, o_ref, sems):
    copy_all(
        [
            pltpu.make_async_copy(k_ref.at[SPAN:], o_ref.at[:SPAN], sems.at[0]),
            pltpu.make_async_copy(v_ref.at[SPAN:], o_ref.at[SPAN:], sems.at[1]),
        ]
    )


def pack_kv(keys, values):
    return pl.pallas_call(
        pack_kv_kernel,
        out_shape=jax.ShapeDtypeStruct((2 * SPAN, keys.shape[1]), keys.dtype),
        in_specs=[ANY] * 2,
        out_specs=VMEM,
        scratch_shapes=[pltpu.SemaphoreType.DMA((2,))],
        compiler_params=pltpu.CompilerParams(vmem_limit_bytes=MOST_VMEM_BYTES),
        cost_estimate=cost_of(1),
    )(keys, values)


def pack_q_kernel(q_ref, o_top, o_bottom, sems):
    half = SPAN // 2
    copy_all(
        [
            pltpu.make_async_copy(q_ref.at[SPAN : SPAN + half], o_top, sems.at[0]),
            pltpu.make_async_copy(q_ref.at[SPAN + half :], o_bottom, sems.at[1]),
        ]
    )


def pack_q(queries):
    half = jax.ShapeDtypeStruct((SPAN // 2, queries.shape[1]), queries.dtype)
    return pl.pallas_call(
        pack_q_kernel,
        out_shape=(half, half),
        in_specs=[ANY],
        out_specs=(VMEM, VMEM),
        scratch_shapes=[pltpu.SemaphoreType.DMA((2,))],
        compiler_params=pltpu.CompilerParams(vmem_limit_bytes=VMEM_BYTES),
        cost_estimate=cost_of(1),
    )(queries)


def places(lengths, slot_prompt, slot_span):
    replicas = lengths.shape[0]
    mine = lax.axis_index("replica")
    ring = jnp.arange(replicas, dtype=jnp.int32)
    place = jnp.where(mine % 2 == 0, mine // 2, replicas - 1 - mine // 2)
    at = (place + replicas - ring) % replicas
    other = jnp.where(at < replicas // 2, 2 * at, 2 * (replicas - at) - 1)
    chosen = other[:, None] == ring[None, :]
    wanted = chosen & (slot_prompt[None, :, 1] == mine) & (ring[:, None] > 0)
    spans = jnp.where(wanted, slot_span[None, :, 1] + 1, 0)
    whole = jnp.where(chosen & (ring[:, None] == 0), lengths[None, :] + 1, 0)
    table = jnp.sum(spans + whole, axis=1, keepdims=True) - 1
    return jnp.broadcast_to(table, (replicas, LANES))


def entry(meta_ref, n):
    return jnp.max(meta_ref[n : n + 1, :])


def entries(meta_ref, offsets):
    found = {offset: entry(meta_ref, offset) for offset in dict.fromkeys(offsets)}
    return [found[offset] for offset in offsets]


def widen(v_ref, wide_ref):
    for at in range(0, v_ref.shape[-1], HDIM):
        wide_ref[:, 2 * at : 2 * at + HDIM] = v_ref[:, at : at + HDIM]
        wide_ref[:, 2 * at + HDIM : 2 * at + 2 * HDIM] = jnp.ones(
            (v_ref.shape[0], HDIM), v_ref.dtype
        )


def stack(q_ref, stacked):
    kv_heads, rows, _ = stacked.shape
    tall = q_ref.shape[0]
    group = rows // tall
    for shared in range(kv_heads):
        for h in range(group):
            at = (shared * group + h) * HDIM
            stacked[shared, h * tall : (h + 1) * tall, :] = q_ref[:, at : at + HDIM]


def divide(mixed, shared, o_ref, bounds):
    tall = o_ref.shape[0]
    group = mixed.shape[0] // tall
    total = mixed[:, HDIM:]
    inverse = pl.reciprocal(total, approx=True)
    inverse = inverse * (2.0 - total * inverse)
    result = (mixed[:, :HDIM] * inverse).astype(o_ref.dtype)
    for h in range(group):
        at = (shared * group + h) * HDIM
        o_ref[:, at : at + HDIM] = result[h * tall : (h + 1) * tall, :]
    total = total.reshape(-1, 8, HDIM)
    bounds[0] = jnp.minimum(bounds[0], jnp.min(total, axis=0))
    bounds[1] = jnp.maximum(bounds[1], jnp.max(total, axis=0))


def attend_piece(span, start, stacked, k_ref, wide_ref, mixed, o_ref, bounds):
    kv_heads, rows, _ = stacked.shape
    heads = range(kv_heads)
    tall = o_ref.shape[0]
    scale = LOG2E / math.sqrt(HDIM)
    blocks = span // BLOCK
    edge = span % PART * SPAN + start

    def keys_of(block, spans):
        return pl.ds(pl.multiple_of(block * BLOCK * SPAN, BLOCK * SPAN), spans * SPAN)

    def scores(shared, block, spans, masked):
        found = lax.dot_general(
            stacked[shared],
            k_ref[keys_of(block, spans), shared * HDIM : (shared + 1) * HDIM],
            (((1,), (1,)), ((), ())),
            preferred_element_type=jnp.float32,
        )
        if masked:
            seen = (spans - PART) * SPAN
            row = lax.broadcasted_iota(jnp.int32, (rows, PART * SPAN), 0) % tall
            column = lax.broadcasted_iota(jnp.int32, (rows, PART * SPAN), 1)
            last = jnp.where(column <= row + edge, found[:, seen:], -jnp.inf)
            found = jnp.concatenate([found[:, :seen], last], axis=1) if seen else last
        return found

    def products(shared, block, spans, found):
        return jnp.dot(
            jnp.exp2(found * scale).astype(jnp.bfloat16),
            wide_ref[keys_of(block, spans), 2 * shared * HDIM : 2 * (shared + 1) * HDIM],
            preferred_element_type=jnp.float32,
        )

    def add(block, carry):
        found = [scores(shared, block, BLOCK, False) for shared in heads]
        for shared in heads:
            before = jnp.where(block > 0, mixed[shared], 0.0)
            mixed[shared] = before + products(shared, block, BLOCK, found[shared])
        return carry

    most = k_ref.shape[0] // SPAN
    if most > BLOCK:
        lax.fori_loop(0, blocks, add, 0)
    for spans in range(PART, min(BLOCK, most) + 1, PART):

        @pl.when(span % BLOCK // PART == spans // PART - 1)
        def _(spans=spans):
            found = [scores(shared, blocks, spans, True) for shared in heads]
            for shared in heads:
                before = jnp.where(blocks > 0, mixed[shared], 0.0)
                whole = before + products(shared, blocks, spans, found[shared])
                divide(whole, shared, o_ref, bounds)


def attend_piece_shifted(span, start, stacked, k_ref, wide_ref, mixed, o_ref, bounds, top):
    kv_heads, rows, _ = stacked.shape
    tall = o_ref.shape[0]
    scale = LOG2E / math.sqrt(HDIM)

    def one_head(shared, carry):
        def scores(block):
            found = lax.dot_general(
                stacked[shared],
                k_ref[rows_of(block), pl.ds(pl.multiple_of(shared * HDIM, HDIM), HDIM)],
                (((1,), (1,)), ((), ())),
                preferred_element_type=jnp.float32,
            )
            row = lax.broadcasted_iota(jnp.int32, (rows, SPAN), 0) % tall
            column = lax.broadcasted_iota(jnp.int32, (rows, SPAN), 1)
            return jnp.where(column <= row + (span - block) * SPAN + start, found, -jnp.inf)

        def look(block, carry):
            top[...] = jnp.maximum(top[...], scores(block))
            return carry

        def add(block, carry):
            weights = jnp.exp2((scores(block) - top[...]) * scale).astype(jnp.bfloat16)
            mixed[shared] += jnp.dot(
                weights,
                wide_ref[
                    rows_of(block), pl.ds(pl.multiple_of(2 * shared * HDIM, 2 * HDIM), 2 * HDIM)
                ],
                preferred_element_type=jnp.float32,
            )
            return carry

        top[...] = jnp.full_like(top, -jnp.inf)
        lax.fori_loop(0, span + 1, look, 0)
        top[...] = jnp.broadcast_to(jnp.max(top[...], axis=1, keepdims=True), top.shape)
        mixed[shared] = jnp.zeros(mixed.shape[1:], mixed.dtype)
        lax.fori_loop(0, span + 1, add, 0)
        return carry

    lax.fori_loop(0, kv_heads, one_head, 0)
    for shared in range(kv_heads):
        divide(mixed[shared], shared, o_ref, bounds)


def twice_if_needed(work, drain, bounds):
    bounds[...] = jnp.ones_like(bounds)
    work(False)
    safe = (bounds[0] > LEAST_SUM) & (bounds[1] < MOST_SUM)
    unsafe = jnp.max(jnp.where(safe, 0.0, 1.0)) > 0.5
    drain()

    @pl.when(unsafe)
    def _():
        work(True)
        drain()


def work_space(count, tall, width, key_width):
    kv_heads = key_width // HDIM
    rows = width // key_width * tall
    return [
        pltpu.VMEM((count, kv_heads, rows, HDIM), jnp.bfloat16),
        pltpu.VMEM((kv_heads, rows, 2 * HDIM), jnp.float32),
        pltpu.VMEM((rows, HDIM), jnp.float32),
        pltpu.VMEM((2, 8, HDIM), jnp.float32),
    ]


def rows_of(span):
    return pl.ds(pl.multiple_of(span * SPAN, SPAN), SPAN)


def half_of(span, start):
    return pl.ds(pl.multiple_of(span * SPAN + start, SPAN // 2), SPAN // 2)


def pick(j, options):
    chosen = options[0]
    for n in range(1, len(options)):
        chosen = jnp.where(j == n, options[n], chosen)
    return chosen


def attend_pieces(dests, starts, q_refs, k_ref, wide_ref, out_buf, store, stacked, mixed, top, bounds):
    count = len(dests)
    for j in range(count):

        @pl.when(dests[j] >= 0)
        def _(j=j):
            stack(q_refs[j], stacked.at[j])

    def work(shifted):
        def one(j, carry):
            dest, start = pick(j, dests), pick(j, starts)

            @pl.when(dest >= 0)
            def _():
                args = (dest, start, stacked.at[j], k_ref, wide_ref, mixed, out_buf.at[j], bounds)
                if shifted:
                    attend_piece_shifted(*args, top)
                else:
                    attend_piece(*args)
                if store is not None:
                    store(j, dest, start).start()

            return carry

        lax.fori_loop(0, count, one, 0)

    def drain():
        if store is not None:
            for j in range(count):
                pl.when(dests[j] >= 0)(store(j, jnp.maximum(dests[j], 0), starts[j]).wait)

    twice_if_needed(work, drain, bounds)


def stores(buf, o_ref, sems):
    return lambda j, span, start: pltpu.make_async_copy(
        buf.at[j], o_ref.at[half_of(span, start)], sems.at[j]
    )


def local_kernel(length_ref, q_ref, k_ref, v_ref, out_buf, wide, *work):
    live = length_ref[lax.axis_index("replica")]
    widen(v_ref, wide)
    half = SPAN // 2
    second = jnp.where(live > 1, 1, -1)
    attend_pieces(
        [jnp.int32(0), jnp.int32(0), second, second],
        [0, half, 0, half],
        [q_ref.at[n * half : (n + 1) * half] for n in range(2 * SLOTS)],
        k_ref,
        wide,
        out_buf,
        None,
        *work,
    )


def attend_local(lengths, queries, keys, values):
    width, key_width = queries.shape[1], keys.shape[1]
    return pl.pallas_call(
        local_kernel,
        out_shape=jax.ShapeDtypeStruct((2 * SLOTS, SPAN // 2, width), queries.dtype),
        in_specs=[SMEM, VMEM, VMEM, VMEM],
        out_specs=VMEM,
        scratch_shapes=[
            pltpu.VMEM((SLOTS * SPAN, 2 * key_width), keys.dtype),
            *work_space(2 * SLOTS, SPAN // 2, width, key_width),
        ],
        compiler_params=pltpu.CompilerParams(vmem_limit_bytes=VMEM_BYTES),
        cost_estimate=cost_of(3.5),
    )(lengths, queries, keys, values)


def any_of(dests):
    return functools.reduce(jnp.maximum, dests) >= 0


def first_kernel(kv_offsets, places, meta_ref, own_k, own_v, *refs):
    blocks, refs = refs[: len(kv_offsets)], refs[len(kv_offsets) :]
    q_refs, refs = refs[: len(places)], refs[len(places) :]
    local, o_k, o_v, k_buf, wide, out_buf, o_ref, v_buf, zeros, out_sems, span_sems, *work = refs
    live = entry(meta_ref, 0)
    half = SPAN // 2
    kv_dests = entries(meta_ref, kv_offsets)

    def each_span(act):
        for span in range(MAXC):
            if span < SLOTS:
                for n in range(2):
                    copy = pltpu.make_async_copy(
                        local.at[2 * span + n],
                        o_ref.at[half_of(span, n * half)],
                        span_sems.at[span, n],
                    )
                    pl.when(span < live)(getattr(copy, act))
            if span > 0:
                copy = pltpu.make_async_copy(zeros, o_ref.at[rows_of(span)], span_sems.at[span, 0])
                pl.when(span >= live)(getattr(copy, act))

    zeros[...] = jnp.zeros_like(zeros)
    each_span("start")
    k_buf[rows_of(0), :] = own_k[:SPAN, :]
    v_buf[rows_of(0), :] = own_v[:SPAN, :]

    @pl.when(live > 1)
    def _():
        k_buf[rows_of(1), :] = own_k[SPAN:, :]
        v_buf[rows_of(1), :] = own_v[SPAN:, :]

    for span in range(1, MAXC):

        @pl.when(span >= live)
        def _(span=span):
            k_buf[rows_of(span), :] = jnp.zeros((SPAN, k_buf.shape[1]), k_buf.dtype)
            v_buf[rows_of(span), :] = jnp.zeros((SPAN, v_buf.shape[1]), v_buf.dtype)

    for block, dest in zip(blocks, kv_dests, strict=True):

        @pl.when(dest >= 0)
        def _(block=block, dest=dest):
            k_buf[rows_of(dest), :] = block[:SPAN, :]
            v_buf[rows_of(dest), :] = block[SPAN:, :]

    copy_k = pltpu.make_async_copy(k_buf, o_k, out_sems.at[0])
    copy_v = pltpu.make_async_copy(v_buf, o_v, out_sems.at[1])
    copy_k.start()
    copy_v.start()
    dests = entries(meta_ref, [offset for offset, _ in places])

    @pl.when(live > 1)
    def _():
        widen(v_buf, wide)

    @pl.when(any_of(dests))
    def _():
        starts = [start for _, start in places]
        attend_pieces(dests, starts, q_refs, k_buf, wide, out_buf, None, *work)

    copy_k.wait()
    copy_v.wait()
    each_span("wait")


def attend_first(meta, keys, values, kv_offsets, kv_blocks, pieces, local):
    rows, key_width = MAXC * SPAN, keys.shape[1]
    queries = [piece[0] for piece in pieces]
    places = [piece[1:] for piece in pieces]
    count, (tall, width) = len(pieces), queries[0].shape
    out = jax.ShapeDtypeStruct((rows, key_width), keys.dtype)
    return pl.pallas_call(
        lambda *refs: first_kernel(kv_offsets, places, *refs),
        out_shape=(
            out,
            out,
            out,
            jax.ShapeDtypeStruct((rows, 2 * key_width), keys.dtype),
            jax.ShapeDtypeStruct((count, tall, width), keys.dtype),
            jax.ShapeDtypeStruct((rows, width), keys.dtype),
        ),
        in_specs=[VMEM] * (len(kv_blocks) + count + 4),
        out_specs=(ANY, ANY, VMEM, VMEM, VMEM, ANY),
        scratch_shapes=[
            pltpu.VMEM((rows, key_width), keys.dtype),
            pltpu.VMEM((SPAN, width), keys.dtype),
            pltpu.SemaphoreType.DMA((2,)),
            pltpu.SemaphoreType.DMA((MAXC, 2)),
            *work_space(count, tall, width, key_width),
        ],
        compiler_params=pltpu.CompilerParams(vmem_limit_bytes=VMEM_BYTES),
        cost_estimate=cost_of(2 + 1.3 * count),
    )(meta, keys, values, *kv_blocks, *queries, local)


def later_kernel(places, meta_ref, *refs):
    q_refs, (k_ref, wide_ref, out_buf, *work) = refs[: len(places)], refs[len(places) :]
    dests = entries(meta_ref, [offset for offset, _ in places])

    @pl.when(any_of(dests))
    def _():
        starts = [start for _, start in places]
        attend_pieces(dests, starts, q_refs, k_ref, wide_ref, out_buf, None, *work)


def attend_later(meta, pieces, ordered_keys, wide_values):
    queries = [piece[0] for piece in pieces]
    places = [piece[1:] for piece in pieces]
    count, (tall, width) = len(pieces), queries[0].shape
    return pl.pallas_call(
        lambda *refs: later_kernel(places, *refs),
        out_shape=jax.ShapeDtypeStruct((count, tall, width), ordered_keys.dtype),
        in_specs=[VMEM] * (count + 3),
        out_specs=VMEM,
        scratch_shapes=work_space(count, tall, width, ordered_keys.shape[1]),
        compiler_params=pltpu.CompilerParams(vmem_limit_bytes=VMEM_BYTES),
        cost_estimate=cost_of(1 + 1.3 * count),
    )(meta, *queries, ordered_keys, wide_values)


def last_kernel(before, places, meta_ref, *refs):
    results, refs = refs[: len(before)], refs[len(before) :]
    q_refs, refs = refs[: len(places)], refs[len(places) :]
    k_ref, wide_ref, _, o_ref, out_buf, sems, out_sems, *work = refs
    known = {
        offset: entry(meta_ref, offset) for its_places in before for offset, _ in its_places
    }

    def each(act):
        for n, (result, its_places) in enumerate(zip(results, before, strict=True)):
            for j, (offset, start) in enumerate(its_places):
                dest = known[offset]
                copy = pltpu.make_async_copy(
                    result.at[j], o_ref.at[half_of(jnp.maximum(dest, 0), start)], sems.at[n, j]
                )
                pl.when(dest >= 0)(getattr(copy, act))

    each("start")
    dests = entries(meta_ref, [offset for offset, _ in places])

    @pl.when(any_of(dests))
    def _():
        starts = [start for _, start in places]
        store = stores(out_buf, o_ref, out_sems)
        attend_pieces(dests, starts, q_refs, k_ref, wide_ref, out_buf, store, *work)

    each("wait")


def attend_last(meta, before, results, pieces, ordered_keys, wide_values, attention):
    queries = [piece[0] for piece in pieces]
    places = [piece[1:] for piece in pieces]
    count, (tall, width) = len(pieces), queries[0].shape
    most = max([1, *(len(its_places) for its_places in before)])
    return pl.pallas_call(
        lambda *refs: last_kernel(before, places, *refs),
        out_shape=jax.ShapeDtypeStruct(attention.shape, attention.dtype),
        in_specs=[VMEM] * (len(results) + count + 3) + [ANY],
        out_specs=ANY,
        input_output_aliases={len(results) + count + 3: 0},
        scratch_shapes=[
            pltpu.VMEM((count, tall, width), attention.dtype),
            pltpu.SemaphoreType.DMA((max(1, len(before)), most)),
            pltpu.SemaphoreType.DMA((count,)),
            *work_space(count, tall, width, ordered_keys.shape[1]),
        ],
        compiler_params=pltpu.CompilerParams(vmem_limit_bytes=VMEM_BYTES),
        cost_estimate=cost_of(2.5),
    )(meta, *results, *queries, ordered_keys, wide_values, attention)


def gathered_kernel(meta_ref, first_ref, later_ref, k_ref, v_ref, o_ref, wide, stacked, mixed, top, bounds):
    at = pl.program_id(1)
    live = meta_ref[0]
    widen(v_ref, wide)

    @pl.when(at == 0)
    def _():
        stack(first_ref, stacked.at[0])

    @pl.when(at > 0)
    def _():
        stack(later_ref.at[0], stacked.at[0])

    def work(shifted):
        args = (at, 0, stacked.at[0], k_ref, wide, mixed, o_ref, bounds)
        if shifted:
            attend_piece_shifted(*args, top)
        else:
            attend_piece(*args)

    @pl.when(at < live)
    def _():
        twice_if_needed(work, lambda: None, bounds)

    @pl.when(at >= live)
    def _():
        o_ref[...] = jnp.zeros_like(o_ref)


def attend_gathered(live, source, first, later, cache_keys, cache_values):
    home_rows, key_width = cache_keys.shape
    width = first.shape[1]
    groups = key_width // HDIM
    part = width // groups
    meta = jnp.concatenate([live.reshape(1), source]).astype(jnp.int32)
    return pl.pallas_call(
        gathered_kernel,
        out_shape=jax.ShapeDtypeStruct((home_rows, width), first.dtype),
        grid_spec=pltpu.PrefetchScalarGridSpec(
            num_scalar_prefetch=1,
            grid=(groups, MAXC),
            in_specs=[
                pl.BlockSpec((SPAN, part), lambda g, m, meta: (0, g)),
                pl.BlockSpec((1, SPAN, part), lambda g, m, meta: (meta[1 + m], 0, g)),
                pl.BlockSpec((home_rows, HDIM), lambda g, m, meta: (0, g)),
                pl.BlockSpec((home_rows, HDIM), lambda g, m, meta: (0, g)),
            ],
            out_specs=pl.BlockSpec((SPAN, part), lambda g, m, meta: (m, g)),
            scratch_shapes=[
                pltpu.VMEM((home_rows, 2 * HDIM), cache_keys.dtype),
                *work_space(1, SPAN, part, HDIM),
            ],
        ),
        compiler_params=pltpu.CompilerParams(vmem_limit_bytes=VMEM_BYTES),
    )(meta, first, later, cache_keys, cache_values)


def gather_all(queries, keys, values, lengths, slot_prompt, slot_span):
    mine = lax.axis_index("replica")
    home_rows, key_width = MAXC * SPAN, keys.shape[1]
    live = lengths[mine]
    spans = jnp.arange(MAXC, dtype=jnp.int32)
    matches = (slot_prompt[None, :, 1] == mine) & (slot_span[None, :, 1] == spans[:, None])
    here = jnp.any(matches, axis=1)
    source = jnp.argmax(matches, axis=1).astype(jnp.int32)
    slots_k = lax.all_gather(keys[SPAN:], "replica")
    slots_v = lax.all_gather(values[SPAN:], "replica")
    slots_q = lax.all_gather(queries[SPAN:], "replica")

    def in_order(first, slots):
        picked = jnp.take(slots, source, axis=0)
        kept = jnp.where(here[:, None, None], picked, jnp.zeros((), slots.dtype))
        return jnp.concatenate([first, kept[1:].reshape(home_rows - SPAN, key_width)], axis=0)

    cache_keys = in_order(keys[:SPAN], slots_k)
    cache_values = in_order(values[:SPAN], slots_v)
    attention = attend_gathered(live, source, queries[:SPAN], slots_q, cache_keys, cache_values)
    return (attention, cache_keys, cache_values)


def per_device(queries, keys, values, lengths, slot_prompt, slot_span):
    replicas = lax.axis_size("replica")
    if replicas != 8:
        return gather_all(queries, keys, values, lengths, slot_prompt, slot_span)
    ring = column_ring(replicas)
    farthest = replicas // 2

    def after(block, *others):
        return lax.optimization_barrier((block, others))[0]

    def joined(both):
        return list(lax.optimization_barrier(tuple(both)))

    def shift(block, step):
        pairs = [(r, ring[(n + step) % replicas]) for n, r in enumerate(ring)]
        return lax.ppermute(block, "replica", pairs)

    def go_on(both):
        return [shift(both[0], 1), shift(both[1], -1)]

    own_kv = pack_kv(keys, values)
    kv = [[own_kv, own_kv]]
    kv.append(go_on(kv[0]))
    own_top, own_bottom = pack_q(after(queries, own_kv))
    first, second = [[own_top, own_bottom]], [[own_bottom, own_top]]
    first.append(joined(go_on(first[0])))
    kv[1] = joined(kv[1])
    kv.append(joined(go_on(kv[1])))
    local = attend_local(lengths, after(queries, kv[1]), keys, values)
    second.append(joined(go_on([after(block, first[1]) for block in second[0]])))
    kv.append(joined(go_on([after(block, local) for block in kv[2]])))
    first.append(joined(go_on([after(block, kv[3]) for block in first[1]])))
    kv.append([shift(kv[3][0], 1)])
    second.append(joined(go_on([after(block, kv[3]) for block in second[1]])))
    meta = places(lengths, slot_prompt, slot_span)
    offsets = [[n, replicas - n] for n in range(1, farthest)]

    def wave(n, which):
        up, down = offsets[n - 1]
        if which is first:
            return [(first[n][0], up, 0), (first[n][1], down, half)]
        return [(second[n][0], up, half), (second[n][1], down, 0)]

    half = SPAN // 2
    cache_keys, cache_values, ordered_keys, wide_values, result, attention = attend_first(
        meta,
        keys,
        values,
        sum(offsets, []) + [farthest],
        sum(kv[1:], []),
        wave(1, first) + wave(1, second),
        local,
    )
    results, before = [result], [wave(1, first) + wave(1, second)]

    def attend(n, which):
        results.append(attend_later(meta, wave(n, which), ordered_keys, wide_values))
        before.append(wave(n, which))

    first.append(joined(go_on(first[2])))
    attend(2, first)
    second.append(joined(go_on([after(block, results[-1]) for block in second[2]])))
    attend(2, second)
    last = [
        (shift(after(first[3][0], results[-1]), 1), farthest, 0),
        (shift(after(first[3][1], results[-1]), -1), farthest, half),
    ]

    def attend_and_store(done, pieces, attention):
        places = [[piece[1:] for piece in its_pieces] for its_pieces in before[done]]
        return attend_last(
            meta, places, results[done], pieces, ordered_keys, wide_values, attention
        )

    attention = attend_and_store(slice(0, 3), wave(3, first), attention)
    attend(3, second)
    attention = attend_and_store(slice(3, 4), last[1:], attention)
    attention = attend_and_store(slice(0, 0), last[:1], attention)
    return (attention, cache_keys, cache_values)


def solution(mesh):
    in_specs = (
        P(("group", "replica"), "tensor"),
        P(("group", "replica"), "tensor"),
        P(("group", "replica"), "tensor"),
        P("group"),
        P("group", None),
        P("group", None),
    )
    out_specs = (
        P(("group", "replica"), "tensor"),
        P(("group", "replica"), "tensor"),
        P(("group", "replica"), "tensor"),
    )
    return jax.shard_map(
        per_device, mesh=mesh, in_specs=in_specs, out_specs=out_specs, check_vma=False
    )
```

```python
import functools
import math

import jax
import jax.numpy as jnp
from jax import lax
from jax.experimental import pallas as pl
from jax.experimental.pallas import tpu as pltpu
from jax.sharding import PartitionSpec as P

HDIM = 128
SPAN = 128
SLOTS = 2
LANES = 128
MAXC = 8
BLOCK = 4
PART = 1
LOG2E = 1.0 / math.log(2.0)
VMEM_BYTES = 40 * 1024 * 1024
MOST_VMEM_BYTES = 60 * 1024 * 1024
LEAST_SUM, MOST_SUM = 1e-20, 1e30
ANY = pl.BlockSpec(memory_space=pl.ANY)
SMEM = pl.BlockSpec(memory_space=pltpu.SMEM)
VMEM = pl.BlockSpec(memory_space=pltpu.VMEM)


def cost_of(us):
    return pl.CostEstimate(flops=int(us * 1.15e9), bytes_accessed=0, transcendentals=0)


def column_ring(replicas):
    return list(range(0, replicas, 2)) + list(range(replicas - 1, 0, -2))


def copy_all(copies):
    for copy in copies:
        copy.start()
    for copy in copies:
        copy.wait()


def pack_kv_kernel(k_ref, v_ref, o_ref, sems):
    copy_all(
        [
            pltpu.make_async_copy(k_ref.at[SPAN:], o_ref.at[:SPAN], sems.at[0]),
            pltpu.make_async_copy(v_ref.at[SPAN:], o_ref.at[SPAN:], sems.at[1]),
        ]
    )


def pack_kv(keys, values):
    return pl.pallas_call(
        pack_kv_kernel,
        out_shape=jax.ShapeDtypeStruct((2 * SPAN, keys.shape[1]), keys.dtype),
        in_specs=[ANY] * 2,
        out_specs=VMEM,
        scratch_shapes=[pltpu.SemaphoreType.DMA((2,))],
        compiler_params=pltpu.CompilerParams(vmem_limit_bytes=MOST_VMEM_BYTES),
        cost_estimate=cost_of(1),
    )(keys, values)


def pack_q_kernel(q_ref, o_top, o_bottom, sems):
    half = SPAN // 2
    copy_all(
        [
            pltpu.make_async_copy(q_ref.at[SPAN : SPAN + half], o_top, sems.at[0]),
            pltpu.make_async_copy(q_ref.at[SPAN + half :], o_bottom, sems.at[1]),
        ]
    )


def pack_q(queries):
    half = jax.ShapeDtypeStruct((SPAN // 2, queries.shape[1]), queries.dtype)
    return pl.pallas_call(
        pack_q_kernel,
        out_shape=(half, half),
        in_specs=[ANY],
        out_specs=(VMEM, VMEM),
        scratch_shapes=[pltpu.SemaphoreType.DMA((2,))],
        compiler_params=pltpu.CompilerParams(vmem_limit_bytes=VMEM_BYTES),
        cost_estimate=cost_of(1),
    )(queries)


def places(lengths, slot_prompt, slot_span):
    replicas = lengths.shape[0]
    mine = lax.axis_index("replica")
    ring = jnp.arange(replicas, dtype=jnp.int32)
    place = jnp.where(mine % 2 == 0, mine // 2, replicas - 1 - mine // 2)
    at = (place + replicas - ring) % replicas
    other = jnp.where(at < replicas // 2, 2 * at, 2 * (replicas - at) - 1)
    chosen = other[:, None] == ring[None, :]
    wanted = chosen & (slot_prompt[None, :, 1] == mine) & (ring[:, None] > 0)
    spans = jnp.where(wanted, slot_span[None, :, 1] + 1, 0)
    whole = jnp.where(chosen & (ring[:, None] == 0), lengths[None, :] + 1, 0)
    table = jnp.sum(spans + whole, axis=1, keepdims=True) - 1
    return jnp.broadcast_to(table, (replicas, LANES))


def entry(meta_ref, n):
    return jnp.max(meta_ref[n : n + 1, :])


def entries(meta_ref, offsets):
    found = {offset: entry(meta_ref, offset) for offset in dict.fromkeys(offsets)}
    return [found[offset] for offset in offsets]


def widen(v_ref, wide_ref):
    for at in range(0, v_ref.shape[-1], HDIM):
        wide_ref[:, 2 * at : 2 * at + HDIM] = v_ref[:, at : at + HDIM]
        wide_ref[:, 2 * at + HDIM : 2 * at + 2 * HDIM] = jnp.ones(
            (v_ref.shape[0], HDIM), v_ref.dtype
        )


def stack(q_ref, stacked):
    kv_heads, rows, _ = stacked.shape
    tall = q_ref.shape[0]
    group = rows // tall
    for shared in range(kv_heads):
        for h in range(group):
            at = (shared * group + h) * HDIM
            stacked[shared, h * tall : (h + 1) * tall, :] = q_ref[:, at : at + HDIM]


def divide(mixed, shared, o_ref, bounds):
    tall = o_ref.shape[0]
    group = mixed.shape[0] // tall
    total = mixed[:, HDIM:]
    inverse = pl.reciprocal(total, approx=True)
    inverse = inverse * (2.0 - total * inverse)
    result = (mixed[:, :HDIM] * inverse).astype(o_ref.dtype)
    for h in range(group):
        at = (shared * group + h) * HDIM
        o_ref[:, at : at + HDIM] = result[h * tall : (h + 1) * tall, :]
    total = total.reshape(-1, 8, HDIM)
    bounds[0] = jnp.minimum(bounds[0], jnp.min(total, axis=0))
    bounds[1] = jnp.maximum(bounds[1], jnp.max(total, axis=0))


def attend_piece(span, start, stacked, k_ref, wide_ref, mixed, o_ref, bounds):
    kv_heads, rows, _ = stacked.shape
    heads = range(kv_heads)
    tall = o_ref.shape[0]
    scale = LOG2E / math.sqrt(HDIM)
    blocks = span // BLOCK
    edge = span % PART * SPAN + start

    def keys_of(block, spans):
        return pl.ds(pl.multiple_of(block * BLOCK * SPAN, BLOCK * SPAN), spans * SPAN)

    def scores(shared, block, spans, masked):
        found = lax.dot_general(
            stacked[shared],
            k_ref[keys_of(block, spans), shared * HDIM : (shared + 1) * HDIM],
            (((1,), (1,)), ((), ())),
            preferred_element_type=jnp.float32,
        )
        if masked:
            seen = (spans - PART) * SPAN
            row = lax.broadcasted_iota(jnp.int32, (rows, PART * SPAN), 0) % tall
            column = lax.broadcasted_iota(jnp.int32, (rows, PART * SPAN), 1)
            last = jnp.where(column <= row + edge, found[:, seen:], -jnp.inf)
            found = jnp.concatenate([found[:, :seen], last], axis=1) if seen else last
        return found

    def products(shared, block, spans, found):
        return jnp.dot(
            jnp.exp2(found * scale).astype(jnp.bfloat16),
            wide_ref[keys_of(block, spans), 2 * shared * HDIM : 2 * (shared + 1) * HDIM],
            preferred_element_type=jnp.float32,
        )

    def add(block, carry):
        found = [scores(shared, block, BLOCK, False) for shared in heads]
        for shared in heads:
            before = jnp.where(block > 0, mixed[shared], 0.0)
            mixed[shared] = before + products(shared, block, BLOCK, found[shared])
        return carry

    most = k_ref.shape[0] // SPAN
    if most > BLOCK:
        lax.fori_loop(0, blocks, add, 0)
    for spans in range(PART, min(BLOCK, most) + 1, PART):

        @pl.when(span % BLOCK // PART == spans // PART - 1)
        def _(spans=spans):
            found = [scores(shared, blocks, spans, True) for shared in heads]
            for shared in heads:
                before = jnp.where(blocks > 0, mixed[shared], 0.0)
                whole = before + products(shared, blocks, spans, found[shared])
                divide(whole, shared, o_ref, bounds)


def attend_piece_shifted(span, start, stacked, k_ref, wide_ref, mixed, o_ref, bounds, top):
    kv_heads, rows, _ = stacked.shape
    tall = o_ref.shape[0]
    scale = LOG2E / math.sqrt(HDIM)

    def one_head(shared, carry):
        def scores(block):
            found = lax.dot_general(
                stacked[shared],
                k_ref[rows_of(block), pl.ds(pl.multiple_of(shared * HDIM, HDIM), HDIM)],
                (((1,), (1,)), ((), ())),
                preferred_element_type=jnp.float32,
            )
            row = lax.broadcasted_iota(jnp.int32, (rows, SPAN), 0) % tall
            column = lax.broadcasted_iota(jnp.int32, (rows, SPAN), 1)
            return jnp.where(column <= row + (span - block) * SPAN + start, found, -jnp.inf)

        def look(block, carry):
            top[...] = jnp.maximum(top[...], scores(block))
            return carry

        def add(block, carry):
            weights = jnp.exp2((scores(block) - top[...]) * scale).astype(jnp.bfloat16)
            mixed[shared] += jnp.dot(
                weights,
                wide_ref[
                    rows_of(block), pl.ds(pl.multiple_of(2 * shared * HDIM, 2 * HDIM), 2 * HDIM)
                ],
                preferred_element_type=jnp.float32,
            )
            return carry

        top[...] = jnp.full_like(top, -jnp.inf)
        lax.fori_loop(0, span + 1, look, 0)
        top[...] = jnp.broadcast_to(jnp.max(top[...], axis=1, keepdims=True), top.shape)
        mixed[shared] = jnp.zeros(mixed.shape[1:], mixed.dtype)
        lax.fori_loop(0, span + 1, add, 0)
        return carry

    lax.fori_loop(0, kv_heads, one_head, 0)
    for shared in range(kv_heads):
        divide(mixed[shared], shared, o_ref, bounds)


def twice_if_needed(work, drain, bounds):
    bounds[...] = jnp.ones_like(bounds)
    work(False)
    safe = (bounds[0] > LEAST_SUM) & (bounds[1] < MOST_SUM)
    unsafe = jnp.max(jnp.where(safe, 0.0, 1.0)) > 0.5
    drain()

    @pl.when(unsafe)
    def _():
        work(True)
        drain()


def work_space(count, tall, width, key_width):
    kv_heads = key_width // HDIM
    rows = width // key_width * tall
    return [
        pltpu.VMEM((count, kv_heads, rows, HDIM), jnp.bfloat16),
        pltpu.VMEM((kv_heads, rows, 2 * HDIM), jnp.float32),
        pltpu.VMEM((rows, HDIM), jnp.float32),
        pltpu.VMEM((2, 8, HDIM), jnp.float32),
    ]


def rows_of(span):
    return pl.ds(pl.multiple_of(span * SPAN, SPAN), SPAN)


def half_of(span, start):
    return pl.ds(pl.multiple_of(span * SPAN + start, SPAN // 2), SPAN // 2)


def pick(j, options):
    chosen = options[0]
    for n in range(1, len(options)):
        chosen = jnp.where(j == n, options[n], chosen)
    return chosen


def attend_pieces(dests, starts, q_refs, k_ref, wide_ref, out_buf, store, stacked, mixed, top, bounds):
    count = len(dests)
    for j in range(count):

        @pl.when(dests[j] >= 0)
        def _(j=j):
            stack(q_refs[j], stacked.at[j])

    def work(shifted):
        def one(j, carry):
            dest, start = pick(j, dests), pick(j, starts)

            @pl.when(dest >= 0)
            def _():
                args = (dest, start, stacked.at[j], k_ref, wide_ref, mixed, out_buf.at[j], bounds)
                if shifted:
                    attend_piece_shifted(*args, top)
                else:
                    attend_piece(*args)
                if store is not None:
                    store(j, dest, start).start()

            return carry

        lax.fori_loop(0, count, one, 0)

    def drain():
        if store is not None:
            for j in range(count):
                pl.when(dests[j] >= 0)(store(j, jnp.maximum(dests[j], 0), starts[j]).wait)

    twice_if_needed(work, drain, bounds)


def stores(buf, o_ref, sems):
    return lambda j, span, start: pltpu.make_async_copy(
        buf.at[j], o_ref.at[half_of(span, start)], sems.at[j]
    )


def local_kernel(length_ref, q_ref, k_ref, v_ref, out_buf, wide, *work):
    live = length_ref[lax.axis_index("replica")]
    widen(v_ref, wide)
    half = SPAN // 2
    second = jnp.where(live > 1, 1, -1)
    attend_pieces(
        [jnp.int32(0), jnp.int32(0), second, second],
        [0, half, 0, half],
        [q_ref.at[n * half : (n + 1) * half] for n in range(2 * SLOTS)],
        k_ref,
        wide,
        out_buf,
        None,
        *work,
    )


def attend_local(lengths, queries, keys, values):
    width, key_width = queries.shape[1], keys.shape[1]
    return pl.pallas_call(
        local_kernel,
        out_shape=jax.ShapeDtypeStruct((2 * SLOTS, SPAN // 2, width), queries.dtype),
        in_specs=[SMEM, VMEM, VMEM, VMEM],
        out_specs=VMEM,
        scratch_shapes=[
            pltpu.VMEM((SLOTS * SPAN, 2 * key_width), keys.dtype),
            *work_space(2 * SLOTS, SPAN // 2, width, key_width),
        ],
        compiler_params=pltpu.CompilerParams(vmem_limit_bytes=VMEM_BYTES),
        cost_estimate=cost_of(3.5),
    )(lengths, queries, keys, values)


def any_of(dests):
    return functools.reduce(jnp.maximum, dests) >= 0


def first_kernel(kv_offsets, places, meta_ref, own_k, own_v, *refs):
    blocks, refs = refs[: len(kv_offsets)], refs[len(kv_offsets) :]
    q_refs, refs = refs[: len(places)], refs[len(places) :]
    local, o_k, o_v, k_buf, wide, out_buf, o_ref, v_buf, zeros, out_sems, span_sems, *work = refs
    live = entry(meta_ref, 0)
    half = SPAN // 2
    kv_dests = entries(meta_ref, kv_offsets)

    def each_span(act):
        for span in range(MAXC):
            if span < SLOTS:
                for n in range(2):
                    copy = pltpu.make_async_copy(
                        local.at[2 * span + n],
                        o_ref.at[half_of(span, n * half)],
                        span_sems.at[span, n],
                    )
                    pl.when(span < live)(getattr(copy, act))
            if span > 0:
                copy = pltpu.make_async_copy(zeros, o_ref.at[rows_of(span)], span_sems.at[span, 0])
                pl.when(span >= live)(getattr(copy, act))

    zeros[...] = jnp.zeros_like(zeros)
    each_span("start")
    k_buf[rows_of(0), :] = own_k[:SPAN, :]
    v_buf[rows_of(0), :] = own_v[:SPAN, :]

    @pl.when(live > 1)
    def _():
        k_buf[rows_of(1), :] = own_k[SPAN:, :]
        v_buf[rows_of(1), :] = own_v[SPAN:, :]

    for span in range(1, MAXC):

        @pl.when(span >= live)
        def _(span=span):
            k_buf[rows_of(span), :] = jnp.zeros((SPAN, k_buf.shape[1]), k_buf.dtype)
            v_buf[rows_of(span), :] = jnp.zeros((SPAN, v_buf.shape[1]), v_buf.dtype)

    for block, dest in zip(blocks, kv_dests, strict=True):

        @pl.when(dest >= 0)
        def _(block=block, dest=dest):
            k_buf[rows_of(dest), :] = block[:SPAN, :]
            v_buf[rows_of(dest), :] = block[SPAN:, :]

    copy_k = pltpu.make_async_copy(k_buf, o_k, out_sems.at[0])
    copy_v = pltpu.make_async_copy(v_buf, o_v, out_sems.at[1])
    copy_k.start()
    copy_v.start()
    dests = entries(meta_ref, [offset for offset, _ in places])

    @pl.when(live > 1)
    def _():
        widen(v_buf, wide)

    @pl.when(any_of(dests))
    def _():
        starts = [start for _, start in places]
        attend_pieces(dests, starts, q_refs, k_buf, wide, out_buf, None, *work)

    copy_k.wait()
    copy_v.wait()
    each_span("wait")


def attend_first(meta, keys, values, kv_offsets, kv_blocks, pieces, local):
    rows, key_width = MAXC * SPAN, keys.shape[1]
    queries = [piece[0] for piece in pieces]
    places = [piece[1:] for piece in pieces]
    count, (tall, width) = len(pieces), queries[0].shape
    out = jax.ShapeDtypeStruct((rows, key_width), keys.dtype)
    return pl.pallas_call(
        lambda *refs: first_kernel(kv_offsets, places, *refs),
        out_shape=(
            out,
            out,
            out,
            jax.ShapeDtypeStruct((rows, 2 * key_width), keys.dtype),
            jax.ShapeDtypeStruct((count, tall, width), keys.dtype),
            jax.ShapeDtypeStruct((rows, width), keys.dtype),
        ),
        in_specs=[VMEM] * (len(kv_blocks) + count + 4),
        out_specs=(ANY, ANY, VMEM, VMEM, VMEM, ANY),
        scratch_shapes=[
            pltpu.VMEM((rows, key_width), keys.dtype),
            pltpu.VMEM((SPAN, width), keys.dtype),
            pltpu.SemaphoreType.DMA((2,)),
            pltpu.SemaphoreType.DMA((MAXC, 2)),
            *work_space(count, tall, width, key_width),
        ],
        compiler_params=pltpu.CompilerParams(vmem_limit_bytes=VMEM_BYTES),
        cost_estimate=cost_of(2 + 1.3 * count),
    )(meta, keys, values, *kv_blocks, *queries, local)


def later_kernel(places, meta_ref, *refs):
    q_refs, (k_ref, wide_ref, out_buf, *work) = refs[: len(places)], refs[len(places) :]
    dests = entries(meta_ref, [offset for offset, _ in places])

    @pl.when(any_of(dests))
    def _():
        starts = [start for _, start in places]
        attend_pieces(dests, starts, q_refs, k_ref, wide_ref, out_buf, None, *work)


def attend_later(meta, pieces, ordered_keys, wide_values):
    queries = [piece[0] for piece in pieces]
    places = [piece[1:] for piece in pieces]
    count, (tall, width) = len(pieces), queries[0].shape
    return pl.pallas_call(
        lambda *refs: later_kernel(places, *refs),
        out_shape=jax.ShapeDtypeStruct((count, tall, width), ordered_keys.dtype),
        in_specs=[VMEM] * (count + 3),
        out_specs=VMEM,
        scratch_shapes=work_space(count, tall, width, ordered_keys.shape[1]),
        compiler_params=pltpu.CompilerParams(vmem_limit_bytes=VMEM_BYTES),
        cost_estimate=cost_of(1 + 1.3 * count),
    )(meta, *queries, ordered_keys, wide_values)


def last_kernel(before, places, meta_ref, *refs):
    results, refs = refs[: len(before)], refs[len(before) :]
    q_refs, refs = refs[: len(places)], refs[len(places) :]
    k_ref, wide_ref, _, o_ref, out_buf, sems, out_sems, *work = refs
    known = {
        offset: entry(meta_ref, offset) for its_places in before for offset, _ in its_places
    }

    def each(act):
        for n, (result, its_places) in enumerate(zip(results, before, strict=True)):
            for j, (offset, start) in enumerate(its_places):
                dest = known[offset]
                copy = pltpu.make_async_copy(
                    result.at[j], o_ref.at[half_of(jnp.maximum(dest, 0), start)], sems.at[n, j]
                )
                pl.when(dest >= 0)(getattr(copy, act))

    each("start")
    dests = entries(meta_ref, [offset for offset, _ in places])

    @pl.when(any_of(dests))
    def _():
        starts = [start for _, start in places]
        store = stores(out_buf, o_ref, out_sems)
        attend_pieces(dests, starts, q_refs, k_ref, wide_ref, out_buf, store, *work)

    each("wait")


def attend_last(meta, before, results, pieces, ordered_keys, wide_values, attention):
    queries = [piece[0] for piece in pieces]
    places = [piece[1:] for piece in pieces]
    count, (tall, width) = len(pieces), queries[0].shape
    most = max([1, *(len(its_places) for its_places in before)])
    return pl.pallas_call(
        lambda *refs: last_kernel(before, places, *refs),
        out_shape=jax.ShapeDtypeStruct(attention.shape, attention.dtype),
        in_specs=[VMEM] * (len(results) + count + 3) + [ANY],
        out_specs=ANY,
        input_output_aliases={len(results) + count + 3: 0},
        scratch_shapes=[
            pltpu.VMEM((count, tall, width), attention.dtype),
            pltpu.SemaphoreType.DMA((max(1, len(before)), most)),
            pltpu.SemaphoreType.DMA((count,)),
            *work_space(count, tall, width, ordered_keys.shape[1]),
        ],
        compiler_params=pltpu.CompilerParams(vmem_limit_bytes=VMEM_BYTES),
        cost_estimate=cost_of(2.5),
    )(meta, *results, *queries, ordered_keys, wide_values, attention)


def gathered_kernel(meta_ref, first_ref, later_ref, k_ref, v_ref, o_ref, wide, stacked, mixed, top, bounds):
    at = pl.program_id(1)
    live = meta_ref[0]
    widen(v_ref, wide)

    @pl.when(at == 0)
    def _():
        stack(first_ref, stacked.at[0])

    @pl.when(at > 0)
    def _():
        stack(later_ref.at[0], stacked.at[0])

    def work(shifted):
        args = (at, 0, stacked.at[0], k_ref, wide, mixed, o_ref, bounds)
        if shifted:
            attend_piece_shifted(*args, top)
        else:
            attend_piece(*args)

    @pl.when(at < live)
    def _():
        twice_if_needed(work, lambda: None, bounds)

    @pl.when(at >= live)
    def _():
        o_ref[...] = jnp.zeros_like(o_ref)


def attend_gathered(live, source, first, later, cache_keys, cache_values):
    home_rows, key_width = cache_keys.shape
    width = first.shape[1]
    groups = key_width // HDIM
    part = width // groups
    meta = jnp.concatenate([live.reshape(1), source]).astype(jnp.int32)
    return pl.pallas_call(
        gathered_kernel,
        out_shape=jax.ShapeDtypeStruct((home_rows, width), first.dtype),
        grid_spec=pltpu.PrefetchScalarGridSpec(
            num_scalar_prefetch=1,
            grid=(groups, MAXC),
            in_specs=[
                pl.BlockSpec((SPAN, part), lambda g, m, meta: (0, g)),
                pl.BlockSpec((1, SPAN, part), lambda g, m, meta: (meta[1 + m], 0, g)),
                pl.BlockSpec((home_rows, HDIM), lambda g, m, meta: (0, g)),
                pl.BlockSpec((home_rows, HDIM), lambda g, m, meta: (0, g)),
            ],
            out_specs=pl.BlockSpec((SPAN, part), lambda g, m, meta: (m, g)),
            scratch_shapes=[
                pltpu.VMEM((home_rows, 2 * HDIM), cache_keys.dtype),
                *work_space(1, SPAN, part, HDIM),
            ],
        ),
        compiler_params=pltpu.CompilerParams(vmem_limit_bytes=VMEM_BYTES),
    )(meta, first, later, cache_keys, cache_values)


def gather_all(queries, keys, values, lengths, slot_prompt, slot_span):
    mine = lax.axis_index("replica")
    home_rows, key_width = MAXC * SPAN, keys.shape[1]
    live = lengths[mine]
    spans = jnp.arange(MAXC, dtype=jnp.int32)
    matches = (slot_prompt[None, :, 1] == mine) & (slot_span[None, :, 1] == spans[:, None])
    here = jnp.any(matches, axis=1)
    source = jnp.argmax(matches, axis=1).astype(jnp.int32)
    slots_k = lax.all_gather(keys[SPAN:], "replica")
    slots_v = lax.all_gather(values[SPAN:], "replica")
    slots_q = lax.all_gather(queries[SPAN:], "replica")

    def in_order(first, slots):
        picked = jnp.take(slots, source, axis=0)
        kept = jnp.where(here[:, None, None], picked, jnp.zeros((), slots.dtype))
        return jnp.concatenate([first, kept[1:].reshape(home_rows - SPAN, key_width)], axis=0)

    cache_keys = in_order(keys[:SPAN], slots_k)
    cache_values = in_order(values[:SPAN], slots_v)
    attention = attend_gathered(live, source, queries[:SPAN], slots_q, cache_keys, cache_values)
    return (attention, cache_keys, cache_values)


def per_device(queries, keys, values, lengths, slot_prompt, slot_span):
    replicas = lax.axis_size("replica")
    if replicas != 8:
        return gather_all(queries, keys, values, lengths, slot_prompt, slot_span)
    ring = column_ring(replicas)
    farthest = replicas // 2

    def after(block, *others):
        return lax.optimization_barrier((block, others))[0]

    def joined(both):
        return list(lax.optimization_barrier(tuple(both)))

    def shift(block, step):
        pairs = [(r, ring[(n + step) % replicas]) for n, r in enumerate(ring)]
        return lax.ppermute(block, "replica", pairs)

    def go_on(both):
        return [shift(both[0], 1), shift(both[1], -1)]

    own_kv = pack_kv(keys, values)
    kv = [[own_kv, own_kv]]
    kv.append(go_on(kv[0]))
    own_top, own_bottom = pack_q(after(queries, own_kv))
    first, second = [[own_top, own_bottom]], [[own_bottom, own_top]]
    first.append(joined(go_on(first[0])))
    kv[1] = joined(kv[1])
    kv.append(joined(go_on(kv[1])))
    local = attend_local(lengths, after(queries, kv[1]), keys, values)
    second.append(joined(go_on([after(block, first[1]) for block in second[0]])))
    kv.append(joined(go_on([after(block, local) for block in kv[2]])))
    first.append(joined(go_on([after(block, kv[3]) for block in first[1]])))
    kv.append([shift(kv[3][0], 1)])
    second.append(joined(go_on([after(block, kv[3]) for block in second[1]])))
    meta = places(lengths, slot_prompt, slot_span)
    offsets = [[n, replicas - n] for n in range(1, farthest)]

    def wave(n, which):
        up, down = offsets[n - 1]
        if which is first:
            return [(first[n][0], up, 0), (first[n][1], down, half)]
        return [(second[n][0], up, half), (second[n][1], down, 0)]

    half = SPAN // 2
    cache_keys, cache_values, ordered_keys, wide_values, result, attention = attend_first(
        meta,
        keys,
        values,
        sum(offsets, []) + [farthest],
        sum(kv[1:], []),
        wave(1, first) + wave(1, second),
        local,
    )
    results, before = [result], [wave(1, first) + wave(1, second)]

    def attend(n, which):
        results.append(attend_later(meta, wave(n, which), ordered_keys, wide_values))
        before.append(wave(n, which))

    first.append(joined(go_on(first[2])))
    attend(2, first)
    second.append(joined(go_on([after(block, results[-1]) for block in second[2]])))
    attend(2, second)
    last = [
        (shift(after(first[3][0], results[-1]), 1), farthest, 0),
        (shift(after(first[3][1], results[-1]), -1), farthest, half),
    ]

    def attend_and_store(done, pieces, attention):
        places = [[piece[1:] for piece in its_pieces] for its_pieces in before[done]]
        return attend_last(
            meta, places, results[done], pieces, ordered_keys, wide_values, attention
        )

    attention = attend_and_store(slice(0, 3), wave(3, first), attention)
    attend(3, second)
    results.append(attend_later(meta, last[1:], ordered_keys, wide_values))
    before.append(last[1:])
    attention = attend_and_store(slice(3, 5), last[:1], attention)
    return (attention, cache_keys, cache_values)


def solution(mesh):
    in_specs = (
        P(("group", "replica"), "tensor"),
        P(("group", "replica"), "tensor"),
        P(("group", "replica"), "tensor"),
        P("group"),
        P("group", None),
        P("group", None),
    )
    out_specs = (
        P(("group", "replica"), "tensor"),
        P(("group", "replica"), "tensor"),
        P(("group", "replica"), "tensor"),
    )
    return jax.shard_map(
        per_device, mesh=mesh, in_specs=in_specs, out_specs=out_specs, check_vma=False
    )
```
